256 devices in a mesh: dp: 2 (over x_hi), lat: 8 (over y, core), lon: 16 (over z, x_lo).
Axes of the slice: x: 4 (x_hi: 2, x_lo: 2; x = x_hi * 2 + x_lo), y: 4, z: 8, core: 2. Of those that a mesh axis runs over, the one named last changes fastest.
Arguments:
- state: float32 [2, 256, 512, 384], P('dp', 'lat', 'lon'), may hold values from -6 to 6
- cotangent: float32 [2, 256, 512, 384], P('dp', 'lat', 'lon'), may hold values from -6 to 6
- counts: int32 [32, 64], P('lat', 'lon'), may hold values from 0 to 64, as said below
- dw_kernel: float32 [1, 49, 384], replicated, may hold values from -0.875 to 0.875
- dw_bias: float32 [1, 384], replicated, may hold values from -3 to 3
- norm_gain: float32 [1, 384], replicated, may hold values from 0.1 to 1.9
- norm_bias: float32 [1, 384], replicated, may hold values from -3 to 3
- w_expand: bfloat16 [1, 1536, 384], replicated, may hold values from -0.3125 to 0.3125
- b_expand: float32 [1, 1536], replicated, may hold values from -3 to 3
- w_reduce: bfloat16 [1, 1536, 384], replicated, may hold values from -0.15625 to 0.15625
Outputs:
- grad_state: float32 [2, 256, 512, 384], P('dp', 'lat', 'lon')
- grad_expand: float32 [1, 1536, 384], P(None, ('dp', 'lat', 'lon'))
- grad_reduce: float32 [1, 1536, 384], P(None, ('dp', 'lat', 'lon'))
The draws below stay inside these ranges and needn't reach their ends.
Inputs may be any that keep to these rules, and one draw needn't show every extreme that they name: `counts`: A tile with count 0 is land. In the tiles of the devices of one lat index (4 x 64 tiles) at most 192 have a positive count, and some such band reaches that number.
All inputs are finite; a program needn't handle non-finite values.
Results may differ from the reference program's by a relative error of at most 0.0056.
Values may be sent and summed in bfloat16 or wider, within the bound.
No kernel may reach another device: no remote copies, remote signals or barrier semaphores. Data moves between devices by JAX's collectives and lax.ppermute only.
A program may use at most 128 MiB of HBM per device.

```python
import math
import jax
import jax.numpy as jnp
from jax import lax

C = 384
H = 1536
TS = 8
TA = 4
TO = 4
BLOCKS = 1
STATES = 2
NLAT = 256
NLON = 512
GA = 32
GO = 64
CAP = 12


def draw_counts(key, part):
    key = jax.random.fold_in(key, 7)
    subkeys = jax.random.split(key, 6)
    band_count = GA // TA
    band_tiles = TA * GO
    lane_total = GO // TO
    continent = jax.random.randint(subkeys[0], (lane_total,), 0, 4)
    lon_level = jnp.repeat(continent, TO)
    jitter = jax.random.randint(subkeys[1], (GA, GO), 0, 1024)
    position = jnp.arange(GA * GO, dtype=jnp.int32).reshape(GA, GO)
    land_score = (jitter + 700 * lon_level[None, :]) * (GA * GO) + position
    banded = land_score.reshape(band_count, band_tiles)
    ordering = jnp.argsort(banded, axis=1)
    band_rank = jnp.argsort(ordering, axis=1)
    chosen = jax.random.randint(subkeys[2], (), 0, band_count)
    deficit = jax.random.randint(subkeys[3], (band_count,), 0, 2 * lane_total + 1)
    deficit = jnp.where(jnp.arange(band_count) == chosen, 0, deficit)
    ocean_limit = CAP * lane_total - deficit
    oceanic = band_rank < ocean_limit[:, None]
    coastal = jax.random.randint(subkeys[4], (band_count, band_tiles), 1, TS * TS + 1)
    interior = jax.random.randint(subkeys[5], (band_count, band_tiles), 0, 4) > 0
    filled = jnp.where(interior, TS * TS, coastal)
    return jnp.where(oceanic, filled, 0).astype(jnp.int32).reshape(GA, GO)


def block_scale(own_key, dims, shards, least, top_value):
    def one(dim, blocks):
        draws = jax.random.uniform(jax.random.fold_in(jax.random.fold_in(own_key, 6), dim), (blocks,), jnp.float32, least / len(shards), top_value / len(shards))
        return jnp.repeat(jnp.exp(draws), dims[dim] // blocks).reshape((-1,) + (1,) * (len(dims) - dim - 1))

    factor_of = one(*shards[0])
    for cut in shards[1:]:
        factor_of = factor_of * one(*cut)
    return factor_of


def noise(stream_key, shape, deviation, most, pieces=(), kind=jnp.bfloat16):
    drawn = deviation * jax.random.normal(stream_key, shape, jnp.float32)
    if pieces:
        drawn = drawn * block_scale(stream_key, shape, pieces, -0.22, 0.18)
    return jnp.clip(drawn, -most, most).astype(kind)


def setup_inputs(seed: int = 0) -> dict:
    key_list = jax.random.split(jax.random.key(seed), 11)
    state = noise(key_list[0], (STATES, NLAT, NLON, C), 1.0, 6.0, ((0, 2), (1, 8), (2, 16)), jnp.float32)
    cotangent = noise(key_list[1], (STATES, NLAT, NLON, C), 1.0, 6.0, ((0, 2), (1, 8), (2, 16)), jnp.float32)
    counts = draw_counts(jax.random.fold_in(key_list[10], 71), 0)
    dw_kernel = noise(key_list[3], (BLOCKS, 49, C), 49 ** -0.5, 0.875, (), jnp.float32)
    dw_bias = noise(key_list[4], (BLOCKS, C), 0.5, 3.0, (), jnp.float32)
    norm_gain = jnp.clip(1.0 + 0.18 * jax.random.normal(key_list[5], (BLOCKS, C), jnp.float32), 0.1, 1.9)
    norm_bias = noise(key_list[6], (BLOCKS, C), 0.5, 3.0, (), jnp.float32)
    w_expand = noise(key_list[7], (BLOCKS, H, C), C ** -0.5, 0.3125)
    b_expand = noise(key_list[8], (BLOCKS, H), 0.5, 3.0, (), jnp.float32)
    w_reduce = noise(key_list[9], (BLOCKS, H, C), H ** -0.5, 0.15625)
    return dict(state=state, cotangent=cotangent, counts=counts, dw_kernel=dw_kernel, dw_bias=dw_bias, norm_gain=norm_gain, norm_bias=norm_bias, w_expand=w_expand, b_expand=b_expand, w_reduce=w_reduce)


norm_eps = 1e-06
root_half = 0.7071067811865476
inv_root_two_pi = 0.3989422804014327

def cell_mask(counts, tile_side):
    per_cell = jnp.repeat(jnp.repeat(counts, tile_side, axis=0), tile_side, axis=1)
    row_place = lax.broadcasted_iota(jnp.int32, per_cell.shape, 0) % tile_side
    col_place = lax.broadcasted_iota(jnp.int32, per_cell.shape, 1) % tile_side
    return (row_place * tile_side + col_place < per_cell).astype(jnp.float32)

def rim_pad(grid):
    wrapped = jnp.concatenate([grid[:, :, -3:], grid, grid[:, :, :3]], axis=2)
    return jnp.pad(wrapped, ((0, 0), (3, 3), (0, 0), (0, 0)))

def conv_apply(padded, kernel, flipped):
    row_count = padded.shape[-3] - 6
    col_count = padded.shape[-2] - 6
    summed = jnp.zeros(padded.shape[:-3] + (row_count, col_count, padded.shape[-1]), jnp.float32)
    for row_off in range(7):
        for col_off in range(7):
            row_start = 6 - row_off if flipped else row_off
            col_start = 6 - col_off if flipped else col_off
            window = padded[..., row_start:row_start + row_count, col_start:col_start + col_count, :]
            summed = summed + kernel[7 * row_off + col_off] * window
    return summed

def layer_stats(mixed_conv):
    mean_value = lax.optimization_barrier(jnp.mean(mixed_conv, axis=-1, keepdims=True))
    centred = mixed_conv - mean_value
    inv_spread = lax.rsqrt(lax.optimization_barrier(jnp.mean(centred * centred, axis=-1, keepdims=True)) + norm_eps)
    return (centred * inv_spread, inv_spread)

def norm_backward(grad_normed, unit_conv, inv_spread, gain):
    grad_unit = grad_normed.astype(jnp.float32) * gain
    mean_grad = lax.optimization_barrier(jnp.mean(grad_unit, axis=-1, keepdims=True))
    mean_cross = lax.optimization_barrier(jnp.mean(grad_unit * unit_conv, axis=-1, keepdims=True))
    return (grad_unit - mean_grad - unit_conv * mean_cross) * inv_spread

def gelu_value(preact):
    return 0.5 * preact * (1.0 + lax.erf(preact * root_half))

def gelu_slope(preact):
    return 0.5 * (1.0 + lax.erf(preact * root_half)) + preact * inv_root_two_pi * jnp.exp(-0.5 * preact * preact)

def mlp_forward(normed_rows, expand_weight, expand_bias, reduce_weight):
    preact = jnp.dot(normed_rows, expand_weight.T, preferred_element_type=jnp.float32) + expand_bias
    hidden = gelu_value(preact).astype(jnp.bfloat16)
    branch = jnp.dot(hidden, reduce_weight, preferred_element_type=jnp.float32).astype(jnp.bfloat16)
    return (preact, hidden, branch)

def mlp_backward(normed_rows, preact, hidden, grad_branch, expand_weight, reduce_weight):
    grad_hidden = jnp.dot(grad_branch, reduce_weight.T, preferred_element_type=jnp.float32)
    grad_pre = (grad_hidden * gelu_slope(preact)).astype(jnp.bfloat16)
    grad_normed = jnp.dot(grad_pre, expand_weight, preferred_element_type=jnp.float32).astype(jnp.bfloat16)
    grad_e = jnp.dot(grad_pre.T, normed_rows, preferred_element_type=jnp.float32)
    grad_r = jnp.dot(hidden.T, grad_branch, preferred_element_type=jnp.float32)
    return (grad_normed, grad_e, grad_r)

def reference(state, cotangent, counts, dw_kernel, dw_bias, norm_gain, norm_bias, w_expand, b_expand, w_reduce):
    wet_cells = cell_mask(counts, TS)[None, :, :, None]
    current = state
    stored = []
    for layer_index in range(BLOCKS):
        stored.append(current)
        mixed_conv = conv_apply(rim_pad(current), dw_kernel[layer_index], False) + dw_bias[layer_index]
        unit_conv, inv_spread = layer_stats(mixed_conv)
        normed = (unit_conv * norm_gain[layer_index] + norm_bias[layer_index]).astype(jnp.bfloat16)
        expand_weight, expand_bias = (w_expand[layer_index], b_expand[layer_index])
        reduce_weight = w_reduce[layer_index]

        def forward_rows(rows_in):
            return mlp_forward(rows_in, expand_weight, expand_bias, reduce_weight)[2]
        branch = lax.map(forward_rows, normed.reshape(STATES * NLAT, NLON, C)).reshape(current.shape)
        current = (current + branch.astype(jnp.float32)) * wet_cells
    gradient = cotangent
    grads_e = [None] * BLOCKS
    grads_r = [None] * BLOCKS
    for layer_index in reversed(range(BLOCKS)):
        entering = stored[layer_index]
        mixed_conv = conv_apply(rim_pad(entering), dw_kernel[layer_index], False) + dw_bias[layer_index]
        unit_conv, inv_spread = layer_stats(mixed_conv)
        normed = (unit_conv * norm_gain[layer_index] + norm_bias[layer_index]).astype(jnp.bfloat16)
        masked = gradient * wet_cells
        grad_branch = masked.astype(jnp.bfloat16)
        expand_weight, expand_bias = (w_expand[layer_index], b_expand[layer_index])
        reduce_weight = w_reduce[layer_index]

        def backward_rows(running, row_pair):
            rows_in, grad_rows = row_pair
            preact, hidden, unused = mlp_forward(rows_in, expand_weight, expand_bias, reduce_weight)
            grad_normed, grad_e, grad_r = mlp_backward(rows_in, preact, hidden, grad_rows, expand_weight, reduce_weight)
            return ((running[0] + grad_e, running[1] + grad_r), grad_normed)
        zero_grad = jnp.zeros((H, C), jnp.float32)
        sums, grad_normed = lax.scan(backward_rows, (zero_grad, zero_grad), (normed.reshape(STATES * NLAT, NLON, C), grad_branch.reshape(STATES * NLAT, NLON, C)))
        grad_conv = norm_backward(grad_normed.reshape(entering.shape), unit_conv, inv_spread, norm_gain[layer_index])
        gradient = masked + conv_apply(rim_pad(grad_conv), dw_kernel[layer_index], True)
        grads_e[layer_index] = sums[0]
        grads_r[layer_index] = sums[1]
    grad_scale = 1.0 / math.sqrt(STATES * NLAT * NLON)
    return (gradient, jnp.stack(grads_e) * grad_scale, jnp.stack(grads_r) * grad_scale)
```

```python
import itertools
import math

import jax
import jax.numpy as jnp
from jax import lax
from jax.sharding import PartitionSpec as P

norm_eps = 1e-06
root_half = 0.7071067811865476
inv_root_two_pi = 0.3989422804014327


def with_halo(cells, sides, width, closed):
    for axis, dim in sides:
        count = lax.axis_size(axis)
        ends = count if closed else count - 1
        head = lax.slice_in_dim(cells, 0, width, axis=dim)
        tail = lax.slice_in_dim(cells, cells.shape[dim] - width, cells.shape[dim], axis=dim)
        cells = jnp.concatenate(
            [
                lax.ppermute(tail, axis, [(i, (i + 1) % count) for i in range(ends)]),
                cells,
                lax.ppermute(head, axis, [((i + 1) % count, i) for i in range(ends)]),
            ],
            axis=dim,
        )
    return cells


def cell_mask(counts, tile_side):
    tile_rows, tile_cols = counts.shape
    shape = (tile_rows, tile_side, tile_cols, tile_side)
    row_place = lax.broadcasted_iota(jnp.int32, shape, 1)
    col_place = lax.broadcasted_iota(jnp.int32, shape, 3)
    wet = (row_place * tile_side + col_place < counts[:, None, :, None]).astype(jnp.float32)
    return wet.reshape(tile_rows * tile_side, tile_cols * tile_side)


def pad_rims(grid):
    beside_all = with_halo(grid, (("lon", 1),), 3, True)
    return with_halo(beside_all, (("lat", 0),), 3, False)


def conv_apply(padded, kernel, flipped):
    row_count = padded.shape[-3] - 6
    col_count = padded.shape[-2] - 6
    summed = jnp.zeros(padded.shape[:-3] + (row_count, col_count, padded.shape[-1]), jnp.float32)
    for row_off in range(7):
        for col_off in range(7):
            row_start = 6 - row_off if flipped else row_off
            col_start = 6 - col_off if flipped else col_off
            window = padded[
                ..., row_start : row_start + row_count, col_start : col_start + col_count, :
            ]
            summed = summed + kernel[7 * row_off + col_off] * window
    return summed


def layer_stats(mixed_conv):
    mean_value = jnp.mean(mixed_conv, axis=-1, keepdims=True)
    centred = mixed_conv - mean_value
    inv_spread = lax.rsqrt(jnp.mean(centred * centred, axis=-1, keepdims=True) + norm_eps)
    return (centred * inv_spread, inv_spread)


def norm_backward(grad_normed, unit_conv, inv_spread, gain):
    grad_unit = grad_normed.astype(jnp.float32) * gain
    mean_grad = jnp.mean(grad_unit, axis=-1, keepdims=True)
    mean_cross = jnp.mean(grad_unit * unit_conv, axis=-1, keepdims=True)
    return (grad_unit - mean_grad - unit_conv * mean_cross) * inv_spread


def gelu_value(preact):
    return 0.5 * preact * (1.0 + lax.erf(preact * root_half))


def gelu_slope(preact):
    return 0.5 * (1.0 + lax.erf(preact * root_half)) + preact * inv_root_two_pi * jnp.exp(
        -0.5 * preact * preact
    )


def mlp_forward(normed_rows, expand_weight, expand_bias, reduce_weight):
    preact = jnp.dot(normed_rows, expand_weight.T, preferred_element_type=jnp.float32) + expand_bias
    hidden = gelu_value(preact).astype(jnp.bfloat16)
    branch = jnp.dot(hidden, reduce_weight, preferred_element_type=jnp.float32).astype(jnp.bfloat16)
    return (preact, hidden, branch)


def mlp_backward(normed_rows, preact, hidden, grad_branch, expand_weight, reduce_weight):
    grad_hidden = jnp.dot(grad_branch, reduce_weight.T, preferred_element_type=jnp.float32)
    grad_pre = (grad_hidden * gelu_slope(preact)).astype(jnp.bfloat16)
    grad_normed = jnp.dot(grad_pre, expand_weight, preferred_element_type=jnp.float32).astype(
        jnp.bfloat16
    )
    grad_e = jnp.dot(grad_pre.T, normed_rows, preferred_element_type=jnp.float32)
    grad_r = jnp.dot(hidden.T, grad_branch, preferred_element_type=jnp.float32)
    return (grad_normed, grad_e, grad_r)


every_axis = ("dp", "lat", "lon")


def device_pairs(move):
    def flat(hi, y, core, z, lo):
        return (hi * 8 + y * 2 + core) * 16 + z * 2 + lo

    found = []
    for hi, y, core, z, lo in itertools.product(range(2), range(4), range(2), range(8), range(2)):
        found.append((flat(hi, y, core, z, lo), flat(*move(hi, y, core, z, lo))))
    return found


def plane_pairs(step, first):
    def move(hi, y, core, z, lo):
        if (core == 0) == first:
            return (hi, (y + step) % 4, core, z, lo)
        x = (2 * hi + lo + step) % 4
        return (x // 2, y, core, z, x % 2)

    return device_pairs(move)


def scatter_direct(rows, place, pairs_of):
    size = rows.shape[0] // 4
    narrow = rows.astype(jnp.bfloat16)
    total = lax.dynamic_slice_in_dim(rows, place * size, size, 0)
    arrived = [
        lax.ppermute(
            lax.dynamic_slice_in_dim(narrow, ((place + step) % 4) * size, size, 0),
            every_axis,
            pairs_of(step),
        )
        for step in range(1, 4)
    ]
    for part in arrived:
        total = total + part.astype(jnp.float32)
    return total


def scatter_halving(rows, z):
    for bit in (4, 2, 1):
        size = rows.shape[0] // 2
        upper = (z // bit) % 2
        arrived = lax.ppermute(
            lax.dynamic_slice_in_dim(rows, (1 - upper) * size, size, 0),
            every_axis,
            device_pairs(lambda hi, y, core, z, lo, bit=bit: (hi, y, core, z ^ bit, lo)),
        )
        rows = lax.dynamic_slice_in_dim(rows, upper * size, size, 0) + arrived
    return rows


def scatter_rows(mine, arrived):
    lat, lon = lax.axis_index("lat"), lax.axis_index("lon")
    y, core, z, lo = lat // 2, lat % 2, lon // 2, lon % 2
    x = 2 * lax.axis_index("dp") + lo
    rows = mine + arrived.astype(jnp.float32)
    rows = scatter_direct(rows, jnp.where(core == 0, y, x), lambda step: plane_pairs(step, True))
    rows = scatter_direct(rows, jnp.where(core == 0, x, y), lambda step: plane_pairs(step, False))
    return scatter_halving(rows, z)


def arrange_rows(rows):
    width = rows.shape[1]
    parts = rows.reshape(2, 4, 2, 8, 2, -1, width)
    first = parts[:, :, 0].transpose(1, 0, 3, 2, 4, 5)
    second = parts[:, :, 1].transpose(0, 3, 1, 2, 4, 5)
    return jnp.concatenate([first.reshape(-1, width), second.reshape(-1, width)])


def local(
    state, cotangent, counts, dw_kernel, dw_bias, norm_gain, norm_bias, w_expand, b_expand, w_reduce
):
    current = state[0]
    row_count, col_count, channels = current.shape
    tile_side = row_count // counts.shape[0]
    wet_cells = cell_mask(counts, tile_side)[:, :, None]
    expand_weight = arrange_rows(w_expand[0])
    reduce_weight = arrange_rows(w_reduce[0])
    expand_bias = arrange_rows(b_expand[0][:, None])[:, 0]
    masked = cotangent[0] * wet_cells
    grad_rows = masked.astype(jnp.bfloat16).reshape(-1, channels)
    mixed_conv = conv_apply(pad_rims(current), dw_kernel[0], False) + dw_bias[0]
    unit_conv, inv_spread = layer_stats(mixed_conv)
    normed = (unit_conv * norm_gain[0] + norm_bias[0]).astype(jnp.bfloat16)
    work_rows = normed.reshape(-1, channels)
    preact = jnp.dot(work_rows, expand_weight.T, preferred_element_type=jnp.float32) + expand_bias
    hidden = gelu_value(preact).astype(jnp.bfloat16)
    grad_hidden = jnp.dot(grad_rows, reduce_weight.T, preferred_element_type=jnp.float32)
    grad_pre = (grad_hidden * gelu_slope(preact)).astype(jnp.bfloat16)
    grad_e = jnp.dot(grad_pre.T, work_rows, preferred_element_type=jnp.float32)
    grad_r = jnp.dot(hidden.T, grad_rows, preferred_element_type=jnp.float32)
    grads = jnp.concatenate([grad_e, grad_r], axis=1)
    core = lax.axis_index("lat") % 2
    half = grads.shape[0] // 2
    send = lax.dynamic_slice_in_dim(grads, (1 - core) * half, half, 0).astype(jnp.bfloat16)
    arrived = lax.ppermute(send, "lat", [(i, i ^ 1) for i in range(8)])
    mine = lax.dynamic_slice_in_dim(grads, core * half, half, 0)
    grad_normed = jnp.dot(grad_pre, expand_weight, preferred_element_type=jnp.float32).astype(
        jnp.bfloat16
    )
    normed_grid = grad_normed.reshape(row_count, col_count, channels)
    grad_conv = norm_backward(normed_grid, unit_conv, inv_spread, norm_gain[0])
    gradient = masked + conv_apply(pad_rims(grad_conv), dw_kernel[0], True)
    kept = scatter_rows(mine, arrived)
    cell_total = (
        lax.axis_size("dp") * lax.axis_size("lat") * lax.axis_size("lon") * row_count * col_count
    )
    kept = kept * (1.0 / math.sqrt(cell_total))
    return (gradient[None], kept[None, :, :channels], kept[None, :, channels:])


def solution(mesh):
    in_specs = (
        P("dp", "lat", "lon", None),
        P("dp", "lat", "lon", None),
        P("lat", "lon"),
        P(),
        P(),
        P(),
        P(),
        P(),
        P(),
        P(),
    )
    out_specs = (
        P("dp", "lat", "lon", None),
        P(None, ("dp", "lat", "lon"), None),
        P(None, ("dp", "lat", "lon"), None),
    )
    return jax.shard_map(local, mesh=mesh, in_specs=in_specs, out_specs=out_specs, check_vma=False)
```

```python
import functools
import itertools
import math

import jax
import jax.numpy as jnp
from jax import lax
from jax.experimental import pallas as pl
from jax.experimental.pallas import tpu as pltpu
from jax.sharding import PartitionSpec as P

norm_eps = 1e-06
inv_root_two_pi = 0.3989422804014327
side = 32
reach = 3
lanes = 128
f32 = jnp.float32
bf16 = jnp.bfloat16
whole = pl.BlockSpec(memory_space=pltpu.VMEM)


def params(mib):
    return pltpu.CompilerParams(vmem_limit_bytes=mib * 1024 * 1024)


def cost(microseconds):
    return pl.CostEstimate(
        flops=int(microseconds * 1.15e9), bytes_accessed=2**20, transcendentals=0
    )


def tap_row(kernel_ref, flipped, p, q, cols):
    index = 7 * p + q
    if flipped:
        index = 48 - index
    return kernel_ref[index : index + 1, cols]


def shift_cols(rows, offset):
    if offset == 0:
        return rows
    count = rows.shape[0]
    turned = pltpu.roll(rows, (-offset) % count, 0)
    place = lax.broadcasted_iota(jnp.int32, (8, rows.shape[1]), 0)
    if offset > 0:
        last = jnp.where(place < 8 - offset, turned[count - 8 :], 0.0)
        return jnp.concatenate([turned[: count - 8], last], axis=0)
    first = jnp.where(place >= -offset, turned[:8], 0.0)
    return jnp.concatenate([first, turned[8:]], axis=0)


def inner_conv_body(flipped, cells_ref, kernel_ref, out_ref, padded):
    edge = reach * side
    total = side * side
    padded[0:edge] = jnp.zeros((edge, lanes), f32)
    padded[edge + total : 2 * edge + total] = jnp.zeros((edge, lanes), f32)
    padded[edge : edge + total] = cells_ref[...]

    def one_row(i, carry):
        base = pl.multiple_of(i * side, side)
        rows = [padded[pl.ds(base + p * side, side), :] for p in range(7)]
        result = None
        for q in range(7):
            summed = None
            for p in range(7):
                term = tap_row(kernel_ref, flipped, p, q, slice(None)) * rows[p]
                summed = term if summed is None else summed + term
            summed = shift_cols(summed, q - reach)
            result = summed if result is None else result + summed
        out_ref[pl.ds(base, side), :] = result
        return carry

    lax.fori_loop(0, side, one_row, 0)


def inner_conv(cells, kernel, flipped):
    total, channels = cells.shape
    block = pl.BlockSpec((total, lanes), lambda c: (0, c))
    return pl.pallas_call(
        functools.partial(inner_conv_body, flipped),
        out_shape=jax.ShapeDtypeStruct((total, channels), f32),
        grid=(channels // lanes,),
        in_specs=[block, pl.BlockSpec((49, lanes), lambda c: (0, c))],
        out_specs=block,
        scratch_shapes=[pltpu.VMEM((total + 2 * reach * side, lanes), f32)],
        compiler_params=params(16),
        cost_estimate=cost(7.8),
        name="inner_conv",
    )(cells, kernel)


def side_cols_body(low_ref, high_ref, first_ref, last_ref):
    for j in range(reach):
        first_ref[j] = low_ref[:, j, :].astype(bf16)
        last_ref[j] = high_ref[:, 8 - reach + j, :].astype(bf16)


def side_cols(cells):
    channels = cells.shape[1]
    grid3 = cells.reshape(side, side, channels)
    shape = jax.ShapeDtypeStruct((reach, side, channels), bf16)
    return pl.pallas_call(
        side_cols_body,
        out_shape=(shape, shape),
        grid=(1,),
        in_specs=[
            pl.BlockSpec((side, 8, channels), lambda g: (0, 0, 0)),
            pl.BlockSpec((side, 8, channels), lambda g: (0, side // 8 - 1, 0)),
        ],
        out_specs=[pl.BlockSpec((reach, side, channels), lambda g: (0, 0, 0))] * 2,
        compiler_params=params(16),
        cost_estimate=cost(1.0),
        name="side_cols",
    )(grid3, grid3)


def side_rows_body(top_ref, bottom_ref, left_ref, right_ref, up_ref, down_ref):
    channels = top_ref.shape[1]
    place = lax.broadcasted_iota(jnp.int32, (8, channels), 0)
    blank = jnp.zeros((8, channels), f32)
    left = [left_ref[h].astype(f32) for h in range(reach)]
    right = [right_ref[h].astype(f32) for h in range(reach)]
    for r in range(reach):
        for source, row, ref in ((top_ref, r, up_ref), (bottom_ref, side - reach + r, down_ref)):
            corner = blank
            for h in range(reach):
                corner = jnp.where(place == h, right[h][row : row + 1], corner)
                corner = jnp.where(place == 8 - reach + h, left[h][row : row + 1], corner)
            body = source[r * side : (r + 1) * side]
            ref[r] = jnp.concatenate([body, corner, blank], axis=0).astype(bf16)


def side_rows(cells, left, right):
    channels = cells.shape[1]
    shape = jax.ShapeDtypeStruct((reach, side + 16, channels), bf16)
    edge = reach * side
    return pl.pallas_call(
        side_rows_body,
        out_shape=(shape, shape),
        in_specs=[whole] * 4,
        out_specs=[whole] * 2,
        compiler_params=params(16),
        cost_estimate=cost(0.8),
        name="side_rows",
    )(cells[:edge], cells[-edge:], left, right)


def add_edges(flipped, kernel_ref, left_ref, right_ref, top_ref, bottom_ref, rows_sum, cols_sum):
    channels = kernel_ref.shape[1]
    for c in range(channels // lanes):
        cols = slice(c * lanes, (c + 1) * lanes)
        for low, ref in ((True, top_ref), (False, bottom_ref)):
            beyond = [ref[h, :, cols].astype(f32)[: side + 8] for h in range(reach)]
            for r in range(reach):
                result = None
                steps = [(h, h - r) for h in range(r, reach)] if low else [
                    (h, 6 + h - r) for h in range(0, r + 1)
                ]
                for q in range(7):
                    summed = None
                    for h, p in steps:
                        term = tap_row(kernel_ref, flipped, p, q, cols) * beyond[h]
                        summed = term if summed is None else summed + term
                    summed = pltpu.roll(summed, (reach - q) % (side + 8), 0) if q != reach else summed
                    result = summed if result is None else result + summed
                rows_sum[r if low else reach + r, :, cols] = result[:side]
        for low, ref in ((True, left_ref), (False, right_ref)):
            beyond = [ref[h, :, cols].astype(f32) for h in range(reach)]
            for r in range(reach):
                steps = [(h, h - r) for h in range(r, reach)] if low else [
                    (h, 6 + h - r) for h in range(0, r + 1)
                ]
                result = None
                for p in range(7):
                    summed = None
                    for h, q in steps:
                        term = tap_row(kernel_ref, flipped, p, q, cols) * beyond[h]
                        summed = term if summed is None else summed + term
                    summed = shift_cols(summed, p - reach)
                    result = summed if result is None else result + summed
                cols_sum[r if low else reach + r, :, cols] = result


def edged_row(i, conv_row, cols_sum):
    channels = conv_row.shape[1]
    place = lax.broadcasted_iota(jnp.int32, (8, channels), 0)
    first, last = conv_row[:8], conv_row[side - 8 :]
    for r in range(reach):
        first = first + jnp.where(place == r, cols_sum[r, pl.ds(i, 1), :], 0.0)
        last = last + jnp.where(place == 8 - reach + r, cols_sum[reach + r, pl.ds(i, 1), :], 0.0)
    return jnp.concatenate([first, conv_row[8 : side - 8], last], axis=0)


def each_row(step):
    def low(i, carry):
        step(i, i)
        return carry

    def middle(i, carry):
        step(i, None)
        return carry

    def high(i, carry):
        step(i, i - (side - 2 * reach))
        return carry

    lax.fori_loop(0, reach, low, 0)
    lax.fori_loop(reach, side - reach, middle, 0, unroll=2)
    lax.fori_loop(side - reach, side, high, 0)


def normalise_body(
    conv_ref, kernel_ref, left_ref, right_ref, top_ref, bottom_ref, bias_ref, gain_ref, shift_ref,
    unit_ref, spread_ref, normed_ref, flipped_ref, rows_sum, cols_sum,
):
    channels = conv_ref.shape[1]
    add_edges(False, kernel_ref, left_ref, right_ref, top_ref, bottom_ref, rows_sum, cols_sum)
    share = 1.0 / channels

    def step(i, outer):
        at = pl.ds(pl.multiple_of(i * side, side), side)
        value = edged_row(i, conv_ref[at, :], cols_sum)
        if outer is not None:
            value = value + rows_sum[outer]
        value = value + bias_ref[...]
        mean = jnp.sum(value, axis=1, keepdims=True) * share
        centred = value - mean
        spread = lax.rsqrt(jnp.sum(centred * centred, axis=1, keepdims=True) * share + norm_eps)
        unit = centred * spread
        unit_ref[at, :] = unit
        spread_ref[at, :] = jnp.broadcast_to(spread, (side, lanes))
        normed_ref[at, :] = (unit * gain_ref[...] + shift_ref[...]).astype(bf16)

    each_row(step)
    turn(normed_ref, flipped_ref)


def turn(source_ref, target_ref):
    for b in range(source_ref.shape[0] // 256):
        at = slice(b * 256, (b + 1) * 256)
        target_ref[:, at] = source_ref[at, :].T


def normalise(conv, kernel, left, right, top, bottom, bias, gain, shift):
    total, channels = conv.shape
    return pl.pallas_call(
        normalise_body,
        out_shape=(
            jax.ShapeDtypeStruct((total, channels), f32),
            jax.ShapeDtypeStruct((total, lanes), f32),
            jax.ShapeDtypeStruct((total, channels), bf16),
            jax.ShapeDtypeStruct((channels, total), bf16),
        ),
        in_specs=[whole] * 9,
        out_specs=[whole] * 4,
        scratch_shapes=[pltpu.VMEM((2 * reach, side, channels), f32)] * 2,
        compiler_params=params(32),
        cost_estimate=cost(6.2),
        name="normalise",
    )(conv, kernel, left, right, top, bottom, bias, gain, shift)


def wet_row(i, counts_ref):
    place = lax.broadcasted_iota(jnp.int32, (8, lanes), 0) + (i % 8) * 8
    pieces = []
    for t in range(side // 8):
        pieces.append(place < counts_ref[i // 8, t])
    return pieces


def masked_row(i, grad_row, counts_ref):
    channels = grad_row.shape[1]
    parts = []
    for t, wet in enumerate(wet_row(i, counts_ref)):
        piece = grad_row[t * 8 : (t + 1) * 8]
        parts.append(
            jnp.concatenate(
                [
                    jnp.where(wet, piece[:, c * lanes : (c + 1) * lanes], 0.0)
                    for c in range(channels // lanes)
                ],
                axis=1,
            )
        )
    return jnp.concatenate(parts, axis=0)


def mask_rows_body(counts_ref, grad_ref, rows_ref, flipped_ref):
    def step(i, carry):
        at = pl.ds(pl.multiple_of(i * side, side), side)
        rows_ref[at, :] = masked_row(i, grad_ref[at, :], counts_ref).astype(bf16)
        return carry

    lax.fori_loop(0, side, step, 0)
    turn(rows_ref, flipped_ref)


def mask_rows(counts, grad):
    total, channels = grad.shape
    return pl.pallas_call(
        mask_rows_body,
        out_shape=(
            jax.ShapeDtypeStruct((total, channels), bf16),
            jax.ShapeDtypeStruct((channels, total), bf16),
        ),
        in_specs=[pl.BlockSpec(memory_space=pltpu.SMEM), whole],
        out_specs=[whole] * 2,
        compiler_params=params(16),
        cost_estimate=cost(2.2),
        name="mask_rows",
    )(counts, grad)


def arrange_body(expand_ref, reduce_ref, bias_ref, expand_out, reduce_out, turned_out, bias_out):
    unit_row = lax.broadcasted_iota(jnp.int32, (48, 96), 0)
    unit_col = lax.broadcasted_iota(jnp.int32, (48, 96), 1)
    picks = [unit_col == (unit_row // 6) * 12 + lo * 6 + unit_row % 6 for lo in range(2)]
    chosen = [pick.astype(f32).astype(bf16) for pick in picks]
    for hi, y, core in itertools.product(range(2), range(4), range(2)):
        unit = (hi * 4 + y) * 2 + core
        at = slice(unit * 96, (unit + 1) * 96)
        expand, reduce = expand_ref[at, :], reduce_ref[at, :]
        bias = bias_ref[unit : unit + 1, :]
        for lo in range(2):
            x = 2 * hi + lo
            place = core * 16 + (y * 4 + x if core == 0 else x * 4 + y)
            to = slice(place * 48, (place + 1) * 48)
            expand_out[to, :] = jnp.dot(chosen[lo], expand, preferred_element_type=f32).astype(bf16)
            reduce_out[to, :] = jnp.dot(chosen[lo], reduce, preferred_element_type=f32).astype(bf16)
            column = jnp.sum(jnp.where(picks[lo], bias, 0.0), axis=1, keepdims=True)
            bias_out[to, :] = jnp.broadcast_to(column, (48, lanes))
    turn(expand_out, turned_out)


def arrange(expand, reduce, bias):
    units, channels = expand.shape
    shape = jax.ShapeDtypeStruct((units, channels), bf16)
    return pl.pallas_call(
        arrange_body,
        out_shape=(
            shape,
            shape,
            jax.ShapeDtypeStruct((channels, units), bf16),
            jax.ShapeDtypeStruct((units, lanes), f32),
        ),
        in_specs=[whole] * 3,
        out_specs=[whole] * 4,
        compiler_params=params(32),
        cost_estimate=cost(3.0),
        name="arrange",
    )(expand, reduce, bias.reshape(16, 96))


tail_slope = 0.3275911 * 0.7071067811865476
tail_terms = [
    0.5 * a for a in (0.254829592, -0.284496736, 1.421413741, -1.453152027, 1.061405429)
]
exp_scale = -0.5 * 1.4426950408889634


def gelu_pair(v):
    d = 1.0 + tail_slope * jnp.abs(v)
    t = pl.reciprocal(d, approx=True)
    t = t * (2.0 - d * t)
    poly = tail_terms[4]
    for a in reversed(tail_terms[:4]):
        poly = poly * t + a
    bell = jnp.exp2(v * v * exp_scale)
    tail = poly * t * bell
    below = jnp.where(v >= 0.0, 1.0 - tail, tail)
    return v * below, below + v * bell * inv_root_two_pi


def hidden_body(
    core_ref, normed_ref, normed_t_ref, grad_ref, grad_t_ref, expand_ref, reduce_ref, bias_ref,
    sums_ref, grad_pre_ref,
):
    channels = normed_ref.shape[1]
    total = normed_ref.shape[0]
    preact = jnp.dot(expand_ref[...], normed_t_ref[...], preferred_element_type=f32)
    grad_hidden = jnp.dot(reduce_ref[...], grad_t_ref[...], preferred_element_type=f32)
    bias = jnp.concatenate([bias_ref[...]] * (total // lanes), axis=1)
    value, slope = gelu_pair(preact + bias)
    hidden = value.astype(bf16)
    grad_pre = (grad_hidden * slope).astype(bf16)
    grad_pre_ref[...] = grad_pre
    sums_ref[:, :channels] = jnp.dot(grad_pre, normed_ref[...], preferred_element_type=f32).astype(
        sums_ref.dtype
    )
    sums_ref[:, channels:] = jnp.dot(hidden, grad_ref[...], preferred_element_type=f32).astype(
        sums_ref.dtype
    )


hidden_block = 256


def hidden_half(core, normed, normed_t, grad, grad_t, expand, reduce, bias, kind):
    total, channels = normed.shape
    half = expand.shape[0] // 2
    steps = half // hidden_block
    keep = lambda i, core: (0, 0)
    pick = lambda i, core: (core[0] * steps + i, 0)
    return pl.pallas_call(
        hidden_body,
        out_shape=(
            jax.ShapeDtypeStruct((half, 2 * channels), kind),
            jax.ShapeDtypeStruct((half, total), bf16),
        ),
        grid_spec=pltpu.PrefetchScalarGridSpec(
            num_scalar_prefetch=1,
            grid=(steps,),
            in_specs=[
                pl.BlockSpec((total, channels), keep),
                pl.BlockSpec((channels, total), keep),
                pl.BlockSpec((total, channels), keep),
                pl.BlockSpec((channels, total), keep),
                pl.BlockSpec((hidden_block, channels), pick),
                pl.BlockSpec((hidden_block, channels), pick),
                pl.BlockSpec((hidden_block, lanes), pick),
            ],
            out_specs=[
                pl.BlockSpec((hidden_block, 2 * channels), lambda i, core: (i, 0)),
                pl.BlockSpec((hidden_block, total), lambda i, core: (i, 0)),
            ],
        ),
        compiler_params=params(40),
        cost_estimate=cost(6.9),
        name="hidden_half",
    )(core, normed, normed_t, grad, grad_t, expand, reduce, bias)


def norm_back_body(
    core_ref, turned_ref, other_ref, mine_ref, unit_ref, spread_ref, gain_ref,
    conv_grad_ref, first_ref, last_ref,
):
    total, channels = unit_ref.shape
    half = turned_ref.shape[1] // 2
    core = core_ref[0]
    block = 256
    share = 1.0 / channels
    mine_weight = turned_ref[:, pl.ds(pl.multiple_of(core * half, half), half)]
    other_weight = turned_ref[:, pl.ds(pl.multiple_of((1 - core) * half, half), half)]
    for b in range(total // block):
        at = slice(b * block, (b + 1) * block)
        summed = jnp.dot(mine_weight, mine_ref[:, at], preferred_element_type=f32)
        summed = summed + jnp.dot(other_weight, other_ref[:, at], preferred_element_type=f32)
        grad_normed = summed.astype(bf16).T.astype(f32)
        unit = unit_ref[at, :]
        grad_unit = grad_normed * gain_ref[...]
        mean_grad = jnp.sum(grad_unit, axis=1, keepdims=True) * share
        mean_cross = jnp.sum(grad_unit * unit, axis=1, keepdims=True) * share
        spread = jnp.concatenate([spread_ref[at, :]] * (channels // lanes), axis=1)
        value = (grad_unit - mean_grad - unit * mean_cross) * spread
        conv_grad_ref[b * 8 : (b + 1) * 8] = value.reshape(block // side, side, channels)
    for j in range(reach):
        first_ref[j] = conv_grad_ref[:, j, :].astype(bf16)
        last_ref[j] = conv_grad_ref[:, side - reach + j, :].astype(bf16)


def norm_back(core, turned, other, mine, unit, spread, gain):
    total, channels = unit.shape
    shape = jax.ShapeDtypeStruct((reach, side, channels), bf16)
    found, first, last = pl.pallas_call(
        norm_back_body,
        out_shape=(jax.ShapeDtypeStruct((side, side, channels), f32), shape, shape),
        in_specs=[pl.BlockSpec(memory_space=pltpu.SMEM)] + [whole] * 6,
        out_specs=[whole] * 3,
        compiler_params=params(40),
        cost_estimate=cost(3.3),
        name="norm_back",
    )(core, turned, other, mine, unit, spread, gain)
    return found.reshape(total, channels), first, last


def finish_body(
    counts_ref, conv_ref, kernel_ref, left_ref, right_ref, top_ref, bottom_ref, grad_ref,
    out_ref, rows_sum, cols_sum,
):
    add_edges(True, kernel_ref, left_ref, right_ref, top_ref, bottom_ref, rows_sum, cols_sum)

    def step(i, outer):
        at = pl.ds(pl.multiple_of(i * side, side), side)
        value = edged_row(i, conv_ref[at, :], cols_sum)
        if outer is not None:
            value = value + rows_sum[outer]
        out_ref[at, :] = value + masked_row(i, grad_ref[at, :], counts_ref)

    each_row(step)


def finish(counts, conv, kernel, left, right, top, bottom, grad):
    total, channels = conv.shape
    return pl.pallas_call(
        finish_body,
        out_shape=jax.ShapeDtypeStruct((total, channels), f32),
        in_specs=[pl.BlockSpec(memory_space=pltpu.SMEM)] + [whole] * 7,
        out_specs=whole,
        scratch_shapes=[pltpu.VMEM((2 * reach, side, channels), f32)] * 2,
        compiler_params=params(32),
        cost_estimate=cost(3.1),
        name="finish",
    )(counts, conv, kernel, left, right, top, bottom, grad)


every_axis = ("dp", "lat", "lon")


def device_pairs(move):
    def flat(hi, y, core, z, lo):
        return (hi * 8 + y * 2 + core) * 16 + z * 2 + lo

    found = []
    for hi, y, core, z, lo in itertools.product(range(2), range(4), range(2), range(8), range(2)):
        found.append((flat(hi, y, core, z, lo), flat(*move(hi, y, core, z, lo))))
    return found


def plane_pairs(step, first):
    def move(hi, y, core, z, lo):
        if (core == 0) == first:
            return (hi, (y + step) % 4, core, z, lo)
        x = (2 * hi + lo + step) % 4
        return (x // 2, y, core, z, x % 2)

    return device_pairs(move)


def scatter_direct(rows, place, pairs_of):
    size = rows.shape[0] // 4
    narrow = rows.astype(jnp.bfloat16)
    total = lax.dynamic_slice_in_dim(rows, place * size, size, 0)
    arrived = [
        lax.ppermute(
            lax.dynamic_slice_in_dim(narrow, ((place + step) % 4) * size, size, 0),
            every_axis,
            pairs_of(step),
        )
        for step in range(1, 4)
    ]
    for part in arrived:
        total = total + part.astype(jnp.float32)
    return total


def scatter_halving(rows, z):
    for bit in (4, 2, 1):
        size = rows.shape[0] // 2
        upper = (z // bit) % 2
        arrived = lax.ppermute(
            lax.dynamic_slice_in_dim(rows, (1 - upper) * size, size, 0),
            every_axis,
            device_pairs(lambda hi, y, core, z, lo, bit=bit: (hi, y, core, z ^ bit, lo)),
        )
        rows = lax.dynamic_slice_in_dim(rows, upper * size, size, 0) + arrived
    return rows


def scatter_rows(mine, arrived):
    lat, lon = lax.axis_index("lat"), lax.axis_index("lon")
    y, core, z, lo = lat // 2, lat % 2, lon // 2, lon % 2
    x = 2 * lax.axis_index("dp") + lo
    rows = mine + arrived.astype(jnp.float32)
    rows = scatter_direct(rows, jnp.where(core == 0, y, x), lambda step: plane_pairs(step, True))
    rows = scatter_direct(rows, jnp.where(core == 0, x, y), lambda step: plane_pairs(step, False))
    return scatter_halving(rows, z)


def shifted(axis, step, closed):
    count = lax.axis_size(axis)
    found = []
    for i in range(count):
        j = i + step
        if closed or 0 <= j < count:
            found.append((i, j % count))
    return found


def lon_halo(first, last):
    left = lax.ppermute(last, "lon", shifted("lon", 1, True))
    right = lax.ppermute(first, "lon", shifted("lon", -1, True))
    return left, right


def lat_halo(up, down):
    top = lax.ppermute(down, "lat", shifted("lat", 1, False))
    bottom = lax.ppermute(up, "lat", shifted("lat", -1, False))
    return top, bottom


def local(
    state, cotangent, counts, dw_kernel, dw_bias, norm_gain, norm_bias, w_expand, b_expand, w_reduce
):
    channels = state.shape[-1]
    cells = state.reshape(-1, channels)
    grad = cotangent.reshape(-1, channels)
    total = cells.shape[0]
    kernel = dw_kernel[0]
    core = lax.axis_index("lat") % 2
    near = core.astype(jnp.int32).reshape(1)
    far = 1 - near

    left, right = lon_halo(*side_cols(cells))
    rows, rows_t = mask_rows(counts, grad)
    expand, reduce, expand_t, bias = arrange(w_expand[0], w_reduce[0], b_expand[0])
    top, bottom = lat_halo(*side_rows(cells, left, right))
    conv = inner_conv(cells, kernel, False)
    unit, spread, normed, normed_t = normalise(
        conv, kernel, left, right, top, bottom, dw_bias, norm_gain, norm_bias
    )

    sent, far_pre = hidden_half(
        far, normed, normed_t, rows, rows_t, expand, reduce, bias, jnp.bfloat16
    )
    arrived = lax.ppermute(sent, "lat", [(i, i ^ 1) for i in range(8)])
    mine, near_pre = hidden_half(
        near, normed, normed_t, rows, rows_t, expand, reduce, bias, jnp.float32
    )
    conv_grad, first, last = norm_back(near, expand_t, far_pre, near_pre, unit, spread, norm_gain)
    kept = scatter_rows(mine, arrived)
    left, right = lon_halo(first, last)
    top, bottom = lat_halo(*side_rows(conv_grad, left, right))
    back = inner_conv(conv_grad, kernel, True)
    gradient = finish(counts, back, kernel, left, right, top, bottom, grad)

    cells_all = lax.axis_size("dp") * lax.axis_size("lat") * lax.axis_size("lon") * total
    kept = kept * (1.0 / math.sqrt(cells_all))
    return (gradient.reshape(state.shape), kept[None, :, :channels], kept[None, :, channels:])


def solution(mesh):
    in_specs = (
        P("dp", "lat", "lon", None),
        P("dp", "lat", "lon", None),
        P("lat", "lon"),
        P(),
        P(),
        P(),
        P(),
        P(),
        P(),
        P(),
    )
    out_specs = (
        P("dp", "lat", "lon", None),
        P(None, ("dp", "lat", "lon"), None),
        P(None, ("dp", "lat", "lon"), None),
    )
    return jax.shard_map(local, mesh=mesh, in_specs=in_specs, out_specs=out_specs, check_vma=False)
```

```python
import functools
import itertools
import math

import jax
import jax.numpy as jnp
from jax import lax
from jax.experimental import pallas as pl
from jax.experimental.pallas import tpu as pltpu
from jax.sharding import PartitionSpec as P

norm_eps = 1e-06
inv_root_two_pi = 0.3989422804014327
side = 32
reach = 3
lanes = 128
f32 = jnp.float32
bf16 = jnp.bfloat16
whole = pl.BlockSpec(memory_space=pltpu.VMEM)


def params(mib):
    return pltpu.CompilerParams(vmem_limit_bytes=mib * 1024 * 1024)


def cost(microseconds):
    return pl.CostEstimate(
        flops=int(microseconds * 1.15e9), bytes_accessed=2**20, transcendentals=0
    )


def tap_row(kernel_ref, flipped, p, q, cols):
    index = 7 * p + q
    if flipped:
        index = 48 - index
    return kernel_ref[index : index + 1, cols]


def shift_cols(rows, offset):
    if offset == 0:
        return rows
    count = rows.shape[0]
    turned = pltpu.roll(rows, (-offset) % count, 0)
    place = lax.broadcasted_iota(jnp.int32, (8, rows.shape[1]), 0)
    if offset > 0:
        last = jnp.where(place < 8 - offset, turned[count - 8 :], 0.0)
        return jnp.concatenate([turned[: count - 8], last], axis=0)
    first = jnp.where(place >= -offset, turned[:8], 0.0)
    return jnp.concatenate([first, turned[8:]], axis=0)


def inner_conv_body(flipped, cells_ref, kernel_ref, out_ref, padded):
    edge = reach * side
    total = side * side
    padded[0:edge] = jnp.zeros((edge, lanes), f32)
    padded[edge + total : 2 * edge + total] = jnp.zeros((edge, lanes), f32)
    padded[edge : edge + total] = cells_ref[...]

    def one_row(i, carry):
        base = pl.multiple_of(i * side, side)
        rows = [padded[pl.ds(base + p * side, side), :] for p in range(7)]
        result = None
        for q in range(7):
            summed = None
            for p in range(7):
                term = tap_row(kernel_ref, flipped, p, q, slice(None)) * rows[p]
                summed = term if summed is None else summed + term
            summed = shift_cols(summed, q - reach)
            result = summed if result is None else result + summed
        out_ref[pl.ds(base, side), :] = result
        return carry

    lax.fori_loop(0, side, one_row, 0)


def inner_conv(cells, kernel, flipped):
    total, channels = cells.shape
    block = pl.BlockSpec((total, lanes), lambda c: (0, c))
    return pl.pallas_call(
        functools.partial(inner_conv_body, flipped),
        out_shape=jax.ShapeDtypeStruct((total, channels), f32),
        grid=(channels // lanes,),
        in_specs=[block, pl.BlockSpec((49, lanes), lambda c: (0, c))],
        out_specs=block,
        scratch_shapes=[pltpu.VMEM((total + 2 * reach * side, lanes), f32)],
        compiler_params=params(6),
        cost_estimate=cost(7.0),
        name="inner_conv",
    )(cells, kernel)


def side_cols_body(low_ref, high_ref, first_ref, last_ref):
    for j in range(reach):
        first_ref[j] = low_ref[:, j, :].astype(bf16)
        last_ref[j] = high_ref[:, 8 - reach + j, :].astype(bf16)


def side_cols(cells):
    channels = cells.shape[1]
    grid3 = cells.reshape(side, side, channels)
    shape = jax.ShapeDtypeStruct((reach, side, channels), bf16)
    return pl.pallas_call(
        side_cols_body,
        out_shape=(shape, shape),
        grid=(1,),
        in_specs=[
            pl.BlockSpec((side, 8, channels), lambda g: (0, 0, 0)),
            pl.BlockSpec((side, 8, channels), lambda g: (0, side // 8 - 1, 0)),
        ],
        out_specs=[pl.BlockSpec((reach, side, channels), lambda g: (0, 0, 0))] * 2,
        compiler_params=params(4),
        cost_estimate=cost(1.0),
        name="side_cols",
    )(grid3, grid3)


def side_rows_body(top_ref, bottom_ref, left_ref, right_ref, up_ref, down_ref):
    channels = top_ref.shape[1]
    place = lax.broadcasted_iota(jnp.int32, (8, channels), 0)
    blank = jnp.zeros((8, channels), f32)
    left = [left_ref[h].astype(f32) for h in range(reach)]
    right = [right_ref[h].astype(f32) for h in range(reach)]
    for r in range(reach):
        for source, row, ref in ((top_ref, r, up_ref), (bottom_ref, side - reach + r, down_ref)):
            corner = blank
            for h in range(reach):
                corner = jnp.where(place == h, right[h][row : row + 1], corner)
                corner = jnp.where(place == 8 - reach + h, left[h][row : row + 1], corner)
            body = source[r * side : (r + 1) * side]
            ref[r] = jnp.concatenate([body, corner, blank], axis=0).astype(bf16)


def side_rows(cells, left, right):
    channels = cells.shape[1]
    shape = jax.ShapeDtypeStruct((reach, side + 16, channels), bf16)
    edge = reach * side
    return pl.pallas_call(
        side_rows_body,
        out_shape=(shape, shape),
        in_specs=[whole] * 4,
        out_specs=[whole] * 2,
        compiler_params=params(6),
        cost_estimate=cost(0.8),
        name="side_rows",
    )(cells[:edge], cells[-edge:], left, right)


def add_edges(flipped, kernel_ref, left_ref, right_ref, top_ref, bottom_ref, rows_sum, cols_sum):
    channels = kernel_ref.shape[1]
    for c in range(channels // lanes):
        cols = slice(c * lanes, (c + 1) * lanes)
        for low, ref in ((True, top_ref), (False, bottom_ref)):
            beyond = [ref[h, :, cols].astype(f32)[: side + 8] for h in range(reach)]
            for r in range(reach):
                result = None
                steps = [(h, h - r) for h in range(r, reach)] if low else [
                    (h, 6 + h - r) for h in range(0, r + 1)
                ]
                for q in range(7):
                    summed = None
                    for h, p in steps:
                        term = tap_row(kernel_ref, flipped, p, q, cols) * beyond[h]
                        summed = term if summed is None else summed + term
                    summed = pltpu.roll(summed, (reach - q) % (side + 8), 0) if q != reach else summed
                    result = summed if result is None else result + summed
                rows_sum[r if low else reach + r, :, cols] = result[:side]
        for low, ref in ((True, left_ref), (False, right_ref)):
            beyond = [ref[h, :, cols].astype(f32) for h in range(reach)]
            for r in range(reach):
                steps = [(h, h - r) for h in range(r, reach)] if low else [
                    (h, 6 + h - r) for h in range(0, r + 1)
                ]
                result = None
                for p in range(7):
                    summed = None
                    for h, q in steps:
                        term = tap_row(kernel_ref, flipped, p, q, cols) * beyond[h]
                        summed = term if summed is None else summed + term
                    summed = shift_cols(summed, p - reach)
                    result = summed if result is None else result + summed
                cols_sum[r if low else reach + r, :, cols] = result


def edged_row(i, conv_row, cols_sum):
    channels = conv_row.shape[1]
    place = lax.broadcasted_iota(jnp.int32, (8, channels), 0)
    first, last = conv_row[:8], conv_row[side - 8 :]
    for r in range(reach):
        first = first + jnp.where(place == r, cols_sum[r, pl.ds(i, 1), :], 0.0)
        last = last + jnp.where(place == 8 - reach + r, cols_sum[reach + r, pl.ds(i, 1), :], 0.0)
    return jnp.concatenate([first, conv_row[8 : side - 8], last], axis=0)


def each_row(step):
    def low(i, carry):
        step(i, i)
        return carry

    def middle(i, carry):
        step(i, None)
        return carry

    def high(i, carry):
        step(i, i - (side - 2 * reach))
        return carry

    lax.fori_loop(0, reach, low, 0)
    lax.fori_loop(reach, side - reach, middle, 0, unroll=2)
    lax.fori_loop(side - reach, side, high, 0)


def normalise_body(
    conv_ref, kernel_ref, left_ref, right_ref, top_ref, bottom_ref, bias_ref, gain_ref, shift_ref,
    unit_ref, spread_ref, normed_ref, flipped_ref, rows_sum, cols_sum,
):
    channels = conv_ref.shape[1]
    add_edges(False, kernel_ref, left_ref, right_ref, top_ref, bottom_ref, rows_sum, cols_sum)
    share = 1.0 / channels

    def step(i, outer):
        at = pl.ds(pl.multiple_of(i * side, side), side)
        value = edged_row(i, conv_ref[at, :], cols_sum)
        if outer is not None:
            value = value + rows_sum[outer]
        value = value + bias_ref[...]
        mean = jnp.sum(value, axis=1, keepdims=True) * share
        centred = value - mean
        spread = lax.rsqrt(jnp.sum(centred * centred, axis=1, keepdims=True) * share + norm_eps)
        unit = centred * spread
        unit_ref[at, :] = unit
        spread_ref[at, :] = jnp.broadcast_to(spread, (side, lanes))
        normed_ref[at, :] = (unit * gain_ref[...] + shift_ref[...]).astype(bf16)

    each_row(step)
    turn(normed_ref, flipped_ref)


def turn(source_ref, target_ref):
    for b in range(source_ref.shape[0] // 256):
        at = slice(b * 256, (b + 1) * 256)
        target_ref[:, at] = source_ref[at, :].T


def normalise(conv, kernel, left, right, top, bottom, bias, gain, shift):
    total, channels = conv.shape
    return pl.pallas_call(
        normalise_body,
        out_shape=(
            jax.ShapeDtypeStruct((total, channels), f32),
            jax.ShapeDtypeStruct((total, lanes), f32),
            jax.ShapeDtypeStruct((total, channels), bf16),
            jax.ShapeDtypeStruct((channels, total), bf16),
        ),
        in_specs=[whole] * 9,
        out_specs=[whole] * 4,
        scratch_shapes=[pltpu.VMEM((2 * reach, side, channels), f32)] * 2,
        compiler_params=params(12),
        cost_estimate=cost(4.8),
        name="normalise",
    )(conv, kernel, left, right, top, bottom, bias, gain, shift)


def wet_row(i, counts_ref):
    place = lax.broadcasted_iota(jnp.int32, (8, lanes), 0) + (i % 8) * 8
    pieces = []
    for t in range(side // 8):
        pieces.append(place < counts_ref[i // 8, t])
    return pieces


def masked_row(i, grad_row, counts_ref):
    channels = grad_row.shape[1]
    parts = []
    for t, wet in enumerate(wet_row(i, counts_ref)):
        piece = grad_row[t * 8 : (t + 1) * 8]
        parts.append(
            jnp.concatenate(
                [
                    jnp.where(wet, piece[:, c * lanes : (c + 1) * lanes], 0.0)
                    for c in range(channels // lanes)
                ],
                axis=1,
            )
        )
    return jnp.concatenate(parts, axis=0)


def mask_rows_body(counts_ref, grad_ref, rows_ref, flipped_ref):
    def step(i, carry):
        at = pl.ds(pl.multiple_of(i * side, side), side)
        rows_ref[at, :] = masked_row(i, grad_ref[at, :], counts_ref).astype(bf16)
        return carry

    lax.fori_loop(0, side, step, 0)
    turn(rows_ref, flipped_ref)


def mask_rows(counts, grad):
    total, channels = grad.shape
    return pl.pallas_call(
        mask_rows_body,
        out_shape=(
            jax.ShapeDtypeStruct((total, channels), bf16),
            jax.ShapeDtypeStruct((channels, total), bf16),
        ),
        in_specs=[pl.BlockSpec(memory_space=pltpu.SMEM), whole],
        out_specs=[whole] * 2,
        compiler_params=params(8),
        cost_estimate=cost(1.3),
        name="mask_rows",
    )(counts, grad)


def arrange_body(expand_ref, reduce_ref, bias_ref, expand_out, reduce_out, turned_out, bias_out):
    unit_row = lax.broadcasted_iota(jnp.int32, (48, 96), 0)
    unit_col = lax.broadcasted_iota(jnp.int32, (48, 96), 1)
    picks = [unit_col == (unit_row // 6) * 12 + lo * 6 + unit_row % 6 for lo in range(2)]
    chosen = [pick.astype(f32).astype(bf16) for pick in picks]
    for hi, y, core in itertools.product(range(2), range(4), range(2)):
        unit = (hi * 4 + y) * 2 + core
        at = slice(unit * 96, (unit + 1) * 96)
        expand, reduce = expand_ref[at, :], reduce_ref[at, :]
        bias = bias_ref[unit : unit + 1, :]
        for lo in range(2):
            x = 2 * hi + lo
            place = core * 16 + (y * 4 + x if core == 0 else x * 4 + y)
            to = slice(place * 48, (place + 1) * 48)
            expand_out[to, :] = jnp.dot(chosen[lo], expand, preferred_element_type=f32).astype(bf16)
            reduce_out[to, :] = jnp.dot(chosen[lo], reduce, preferred_element_type=f32).astype(bf16)
            column = jnp.sum(jnp.where(picks[lo], bias, 0.0), axis=1, keepdims=True)
            bias_out[to, :] = jnp.broadcast_to(column, (48, lanes))
    turn(expand_out, turned_out)


def arrange(expand, reduce, bias):
    units, channels = expand.shape
    shape = jax.ShapeDtypeStruct((units, channels), bf16)
    return pl.pallas_call(
        arrange_body,
        out_shape=(
            shape,
            shape,
            jax.ShapeDtypeStruct((channels, units), bf16),
            jax.ShapeDtypeStruct((units, lanes), f32),
        ),
        in_specs=[whole] * 3,
        out_specs=[whole] * 4,
        compiler_params=params(12),
        cost_estimate=cost(1.1),
        name="arrange",
    )(expand, reduce, bias.reshape(16, 96))


tail_slope = 0.3275911 * 0.7071067811865476
tail_terms = [
    0.5 * a for a in (0.254829592, -0.284496736, 1.421413741, -1.453152027, 1.061405429)
]
exp_scale = -0.5 * 1.4426950408889634


def gelu_pair(v):
    d = 1.0 + tail_slope * jnp.abs(v)
    t = pl.reciprocal(d, approx=True)
    t = t * (2.0 - d * t)
    poly = tail_terms[4]
    for a in reversed(tail_terms[:4]):
        poly = poly * t + a
    bell = jnp.exp2(v * v * exp_scale)
    tail = poly * t * bell
    below = jnp.where(v >= 0.0, 1.0 - tail, tail)
    return v * below, below + v * bell * inv_root_two_pi


def hidden_body(
    core_ref, normed_ref, normed_t_ref, grad_ref, grad_t_ref, expand_ref, reduce_ref, bias_ref,
    sums_ref, grad_pre_ref,
):
    channels = normed_ref.shape[1]
    total = normed_ref.shape[0]
    preact = jnp.dot(expand_ref[...], normed_t_ref[...], preferred_element_type=f32)
    grad_hidden = jnp.dot(reduce_ref[...], grad_t_ref[...], preferred_element_type=f32)
    bias = jnp.concatenate([bias_ref[...]] * (total // lanes), axis=1)
    value, slope = gelu_pair(preact + bias)
    hidden = value.astype(bf16)
    grad_pre = (grad_hidden * slope).astype(bf16)
    grad_pre_ref[...] = grad_pre
    sums_ref[:, :channels] = jnp.dot(grad_pre, normed_ref[...], preferred_element_type=f32).astype(
        sums_ref.dtype
    )
    sums_ref[:, channels:] = jnp.dot(hidden, grad_ref[...], preferred_element_type=f32).astype(
        sums_ref.dtype
    )


hidden_block = 256


def hidden_half(core, normed, normed_t, grad, grad_t, expand, reduce, bias, kind):
    total, channels = normed.shape
    half = expand.shape[0] // 2
    steps = half // hidden_block
    keep = lambda i, core: (0, 0)
    pick = lambda i, core: (core[0] * steps + i, 0)
    return pl.pallas_call(
        hidden_body,
        out_shape=(
            jax.ShapeDtypeStruct((half, 2 * channels), kind),
            jax.ShapeDtypeStruct((half, total), bf16),
        ),
        grid_spec=pltpu.PrefetchScalarGridSpec(
            num_scalar_prefetch=1,
            grid=(steps,),
            in_specs=[
                pl.BlockSpec((total, channels), keep),
                pl.BlockSpec((channels, total), keep),
                pl.BlockSpec((total, channels), keep),
                pl.BlockSpec((channels, total), keep),
                pl.BlockSpec((hidden_block, channels), pick),
                pl.BlockSpec((hidden_block, channels), pick),
                pl.BlockSpec((hidden_block, lanes), pick),
            ],
            out_specs=[
                pl.BlockSpec((hidden_block, 2 * channels), lambda i, core: (i, 0)),
                pl.BlockSpec((hidden_block, total), lambda i, core: (i, 0)),
            ],
        ),
        compiler_params=params(20),
        cost_estimate=cost(6.1),
        name="hidden_half",
    )(core, normed, normed_t, grad, grad_t, expand, reduce, bias)


def norm_back_body(
    core_ref, turned_ref, other_ref, mine_ref, unit_ref, spread_ref, gain_ref,
    conv_grad_ref, first_ref, last_ref,
):
    total, channels = unit_ref.shape
    half = turned_ref.shape[1] // 2
    core = core_ref[0]
    block = 256
    share = 1.0 / channels
    mine_weight = turned_ref[:, pl.ds(pl.multiple_of(core * half, half), half)]
    other_weight = turned_ref[:, pl.ds(pl.multiple_of((1 - core) * half, half), half)]
    for b in range(total // block):
        at = slice(b * block, (b + 1) * block)
        summed = jnp.dot(mine_weight, mine_ref[:, at], preferred_element_type=f32)
        summed = summed + jnp.dot(other_weight, other_ref[:, at], preferred_element_type=f32)
        grad_normed = summed.astype(bf16).T.astype(f32)
        unit = unit_ref[at, :]
        grad_unit = grad_normed * gain_ref[...]
        mean_grad = jnp.sum(grad_unit, axis=1, keepdims=True) * share
        mean_cross = jnp.sum(grad_unit * unit, axis=1, keepdims=True) * share
        spread = jnp.concatenate([spread_ref[at, :]] * (channels // lanes), axis=1)
        value = (grad_unit - mean_grad - unit * mean_cross) * spread
        conv_grad_ref[b * 8 : (b + 1) * 8] = value.reshape(block // side, side, channels)
    for j in range(reach):
        first_ref[j] = conv_grad_ref[:, j, :].astype(bf16)
        last_ref[j] = conv_grad_ref[:, side - reach + j, :].astype(bf16)


def norm_back(core, turned, other, mine, unit, spread, gain):
    total, channels = unit.shape
    shape = jax.ShapeDtypeStruct((reach, side, channels), bf16)
    found, first, last = pl.pallas_call(
        norm_back_body,
        out_shape=(jax.ShapeDtypeStruct((side, side, channels), f32), shape, shape),
        in_specs=[pl.BlockSpec(memory_space=pltpu.SMEM)] + [whole] * 6,
        out_specs=[whole] * 3,
        compiler_params=params(14),
        cost_estimate=cost(2.2),
        name="norm_back",
    )(core, turned, other, mine, unit, spread, gain)
    return found.reshape(total, channels), first, last


def finish_body(
    counts_ref, conv_ref, kernel_ref, left_ref, right_ref, top_ref, bottom_ref, grad_ref,
    out_ref, rows_sum, cols_sum,
):
    add_edges(True, kernel_ref, left_ref, right_ref, top_ref, bottom_ref, rows_sum, cols_sum)

    def step(i, outer):
        at = pl.ds(pl.multiple_of(i * side, side), side)
        value = edged_row(i, conv_ref[at, :], cols_sum)
        if outer is not None:
            value = value + rows_sum[outer]
        out_ref[at, :] = value + masked_row(i, grad_ref[at, :], counts_ref)

    each_row(step)


def finish(counts, conv, kernel, left, right, top, bottom, grad):
    total, channels = conv.shape
    return pl.pallas_call(
        finish_body,
        out_shape=jax.ShapeDtypeStruct((total, channels), f32),
        in_specs=[pl.BlockSpec(memory_space=pltpu.SMEM)] + [whole] * 7,
        out_specs=whole,
        scratch_shapes=[pltpu.VMEM((2 * reach, side, channels), f32)] * 2,
        compiler_params=params(12),
        cost_estimate=cost(3.1),
        name="finish",
    )(counts, conv, kernel, left, right, top, bottom, grad)


def combine_body(place_ref, mine_ref, arrived_ref, own_ref, *sent_refs):
    size = own_ref.shape[0]
    for step in range(4):
        chunk = lax.rem(place_ref[0] + step, 4)
        at = pl.ds(pl.multiple_of(chunk * size, size), size)
        total = mine_ref[at, :] + arrived_ref[at, :].astype(f32)
        if step == 0:
            own_ref[...] = total
        else:
            sent_refs[step - 1][...] = total.astype(bf16)


def combine(place, mine, arrived):
    size, width = mine.shape[0] // 4, mine.shape[1]
    sent = jax.ShapeDtypeStruct((size, width), bf16)
    return pl.pallas_call(
        combine_body,
        out_shape=(jax.ShapeDtypeStruct((size, width), f32), sent, sent, sent),
        in_specs=[pl.BlockSpec(memory_space=pltpu.SMEM), whole, whole],
        out_specs=[whole] * 4,
        compiler_params=params(10),
        cost_estimate=cost(0.7),
        name="combine",
    )(place, mine, arrived)


def last_sum_body(scale, place_ref, rows_ref, arrived_ref, expand_ref, reduce_ref):
    size = arrived_ref.shape[0]
    channels = expand_ref.shape[2]
    low, high = rows_ref[:size], rows_ref[size:]
    total = (jnp.where(place_ref[0] == 0, low, high) + arrived_ref[...]) * scale
    for r in range(size):
        expand_ref[r] = total[r : r + 1, :channels]
        reduce_ref[r] = total[r : r + 1, channels:]


def last_sum(place, rows, arrived, scale):
    size, width = arrived.shape
    shape = jax.ShapeDtypeStruct((size, 1, width // 2), f32)
    expand, reduce = pl.pallas_call(
        functools.partial(last_sum_body, scale),
        out_shape=(shape, shape),
        in_specs=[pl.BlockSpec(memory_space=pltpu.SMEM), whole, whole],
        out_specs=[whole] * 2,
        compiler_params=params(4),
        cost_estimate=cost(0.5),
        name="last_sum",
    )(place, rows, arrived)
    return expand.transpose(1, 0, 2), reduce.transpose(1, 0, 2)


every_axis = ("dp", "lat", "lon")


def device_pairs(move):
    def flat(hi, y, core, z, lo):
        return (hi * 8 + y * 2 + core) * 16 + z * 2 + lo

    found = []
    for hi, y, core, z, lo in itertools.product(range(2), range(4), range(2), range(8), range(2)):
        found.append((flat(hi, y, core, z, lo), flat(*move(hi, y, core, z, lo))))
    return found


def plane_pairs(step, first):
    def move(hi, y, core, z, lo):
        if (core == 0) == first:
            return (hi, (y + step) % 4, core, z, lo)
        x = (2 * hi + lo + step) % 4
        return (x // 2, y, core, z, x % 2)

    return device_pairs(move)


def add_parts(own, parts):
    for part in parts:
        own = own + part.astype(jnp.float32)
    return own


def scatter_direct(rows, place, pairs_of):
    size = rows.shape[0] // 4
    narrow = rows.astype(jnp.bfloat16)
    own = lax.dynamic_slice_in_dim(rows, place * size, size, 0)
    arrived = [
        lax.ppermute(
            lax.dynamic_slice_in_dim(narrow, ((place + step) % 4) * size, size, 0),
            every_axis,
            pairs_of(step),
        )
        for step in range(1, 4)
    ]
    return add_parts(own, arrived)


def scatter_halving(rows, z):
    for bit in (4, 2, 1):
        size = rows.shape[0] // 2
        upper = (z // bit) % 2
        arrived = lax.ppermute(
            lax.dynamic_slice_in_dim(rows, (1 - upper) * size, size, 0),
            every_axis,
            device_pairs(lambda hi, y, core, z, lo, bit=bit: (hi, y, core, z ^ bit, lo)),
        )
        if bit > 1:
            rows = lax.dynamic_slice_in_dim(rows, upper * size, size, 0) + arrived
    return rows, arrived, upper


def shifted(axis, step, closed):
    count = lax.axis_size(axis)
    found = []
    for i in range(count):
        j = i + step
        if closed or 0 <= j < count:
            found.append((i, j % count))
    return found


def lon_halo(first, last):
    left = lax.ppermute(last, "lon", shifted("lon", 1, True))
    right = lax.ppermute(first, "lon", shifted("lon", -1, True))
    return left, right


def lat_halo(up, down):
    top = lax.ppermute(down, "lat", shifted("lat", 1, False))
    bottom = lax.ppermute(up, "lat", shifted("lat", -1, False))
    return top, bottom


def local(
    state, cotangent, counts, dw_kernel, dw_bias, norm_gain, norm_bias, w_expand, b_expand, w_reduce
):
    channels = state.shape[-1]
    cells = state.reshape(-1, channels)
    grad = cotangent.reshape(-1, channels)
    total = cells.shape[0]
    kernel = dw_kernel[0]
    core = lax.axis_index("lat") % 2
    near = core.astype(jnp.int32).reshape(1)
    far = 1 - near

    left, right = lon_halo(*side_cols(cells))
    rows, rows_t = mask_rows(counts, grad)
    expand, reduce, expand_t, bias = arrange(w_expand[0], w_reduce[0], b_expand[0])
    top, bottom = lat_halo(*side_rows(cells, left, right))
    conv = inner_conv(cells, kernel, False)
    unit, spread, normed, normed_t = normalise(
        conv, kernel, left, right, top, bottom, dw_bias, norm_gain, norm_bias
    )

    sent, far_pre = hidden_half(
        far, normed, normed_t, rows, rows_t, expand, reduce, bias, jnp.bfloat16
    )
    arrived = lax.ppermute(sent, "lat", [(i, i ^ 1) for i in range(8)])
    mine, near_pre = hidden_half(
        near, normed, normed_t, rows, rows_t, expand, reduce, bias, jnp.float32
    )
    lon = lax.axis_index("lon")
    z, x = lon // 2, 2 * lax.axis_index("dp") + lon % 2
    y = lax.axis_index("lat") // 2
    first_place, second_place = jnp.where(core == 0, y, x), jnp.where(core == 0, x, y)
    own, *sent = combine(first_place.astype(jnp.int32).reshape(1), mine, arrived)
    sent, near_pre = lax.optimization_barrier((sent, near_pre))
    parts = [lax.ppermute(s, every_axis, plane_pairs(i + 1, True)) for i, s in enumerate(sent)]
    conv_grad, first, last = norm_back(near, expand_t, far_pre, near_pre, unit, spread, norm_gain)
    left, right = lon_halo(first, last)
    back = inner_conv(conv_grad, kernel, True)
    own, parts, back, left, right = lax.optimization_barrier((own, parts, back, left, right))
    summed = add_parts(own, parts)
    top, bottom = lat_halo(*side_rows(conv_grad, left, right))
    summed = scatter_direct(summed, second_place, lambda step: plane_pairs(step, False))
    summed, arrived, upper = scatter_halving(summed, z)
    gradient = finish(counts, back, kernel, left, right, top, bottom, grad)

    cells_all = lax.axis_size("dp") * lax.axis_size("lat") * lax.axis_size("lon") * total
    kept = last_sum(
        upper.astype(jnp.int32).reshape(1), summed, arrived, 1.0 / math.sqrt(cells_all)
    )
    return (gradient.reshape(state.shape), *kept)


def solution(mesh):
    in_specs = (
        P("dp", "lat", "lon", None),
        P("dp", "lat", "lon", None),
        P("lat", "lon"),
        P(),
        P(),
        P(),
        P(),
        P(),
        P(),
        P(),
    )
    out_specs = (
        P("dp", "lat", "lon", None),
        P(None, ("dp", "lat", "lon"), None),
        P(None, ("dp", "lat", "lon"), None),
    )
    return jax.shard_map(local, mesh=mesh, in_specs=in_specs, out_specs=out_specs, check_vma=False)
```

```python
import functools
import itertools
import math

import jax
import jax.numpy as jnp
from jax import lax
from jax.experimental import pallas as pl
from jax.experimental.pallas import tpu as pltpu
from jax.sharding import PartitionSpec as P

norm_eps = 1e-06
inv_root_two_pi = 0.3989422804014327
side = 32
reach = 3
lanes = 128
f32 = jnp.float32
bf16 = jnp.bfloat16
whole = pl.BlockSpec(memory_space=pltpu.VMEM)


def params(mib):
    return pltpu.CompilerParams(vmem_limit_bytes=mib * 1024 * 1024)


def cost(microseconds):
    return pl.CostEstimate(
        flops=int(microseconds * 1.15e9), bytes_accessed=2**20, transcendentals=0
    )


def tap_row(kernel_ref, flipped, p, q, cols):
    index = 7 * p + q
    if flipped:
        index = 48 - index
    return kernel_ref[index, :, cols]


def shift_cols(rows, offset):
    if offset == 0:
        return rows
    count = rows.shape[0]
    turned = pltpu.roll(rows, (-offset) % count, 0)
    place = lax.broadcasted_iota(jnp.int32, (8, rows.shape[1]), 0)
    if offset > 0:
        last = jnp.where(place < 8 - offset, turned[count - 8 :], 0.0)
        return jnp.concatenate([turned[: count - 8], last], axis=0)
    first = jnp.where(place >= -offset, turned[:8], 0.0)
    return jnp.concatenate([first, turned[8:]], axis=0)


def inner_conv_body(flipped, parts, cells_ref, kernel_ref, *refs):
    outs, padded = refs[:-1], refs[-1]
    edge = reach * side
    total = side * side
    padded[0:edge] = jnp.zeros((edge, lanes), f32)
    padded[edge + total : 2 * edge + total] = jnp.zeros((edge, lanes), f32)
    for part, out_ref in zip(parts, outs):
        cols = slice(part * lanes, (part + 1) * lanes)
        padded[edge : edge + total] = cells_ref[:, cols]

        def two_rows(i, carry):
            base = pl.multiple_of(i * (2 * side), 2 * side)
            rows = [padded[pl.ds(base + p * side, side), :] for p in range(8)]
            results = [None, None]
            for q in range(7):
                sums = [None, None]
                for p in range(7):
                    tap = tap_row(kernel_ref, flipped, p, q, cols)
                    for g in range(2):
                        term = tap * rows[p + g]
                        sums[g] = term if sums[g] is None else sums[g] + term
                for g in range(2):
                    moved = shift_cols(sums[g], q - reach)
                    results[g] = moved if results[g] is None else results[g] + moved
            for g in range(2):
                out_ref[pl.ds(base + g * side, side), :] = results[g]
            return carry

        lax.fori_loop(0, side // 2, two_rows, 0)


def inner_conv(cells, kernel, flipped, parts):
    total = cells.shape[0]
    shape = jax.ShapeDtypeStruct((total, lanes), f32)
    return pl.pallas_call(
        functools.partial(inner_conv_body, flipped, parts),
        out_shape=(shape,) * len(parts),
        in_specs=[whole] * 2,
        out_specs=[whole] * len(parts),
        scratch_shapes=[pltpu.VMEM((total + 2 * reach * side, lanes), f32)],
        compiler_params=params(6),
        cost_estimate=cost(2.3 * len(parts)),
        name="inner_conv",
    )(cells, kernel)


def side_cols_body(low_ref, high_ref, first_ref, last_ref):
    for j in range(reach):
        first_ref[j] = low_ref[:, j, :].astype(bf16)
        last_ref[j] = high_ref[:, 8 - reach + j, :].astype(bf16)


def side_cols(cells):
    channels = cells.shape[1]
    grid3 = cells.reshape(side, side, channels)
    shape = jax.ShapeDtypeStruct((reach, side, channels), bf16)
    return pl.pallas_call(
        side_cols_body,
        out_shape=(shape, shape),
        grid=(1,),
        in_specs=[
            pl.BlockSpec((side, 8, channels), lambda g: (0, 0, 0)),
            pl.BlockSpec((side, 8, channels), lambda g: (0, side // 8 - 1, 0)),
        ],
        out_specs=[pl.BlockSpec((reach, side, channels), lambda g: (0, 0, 0))] * 2,
        compiler_params=params(4),
        cost_estimate=cost(0.5),
        name="side_cols",
    )(grid3, grid3)


def side_rows_body(cells_ref, left_ref, right_ref, up_ref, down_ref):
    channels = cells_ref.shape[1]
    place = lax.broadcasted_iota(jnp.int32, (8, channels), 0)
    blank = jnp.zeros((8, channels), f32)
    left = [left_ref[h].astype(f32) for h in range(reach)]
    right = [right_ref[h].astype(f32) for h in range(reach)]
    for r in range(reach):
        for row, ref in ((r, up_ref), (side - reach + r, down_ref)):
            corner = blank
            for h in range(reach):
                corner = jnp.where(place == h, right[h][row : row + 1], corner)
                corner = jnp.where(place == 8 - reach + h, left[h][row : row + 1], corner)
            body = cells_ref[row * side : (row + 1) * side]
            ref[r] = jnp.concatenate([body, corner, blank], axis=0).astype(bf16)


def side_rows(cells, left, right):
    channels = cells.shape[1]
    shape = jax.ShapeDtypeStruct((reach, side + 16, channels), bf16)
    return pl.pallas_call(
        side_rows_body,
        out_shape=(shape, shape),
        in_specs=[whole] * 3,
        out_specs=[whole] * 2,
        compiler_params=params(6),
        cost_estimate=cost(0.5),
        name="side_rows",
    )(cells, left, right)


def add_edges(flipped, kernel_ref, left_ref, right_ref, top_ref, bottom_ref, rows_sum, cols_sum):
    channels = kernel_ref.shape[2]
    for c in range(channels // lanes):
        cols = slice(c * lanes, (c + 1) * lanes)
        for low, ref in ((True, top_ref), (False, bottom_ref)):
            beyond = [ref[h, :, cols].astype(f32)[: side + 8] for h in range(reach)]
            for r in range(reach):
                result = None
                steps = [(h, h - r) for h in range(r, reach)] if low else [
                    (h, 6 + h - r) for h in range(0, r + 1)
                ]
                for q in range(7):
                    summed = None
                    for h, p in steps:
                        term = tap_row(kernel_ref, flipped, p, q, cols) * beyond[h]
                        summed = term if summed is None else summed + term
                    summed = pltpu.roll(summed, (reach - q) % (side + 8), 0) if q != reach else summed
                    result = summed if result is None else result + summed
                rows_sum[r if low else reach + r, :, cols] = result[:side]
        for low, ref in ((True, left_ref), (False, right_ref)):
            beyond = [ref[h, :, cols].astype(f32) for h in range(reach)]
            for r in range(reach):
                steps = [(h, h - r) for h in range(r, reach)] if low else [
                    (h, 6 + h - r) for h in range(0, r + 1)
                ]
                result = None
                for p in range(7):
                    summed = None
                    for h, q in steps:
                        term = tap_row(kernel_ref, flipped, p, q, cols) * beyond[h]
                        summed = term if summed is None else summed + term
                    summed = shift_cols(summed, p - reach)
                    result = summed if result is None else result + summed
                cols_sum[r if low else reach + r, :, cols] = result


def edged_row(i, conv_row, cols_sum):
    channels = conv_row.shape[1]
    place = lax.broadcasted_iota(jnp.int32, (8, channels), 0)
    first, last = conv_row[:8], conv_row[side - 8 :]
    for r in range(reach):
        first = first + jnp.where(place == r, cols_sum[r, pl.ds(i, 1), :], 0.0)
        last = last + jnp.where(place == 8 - reach + r, cols_sum[reach + r, pl.ds(i, 1), :], 0.0)
    return jnp.concatenate([first, conv_row[8 : side - 8], last], axis=0)


def each_row(step):
    def low(i, carry):
        step(i, i)
        return carry

    def middle(i, carry):
        step(i, None)
        return carry

    def high(i, carry):
        step(i, i - (side - 2 * reach))
        return carry

    lax.fori_loop(0, reach, low, 0)
    lax.fori_loop(reach, side - reach, middle, 0, unroll=2)
    lax.fori_loop(side - reach, side, high, 0)


def conv_rows(refs, at):
    return jnp.concatenate([ref[at, :] for ref in refs], axis=1)


def normalise_body(
    conv0_ref, conv1_ref, conv2_ref, kernel_ref, left_ref, right_ref, top_ref, bottom_ref, bias_ref, gain_ref, shift_ref,
    unit_ref, spread_ref, normed_ref, flipped_ref, rows_sum, cols_sum,
):
    channels = kernel_ref.shape[2]
    conv_refs = (conv0_ref, conv1_ref, conv2_ref)
    add_edges(False, kernel_ref, left_ref, right_ref, top_ref, bottom_ref, rows_sum, cols_sum)
    share = 1.0 / channels

    def step(i, outer):
        at = pl.ds(pl.multiple_of(i * side, side), side)
        value = edged_row(i, conv_rows(conv_refs, at), cols_sum)
        if outer is not None:
            value = value + rows_sum[outer]
        value = value + bias_ref[...]
        mean = jnp.sum(value, axis=1, keepdims=True) * share
        centred = value - mean
        spread = lax.rsqrt(jnp.sum(centred * centred, axis=1, keepdims=True) * share + norm_eps)
        unit = centred * spread
        unit_ref[at, :] = unit
        spread_ref[at, :] = jnp.broadcast_to(spread, (side, lanes))
        normed_ref[at, :] = (unit * gain_ref[...] + shift_ref[...]).astype(bf16)

    each_row(step)
    turn(normed_ref, flipped_ref)


def turn(source_ref, target_ref):
    for b in range(source_ref.shape[0] // 256):
        at = slice(b * 256, (b + 1) * 256)
        target_ref[:, at] = source_ref[at, :].T


def normalise(conv, kernel, left, right, top, bottom, bias, gain, shift):
    total, channels = conv[0].shape[0], kernel.shape[2]
    return pl.pallas_call(
        normalise_body,
        out_shape=(
            jax.ShapeDtypeStruct((total, channels), f32),
            jax.ShapeDtypeStruct((total, lanes), f32),
            jax.ShapeDtypeStruct((total, channels), bf16),
            jax.ShapeDtypeStruct((channels, total), bf16),
        ),
        in_specs=[whole] * 11,
        out_specs=[whole] * 4,
        scratch_shapes=[pltpu.VMEM((2 * reach, side, channels), f32)] * 2,
        compiler_params=params(12),
        cost_estimate=cost(4.8),
        name="normalise",
    )(*conv, kernel, left, right, top, bottom, bias, gain, shift)


def wet_row(i, counts_ref):
    place = lax.broadcasted_iota(jnp.int32, (8, lanes), 0) + (i % 8) * 8
    pieces = []
    for t in range(side // 8):
        pieces.append(place < counts_ref[i // 8, t])
    return pieces


def masked_row(i, grad_row, counts_ref):
    channels = grad_row.shape[1]
    parts = []
    for t, wet in enumerate(wet_row(i, counts_ref)):
        piece = grad_row[t * 8 : (t + 1) * 8]
        parts.append(
            jnp.concatenate(
                [
                    jnp.where(wet, piece[:, c * lanes : (c + 1) * lanes], 0.0)
                    for c in range(channels // lanes)
                ],
                axis=1,
            )
        )
    return jnp.concatenate(parts, axis=0)


def mask_rows_body(counts_ref, grad_ref, rows_ref, flipped_ref):
    def step(i, carry):
        at = pl.ds(pl.multiple_of(i * side, side), side)
        rows_ref[at, :] = masked_row(i, grad_ref[at, :], counts_ref).astype(bf16)
        return carry

    lax.fori_loop(0, side, step, 0)
    turn(rows_ref, flipped_ref)


def mask_rows(counts, grad):
    total, channels = grad.shape
    return pl.pallas_call(
        mask_rows_body,
        out_shape=(
            jax.ShapeDtypeStruct((total, channels), bf16),
            jax.ShapeDtypeStruct((channels, total), bf16),
        ),
        in_specs=[pl.BlockSpec(memory_space=pltpu.SMEM), whole],
        out_specs=[whole] * 2,
        compiler_params=params(8),
        cost_estimate=cost(1.3),
        name="mask_rows",
    )(counts, grad)


def arrange_body(expand_ref, reduce_ref, bias_ref, expand_out, reduce_out, turned_out, bias_out):
    unit_row = lax.broadcasted_iota(jnp.int32, (48, 96), 0)
    unit_col = lax.broadcasted_iota(jnp.int32, (48, 96), 1)
    picks = [unit_col == (unit_row // 6) * 12 + lo * 6 + unit_row % 6 for lo in range(2)]
    chosen = [pick.astype(f32).astype(bf16) for pick in picks]
    for hi, y, core in itertools.product(range(2), range(4), range(2)):
        unit = (hi * 4 + y) * 2 + core
        at = slice(unit * 96, (unit + 1) * 96)
        expand, reduce = expand_ref[at, :], reduce_ref[at, :]
        bias = bias_ref[:, at]
        for lo in range(2):
            x = 2 * hi + lo
            place = core * 16 + (y * 4 + x if core == 0 else x * 4 + y)
            to = slice(place * 48, (place + 1) * 48)
            expand_out[to, :] = jnp.dot(chosen[lo], expand, preferred_element_type=f32).astype(bf16)
            reduce_out[to, :] = jnp.dot(chosen[lo], reduce, preferred_element_type=f32).astype(bf16)
            column = jnp.sum(jnp.where(picks[lo], bias, 0.0), axis=1, keepdims=True)
            bias_out[to, :] = jnp.broadcast_to(column, (48, lanes))
    turn(expand_out, turned_out)


def arrange(expand, reduce, bias):
    units, channels = expand.shape
    shape = jax.ShapeDtypeStruct((units, channels), bf16)
    return pl.pallas_call(
        arrange_body,
        out_shape=(
            shape,
            shape,
            jax.ShapeDtypeStruct((channels, units), bf16),
            jax.ShapeDtypeStruct((units, lanes), f32),
        ),
        in_specs=[whole] * 3,
        out_specs=[whole] * 4,
        compiler_params=params(12),
        cost_estimate=cost(1.1),
        name="arrange",
    )(expand, reduce, bias)


tail_slope = 0.3275911 * 0.7071067811865476
tail_terms = [
    0.5 * a for a in (0.254829592, -0.284496736, 1.421413741, -1.453152027, 1.061405429)
]
exp_scale = -0.5 * 1.4426950408889634


def gelu_pair(v):
    d = 1.0 + tail_slope * jnp.abs(v)
    t = pltpu.reciprocal(d, approx=True)
    poly = tail_terms[4]
    for a in reversed(tail_terms[:4]):
        poly = poly * t + a
    bell = jnp.exp2(v * v * exp_scale)
    tail = poly * t * bell
    below = jnp.where(v >= 0.0, 1.0 - tail, tail)
    return v * below, below + v * bell * inv_root_two_pi


def own_place():
    lat, lon = lax.axis_index("lat"), lax.axis_index("lon")
    x = 2 * lax.axis_index("dp") + (lon & 1)
    return lat & 1, x, lat >> 1, lon >> 1


def phase_place(second):
    core, x, y, _ = own_place()
    along_y = core == (1 if second else 0)
    return jnp.where(along_y, y, x)


def hidden_rows(cells, source, rows, grad_pre_ref, to):
    normed_ref, normed_t_ref, grad_ref, grad_t_ref, expand_ref, reduce_ref, bias_ref = cells
    total = normed_ref.shape[0]
    at = pl.ds(source, rows)
    preact = jnp.dot(expand_ref[at, :], normed_t_ref[...], preferred_element_type=f32)
    grad_hidden = jnp.dot(reduce_ref[at, :], grad_t_ref[...], preferred_element_type=f32)
    bias = jnp.concatenate([bias_ref[at, :]] * (total // lanes), axis=1)
    value, slope = gelu_pair(preact + bias)
    hidden = value.astype(bf16)
    grad_pre = (grad_hidden * slope).astype(bf16)
    grad_pre_ref[pl.ds(to, rows), :] = grad_pre
    return (
        jnp.dot(grad_pre, normed_ref[...], preferred_element_type=f32),
        jnp.dot(hidden, grad_ref[...], preferred_element_type=f32),
    )


def far_body(*refs):
    cells, (sent_ref, grad_pre_ref) = refs[:7], refs[7:]
    half = grad_pre_ref.shape[0]
    channels = refs[0].shape[1]
    base = (1 - own_place()[0]) * half
    rows = 256
    for b in range(half // rows):
        source = pl.multiple_of(base + b * rows, rows)
        expand, reduce = hidden_rows(cells, source, rows, grad_pre_ref, b * rows)
        at = slice(b * rows, (b + 1) * rows)
        sent_ref[at, :channels] = expand.astype(bf16)
        sent_ref[at, channels:] = reduce.astype(bf16)


def hidden_far(*cells):
    total, channels = cells[0].shape
    half = cells[4].shape[0] // 2
    return pl.pallas_call(
        far_body,
        out_shape=(
            jax.ShapeDtypeStruct((half, 2 * channels), bf16),
            jax.ShapeDtypeStruct((half, total), bf16),
        ),
        in_specs=[whole] * 7,
        out_specs=[whole] * 2,
        compiler_params=params(16),
        cost_estimate=cost(5.8),
        name="hidden_far",
    )(*cells)


def near_first_body(*refs):
    cells, (sums_ref, grad_pre_ref) = refs[:7], refs[7:]
    half = grad_pre_ref.shape[0]
    channels = refs[0].shape[1]
    size = half // 4
    core, place = own_place()[0], phase_place(False)
    for step in (1, 2):
        chunk = pl.multiple_of(lax.rem(place + step, 4) * size, size)
        source = pl.multiple_of(core * half + chunk, size)
        expand, reduce = hidden_rows(cells, source, size, grad_pre_ref, chunk)
        at = slice((step - 1) * size, step * size)
        sums_ref[at, :channels] = expand
        sums_ref[at, channels:] = reduce


def near_first(*cells):
    total, channels = cells[0].shape
    half = cells[4].shape[0] // 2
    return pl.pallas_call(
        near_first_body,
        out_shape=(
            jax.ShapeDtypeStruct((half // 2, 2 * channels), f32),
            jax.ShapeDtypeStruct((half, total), bf16),
        ),
        in_specs=[whole] * 7,
        out_specs=[whole] * 2,
        compiler_params=params(16),
        cost_estimate=cost(3.0),
        name="near_first",
    )(*cells)


def near_sends_body(sums_ref, arrived_ref, *sent_refs):
    size = sent_refs[0].shape[0]
    place = phase_place(False)
    for step in (1, 2):
        chunk = pl.multiple_of(lax.rem(place + step, 4) * size, size)
        total = sums_ref[(step - 1) * size : step * size] + arrived_ref[pl.ds(chunk, size), :].astype(f32)
        sent_refs[step - 1][...] = total.astype(bf16)


def near_sends(sums, arrived):
    size, width = sums.shape[0] // 2, sums.shape[1]
    sent = jax.ShapeDtypeStruct((size, width), bf16)
    return pl.pallas_call(
        near_sends_body,
        out_shape=(sent, sent),
        in_specs=[whole] * 2,
        out_specs=[whole] * 2,
        compiler_params=params(6),
        cost_estimate=cost(0.3),
        name="near_sends",
    )(sums, arrived)


def near_last_body(*refs):
    cells, (arrived_ref, _, own_ref, sent_ref, grad_pre_ref) = refs[:7], refs[7:]
    half = grad_pre_ref.shape[0]
    channels = refs[0].shape[1]
    size = half // 4
    core, place = own_place()[0], phase_place(False)
    for step, ref in ((3, sent_ref), (0, own_ref)):
        chunk = pl.multiple_of(lax.rem(place + step, 4) * size, size)
        source = pl.multiple_of(core * half + chunk, size)
        expand, reduce = hidden_rows(cells, source, size, grad_pre_ref, chunk)
        other = arrived_ref[pl.ds(chunk, size), :].astype(f32)
        ref[:, :channels] = (expand + other[:, :channels]).astype(ref.dtype)
        ref[:, channels:] = (reduce + other[:, channels:]).astype(ref.dtype)


def near_last(*inputs):
    cells, grad_pre = inputs[:7], inputs[8]
    channels = cells[0].shape[1]
    size = cells[4].shape[0] // 8
    return pl.pallas_call(
        near_last_body,
        out_shape=(
            jax.ShapeDtypeStruct((size, 2 * channels), f32),
            jax.ShapeDtypeStruct((size, 2 * channels), bf16),
            jax.ShapeDtypeStruct(grad_pre.shape, bf16),
        ),
        in_specs=[whole] * 9,
        out_specs=[whole] * 3,
        input_output_aliases={8: 2},
        compiler_params=params(16),
        cost_estimate=cost(3.0),
        name="near_last",
    )(*inputs)


def norm_back_body(
    turned_ref, other_ref, mine_ref, unit_ref, spread_ref, gain_ref,
    conv_grad_ref, first_ref, last_ref,
):
    total, channels = unit_ref.shape
    half = turned_ref.shape[1] // 2
    core = own_place()[0]
    block = 256
    share = 1.0 / channels
    mine_weight = turned_ref[:, pl.ds(pl.multiple_of(core * half, half), half)]
    other_weight = turned_ref[:, pl.ds(pl.multiple_of((1 - core) * half, half), half)]
    for b in range(total // block):
        at = slice(b * block, (b + 1) * block)
        summed = jnp.dot(mine_weight, mine_ref[:, at], preferred_element_type=f32)
        summed = summed + jnp.dot(other_weight, other_ref[:, at], preferred_element_type=f32)
        grad_normed = summed.astype(bf16).T.astype(f32)
        unit = unit_ref[at, :]
        grad_unit = grad_normed * gain_ref[...]
        mean_grad = jnp.sum(grad_unit, axis=1, keepdims=True) * share
        mean_cross = jnp.sum(grad_unit * unit, axis=1, keepdims=True) * share
        spread = jnp.concatenate([spread_ref[at, :]] * (channels // lanes), axis=1)
        value = (grad_unit - mean_grad - unit * mean_cross) * spread
        conv_grad_ref[b * 8 : (b + 1) * 8] = value.reshape(block // side, side, channels)
    for j in range(reach):
        first_ref[j] = conv_grad_ref[:, j, :].astype(bf16)
        last_ref[j] = conv_grad_ref[:, side - reach + j, :].astype(bf16)


def norm_back(turned, other, mine, unit, spread, gain):
    total, channels = unit.shape
    shape = jax.ShapeDtypeStruct((reach, side, channels), bf16)
    found, first, last = pl.pallas_call(
        norm_back_body,
        out_shape=(jax.ShapeDtypeStruct((side, side, channels), f32), shape, shape),
        in_specs=[whole] * 6,
        out_specs=[whole] * 3,
        compiler_params=params(14),
        cost_estimate=cost(2.2),
        name="norm_back",
    )(turned, other, mine, unit, spread, gain)
    return found.reshape(total, channels), first, last


def finish_body(
    counts_ref, conv0_ref, conv1_ref, conv2_ref, kernel_ref, left_ref, right_ref, top_ref, bottom_ref,
    grad_ref, out_ref, rows_sum, cols_sum,
):
    conv_refs = (conv0_ref, conv1_ref, conv2_ref)
    add_edges(True, kernel_ref, left_ref, right_ref, top_ref, bottom_ref, rows_sum, cols_sum)

    def step(i, outer):
        at = pl.ds(pl.multiple_of(i * side, side), side)
        value = edged_row(i, conv_rows(conv_refs, at), cols_sum)
        if outer is not None:
            value = value + rows_sum[outer]
        out_ref[at, :] = value + masked_row(i, grad_ref[at, :], counts_ref)

    each_row(step)


def finish(counts, conv, kernel, left, right, top, bottom, grad):
    total, channels = grad.shape
    return pl.pallas_call(
        finish_body,
        out_shape=jax.ShapeDtypeStruct((total, channels), f32),
        in_specs=[pl.BlockSpec(memory_space=pltpu.SMEM)] + [whole] * 9,
        out_specs=whole,
        scratch_shapes=[pltpu.VMEM((2 * reach, side, channels), f32)] * 2,
        compiler_params=params(12),
        cost_estimate=cost(3.1),
        name="finish",
    )(counts, *conv, kernel, left, right, top, bottom, grad)


def split_four_body(own_ref, first_ref, second_ref, third_ref, kept_ref, *sent_refs):
    size = kept_ref.shape[0]
    place = phase_place(True)
    for step in range(4):
        at = pl.ds(pl.multiple_of(lax.rem(place + step, 4) * size, size), size)
        total = own_ref[at, :]
        for ref in (first_ref, second_ref, third_ref):
            total = total + ref[at, :].astype(f32)
        if step == 0:
            kept_ref[...] = total
        else:
            sent_refs[step - 1][...] = total.astype(bf16)


def split_four(own, parts):
    size, width = own.shape[0] // 4, own.shape[1]
    sent = jax.ShapeDtypeStruct((size, width), bf16)
    return pl.pallas_call(
        split_four_body,
        out_shape=(jax.ShapeDtypeStruct((size, width), f32), sent, sent, sent),
        in_specs=[whole] * 4,
        out_specs=[whole] * 4,
        compiler_params=params(4),
        cost_estimate=cost(0.3),
        name="split_four",
    )(own, *parts)


def split_two_body(bit, own_ref, *refs):
    part_refs, (kept_ref, sent_ref) = refs[:-2], refs[-2:]
    size = kept_ref.shape[0]
    total = own_ref[...]
    for ref in part_refs:
        total = total + ref[...].astype(f32)
    low, high = total[:size], total[size:]
    upper = (own_place()[3] & bit) != 0
    kept_ref[...] = jnp.where(upper, high, low)
    sent_ref[...] = jnp.where(upper, low, high)


def split_two(bit, own, parts):
    shape = jax.ShapeDtypeStruct((own.shape[0] // 2, own.shape[1]), f32)
    return pl.pallas_call(
        functools.partial(split_two_body, bit),
        out_shape=(shape, shape),
        in_specs=[whole] * (1 + len(parts)),
        out_specs=[whole] * 2,
        compiler_params=params(4),
        cost_estimate=cost(0.2),
        name="split_two",
    )(own, *parts)


def last_sum_body(scale, own_ref, arrived_ref, expand_ref, reduce_ref):
    channels = expand_ref.shape[2]
    total = (own_ref[...] + arrived_ref[...]) * scale
    for r in range(total.shape[0]):
        expand_ref[r] = total[r : r + 1, :channels]
        reduce_ref[r] = total[r : r + 1, channels:]


def last_sum(own, arrived, scale):
    size, width = own.shape
    shape = jax.ShapeDtypeStruct((size, 1, width // 2), f32)
    expand, reduce = pl.pallas_call(
        functools.partial(last_sum_body, scale),
        out_shape=(shape, shape),
        in_specs=[whole] * 2,
        out_specs=[whole] * 2,
        compiler_params=params(4),
        cost_estimate=cost(0.4),
        name="last_sum",
    )(own, arrived)
    return expand.transpose(1, 0, 2), reduce.transpose(1, 0, 2)


every_axis = ("dp", "lat", "lon")


def device_pairs(move):
    def flat(hi, y, core, z, lo):
        return (hi * 8 + y * 2 + core) * 16 + z * 2 + lo

    found = []
    for hi, y, core, z, lo in itertools.product(range(2), range(4), range(2), range(8), range(2)):
        found.append((flat(hi, y, core, z, lo), flat(*move(hi, y, core, z, lo))))
    return found


def plane_pairs(step, first):
    def move(hi, y, core, z, lo):
        if (core == 0) == first:
            return (hi, (y + step) % 4, core, z, lo)
        x = (2 * hi + lo + step) % 4
        return (x // 2, y, core, z, x % 2)

    return device_pairs(move)


def halving_pairs(bit):
    return device_pairs(lambda hi, y, core, z, lo: (hi, y, core, z ^ bit, lo))


def shifted(axis, step, closed):
    count = lax.axis_size(axis)
    found = []
    for i in range(count):
        j = i + step
        if closed or 0 <= j < count:
            found.append((i, j % count))
    return found


def lon_halo(first, last):
    left = lax.ppermute(last, "lon", shifted("lon", 1, True))
    right = lax.ppermute(first, "lon", shifted("lon", -1, True))
    return left, right


def lat_halo(up, down):
    top = lax.ppermute(down, "lat", shifted("lat", 1, False))
    bottom = lax.ppermute(up, "lat", shifted("lat", -1, False))
    return top, bottom


def after(value, *others):
    return lax.optimization_barrier((value, others))[0]


def local(
    state, cotangent, counts, dw_kernel, dw_bias, norm_gain, norm_bias, w_expand, b_expand, w_reduce
):
    channels = state.shape[-1]
    cells = state.reshape(-1, channels)
    grad = cotangent.reshape(-1, channels)
    total = cells.shape[0]
    kernel = dw_kernel.transpose(1, 0, 2)

    left, right = lon_halo(*side_cols(cells))
    conv = inner_conv(cells, kernel, False, (0, 1, 2))
    rows, rows_t = mask_rows(counts, grad)
    top, bottom = lat_halo(*side_rows(cells, left, right))
    expand, reduce, expand_t, bias = arrange(w_expand[0], w_reduce[0], b_expand)
    unit, spread, normed, normed_t = normalise(
        conv, kernel, left, right, top, bottom, dw_bias, norm_gain, norm_bias
    )

    inputs = (normed, normed_t, rows, rows_t, expand, reduce, bias)
    sent, far_pre = hidden_far(*inputs)
    arrived = lax.ppermute(sent, "lat", [(i, i ^ 1) for i in range(8)])
    sums, near_pre = near_first(*inputs)
    one, two = near_sends(sums, arrived)
    part_one = lax.ppermute(one, every_axis, plane_pairs(1, True))
    part_two = lax.ppermute(two, every_axis, plane_pairs(2, True))
    own, three, near_pre = near_last(*inputs, arrived, after(near_pre, one, two))
    part_three = lax.ppermute(three, every_axis, plane_pairs(3, True))

    far_pre = after(far_pre, three)
    conv_grad, first, last = norm_back(expand_t, far_pre, near_pre, unit, spread, norm_gain)
    left, right = lon_halo(first, last)

    own, parts = after((own, (part_one, part_two, part_three)), left, right)
    own, *sent = split_four(own, parts)
    parts = [lax.ppermute(s, every_axis, plane_pairs(i + 1, False)) for i, s in enumerate(sent)]
    conv_grad = after(conv_grad, sent)
    up, down = side_rows(conv_grad, left, right)
    back = inner_conv(conv_grad, kernel, True, (0,))

    own, sent = split_two(4, *after((own, parts), up, down, back))
    top, bottom = lat_halo(up, down)
    arrived = lax.ppermute(sent, every_axis, halving_pairs(4))
    conv_grad = after(conv_grad, sent)
    back += inner_conv(conv_grad, kernel, True, (1,))

    own, sent = split_two(2, *after((own, [arrived]), back))
    arrived = lax.ppermute(sent, every_axis, halving_pairs(2))
    conv_grad = after(conv_grad, sent)
    back += inner_conv(conv_grad, kernel, True, (2,))

    own, sent = split_two(1, *after((own, [arrived]), back, top, bottom))
    arrived = lax.ppermute(sent, every_axis, halving_pairs(1))
    grad = after(grad, sent)
    gradient = finish(counts, back, kernel, left, right, top, bottom, grad)

    cells_all = lax.axis_size("dp") * lax.axis_size("lat") * lax.axis_size("lon") * total
    kept = last_sum(own, arrived, 1.0 / math.sqrt(cells_all))
    return (gradient.reshape(state.shape), *kept)


def solution(mesh):
    in_specs = (
        P("dp", "lat", "lon", None),
        P("dp", "lat", "lon", None),
        P("lat", "lon"),
        P(),
        P(),
        P(),
        P(),
        P(),
        P(),
        P(),
    )
    out_specs = (
        P("dp", "lat", "lon", None),
        P(None, ("dp", "lat", "lon"), None),
        P(None, ("dp", "lat", "lon"), None),
    )
    return jax.shard_map(local, mesh=mesh, in_specs=in_specs, out_specs=out_specs, check_vma=False)
```

```python
import functools
import itertools
import math

import jax
import jax.numpy as jnp
from jax import lax
from jax.experimental import pallas as pl
from jax.experimental.pallas import tpu as pltpu
from jax.sharding import PartitionSpec as P

norm_eps = 1e-06
inv_root_two_pi = 0.3989422804014327
side = 32
reach = 3
lanes = 128
f32 = jnp.float32
bf16 = jnp.bfloat16
whole = pl.BlockSpec(memory_space=pltpu.VMEM)


def params(mib):
    return pltpu.CompilerParams(vmem_limit_bytes=mib * 1024 * 1024)


def cost(microseconds):
    return pl.CostEstimate(
        flops=int(microseconds * 1.15e9), bytes_accessed=2**20, transcendentals=0
    )


def tap_row(kernel_ref, flipped, p, q, cols):
    index = 7 * p + q
    if flipped:
        index = 48 - index
    return kernel_ref[index, :, cols]


def shift_cols(rows, offset):
    if offset == 0:
        return rows
    count = rows.shape[0]
    turned = pltpu.roll(rows, (-offset) % count, 0)
    place = lax.broadcasted_iota(jnp.int32, (8, rows.shape[1]), 0)
    if offset > 0:
        last = jnp.where(place < 8 - offset, turned[count - 8 :], 0.0)
        return jnp.concatenate([turned[: count - 8], last], axis=0)
    first = jnp.where(place >= -offset, turned[:8], 0.0)
    return jnp.concatenate([first, turned[8:]], axis=0)


def inner_conv_body(flipped, parts, cells_ref, kernel_ref, *refs):
    outs, padded = refs[:-1], refs[-1]
    edge = reach * side
    total = side * side
    padded[0:edge] = jnp.zeros((edge, lanes), f32)
    padded[edge + total : 2 * edge + total] = jnp.zeros((edge, lanes), f32)
    for part, out_ref in zip(parts, outs):
        cols = slice(part * lanes, (part + 1) * lanes)
        padded[edge : edge + total] = cells_ref[:, cols]

        def two_rows(i, carry):
            base = pl.multiple_of(i * (2 * side), 2 * side)
            rows = [padded[pl.ds(base + p * side, side), :] for p in range(8)]
            results = [None, None]
            for q in range(7):
                sums = [None, None]
                for p in range(7):
                    tap = tap_row(kernel_ref, flipped, p, q, cols)
                    for g in range(2):
                        term = tap * rows[p + g]
                        sums[g] = term if sums[g] is None else sums[g] + term
                for g in range(2):
                    moved = shift_cols(sums[g], q - reach)
                    results[g] = moved if results[g] is None else results[g] + moved
            for g in range(2):
                out_ref[pl.ds(base + g * side, side), :] = results[g]
            return carry

        lax.fori_loop(0, side // 2, two_rows, 0)


def inner_conv(cells, kernel, flipped, parts):
    total = cells.shape[0]
    shape = jax.ShapeDtypeStruct((total, lanes), f32)
    return pl.pallas_call(
        functools.partial(inner_conv_body, flipped, parts),
        out_shape=(shape,) * len(parts),
        in_specs=[whole] * 2,
        out_specs=[whole] * len(parts),
        scratch_shapes=[pltpu.VMEM((total + 2 * reach * side, lanes), f32)],
        compiler_params=params(6),
        cost_estimate=cost(2.3 * len(parts)),
        name="inner_conv",
    )(cells, kernel)


def side_cols_body(cells_ref, first_ref, last_ref, low, high, sems):
    copies = [
        pltpu.make_async_copy(cells_ref.at[:, pl.ds(0, 8), :], low, sems.at[0]),
        pltpu.make_async_copy(cells_ref.at[:, pl.ds(side - 8, 8), :], high, sems.at[1]),
    ]
    for copy in copies:
        copy.start()
    copies[0].wait()
    for j in range(reach):
        first_ref[j] = low[:, j, :].astype(bf16)
    copies[1].wait()
    for j in range(reach):
        last_ref[j] = high[:, 8 - reach + j, :].astype(bf16)


def side_cols(cells):
    channels = cells.shape[1]
    shape = jax.ShapeDtypeStruct((reach, side, channels), bf16)
    return pl.pallas_call(
        side_cols_body,
        out_shape=(shape, shape),
        in_specs=[pl.BlockSpec(memory_space=pltpu.HBM)],
        out_specs=[whole] * 2,
        scratch_shapes=[pltpu.VMEM((side, 8, channels), f32)] * 2 + [pltpu.SemaphoreType.DMA((2,))],
        compiler_params=params(58),
        cost_estimate=cost(1.0),
        name="side_cols",
    )(cells.reshape(side, side, channels))


def side_rows_body(cells_ref, left_ref, right_ref, up_ref, down_ref):
    channels = cells_ref.shape[1]
    place = lax.broadcasted_iota(jnp.int32, (8, channels), 0)
    blank = jnp.zeros((8, channels), f32)
    left = [left_ref[h].astype(f32) for h in range(reach)]
    right = [right_ref[h].astype(f32) for h in range(reach)]
    for r in range(reach):
        for row, ref in ((r, up_ref), (side - reach + r, down_ref)):
            corner = blank
            for h in range(reach):
                corner = jnp.where(place == h, right[h][row : row + 1], corner)
                corner = jnp.where(place == 8 - reach + h, left[h][row : row + 1], corner)
            body = cells_ref[row * side : (row + 1) * side]
            ref[r] = jnp.concatenate([body, corner, blank], axis=0).astype(bf16)


def side_rows(cells, left, right):
    channels = cells.shape[1]
    shape = jax.ShapeDtypeStruct((reach, side + 16, channels), bf16)
    return pl.pallas_call(
        side_rows_body,
        out_shape=(shape, shape),
        in_specs=[whole] * 3,
        out_specs=[whole] * 2,
        compiler_params=params(6),
        cost_estimate=cost(0.5),
        name="side_rows",
    )(cells, left, right)


def add_edges(flipped, kernel_ref, left_ref, right_ref, top_ref, bottom_ref, rows_sum, cols_sum):
    channels = kernel_ref.shape[2]
    for c in range(channels // lanes):
        cols = slice(c * lanes, (c + 1) * lanes)
        for low, ref in ((True, top_ref), (False, bottom_ref)):
            beyond = [ref[h, :, cols].astype(f32)[: side + 8] for h in range(reach)]
            for r in range(reach):
                result = None
                steps = [(h, h - r) for h in range(r, reach)] if low else [
                    (h, 6 + h - r) for h in range(0, r + 1)
                ]
                for q in range(7):
                    summed = None
                    for h, p in steps:
                        term = tap_row(kernel_ref, flipped, p, q, cols) * beyond[h]
                        summed = term if summed is None else summed + term
                    summed = pltpu.roll(summed, (reach - q) % (side + 8), 0) if q != reach else summed
                    result = summed if result is None else result + summed
                rows_sum[r if low else reach + r, :, cols] = result[:side]
        for low, ref in ((True, left_ref), (False, right_ref)):
            beyond = [ref[h, :, cols].astype(f32) for h in range(reach)]
            for r in range(reach):
                steps = [(h, h - r) for h in range(r, reach)] if low else [
                    (h, 6 + h - r) for h in range(0, r + 1)
                ]
                result = None
                for p in range(7):
                    summed = None
                    for h, q in steps:
                        term = tap_row(kernel_ref, flipped, p, q, cols) * beyond[h]
                        summed = term if summed is None else summed + term
                    summed = shift_cols(summed, p - reach)
                    result = summed if result is None else result + summed
                cols_sum[r if low else reach + r, :, cols] = result


def edged_row(i, conv_row, cols_sum):
    channels = conv_row.shape[1]
    place = lax.broadcasted_iota(jnp.int32, (8, channels), 0)
    first, last = conv_row[:8], conv_row[side - 8 :]
    for r in range(reach):
        first = first + jnp.where(place == r, cols_sum[r, pl.ds(i, 1), :], 0.0)
        last = last + jnp.where(place == 8 - reach + r, cols_sum[reach + r, pl.ds(i, 1), :], 0.0)
    return jnp.concatenate([first, conv_row[8 : side - 8], last], axis=0)


def each_row(step):
    def low(i, carry):
        step(i, i)
        return carry

    def middle(i, carry):
        step(i, None)
        return carry

    def high(i, carry):
        step(i, i - (side - 2 * reach))
        return carry

    lax.fori_loop(0, reach, low, 0, unroll=reach)
    lax.fori_loop(reach, side - reach, middle, 0, unroll=side // 2 - reach)
    lax.fori_loop(side - reach, side, high, 0, unroll=reach)


def conv_rows(refs, at):
    return jnp.concatenate([ref[at, :] for ref in refs], axis=1)


def normalise_body(
    conv0_ref, conv1_ref, conv2_ref, kernel_ref, left_ref, right_ref, top_ref, bottom_ref, bias_ref, gain_ref, shift_ref,
    unit_ref, spread_ref, normed_ref, rows_sum, cols_sum,
):
    channels = kernel_ref.shape[2]
    conv_refs = (conv0_ref, conv1_ref, conv2_ref)
    add_edges(False, kernel_ref, left_ref, right_ref, top_ref, bottom_ref, rows_sum, cols_sum)
    share = 1.0 / channels

    def step(i, outer):
        at = pl.ds(pl.multiple_of(i * side, side), side)
        value = edged_row(i, conv_rows(conv_refs, at), cols_sum)
        if outer is not None:
            value = value + rows_sum[outer]
        value = value + bias_ref[...]
        mean = jnp.sum(value, axis=1, keepdims=True) * share
        centred = value - mean
        spread = lax.rsqrt(jnp.sum(centred * centred, axis=1, keepdims=True) * share + norm_eps)
        unit = centred * spread
        unit_ref[at, :] = unit
        spread_ref[at, :] = jnp.broadcast_to(spread, (side, lanes))
        normed_ref[at, :] = (unit * gain_ref[...] + shift_ref[...]).astype(bf16)

    each_row(step)


def turn(source_ref, target_ref):
    for b in range(source_ref.shape[0] // 256):
        at = slice(b * 256, (b + 1) * 256)
        target_ref[:, at] = source_ref[at, :].T


def normalise(conv, kernel, left, right, top, bottom, bias, gain, shift):
    total, channels = conv[0].shape[0], kernel.shape[2]
    return pl.pallas_call(
        normalise_body,
        out_shape=(
            jax.ShapeDtypeStruct((total, channels), f32),
            jax.ShapeDtypeStruct((total, lanes), f32),
            jax.ShapeDtypeStruct((total, channels), bf16),
        ),
        in_specs=[whole] * 11,
        out_specs=[whole] * 3,
        scratch_shapes=[pltpu.VMEM((2 * reach, side, channels), f32)] * 2,
        compiler_params=params(12),
        cost_estimate=cost(2.8),
        name="normalise",
    )(*conv, kernel, left, right, top, bottom, bias, gain, shift)


def wet_row(i, counts_ref):
    place = lax.broadcasted_iota(jnp.int32, (8, lanes), 0) + (i % 8) * 8
    pieces = []
    for t in range(side // 8):
        pieces.append(place < counts_ref[i // 8, t])
    return pieces


def masked_row(i, grad_row, counts_ref):
    channels = grad_row.shape[1]
    parts = []
    for t, wet in enumerate(wet_row(i, counts_ref)):
        piece = grad_row[t * 8 : (t + 1) * 8]
        parts.append(
            jnp.concatenate(
                [
                    jnp.where(wet, piece[:, c * lanes : (c + 1) * lanes], 0.0)
                    for c in range(channels // lanes)
                ],
                axis=1,
            )
        )
    return jnp.concatenate(parts, axis=0)


def mask_rows_body(counts_ref, grad_ref, rows_ref):
    def step(i, carry):
        at = pl.ds(pl.multiple_of(i * side, side), side)
        rows_ref[at, :] = masked_row(i, grad_ref[at, :], counts_ref).astype(bf16)
        return carry

    lax.fori_loop(0, side, step, 0, unroll=2)


def mask_rows(counts, grad):
    total, channels = grad.shape
    return pl.pallas_call(
        mask_rows_body,
        out_shape=jax.ShapeDtypeStruct((total, channels), bf16),
        in_specs=[pl.BlockSpec(memory_space=pltpu.SMEM), whole],
        out_specs=whole,
        compiler_params=params(8),
        cost_estimate=cost(0.9),
        name="mask_rows",
    )(counts, grad)


def arrange_body(expand_ref, reduce_ref, bias_ref, expand_out, reduce_out, turned_out, bias_out):
    unit_row = lax.broadcasted_iota(jnp.int32, (48, 96), 0)
    unit_col = lax.broadcasted_iota(jnp.int32, (48, 96), 1)
    picks = [unit_col == (unit_row // 6) * 12 + lo * 6 + unit_row % 6 for lo in range(2)]
    chosen = [pick.astype(f32).astype(bf16) for pick in picks]
    for hi, y, core in itertools.product(range(2), range(4), range(2)):
        unit = (hi * 4 + y) * 2 + core
        at = slice(unit * 96, (unit + 1) * 96)
        expand, reduce = expand_ref[at, :], reduce_ref[at, :]
        bias = bias_ref[:, at]
        for lo in range(2):
            x = 2 * hi + lo
            place = core * 16 + (y * 4 + x if core == 0 else x * 4 + y)
            to = slice(place * 48, (place + 1) * 48)
            expand_out[to, :] = jnp.dot(chosen[lo], expand, preferred_element_type=f32).astype(bf16)
            reduce_out[to, :] = jnp.dot(chosen[lo], reduce, preferred_element_type=f32).astype(bf16)
            column = jnp.sum(jnp.where(picks[lo], bias, 0.0), axis=1, keepdims=True)
            bias_out[to, :] = jnp.broadcast_to(column, (48, lanes))
    turn(expand_out, turned_out)


def arrange(expand, reduce, bias):
    units, channels = expand.shape
    shape = jax.ShapeDtypeStruct((units, channels), bf16)
    return pl.pallas_call(
        arrange_body,
        out_shape=(
            shape,
            shape,
            jax.ShapeDtypeStruct((channels, units), bf16),
            jax.ShapeDtypeStruct((units, lanes), f32),
        ),
        in_specs=[whole] * 3,
        out_specs=[whole] * 4,
        compiler_params=params(12),
        cost_estimate=cost(1.5),
        name="arrange",
    )(expand, reduce, bias)


tail_slope = 0.3275911 * 0.7071067811865476
tail_terms = [
    0.5 * a for a in (0.254829592, -0.284496736, 1.421413741, -1.453152027, 1.061405429)
]
exp_scale = -0.5 * 1.4426950408889634


def gelu_pair(v):
    d = 1.0 + tail_slope * jnp.abs(v)
    t = pltpu.reciprocal(d, approx=True)
    poly = tail_terms[4]
    for a in reversed(tail_terms[:4]):
        poly = poly * t + a
    bell = jnp.exp2(v * v * exp_scale)
    tail = poly * t * bell
    below = jnp.where(v >= 0.0, 1.0 - tail, tail)
    return v * below, below + v * bell * inv_root_two_pi


def own_place():
    lat, lon = lax.axis_index("lat"), lax.axis_index("lon")
    x = 2 * lax.axis_index("dp") + (lon & 1)
    return lat & 1, x, lat >> 1, lon >> 1


def phase_place(second):
    core, x, y, _ = own_place()
    along_y = core == (1 if second else 0)
    return jnp.where(along_y, y, x)


def dot_rows(left, right):
    return lax.dot_general(left, right, (((1,), (1,)), ((), ())), preferred_element_type=f32)


def hidden_rows(cells, source, rows, grad_pre_ref, to):
    normed_ref, grad_ref, expand_ref, reduce_ref, bias_ref = cells
    total = normed_ref.shape[0]
    at = pl.ds(source, rows)
    preact = dot_rows(expand_ref[at, :], normed_ref[...])
    grad_hidden = dot_rows(reduce_ref[at, :], grad_ref[...])
    bias = jnp.concatenate([bias_ref[at, :]] * (total // lanes), axis=1)
    value, slope = gelu_pair(preact + bias)
    hidden = value.astype(bf16)
    grad_pre = (grad_hidden * slope).astype(bf16)
    grad_pre_ref[pl.ds(to, rows), :] = grad_pre
    return (
        jnp.dot(grad_pre, normed_ref[...], preferred_element_type=f32),
        jnp.dot(hidden, grad_ref[...], preferred_element_type=f32),
    )


def far_body(*refs):
    cells, (sent_ref, grad_pre_ref) = refs[:5], refs[5:]
    half = grad_pre_ref.shape[0]
    channels = refs[0].shape[1]
    base = (1 - own_place()[0]) * half
    rows = 256
    for b in range(half // rows):
        source = pl.multiple_of(base + b * rows, rows)
        expand, reduce = hidden_rows(cells, source, rows, grad_pre_ref, b * rows)
        at = slice(b * rows, (b + 1) * rows)
        sent_ref[at, :channels] = expand.astype(bf16)
        sent_ref[at, channels:] = reduce.astype(bf16)


def hidden_far(*cells):
    total, channels = cells[0].shape
    half = cells[2].shape[0] // 2
    return pl.pallas_call(
        far_body,
        out_shape=(
            jax.ShapeDtypeStruct((half, 2 * channels), bf16),
            jax.ShapeDtypeStruct((half, total), bf16),
        ),
        in_specs=[whole] * 5,
        out_specs=[whole] * 2,
        compiler_params=params(16),
        cost_estimate=cost(5.8),
        name="hidden_far",
    )(*cells)


def near_first_body(*refs):
    cells, (sums_ref, grad_pre_ref) = refs[:5], refs[5:]
    half = grad_pre_ref.shape[0]
    channels = refs[0].shape[1]
    size = half // 4
    core, place = own_place()[0], phase_place(False)
    for step in (1, 2):
        chunk = pl.multiple_of(lax.rem(place + step, 4) * size, size)
        source = pl.multiple_of(core * half + chunk, size)
        expand, reduce = hidden_rows(cells, source, size, grad_pre_ref, chunk)
        at = slice((step - 1) * size, step * size)
        sums_ref[at, :channels] = expand
        sums_ref[at, channels:] = reduce


def near_first(*cells):
    total, channels = cells[0].shape
    half = cells[2].shape[0] // 2
    return pl.pallas_call(
        near_first_body,
        out_shape=(
            jax.ShapeDtypeStruct((half // 2, 2 * channels), f32),
            jax.ShapeDtypeStruct((half, total), bf16),
        ),
        in_specs=[whole] * 5,
        out_specs=[whole] * 2,
        compiler_params=params(16),
        cost_estimate=cost(3.0),
        name="near_first",
    )(*cells)


def near_sends_body(sums_ref, arrived_ref, *sent_refs):
    size = sent_refs[0].shape[0]
    place = phase_place(False)
    for step in (1, 2):
        chunk = pl.multiple_of(lax.rem(place + step, 4) * size, size)
        total = sums_ref[(step - 1) * size : step * size] + arrived_ref[pl.ds(chunk, size), :].astype(f32)
        sent_refs[step - 1][...] = total.astype(bf16)


def near_sends(sums, arrived):
    size, width = sums.shape[0] // 2, sums.shape[1]
    sent = jax.ShapeDtypeStruct((size, width), bf16)
    return pl.pallas_call(
        near_sends_body,
        out_shape=(sent, sent),
        in_specs=[whole] * 2,
        out_specs=[whole] * 2,
        compiler_params=params(6),
        cost_estimate=cost(0.3),
        name="near_sends",
    )(sums, arrived)


def near_last_body(*refs):
    cells, (arrived_ref, _, own_ref, sent_ref, grad_pre_ref) = refs[:5], refs[5:]
    half = grad_pre_ref.shape[0]
    channels = refs[0].shape[1]
    size = half // 4
    core, place = own_place()[0], phase_place(False)
    for step, ref in ((3, sent_ref), (0, own_ref)):
        chunk = pl.multiple_of(lax.rem(place + step, 4) * size, size)
        source = pl.multiple_of(core * half + chunk, size)
        expand, reduce = hidden_rows(cells, source, size, grad_pre_ref, chunk)
        other = arrived_ref[pl.ds(chunk, size), :].astype(f32)
        ref[:, :channels] = (expand + other[:, :channels]).astype(ref.dtype)
        ref[:, channels:] = (reduce + other[:, channels:]).astype(ref.dtype)


def near_last(*inputs):
    cells, grad_pre = inputs[:5], inputs[6]
    channels = cells[0].shape[1]
    size = cells[2].shape[0] // 8
    return pl.pallas_call(
        near_last_body,
        out_shape=(
            jax.ShapeDtypeStruct((size, 2 * channels), f32),
            jax.ShapeDtypeStruct((size, 2 * channels), bf16),
            jax.ShapeDtypeStruct(grad_pre.shape, bf16),
        ),
        in_specs=[whole] * 7,
        out_specs=[whole] * 3,
        input_output_aliases={6: 2},
        compiler_params=params(16),
        cost_estimate=cost(3.0),
        name="near_last",
    )(*inputs)


def norm_back_body(
    turned_ref, other_ref, mine_ref, unit_ref, spread_ref, gain_ref,
    conv_grad_ref, first_ref, last_ref,
):
    total, channels = unit_ref.shape
    half = turned_ref.shape[1] // 2
    core = own_place()[0]
    block = 256
    share = 1.0 / channels
    mine_weight = turned_ref[:, pl.ds(pl.multiple_of(core * half, half), half)]
    other_weight = turned_ref[:, pl.ds(pl.multiple_of((1 - core) * half, half), half)]
    for b in range(total // block):
        at = slice(b * block, (b + 1) * block)
        summed = jnp.dot(mine_weight, mine_ref[:, at], preferred_element_type=f32)
        summed = summed + jnp.dot(other_weight, other_ref[:, at], preferred_element_type=f32)
        grad_normed = summed.astype(bf16).T.astype(f32)
        unit = unit_ref[at, :]
        grad_unit = grad_normed * gain_ref[...]
        mean_grad = jnp.sum(grad_unit, axis=1, keepdims=True) * share
        mean_cross = jnp.sum(grad_unit * unit, axis=1, keepdims=True) * share
        spread = jnp.concatenate([spread_ref[at, :]] * (channels // lanes), axis=1)
        value = (grad_unit - mean_grad - unit * mean_cross) * spread
        conv_grad_ref[b * 8 : (b + 1) * 8] = value.reshape(block // side, side, channels)
    for j in range(reach):
        first_ref[j] = conv_grad_ref[:, j, :].astype(bf16)
        last_ref[j] = conv_grad_ref[:, side - reach + j, :].astype(bf16)


def norm_back(turned, other, mine, unit, spread, gain):
    total, channels = unit.shape
    shape = jax.ShapeDtypeStruct((reach, side, channels), bf16)
    found, first, last = pl.pallas_call(
        norm_back_body,
        out_shape=(jax.ShapeDtypeStruct((side, side, channels), f32), shape, shape),
        in_specs=[whole] * 6,
        out_specs=[whole] * 3,
        compiler_params=params(14),
        cost_estimate=cost(2.2),
        name="norm_back",
    )(turned, other, mine, unit, spread, gain)
    return found.reshape(total, channels), first, last


def finish_body(
    counts_ref, conv0_ref, conv1_ref, conv2_ref, kernel_ref, left_ref, right_ref, top_ref, bottom_ref,
    grad_ref, out_ref, rows_sum, cols_sum,
):
    conv_refs = (conv0_ref, conv1_ref, conv2_ref)
    rows = out_ref.shape[0] // side
    steps = side // rows
    block = pl.program_id(0)

    @pl.when(block == 0)
    def _():
        add_edges(True, kernel_ref, left_ref, right_ref, top_ref, bottom_ref, rows_sum, cols_sum)

    def write(outer_of):
        for r in range(rows):
            i = block * rows + r
            at = pl.ds(pl.multiple_of(i * side, side), side)
            value = edged_row(i, conv_rows(conv_refs, at), cols_sum)
            outer = outer_of(r)
            if outer is not None:
                value = value + rows_sum[outer]
            out_ref[r * side : (r + 1) * side, :] = value + masked_row(i, grad_ref[at, :], counts_ref)

    @pl.when(block == 0)
    def _():
        write(lambda r: r if r < reach else None)

    @pl.when(jnp.logical_and(block > 0, block < steps - 1))
    def _():
        write(lambda r: None)

    @pl.when(block == steps - 1)
    def _():
        write(lambda r: r - (rows - 2 * reach) if r >= rows - reach else None)


def finish(counts, conv, kernel, left, right, top, bottom, grad):
    total, channels = grad.shape
    rows = 8
    return pl.pallas_call(
        finish_body,
        out_shape=jax.ShapeDtypeStruct((total, channels), f32),
        grid=(side // rows,),
        in_specs=[pl.BlockSpec(memory_space=pltpu.SMEM)] + [whole] * 9,
        out_specs=pl.BlockSpec((rows * side, channels), lambda b: (b, 0)),
        scratch_shapes=[pltpu.VMEM((2 * reach, side, channels), f32)] * 2,
        compiler_params=params(12),
        cost_estimate=cost(2.2),
        name="finish",
    )(counts, *conv, kernel, left, right, top, bottom, grad)


def split_four_body(own_ref, first_ref, second_ref, third_ref, kept_ref, *sent_refs):
    size = kept_ref.shape[0]
    place = phase_place(True)
    for step in range(4):
        at = pl.ds(pl.multiple_of(lax.rem(place + step, 4) * size, size), size)
        total = own_ref[at, :]
        for ref in (first_ref, second_ref, third_ref):
            total = total + ref[at, :].astype(f32)
        if step == 0:
            kept_ref[...] = total
        else:
            sent_refs[step - 1][...] = total.astype(bf16)


def split_four(own, parts):
    size, width = own.shape[0] // 4, own.shape[1]
    sent = jax.ShapeDtypeStruct((size, width), bf16)
    return pl.pallas_call(
        split_four_body,
        out_shape=(jax.ShapeDtypeStruct((size, width), f32), sent, sent, sent),
        in_specs=[whole] * 4,
        out_specs=[whole] * 4,
        compiler_params=params(4),
        cost_estimate=cost(0.3),
        name="split_four",
    )(own, *parts)


def split_two_body(bit, own_ref, *refs):
    part_refs, (kept_ref, sent_ref) = refs[:-2], refs[-2:]
    size = kept_ref.shape[0]
    total = own_ref[...]
    for ref in part_refs:
        total = total + ref[...].astype(f32)
    low, high = total[:size], total[size:]
    upper = (own_place()[3] & bit) != 0
    kept_ref[...] = jnp.where(upper, high, low)
    sent_ref[...] = jnp.where(upper, low, high)


def split_two(bit, own, parts):
    shape = jax.ShapeDtypeStruct((own.shape[0] // 2, own.shape[1]), f32)
    return pl.pallas_call(
        functools.partial(split_two_body, bit),
        out_shape=(shape, shape),
        in_specs=[whole] * (1 + len(parts)),
        out_specs=[whole] * 2,
        compiler_params=params(4),
        cost_estimate=cost(0.2),
        name="split_two",
    )(own, *parts)


def last_sum_body(scale, own_ref, arrived_ref, expand_ref, reduce_ref):
    channels = expand_ref.shape[2]
    total = (own_ref[...] + arrived_ref[...]) * scale
    for r in range(total.shape[0]):
        expand_ref[r] = total[r : r + 1, :channels]
        reduce_ref[r] = total[r : r + 1, channels:]


def last_sum(own, arrived, scale):
    size, width = own.shape
    shape = jax.ShapeDtypeStruct((size, 1, width // 2), f32)
    expand, reduce = pl.pallas_call(
        functools.partial(last_sum_body, scale),
        out_shape=(shape, shape),
        in_specs=[whole] * 2,
        out_specs=[whole] * 2,
        compiler_params=params(4),
        cost_estimate=cost(0.4),
        name="last_sum",
    )(own, arrived)
    return expand.transpose(1, 0, 2), reduce.transpose(1, 0, 2)


every_axis = ("dp", "lat", "lon")


def device_pairs(move):
    def flat(hi, y, core, z, lo):
        return (hi * 8 + y * 2 + core) * 16 + z * 2 + lo

    found = []
    for hi, y, core, z, lo in itertools.product(range(2), range(4), range(2), range(8), range(2)):
        found.append((flat(hi, y, core, z, lo), flat(*move(hi, y, core, z, lo))))
    return found


def plane_pairs(step, first):
    def move(hi, y, core, z, lo):
        if (core == 0) == first:
            return (hi, (y + step) % 4, core, z, lo)
        x = (2 * hi + lo + step) % 4
        return (x // 2, y, core, z, x % 2)

    return device_pairs(move)


def halving_pairs(bit):
    return device_pairs(lambda hi, y, core, z, lo: (hi, y, core, z ^ bit, lo))


def shifted(axis, step, closed):
    count = lax.axis_size(axis)
    found = []
    for i in range(count):
        j = i + step
        if closed or 0 <= j < count:
            found.append((i, j % count))
    return found


def lon_halo(first, last):
    left = lax.ppermute(last, "lon", shifted("lon", 1, True))
    right = lax.ppermute(first, "lon", shifted("lon", -1, True))
    return left, right


def lat_halo(up, down):
    top = lax.ppermute(down, "lat", shifted("lat", 1, False))
    bottom = lax.ppermute(up, "lat", shifted("lat", -1, False))
    return top, bottom


def after(value, *others):
    return lax.optimization_barrier((value, others))[0]


def local(
    state, cotangent, counts, dw_kernel, dw_bias, norm_gain, norm_bias, w_expand, b_expand, w_reduce
):
    channels = state.shape[-1]
    cells = state.reshape(-1, channels)
    grad = cotangent.reshape(-1, channels)
    total = cells.shape[0]
    kernel = dw_kernel.transpose(1, 0, 2)

    left, right = lon_halo(*side_cols(cells))
    rows = mask_rows(counts, grad)
    expand, reduce, expand_t, bias = arrange(w_expand[0], w_reduce[0], b_expand)
    left, right = after((left, right), rows, bias)
    up, down = side_rows(cells, left, right)
    top, bottom = lat_halo(up, down)
    conv = inner_conv(after(cells, up, down), kernel, False, (0, 1, 2))
    unit, spread, normed = normalise(
        conv, kernel, left, right, top, bottom, dw_bias, norm_gain, norm_bias
    )

    inputs = (normed, rows, expand, reduce, bias)
    sent, far_pre = hidden_far(*inputs)
    arrived = lax.ppermute(sent, "lat", [(i, i ^ 1) for i in range(8)])
    sums, near_pre = near_first(*inputs)
    one, two = near_sends(sums, arrived)
    part_one = lax.ppermute(one, every_axis, plane_pairs(1, True))
    part_two = lax.ppermute(two, every_axis, plane_pairs(2, True))
    own, three, near_pre = near_last(*inputs, arrived, after(near_pre, one, two))
    part_three = lax.ppermute(three, every_axis, plane_pairs(3, True))

    far_pre = after(far_pre, three)
    conv_grad, first, last = norm_back(expand_t, far_pre, near_pre, unit, spread, norm_gain)
    left, right = lon_halo(first, last)
    back = inner_conv(after(conv_grad, first, last), kernel, True, (0,))

    own, parts = after((own, (part_one, part_two, part_three)), left, right, back)
    own, *sent = split_four(own, parts)
    parts = [lax.ppermute(s, every_axis, plane_pairs(i + 1, False)) for i, s in enumerate(sent)]
    conv_grad = after(conv_grad, sent)
    up, down = side_rows(conv_grad, left, right)

    own, sent = split_two(4, *after((own, parts), up, down))
    top, bottom = lat_halo(up, down)
    arrived = lax.ppermute(sent, every_axis, halving_pairs(4))
    conv_grad = after(conv_grad, sent)
    back += inner_conv(conv_grad, kernel, True, (1,))

    own, sent = split_two(2, *after((own, [arrived]), back))
    arrived = lax.ppermute(sent, every_axis, halving_pairs(2))
    conv_grad = after(conv_grad, sent)
    back += inner_conv(conv_grad, kernel, True, (2,))

    own, sent = split_two(1, *after((own, [arrived]), back, top, bottom))
    arrived = lax.ppermute(sent, every_axis, halving_pairs(1))
    grad = after(grad, sent)
    gradient = finish(counts, back, kernel, left, right, top, bottom, grad)

    cells_all = lax.axis_size("dp") * lax.axis_size("lat") * lax.axis_size("lon") * total
    kept = last_sum(own, arrived, 1.0 / math.sqrt(cells_all))
    return (gradient.reshape(state.shape), *kept)


def solution(mesh):
    in_specs = (
        P("dp", "lat", "lon", None),
        P("dp", "lat", "lon", None),
        P("lat", "lon"),
        P(),
        P(),
        P(),
        P(),
        P(),
        P(),
        P(),
    )
    out_specs = (
        P("dp", "lat", "lon", None),
        P(None, ("dp", "lat", "lon"), None),
        P(None, ("dp", "lat", "lon"), None),
    )
    return jax.shard_map(local, mesh=mesh, in_specs=in_specs, out_specs=out_specs, check_vma=False)
```

```python
import functools
import itertools
import math

import jax
import jax.numpy as jnp
from jax import lax
from jax.experimental import pallas as pl
from jax.experimental.pallas import tpu as pltpu
from jax.sharding import PartitionSpec as P

norm_eps = 1e-06
inv_root_two_pi = 0.3989422804014327
side = 32
reach = 3
lanes = 128
f32 = jnp.float32
bf16 = jnp.bfloat16
whole = pl.BlockSpec(memory_space=pltpu.VMEM)


def params(mib):
    return pltpu.CompilerParams(vmem_limit_bytes=mib * 1024 * 1024)


def cost(microseconds):
    return pl.CostEstimate(
        flops=int(microseconds * 1.15e9), bytes_accessed=2**20, transcendentals=0
    )


def tap_row(kernel_ref, flipped, p, q, cols):
    index = 7 * p + q
    if flipped:
        index = 48 - index
    return kernel_ref[index, :, cols]


def shift_cols(rows, offset):
    if offset == 0:
        return rows
    count = rows.shape[0]
    turned = pltpu.roll(rows, (-offset) % count, 0)
    place = lax.broadcasted_iota(jnp.int32, (8, rows.shape[1]), 0)
    if offset > 0:
        last = jnp.where(place < 8 - offset, turned[count - 8 :], 0.0)
        return jnp.concatenate([turned[: count - 8], last], axis=0)
    first = jnp.where(place >= -offset, turned[:8], 0.0)
    return jnp.concatenate([first, turned[8:]], axis=0)


def inner_conv_body(flipped, parts, cells_ref, kernel_ref, *refs):
    outs, padded = refs[:-1], refs[-1]
    edge = reach * side
    total = side * side
    padded[0:edge] = jnp.zeros((edge, lanes), f32)
    padded[edge + total : 2 * edge + total] = jnp.zeros((edge, lanes), f32)
    for part, out_ref in zip(parts, outs):
        cols = slice(part * lanes, (part + 1) * lanes)
        padded[edge : edge + total] = cells_ref[:, cols]

        def two_rows(i, carry):
            base = pl.multiple_of(i * (2 * side), 2 * side)
            rows = [padded[pl.ds(base + p * side, side), :] for p in range(8)]
            results = [None, None]
            for q in range(7):
                sums = [None, None]
                for p in range(7):
                    tap = tap_row(kernel_ref, flipped, p, q, cols)
                    for g in range(2):
                        term = tap * rows[p + g]
                        sums[g] = term if sums[g] is None else sums[g] + term
                for g in range(2):
                    moved = shift_cols(sums[g], q - reach)
                    results[g] = moved if results[g] is None else results[g] + moved
            for g in range(2):
                out_ref[pl.ds(base + g * side, side), :] = results[g]
            return carry

        lax.fori_loop(0, side // 2, two_rows, 0)


def inner_conv(cells, kernel, flipped, parts):
    total = cells.shape[0]
    shape = jax.ShapeDtypeStruct((total, lanes), f32)
    return pl.pallas_call(
        functools.partial(inner_conv_body, flipped, parts),
        out_shape=(shape,) * len(parts),
        in_specs=[whole] * 2,
        out_specs=[whole] * len(parts),
        scratch_shapes=[pltpu.VMEM((total + 2 * reach * side, lanes), f32)],
        compiler_params=params(6),
        cost_estimate=cost(2.3 * len(parts)),
        name="inner_conv",
    )(cells, kernel)


def side_cols_body(cells_ref, first_ref, last_ref, low, high, sems):
    copies = [
        pltpu.make_async_copy(cells_ref.at[:, pl.ds(0, 8), :], low, sems.at[0]),
        pltpu.make_async_copy(cells_ref.at[:, pl.ds(side - 8, 8), :], high, sems.at[1]),
    ]
    for copy in copies:
        copy.start()
    copies[0].wait()
    for j in range(reach):
        first_ref[j] = low[:, j, :].astype(bf16)
    copies[1].wait()
    for j in range(reach):
        last_ref[j] = high[:, 8 - reach + j, :].astype(bf16)


def side_cols(cells):
    channels = cells.shape[1]
    shape = jax.ShapeDtypeStruct((reach, side, channels), bf16)
    return pl.pallas_call(
        side_cols_body,
        out_shape=(shape, shape),
        in_specs=[pl.BlockSpec(memory_space=pltpu.HBM)],
        out_specs=[whole] * 2,
        scratch_shapes=[pltpu.VMEM((side, 8, channels), f32)] * 2 + [pltpu.SemaphoreType.DMA((2,))],
        compiler_params=params(58),
        cost_estimate=cost(1.0),
        name="side_cols",
    )(cells.reshape(side, side, channels))


def side_rows_body(cells_ref, left_ref, right_ref, up_ref, down_ref):
    channels = cells_ref.shape[1]
    place = lax.broadcasted_iota(jnp.int32, (8, channels), 0)
    blank = jnp.zeros((8, channels), f32)
    left = [left_ref[h].astype(f32) for h in range(reach)]
    right = [right_ref[h].astype(f32) for h in range(reach)]
    for r in range(reach):
        for row, ref in ((r, up_ref), (side - reach + r, down_ref)):
            corner = blank
            for h in range(reach):
                corner = jnp.where(place == h, right[h][row : row + 1], corner)
                corner = jnp.where(place == 8 - reach + h, left[h][row : row + 1], corner)
            body = cells_ref[row * side : (row + 1) * side]
            ref[r] = jnp.concatenate([body, corner, blank], axis=0).astype(bf16)


def side_rows(cells, left, right):
    channels = cells.shape[1]
    shape = jax.ShapeDtypeStruct((reach, side + 16, channels), bf16)
    return pl.pallas_call(
        side_rows_body,
        out_shape=(shape, shape),
        in_specs=[whole] * 3,
        out_specs=[whole] * 2,
        compiler_params=params(6),
        cost_estimate=cost(0.5),
        name="side_rows",
    )(cells, left, right)


def add_edges(flipped, kernel_ref, left_ref, right_ref, top_ref, bottom_ref, rows_sum, cols_sum):
    lat = lax.axis_index("lat")
    channels = kernel_ref.shape[2]
    for c in range(channels // lanes):
        cols = slice(c * lanes, (c + 1) * lanes)
        for low, ref in ((True, top_ref), (False, bottom_ref)):
            outside = lat == (0 if low else lax.axis_size("lat") - 1)
            beyond = [
                jnp.where(outside, 0.0, ref[h, :, cols].astype(f32)[: side + 8]) for h in range(reach)
            ]
            for r in range(reach):
                result = None
                steps = [(h, h - r) for h in range(r, reach)] if low else [
                    (h, 6 + h - r) for h in range(0, r + 1)
                ]
                for q in range(7):
                    summed = None
                    for h, p in steps:
                        term = tap_row(kernel_ref, flipped, p, q, cols) * beyond[h]
                        summed = term if summed is None else summed + term
                    summed = pltpu.roll(summed, (reach - q) % (side + 8), 0) if q != reach else summed
                    result = summed if result is None else result + summed
                rows_sum[r if low else reach + r, :, cols] = result[:side]
        for low, ref in ((True, left_ref), (False, right_ref)):
            beyond = [ref[h, :, cols].astype(f32) for h in range(reach)]
            for r in range(reach):
                steps = [(h, h - r) for h in range(r, reach)] if low else [
                    (h, 6 + h - r) for h in range(0, r + 1)
                ]
                result = None
                for p in range(7):
                    summed = None
                    for h, q in steps:
                        term = tap_row(kernel_ref, flipped, p, q, cols) * beyond[h]
                        summed = term if summed is None else summed + term
                    summed = shift_cols(summed, p - reach)
                    result = summed if result is None else result + summed
                cols_sum[r if low else reach + r, :, cols] = result


def edged_row(i, conv_row, cols_sum):
    channels = conv_row.shape[1]
    place = lax.broadcasted_iota(jnp.int32, (8, channels), 0)
    first, last = conv_row[:8], conv_row[side - 8 :]
    for r in range(reach):
        first = first + jnp.where(place == r, cols_sum[r, pl.ds(i, 1), :], 0.0)
        last = last + jnp.where(place == 8 - reach + r, cols_sum[reach + r, pl.ds(i, 1), :], 0.0)
    return jnp.concatenate([first, conv_row[8 : side - 8], last], axis=0)


def each_row(step):
    def low(i, carry):
        step(i, i)
        return carry

    def middle(i, carry):
        step(i, None)
        return carry

    def high(i, carry):
        step(i, i - (side - 2 * reach))
        return carry

    lax.fori_loop(0, reach, low, 0, unroll=reach)
    lax.fori_loop(reach, side - reach, middle, 0, unroll=side // 2 - reach)
    lax.fori_loop(side - reach, side, high, 0, unroll=reach)


def conv_rows(refs, at):
    return jnp.concatenate([ref[at, :] for ref in refs], axis=1)


def normalise_body(
    conv0_ref, conv1_ref, conv2_ref, kernel_ref, left_ref, right_ref, top_ref, bottom_ref, bias_ref, gain_ref, shift_ref,
    unit_ref, spread_ref, normed_ref, rows_sum, cols_sum,
):
    channels = kernel_ref.shape[2]
    conv_refs = (conv0_ref, conv1_ref, conv2_ref)
    add_edges(False, kernel_ref, left_ref, right_ref, top_ref, bottom_ref, rows_sum, cols_sum)
    share = 1.0 / channels

    def step(i, outer):
        at = pl.ds(pl.multiple_of(i * side, side), side)
        value = edged_row(i, conv_rows(conv_refs, at), cols_sum)
        if outer is not None:
            value = value + rows_sum[outer]
        value = value + bias_ref[...]
        mean = jnp.sum(value, axis=1, keepdims=True) * share
        centred = value - mean
        spread = lax.rsqrt(jnp.sum(centred * centred, axis=1, keepdims=True) * share + norm_eps)
        unit = centred * spread
        unit_ref[at, :] = unit
        spread_ref[at, :] = jnp.broadcast_to(spread, (side, lanes))
        normed_ref[at, :] = (unit * gain_ref[...] + shift_ref[...]).astype(bf16)

    each_row(step)


def turn(source_ref, target_ref):
    for b in range(source_ref.shape[0] // 256):
        at = slice(b * 256, (b + 1) * 256)
        target_ref[:, at] = source_ref[at, :].T


def normalise(conv, kernel, left, right, top, bottom, bias, gain, shift):
    total, channels = conv[0].shape[0], kernel.shape[2]
    return pl.pallas_call(
        normalise_body,
        out_shape=(
            jax.ShapeDtypeStruct((total, channels), f32),
            jax.ShapeDtypeStruct((total, lanes), f32),
            jax.ShapeDtypeStruct((total, channels), bf16),
        ),
        in_specs=[whole] * 11,
        out_specs=[whole] * 3,
        scratch_shapes=[pltpu.VMEM((2 * reach, side, channels), f32)] * 2,
        compiler_params=params(12),
        cost_estimate=cost(2.8),
        name="normalise",
    )(*conv, kernel, left, right, top, bottom, bias, gain, shift)


def wet_row(i, counts_ref):
    place = lax.broadcasted_iota(jnp.int32, (8, lanes), 0) + (i % 8) * 8
    pieces = []
    for t in range(side // 8):
        pieces.append(place < counts_ref[i // 8, t])
    return pieces


def masked_row(i, grad_row, counts_ref):
    channels = grad_row.shape[1]
    parts = []
    for t, wet in enumerate(wet_row(i, counts_ref)):
        piece = grad_row[t * 8 : (t + 1) * 8]
        parts.append(
            jnp.concatenate(
                [
                    jnp.where(wet, piece[:, c * lanes : (c + 1) * lanes], 0.0)
                    for c in range(channels // lanes)
                ],
                axis=1,
            )
        )
    return jnp.concatenate(parts, axis=0)


def mask_rows_body(counts_ref, grad_ref, rows_ref):
    def step(i, carry):
        at = pl.ds(pl.multiple_of(i * side, side), side)
        rows_ref[at, :] = masked_row(i, grad_ref[at, :], counts_ref).astype(bf16)
        return carry

    lax.fori_loop(0, side, step, 0, unroll=2)


def mask_rows(counts, grad):
    total, channels = grad.shape
    return pl.pallas_call(
        mask_rows_body,
        out_shape=jax.ShapeDtypeStruct((total, channels), bf16),
        in_specs=[pl.BlockSpec(memory_space=pltpu.SMEM), whole],
        out_specs=whole,
        compiler_params=params(8),
        cost_estimate=cost(0.9),
        name="mask_rows",
    )(counts, grad)


def arrange_body(expand_ref, reduce_ref, bias_ref, expand_out, reduce_out, turned_out, bias_out):
    unit_row = lax.broadcasted_iota(jnp.int32, (48, 96), 0)
    unit_col = lax.broadcasted_iota(jnp.int32, (48, 96), 1)
    picks = [unit_col == (unit_row // 6) * 12 + lo * 6 + unit_row % 6 for lo in range(2)]
    chosen = [pick.astype(f32).astype(bf16) for pick in picks]
    for hi, y, core in itertools.product(range(2), range(4), range(2)):
        unit = (hi * 4 + y) * 2 + core
        at = slice(unit * 96, (unit + 1) * 96)
        expand, reduce = expand_ref[at, :], reduce_ref[at, :]
        bias = bias_ref[:, at]
        for lo in range(2):
            x = 2 * hi + lo
            place = core * 16 + (y * 4 + x if core == 0 else x * 4 + y)
            to = slice(place * 48, (place + 1) * 48)
            expand_out[to, :] = jnp.dot(chosen[lo], expand, preferred_element_type=f32).astype(bf16)
            reduce_out[to, :] = jnp.dot(chosen[lo], reduce, preferred_element_type=f32).astype(bf16)
            column = jnp.sum(jnp.where(picks[lo], bias, 0.0), axis=1, keepdims=True)
            bias_out[to, :] = jnp.broadcast_to(column, (48, lanes))
    turn(expand_out, turned_out)


def arrange(expand, reduce, bias):
    units, channels = expand.shape
    shape = jax.ShapeDtypeStruct((units, channels), bf16)
    return pl.pallas_call(
        arrange_body,
        out_shape=(
            shape,
            shape,
            jax.ShapeDtypeStruct((channels, units), bf16),
            jax.ShapeDtypeStruct((units, lanes), f32),
        ),
        in_specs=[whole] * 3,
        out_specs=[whole] * 4,
        compiler_params=params(12),
        cost_estimate=cost(1.5),
        name="arrange",
    )(expand, reduce, bias)


tail_slope = 0.3275911 * 0.7071067811865476
tail_terms = [
    0.5 * a for a in (0.254829592, -0.284496736, 1.421413741, -1.453152027, 1.061405429)
]
exp_scale = -0.5 * 1.4426950408889634


def gelu_pair(v):
    d = 1.0 + tail_slope * jnp.abs(v)
    t = pltpu.reciprocal(d, approx=True)
    poly = tail_terms[4]
    for a in reversed(tail_terms[:4]):
        poly = poly * t + a
    bell = jnp.exp2(v * v * exp_scale)
    tail = poly * t * bell
    below = jnp.where(v >= 0.0, 1.0 - tail, tail)
    return v * below, below + v * bell * inv_root_two_pi


def own_place():
    lat, lon = lax.axis_index("lat"), lax.axis_index("lon")
    x = 2 * lax.axis_index("dp") + (lon & 1)
    return lat & 1, x, lat >> 1, lon >> 1


def phase_place(second):
    core, x, y, _ = own_place()
    along_y = core == (1 if second else 0)
    return jnp.where(along_y, y, x)


def dot_rows(left, right):
    return lax.dot_general(left, right, (((1,), (1,)), ((), ())), preferred_element_type=f32)


def hidden_rows(cells, sources, rows, grad_pre_ref, places):
    normed_ref, grad_ref, expand_ref, reduce_ref, bias_ref = cells
    total = normed_ref.shape[0]

    def gather(ref):
        return jnp.concatenate([ref[pl.ds(source, rows), :] for source in sources], axis=0)

    preact = dot_rows(gather(expand_ref), normed_ref[...])
    grad_hidden = dot_rows(gather(reduce_ref), grad_ref[...])
    bias = jnp.concatenate([gather(bias_ref)] * (total // lanes), axis=1)
    value, slope = gelu_pair(preact + bias)
    hidden = value.astype(bf16)
    grad_pre = (grad_hidden * slope).astype(bf16)
    for n, place in enumerate(places):
        grad_pre_ref[pl.ds(place, rows), :] = grad_pre[n * rows : (n + 1) * rows]
    return (
        jnp.dot(grad_pre, normed_ref[...], preferred_element_type=f32),
        jnp.dot(hidden, grad_ref[...], preferred_element_type=f32),
    )


def far_body(*refs):
    cells, (sent_ref, grad_pre_ref) = refs[:5], refs[5:]
    half = grad_pre_ref.shape[0]
    channels = refs[0].shape[1]
    base = (1 - own_place()[0]) * half
    rows = half // 2
    for b in range(half // rows):
        source = pl.multiple_of(base + b * rows, rows)
        expand, reduce = hidden_rows(cells, [source], rows, grad_pre_ref, [b * rows])
        at = slice(b * rows, (b + 1) * rows)
        sent_ref[at, :channels] = expand.astype(bf16)
        sent_ref[at, channels:] = reduce.astype(bf16)


def hidden_far(*cells):
    total, channels = cells[0].shape
    half = cells[2].shape[0] // 2
    return pl.pallas_call(
        far_body,
        out_shape=(
            jax.ShapeDtypeStruct((half, 2 * channels), bf16),
            jax.ShapeDtypeStruct((half, total), bf16),
        ),
        in_specs=[whole] * 5,
        out_specs=[whole] * 2,
        compiler_params=params(16),
        cost_estimate=cost(5.8),
        name="hidden_far",
    )(*cells)


def near_first_body(*refs):
    cells, (sums_ref, grad_pre_ref) = refs[:5], refs[5:]
    half = grad_pre_ref.shape[0]
    channels = refs[0].shape[1]
    size = half // 4
    core, place = own_place()[0], phase_place(False)
    chunks = [pl.multiple_of(lax.rem(place + step, 4) * size, size) for step in (1, 2)]
    sources = [pl.multiple_of(core * half + chunk, size) for chunk in chunks]
    expand, reduce = hidden_rows(cells, sources, size, grad_pre_ref, chunks)
    sums_ref[:, :channels] = expand
    sums_ref[:, channels:] = reduce


def near_first(*cells):
    total, channels = cells[0].shape
    half = cells[2].shape[0] // 2
    return pl.pallas_call(
        near_first_body,
        out_shape=(
            jax.ShapeDtypeStruct((half // 2, 2 * channels), f32),
            jax.ShapeDtypeStruct((half, total), bf16),
        ),
        in_specs=[whole] * 5,
        out_specs=[whole] * 2,
        compiler_params=params(16),
        cost_estimate=cost(3.0),
        name="near_first",
    )(*cells)


def near_sends_body(sums_ref, arrived_ref, *sent_refs):
    size = sent_refs[0].shape[0]
    place = phase_place(False)
    for step in (1, 2):
        chunk = pl.multiple_of(lax.rem(place + step, 4) * size, size)
        total = sums_ref[(step - 1) * size : step * size] + arrived_ref[pl.ds(chunk, size), :].astype(f32)
        sent_refs[step - 1][...] = total.astype(bf16)


def near_sends(sums, arrived):
    size, width = sums.shape[0] // 2, sums.shape[1]
    sent = jax.ShapeDtypeStruct((size, width), bf16)
    return pl.pallas_call(
        near_sends_body,
        out_shape=(sent, sent),
        in_specs=[whole] * 2,
        out_specs=[whole] * 2,
        compiler_params=params(6),
        cost_estimate=cost(0.3),
        name="near_sends",
    )(sums, arrived)


def near_last_body(*refs):
    cells, (arrived_ref, _, own_ref, sent_ref, grad_pre_ref) = refs[:5], refs[5:]
    half = grad_pre_ref.shape[0]
    channels = refs[0].shape[1]
    size = half // 4
    core, place = own_place()[0], phase_place(False)
    chunks = [pl.multiple_of(lax.rem(place + step, 4) * size, size) for step in (3, 0)]
    sources = [pl.multiple_of(core * half + chunk, size) for chunk in chunks]
    expand, reduce = hidden_rows(cells, sources, size, grad_pre_ref, chunks)
    for n, (chunk, ref) in enumerate(zip(chunks, (sent_ref, own_ref))):
        at = slice(n * size, (n + 1) * size)
        other = arrived_ref[pl.ds(chunk, size), :].astype(f32)
        ref[:, :channels] = (expand[at] + other[:, :channels]).astype(ref.dtype)
        ref[:, channels:] = (reduce[at] + other[:, channels:]).astype(ref.dtype)


def near_last(*inputs):
    cells, grad_pre = inputs[:5], inputs[6]
    channels = cells[0].shape[1]
    size = cells[2].shape[0] // 8
    return pl.pallas_call(
        near_last_body,
        out_shape=(
            jax.ShapeDtypeStruct((size, 2 * channels), f32),
            jax.ShapeDtypeStruct((size, 2 * channels), bf16),
            jax.ShapeDtypeStruct(grad_pre.shape, bf16),
        ),
        in_specs=[whole] * 7,
        out_specs=[whole] * 3,
        input_output_aliases={6: 2},
        compiler_params=params(16),
        cost_estimate=cost(3.0),
        name="near_last",
    )(*inputs)


def norm_back_body(
    turned_ref, other_ref, mine_ref, unit_ref, spread_ref, gain_ref,
    conv_grad_ref, first_ref, last_ref,
):
    total, channels = unit_ref.shape
    half = turned_ref.shape[1] // 2
    core = own_place()[0]
    block = 256
    share = 1.0 / channels
    mine_weight = turned_ref[:, pl.ds(pl.multiple_of(core * half, half), half)]
    other_weight = turned_ref[:, pl.ds(pl.multiple_of((1 - core) * half, half), half)]
    for b in range(total // block):
        at = slice(b * block, (b + 1) * block)
        summed = jnp.dot(mine_weight, mine_ref[:, at], preferred_element_type=f32)
        summed = summed + jnp.dot(other_weight, other_ref[:, at], preferred_element_type=f32)
        grad_normed = summed.astype(bf16).T.astype(f32)
        unit = unit_ref[at, :]
        grad_unit = grad_normed * gain_ref[...]
        mean_grad = jnp.sum(grad_unit, axis=1, keepdims=True) * share
        mean_cross = jnp.sum(grad_unit * unit, axis=1, keepdims=True) * share
        spread = jnp.concatenate([spread_ref[at, :]] * (channels // lanes), axis=1)
        value = (grad_unit - mean_grad - unit * mean_cross) * spread
        conv_grad_ref[b * 8 : (b + 1) * 8] = value.reshape(block // side, side, channels)
    for j in range(reach):
        first_ref[j] = conv_grad_ref[:, j, :].astype(bf16)
        last_ref[j] = conv_grad_ref[:, side - reach + j, :].astype(bf16)


def norm_back(turned, other, mine, unit, spread, gain):
    total, channels = unit.shape
    shape = jax.ShapeDtypeStruct((reach, side, channels), bf16)
    found, first, last = pl.pallas_call(
        norm_back_body,
        out_shape=(jax.ShapeDtypeStruct((side, side, channels), f32), shape, shape),
        in_specs=[whole] * 6,
        out_specs=[whole] * 3,
        compiler_params=params(14),
        cost_estimate=cost(0.2),
        name="norm_back",
    )(turned, other, mine, unit, spread, gain)
    return found.reshape(total, channels), first, last


def finish_body(
    counts_ref, conv0_ref, conv1_ref, conv2_ref, kernel_ref, left_ref, right_ref, top_ref, bottom_ref,
    grad_ref, out_ref, rows_sum, cols_sum,
):
    conv_refs = (conv0_ref, conv1_ref, conv2_ref)
    rows = out_ref.shape[0] // side
    steps = side // rows
    block = pl.program_id(0)

    @pl.when(block == 0)
    def _():
        add_edges(True, kernel_ref, left_ref, right_ref, top_ref, bottom_ref, rows_sum, cols_sum)

    def write(outer_of):
        for r in range(rows):
            i = block * rows + r
            at = pl.ds(pl.multiple_of(i * side, side), side)
            value = edged_row(i, conv_rows(conv_refs, at), cols_sum)
            outer = outer_of(r)
            if outer is not None:
                value = value + rows_sum[outer]
            out_ref[r * side : (r + 1) * side, :] = value + masked_row(i, grad_ref[at, :], counts_ref)

    @pl.when(block == 0)
    def _():
        write(lambda r: r if r < reach else None)

    @pl.when(jnp.logical_and(block > 0, block < steps - 1))
    def _():
        write(lambda r: None)

    @pl.when(block == steps - 1)
    def _():
        write(lambda r: r - (rows - 2 * reach) if r >= rows - reach else None)


def finish(counts, conv, kernel, left, right, top, bottom, grad):
    total, channels = grad.shape
    rows = 8
    return pl.pallas_call(
        finish_body,
        out_shape=jax.ShapeDtypeStruct((total, channels), f32),
        grid=(side // rows,),
        in_specs=[pl.BlockSpec(memory_space=pltpu.SMEM)] + [whole] * 9,
        out_specs=pl.BlockSpec((rows * side, channels), lambda b: (b, 0)),
        scratch_shapes=[pltpu.VMEM((2 * reach, side, channels), f32)] * 2,
        compiler_params=params(12),
        cost_estimate=cost(2.2),
        name="finish",
    )(counts, *conv, kernel, left, right, top, bottom, grad)


def split_four_body(own_ref, first_ref, second_ref, third_ref, kept_ref, *sent_refs):
    size = kept_ref.shape[0]
    place = phase_place(True)
    for step in range(4):
        at = pl.ds(pl.multiple_of(lax.rem(place + step, 4) * size, size), size)
        total = own_ref[at, :]
        for ref in (first_ref, second_ref, third_ref):
            total = total + ref[at, :].astype(f32)
        if step == 0:
            kept_ref[...] = total
        else:
            sent_refs[step - 1][...] = total.astype(bf16)


def split_four(own, parts):
    size, width = own.shape[0] // 4, own.shape[1]
    sent = jax.ShapeDtypeStruct((size, width), bf16)
    return pl.pallas_call(
        split_four_body,
        out_shape=(jax.ShapeDtypeStruct((size, width), f32), sent, sent, sent),
        in_specs=[whole] * 4,
        out_specs=[whole] * 4,
        compiler_params=params(4),
        cost_estimate=cost(0.3),
        name="split_four",
    )(own, *parts)


def split_two_body(own_ref, *refs):
    part_refs, (kept_ref, sent_ref) = refs[:-2], refs[-2:]
    size = kept_ref.shape[0]
    total = own_ref[...]
    for ref in part_refs:
        total = total + ref[...].astype(f32)
    low, high = total[:size], total[size:]
    upper = (own_place()[3] & 1) != 0
    kept_ref[...] = jnp.where(upper, high, low)
    sent_ref[...] = jnp.where(upper, low, high)


def split_two(own, parts):
    shape = jax.ShapeDtypeStruct((own.shape[0] // 2, own.shape[1]), f32)
    return pl.pallas_call(
        split_two_body,
        out_shape=(shape, shape),
        in_specs=[whole] * (1 + len(parts)),
        out_specs=[whole] * 2,
        compiler_params=params(4),
        cost_estimate=cost(0.2),
        name="split_two",
    )(own, *parts)


def split_ring_body(own_ref, first_ref, second_ref, third_ref, kept_ref, *sent_refs):
    size = kept_ref.shape[0]
    total = own_ref[...]
    for ref in (first_ref, second_ref, third_ref):
        total = total + ref[...].astype(f32)
    chunks = [total[c * size : (c + 1) * size] for c in range(4)]
    place = own_place()[3] >> 1
    for step, ref in enumerate((kept_ref, *sent_refs)):
        wanted = (place + step) & 3
        found = chunks[0]
        for c in range(1, 4):
            found = jnp.where(wanted == c, chunks[c], found)
        ref[...] = found


def split_ring(own, parts):
    shape = jax.ShapeDtypeStruct((own.shape[0] // 4, own.shape[1]), f32)
    return pl.pallas_call(
        split_ring_body,
        out_shape=(shape,) * 4,
        in_specs=[whole] * 4,
        out_specs=[whole] * 4,
        compiler_params=params(4),
        cost_estimate=cost(0.2),
        name="split_ring",
    )(own, *parts)


def last_sum_body(scale, own_ref, arrived_ref, expand_ref, reduce_ref):
    channels = expand_ref.shape[2]
    total = (own_ref[...] + arrived_ref[...]) * scale
    for r in range(total.shape[0]):
        expand_ref[r] = total[r : r + 1, :channels]
        reduce_ref[r] = total[r : r + 1, channels:]


def last_sum(own, arrived, scale):
    size, width = own.shape
    shape = jax.ShapeDtypeStruct((size, 1, width // 2), f32)
    expand, reduce = pl.pallas_call(
        functools.partial(last_sum_body, scale),
        out_shape=(shape, shape),
        in_specs=[whole] * 2,
        out_specs=[whole] * 2,
        compiler_params=params(4),
        cost_estimate=cost(0.4),
        name="last_sum",
    )(own, arrived)
    return expand.transpose(1, 0, 2), reduce.transpose(1, 0, 2)


every_axis = ("dp", "lat", "lon")


def device_pairs(move):
    def flat(hi, y, core, z, lo):
        return (hi * 8 + y * 2 + core) * 16 + z * 2 + lo

    found = []
    for hi, y, core, z, lo in itertools.product(range(2), range(4), range(2), range(8), range(2)):
        found.append((flat(hi, y, core, z, lo), flat(*move(hi, y, core, z, lo))))
    return found


def plane_pairs(step, first):
    def move(hi, y, core, z, lo):
        if (core == 0) == first:
            return (hi, (y + step) % 4, core, z, lo)
        x = (2 * hi + lo + step) % 4
        return (x // 2, y, core, z, x % 2)

    return device_pairs(move)


def ring_pairs(step):
    return device_pairs(lambda hi, y, core, z, lo: (hi, y, core, (z + 2 * step) % 8, lo))


def last_pairs():
    return device_pairs(lambda hi, y, core, z, lo: (hi, y, core, z ^ 1, lo))


def shifted(axis, step):
    count = lax.axis_size(axis)
    return [(i, (i + step) % count) for i in range(count)]


def lon_halo(first, last):
    left = lax.ppermute(last, "lon", shifted("lon", 1))
    right = lax.ppermute(first, "lon", shifted("lon", -1))
    return left, right


def lat_halo(up, down):
    top = lax.ppermute(down, "lat", shifted("lat", 1))
    bottom = lax.ppermute(up, "lat", shifted("lat", -1))
    return top, bottom


def after(value, *others):
    return lax.optimization_barrier((value, others))[0]


def local(
    state, cotangent, counts, dw_kernel, dw_bias, norm_gain, norm_bias, w_expand, b_expand, w_reduce
):
    channels = state.shape[-1]
    cells = state.reshape(-1, channels)
    grad = cotangent.reshape(-1, channels)
    total = cells.shape[0]
    kernel = dw_kernel.transpose(1, 0, 2)

    left, right = lon_halo(*side_cols(cells))
    rows = mask_rows(counts, grad)
    expand, reduce, expand_t, bias = arrange(w_expand[0], w_reduce[0], b_expand)
    conv = inner_conv(after(cells, rows), kernel, False, (0,))
    left, right = after((left, right), rows, bias, conv)
    up, down = side_rows(cells, left, right)
    top, bottom = lat_halo(up, down)
    conv += inner_conv(after(cells, up, down), kernel, False, (1, 2))
    unit, spread, normed = normalise(
        conv, kernel, left, right, top, bottom, dw_bias, norm_gain, norm_bias
    )

    inputs = (normed, rows, expand, reduce, bias)
    sent, far_pre = hidden_far(*inputs)
    arrived = lax.ppermute(sent, "lat", [(i, i ^ 1) for i in range(8)])
    sums, near_pre = near_first(*inputs)
    one, two = near_sends(sums, arrived)
    part_one = lax.ppermute(one, every_axis, plane_pairs(1, True))
    part_two = lax.ppermute(two, every_axis, plane_pairs(2, True))
    own, three, near_pre = near_last(*inputs, arrived, after(near_pre, one, two))
    part_three = lax.ppermute(three, every_axis, plane_pairs(3, True))

    far_pre, part_one, part_two = after((far_pre, part_one, part_two), three)
    conv_grad, first, last = norm_back(expand_t, far_pre, near_pre, unit, spread, norm_gain)
    left, right = lon_halo(first, last)
    own, parts = after((own, (part_one, part_two, part_three)), first, last)
    own, *sent = split_four(own, parts)
    parts = [lax.ppermute(s, every_axis, plane_pairs(i + 1, False)) for i, s in enumerate(sent)]
    back = inner_conv(after(conv_grad, sent), kernel, True, (0, 1))
    up, down = side_rows(*after((conv_grad, left, right), back))

    own, *sent = split_ring(*after((own, parts), up, down))
    parts = [lax.ppermute(s, every_axis, ring_pairs(i + 1)) for i, s in enumerate(sent)]
    top, bottom = lat_halo(up, down)
    back += inner_conv(after(conv_grad, sent), kernel, True, (2,))

    own, sent = split_two(*after((own, parts), back, top, bottom))
    arrived = lax.ppermute(sent, every_axis, last_pairs())
    grad = after(grad, sent)
    gradient = finish(counts, back, kernel, left, right, top, bottom, grad)

    cells_all = lax.axis_size("dp") * lax.axis_size("lat") * lax.axis_size("lon") * total
    kept = last_sum(own, arrived, 1.0 / math.sqrt(cells_all))
    return (gradient.reshape(state.shape), *kept)


def solution(mesh):
    in_specs = (
        P("dp", "lat", "lon", None),
        P("dp", "lat", "lon", None),
        P("lat", "lon"),
        P(),
        P(),
        P(),
        P(),
        P(),
        P(),
        P(),
    )
    out_specs = (
        P("dp", "lat", "lon", None),
        P(None, ("dp", "lat", "lon"), None),
        P(None, ("dp", "lat", "lon"), None),
    )
    return jax.shard_map(local, mesh=mesh, in_specs=in_specs, out_specs=out_specs, check_vma=False)
```

```python
import functools
import itertools
import math

import jax
import jax.numpy as jnp
from jax import lax
from jax.experimental import pallas as pl
from jax.experimental.pallas import tpu as pltpu
from jax.sharding import PartitionSpec as P

norm_eps = 1e-06
inv_root_two_pi = 0.3989422804014327
side = 32
reach = 3
lanes = 128
f32 = jnp.float32
bf16 = jnp.bfloat16
whole = pl.BlockSpec(memory_space=pltpu.VMEM)


def params(mib):
    return pltpu.CompilerParams(vmem_limit_bytes=mib * 1024 * 1024)


def cost(microseconds):
    return pl.CostEstimate(
        flops=int(microseconds * 1.15e9), bytes_accessed=2**20, transcendentals=0
    )


def tap_row(kernel_ref, flipped, p, q, cols):
    index = 7 * p + q
    if flipped:
        index = 48 - index
    return kernel_ref[index, :, cols]


def shift_cols(rows, offset):
    if offset == 0:
        return rows
    count = rows.shape[0]
    turned = pltpu.roll(rows, (-offset) % count, 0)
    place = lax.broadcasted_iota(jnp.int32, (8, rows.shape[1]), 0)
    if offset > 0:
        last = jnp.where(place < 8 - offset, turned[count - 8 :], 0.0)
        return jnp.concatenate([turned[: count - 8], last], axis=0)
    first = jnp.where(place >= -offset, turned[:8], 0.0)
    return jnp.concatenate([first, turned[8:]], axis=0)


def inner_conv_body(parts, cells_ref, kernel_ref, *refs):
    outs, padded = refs[:-1], refs[-1]
    edge = reach * side
    total = side * side
    padded[0:edge] = jnp.zeros((edge, lanes), f32)
    padded[edge + total : 2 * edge + total] = jnp.zeros((edge, lanes), f32)
    for part, out_ref in zip(parts, outs):
        cols = slice(part * lanes, (part + 1) * lanes)
        padded[edge : edge + total] = cells_ref[:, cols]

        def two_rows(i, carry):
            base = pl.multiple_of(i * (2 * side), 2 * side)
            rows = [padded[pl.ds(base + p * side, side), :] for p in range(8)]
            results = [None, None]
            for q in range(7):
                sums = [None, None]
                for p in range(7):
                    tap = tap_row(kernel_ref, False, p, q, cols)
                    for g in range(2):
                        term = tap * rows[p + g]
                        sums[g] = term if sums[g] is None else sums[g] + term
                for g in range(2):
                    moved = shift_cols(sums[g], q - reach)
                    results[g] = moved if results[g] is None else results[g] + moved
            for g in range(2):
                out_ref[pl.ds(base + g * side, side), :] = results[g]
            return carry

        lax.fori_loop(0, side // 2, two_rows, 0)


def inner_conv(cells, kernel, parts):
    total = cells.shape[0]
    shape = jax.ShapeDtypeStruct((total, lanes), f32)
    return pl.pallas_call(
        functools.partial(inner_conv_body, parts),
        out_shape=(shape,) * len(parts),
        in_specs=[whole] * 2,
        out_specs=[whole] * len(parts),
        scratch_shapes=[pltpu.VMEM((total + 2 * reach * side, lanes), f32)],
        compiler_params=params(6),
        cost_estimate=cost(2.2 * len(parts)),
        name="inner_conv",
    )(cells, kernel)


def back_conv_body(parts, cells_ref, kernel_ref, *refs):
    outs, (padded, taps) = refs[:-2], refs[-2:]
    edge = reach * side
    total = side * side
    group = 4
    padded[0:edge] = jnp.zeros((edge, lanes), bf16)
    padded[edge + total : 2 * edge + total] = jnp.zeros((edge, lanes), bf16)
    for part, out_ref in zip(parts, outs):
        cols = slice(part * lanes, (part + 1) * lanes)
        padded[edge : edge + total] = cells_ref[:, cols].astype(bf16)
        for p, q in itertools.product(range(7), range(7)):
            tap = jnp.broadcast_to(tap_row(kernel_ref, True, p, q, cols), (16, lanes))
            taps[7 * p + q] = tap.astype(bf16)

        def some_rows(i, carry):
            base = pl.multiple_of(i * (group * side), group * side)
            rows = [padded[pl.ds(base + p * side, side), :] for p in range(6 + group)]
            results = [None] * group
            for q in range(7):
                sums = [None] * group
                for p in range(7):
                    tap = jnp.concatenate([taps[7 * p + q]] * (side // 16), axis=0)
                    for g in range(group):
                        term = tap * rows[p + g]
                        sums[g] = term if sums[g] is None else sums[g] + term
                for g in range(group):
                    moved = shift_cols(sums[g].astype(f32), q - reach)
                    results[g] = moved if results[g] is None else results[g] + moved
            for g in range(group):
                out_ref[pl.ds(base + g * side, side), :] = results[g]
            return carry

        lax.fori_loop(0, side // group, some_rows, 0)


def back_conv(cells, kernel, parts):
    total = cells.shape[0]
    shape = jax.ShapeDtypeStruct((total, lanes), f32)
    return pl.pallas_call(
        functools.partial(back_conv_body, parts),
        out_shape=(shape,) * len(parts),
        in_specs=[whole] * 2,
        out_specs=[whole] * len(parts),
        scratch_shapes=[
            pltpu.VMEM((total + 2 * reach * side, lanes), bf16),
            pltpu.VMEM((49, 16, lanes), bf16),
        ],
        compiler_params=params(6),
        cost_estimate=cost(1.5 * len(parts)),
        name="back_conv",
    )(cells, kernel)


def side_cols_body(cells_ref, first_ref, last_ref, low, high, sems):
    copies = [
        pltpu.make_async_copy(cells_ref.at[:, pl.ds(0, 8), :], low, sems.at[0]),
        pltpu.make_async_copy(cells_ref.at[:, pl.ds(side - 8, 8), :], high, sems.at[1]),
    ]
    for copy in copies:
        copy.start()
    copies[0].wait()
    for j in range(reach):
        first_ref[j] = low[:, j, :].astype(bf16)
    copies[1].wait()
    for j in range(reach):
        last_ref[j] = high[:, 8 - reach + j, :].astype(bf16)


def side_cols(cells):
    channels = cells.shape[1]
    shape = jax.ShapeDtypeStruct((reach, side, channels), bf16)
    return pl.pallas_call(
        side_cols_body,
        out_shape=(shape, shape),
        in_specs=[pl.BlockSpec(memory_space=pltpu.HBM)],
        out_specs=[whole] * 2,
        scratch_shapes=[pltpu.VMEM((side, 8, channels), f32)] * 2 + [pltpu.SemaphoreType.DMA((2,))],
        compiler_params=params(58),
        cost_estimate=cost(1.0),
        name="side_cols",
    )(cells.reshape(side, side, channels))


def side_rows_body(cells_ref, left_ref, right_ref, up_ref, down_ref):
    channels = cells_ref.shape[1]
    place = lax.broadcasted_iota(jnp.int32, (8, channels), 0)
    blank = jnp.zeros((8, channels), f32)
    left = [left_ref[h].astype(f32) for h in range(reach)]
    right = [right_ref[h].astype(f32) for h in range(reach)]
    for r in range(reach):
        for row, ref in ((r, up_ref), (side - reach + r, down_ref)):
            corner = blank
            for h in range(reach):
                corner = jnp.where(place == h, right[h][row : row + 1], corner)
                corner = jnp.where(place == 8 - reach + h, left[h][row : row + 1], corner)
            body = cells_ref[row * side : (row + 1) * side]
            ref[r] = jnp.concatenate([body, corner, blank], axis=0).astype(bf16)


def side_rows(cells, left, right):
    channels = cells.shape[1]
    shape = jax.ShapeDtypeStruct((reach, side + 16, channels), bf16)
    return pl.pallas_call(
        side_rows_body,
        out_shape=(shape, shape),
        in_specs=[whole] * 3,
        out_specs=[whole] * 2,
        compiler_params=params(6),
        cost_estimate=cost(0.5),
        name="side_rows",
    )(cells, left, right)


def add_edges(flipped, kernel_ref, left_ref, right_ref, top_ref, bottom_ref, rows_sum, cols_sum):
    lat = lax.axis_index("lat")
    channels = kernel_ref.shape[2]
    for c in range(channels // lanes):
        cols = slice(c * lanes, (c + 1) * lanes)
        for low, ref in ((True, top_ref), (False, bottom_ref)):
            outside = lat == (0 if low else lax.axis_size("lat") - 1)
            beyond = [
                jnp.where(outside, 0.0, ref[h, :, cols].astype(f32)[: side + 8]) for h in range(reach)
            ]
            for r in range(reach):
                result = None
                steps = [(h, h - r) for h in range(r, reach)] if low else [
                    (h, 6 + h - r) for h in range(0, r + 1)
                ]
                for q in range(7):
                    summed = None
                    for h, p in steps:
                        term = tap_row(kernel_ref, flipped, p, q, cols) * beyond[h]
                        summed = term if summed is None else summed + term
                    summed = pltpu.roll(summed, (reach - q) % (side + 8), 0) if q != reach else summed
                    result = summed if result is None else result + summed
                rows_sum[r if low else reach + r, :, cols] = result[:side]
        for low, ref in ((True, left_ref), (False, right_ref)):
            beyond = [ref[h, :, cols].astype(f32) for h in range(reach)]
            for r in range(reach):
                steps = [(h, h - r) for h in range(r, reach)] if low else [
                    (h, 6 + h - r) for h in range(0, r + 1)
                ]
                result = None
                for p in range(7):
                    summed = None
                    for h, q in steps:
                        term = tap_row(kernel_ref, flipped, p, q, cols) * beyond[h]
                        summed = term if summed is None else summed + term
                    summed = shift_cols(summed, p - reach)
                    result = summed if result is None else result + summed
                cols_sum[r if low else reach + r, :, cols] = result


def edged_row(i, conv_row, cols_sum):
    channels = conv_row.shape[1]
    place = lax.broadcasted_iota(jnp.int32, (8, channels), 0)
    first, last = conv_row[:8], conv_row[side - 8 :]
    for r in range(reach):
        first = first + jnp.where(place == r, cols_sum[r, pl.ds(i, 1), :], 0.0)
        last = last + jnp.where(place == 8 - reach + r, cols_sum[reach + r, pl.ds(i, 1), :], 0.0)
    return jnp.concatenate([first, conv_row[8 : side - 8], last], axis=0)


def each_row(step):
    def low(i, carry):
        step(i, i)
        return carry

    def middle(i, carry):
        step(i, None)
        return carry

    def high(i, carry):
        step(i, i - (side - 2 * reach))
        return carry

    lax.fori_loop(0, reach, low, 0, unroll=reach)
    lax.fori_loop(reach, side - reach, middle, 0, unroll=side // 2 - reach)
    lax.fori_loop(side - reach, side, high, 0, unroll=reach)


def conv_rows(refs, at):
    return jnp.concatenate([ref[at, :] for ref in refs], axis=1)


def normalise_body(
    conv0_ref, conv1_ref, conv2_ref, kernel_ref, left_ref, right_ref, top_ref, bottom_ref, bias_ref, gain_ref, shift_ref,
    unit_ref, spread_ref, normed_ref, rows_sum, cols_sum,
):
    channels = kernel_ref.shape[2]
    conv_refs = (conv0_ref, conv1_ref, conv2_ref)
    add_edges(False, kernel_ref, left_ref, right_ref, top_ref, bottom_ref, rows_sum, cols_sum)
    share = 1.0 / channels

    def step(i, outer):
        at = pl.ds(pl.multiple_of(i * side, side), side)
        value = edged_row(i, conv_rows(conv_refs, at), cols_sum)
        if outer is not None:
            value = value + rows_sum[outer]
        value = value + bias_ref[...]
        mean = jnp.sum(value, axis=1, keepdims=True) * share
        centred = value - mean
        spread = lax.rsqrt(jnp.sum(centred * centred, axis=1, keepdims=True) * share + norm_eps)
        unit = centred * spread
        unit_ref[at, :] = unit
        spread_ref[at, :] = jnp.broadcast_to(spread, (side, lanes))
        normed_ref[at, :] = (unit * gain_ref[...] + shift_ref[...]).astype(bf16)

    each_row(step)


def turn(source_ref, target_ref):
    for b in range(source_ref.shape[0] // 256):
        at = slice(b * 256, (b + 1) * 256)
        target_ref[:, at] = source_ref[at, :].T


def normalise(conv, kernel, left, right, top, bottom, bias, gain, shift):
    total, channels = conv[0].shape[0], kernel.shape[2]
    return pl.pallas_call(
        normalise_body,
        out_shape=(
            jax.ShapeDtypeStruct((total, channels), f32),
            jax.ShapeDtypeStruct((total, lanes), f32),
            jax.ShapeDtypeStruct((total, channels), bf16),
        ),
        in_specs=[whole] * 11,
        out_specs=[whole] * 3,
        scratch_shapes=[pltpu.VMEM((2 * reach, side, channels), f32)] * 2,
        compiler_params=params(12),
        cost_estimate=cost(2.8),
        name="normalise",
    )(*conv, kernel, left, right, top, bottom, bias, gain, shift)


def wet_row(i, counts_ref):
    place = lax.broadcasted_iota(jnp.int32, (8, lanes), 0) + (i % 8) * 8
    pieces = []
    for t in range(side // 8):
        pieces.append(place < counts_ref[i // 8, t])
    return pieces


def masked_row(i, grad_row, counts_ref):
    channels = grad_row.shape[1]
    parts = []
    for t, wet in enumerate(wet_row(i, counts_ref)):
        piece = grad_row[t * 8 : (t + 1) * 8]
        parts.append(
            jnp.concatenate(
                [
                    jnp.where(wet, piece[:, c * lanes : (c + 1) * lanes], 0.0)
                    for c in range(channels // lanes)
                ],
                axis=1,
            )
        )
    return jnp.concatenate(parts, axis=0)


def mask_rows_body(counts_ref, grad_ref, rows_ref):
    def step(i, carry):
        at = pl.ds(pl.multiple_of(i * side, side), side)
        rows_ref[at, :] = masked_row(i, grad_ref[at, :], counts_ref).astype(bf16)
        return carry

    lax.fori_loop(0, side, step, 0, unroll=2)


def mask_rows(counts, grad):
    total, channels = grad.shape
    return pl.pallas_call(
        mask_rows_body,
        out_shape=jax.ShapeDtypeStruct((total, channels), bf16),
        in_specs=[pl.BlockSpec(memory_space=pltpu.SMEM), whole],
        out_specs=whole,
        compiler_params=params(8),
        cost_estimate=cost(0.9),
        name="mask_rows",
    )(counts, grad)


def arrange_body(expand_ref, reduce_ref, bias_ref, expand_out, reduce_out, turned_out, bias_out):
    unit_row = lax.broadcasted_iota(jnp.int32, (48, 96), 0)
    unit_col = lax.broadcasted_iota(jnp.int32, (48, 96), 1)
    picks = [unit_col == (unit_row // 6) * 12 + lo * 6 + unit_row % 6 for lo in range(2)]
    chosen = [pick.astype(f32).astype(bf16) for pick in picks]
    for hi, y, core in itertools.product(range(2), range(4), range(2)):
        unit = (hi * 4 + y) * 2 + core
        at = slice(unit * 96, (unit + 1) * 96)
        expand, reduce = expand_ref[at, :], reduce_ref[at, :]
        bias = bias_ref[:, at]
        for lo in range(2):
            x = 2 * hi + lo
            place = core * 16 + (y * 4 + x if core == 0 else x * 4 + y)
            to = slice(place * 48, (place + 1) * 48)
            expand_out[to, :] = jnp.dot(chosen[lo], expand, preferred_element_type=f32).astype(bf16)
            reduce_out[to, :] = jnp.dot(chosen[lo], reduce, preferred_element_type=f32).astype(bf16)
            column = jnp.sum(jnp.where(picks[lo], bias, 0.0), axis=1, keepdims=True)
            bias_out[to, :] = jnp.broadcast_to(column, (48, lanes))
    turn(expand_out, turned_out)


def arrange(expand, reduce, bias):
    units, channels = expand.shape
    shape = jax.ShapeDtypeStruct((units, channels), bf16)
    return pl.pallas_call(
        arrange_body,
        out_shape=(
            shape,
            shape,
            jax.ShapeDtypeStruct((channels, units), bf16),
            jax.ShapeDtypeStruct((units, lanes), f32),
        ),
        in_specs=[whole] * 3,
        out_specs=[whole] * 4,
        compiler_params=params(12),
        cost_estimate=cost(1.5),
        name="arrange",
    )(expand, reduce, bias)


tail_slope = 0.3275911 * 0.7071067811865476
tail_terms = [
    0.5 * a for a in (0.254829592, -0.284496736, 1.421413741, -1.453152027, 1.061405429)
]
exp_scale = -0.5 * 1.4426950408889634


def gelu_pair(v):
    d = 1.0 + tail_slope * jnp.abs(v)
    t = pltpu.reciprocal(d, approx=True)
    poly = tail_terms[4]
    for a in reversed(tail_terms[:4]):
        poly = poly * t + a
    bell = jnp.exp2(v * v * exp_scale)
    tail = poly * t * bell
    below = jnp.where(v >= 0.0, 1.0 - tail, tail)
    return v * below, below + v * bell * inv_root_two_pi


def own_place():
    lat, lon = lax.axis_index("lat"), lax.axis_index("lon")
    x = 2 * lax.axis_index("dp") + (lon & 1)
    return lat & 1, x, lat >> 1, lon >> 1


def phase_place(second):
    core, x, y, _ = own_place()
    along_y = core == (1 if second else 0)
    return jnp.where(along_y, y, x)


def dot_rows(left, right):
    return lax.dot_general(left, right, (((1,), (1,)), ((), ())), preferred_element_type=f32)


def hidden_rows(cells, sources, rows, grad_pre_ref, places):
    normed_ref, grad_ref, expand_ref, reduce_ref, bias_ref = cells
    total = normed_ref.shape[0]

    def gather(ref):
        return jnp.concatenate([ref[pl.ds(source, rows), :] for source in sources], axis=0)

    preact = dot_rows(gather(expand_ref), normed_ref[...])
    grad_hidden = dot_rows(gather(reduce_ref), grad_ref[...])
    bias = jnp.concatenate([gather(bias_ref)] * (total // lanes), axis=1)
    value, slope = gelu_pair(preact + bias)
    hidden = value.astype(bf16)
    grad_pre = (grad_hidden * slope).astype(bf16)
    for n, place in enumerate(places):
        grad_pre_ref[pl.ds(place, rows), :] = grad_pre[n * rows : (n + 1) * rows]
    return (
        jnp.dot(grad_pre, normed_ref[...], preferred_element_type=f32),
        jnp.dot(hidden, grad_ref[...], preferred_element_type=f32),
    )


def far_body(*refs):
    cells, (sent_ref, grad_pre_ref) = refs[:5], refs[5:]
    half = grad_pre_ref.shape[0]
    channels = refs[0].shape[1]
    base = (1 - own_place()[0]) * half
    rows = half // 2
    for b in range(half // rows):
        source = pl.multiple_of(base + b * rows, rows)
        expand, reduce = hidden_rows(cells, [source], rows, grad_pre_ref, [b * rows])
        at = slice(b * rows, (b + 1) * rows)
        sent_ref[at, :channels] = expand.astype(bf16)
        sent_ref[at, channels:] = reduce.astype(bf16)


def hidden_far(*cells):
    total, channels = cells[0].shape
    half = cells[2].shape[0] // 2
    return pl.pallas_call(
        far_body,
        out_shape=(
            jax.ShapeDtypeStruct((half, 2 * channels), bf16),
            jax.ShapeDtypeStruct((half, total), bf16),
        ),
        in_specs=[whole] * 5,
        out_specs=[whole] * 2,
        compiler_params=params(16),
        cost_estimate=cost(5.8),
        name="hidden_far",
    )(*cells)


def near_first_body(*refs):
    cells, (sums_ref, grad_pre_ref) = refs[:5], refs[5:]
    half = grad_pre_ref.shape[0]
    channels = refs[0].shape[1]
    size = half // 4
    core, place = own_place()[0], phase_place(False)
    chunks = [pl.multiple_of(lax.rem(place + step, 4) * size, size) for step in (2, 1)]
    sources = [pl.multiple_of(core * half + chunk, size) for chunk in chunks]
    expand, reduce = hidden_rows(cells, sources, size, grad_pre_ref, chunks)
    sums_ref[:, :channels] = expand
    sums_ref[:, channels:] = reduce


def near_first(*cells):
    total, channels = cells[0].shape
    half = cells[2].shape[0] // 2
    return pl.pallas_call(
        near_first_body,
        out_shape=(
            jax.ShapeDtypeStruct((half // 2, 2 * channels), f32),
            jax.ShapeDtypeStruct((half, total), bf16),
        ),
        in_specs=[whole] * 5,
        out_specs=[whole] * 2,
        compiler_params=params(16),
        cost_estimate=cost(3.0),
        name="near_first",
    )(*cells)


def near_sends_body(sums_ref, arrived_ref, *sent_refs):
    size = sent_refs[0].shape[0]
    place = phase_place(False)
    for n, step in enumerate((2, 1)):
        chunk = pl.multiple_of(lax.rem(place + step, 4) * size, size)
        total = sums_ref[n * size : (n + 1) * size] + arrived_ref[pl.ds(chunk, size), :].astype(f32)
        sent_refs[n][...] = total.astype(bf16)


def near_sends(sums, arrived):
    size, width = sums.shape[0] // 2, sums.shape[1]
    sent = jax.ShapeDtypeStruct((size, width), bf16)
    return pl.pallas_call(
        near_sends_body,
        out_shape=(sent, sent),
        in_specs=[whole] * 2,
        out_specs=[whole] * 2,
        compiler_params=params(6),
        cost_estimate=cost(0.3),
        name="near_sends",
    )(sums, arrived)


def near_last_body(*refs):
    cells, (arrived_ref, _, own_ref, sent_ref, grad_pre_ref) = refs[:5], refs[5:]
    half = grad_pre_ref.shape[0]
    channels = refs[0].shape[1]
    size = half // 4
    core, place = own_place()[0], phase_place(False)
    chunks = [pl.multiple_of(lax.rem(place + step, 4) * size, size) for step in (3, 0)]
    sources = [pl.multiple_of(core * half + chunk, size) for chunk in chunks]
    expand, reduce = hidden_rows(cells, sources, size, grad_pre_ref, chunks)
    for n, (chunk, ref) in enumerate(zip(chunks, (sent_ref, own_ref))):
        at = slice(n * size, (n + 1) * size)
        other = arrived_ref[pl.ds(chunk, size), :].astype(f32)
        ref[:, :channels] = (expand[at] + other[:, :channels]).astype(ref.dtype)
        ref[:, channels:] = (reduce[at] + other[:, channels:]).astype(ref.dtype)


def near_last(*inputs):
    cells, grad_pre = inputs[:5], inputs[6]
    channels = cells[0].shape[1]
    size = cells[2].shape[0] // 8
    return pl.pallas_call(
        near_last_body,
        out_shape=(
            jax.ShapeDtypeStruct((size, 2 * channels), f32),
            jax.ShapeDtypeStruct((size, 2 * channels), bf16),
            jax.ShapeDtypeStruct(grad_pre.shape, bf16),
        ),
        in_specs=[whole] * 7,
        out_specs=[whole] * 3,
        input_output_aliases={6: 2},
        compiler_params=params(16),
        cost_estimate=cost(3.0),
        name="near_last",
    )(*inputs)


def norm_back_body(
    turned_ref, other_ref, mine_ref, unit_ref, spread_ref, gain_ref,
    conv_grad_ref, first_ref, last_ref,
):
    total, channels = unit_ref.shape
    half = turned_ref.shape[1] // 2
    core = own_place()[0]
    block = 256
    share = 1.0 / channels
    mine_weight = turned_ref[:, pl.ds(pl.multiple_of(core * half, half), half)]
    other_weight = turned_ref[:, pl.ds(pl.multiple_of((1 - core) * half, half), half)]
    for b in range(total // block):
        at = slice(b * block, (b + 1) * block)
        summed = jnp.dot(mine_weight, mine_ref[:, at], preferred_element_type=f32)
        summed = summed + jnp.dot(other_weight, other_ref[:, at], preferred_element_type=f32)
        grad_normed = summed.astype(bf16).T.astype(f32)
        unit = unit_ref[at, :]
        grad_unit = grad_normed * gain_ref[...]
        mean_grad = jnp.sum(grad_unit, axis=1, keepdims=True) * share
        mean_cross = jnp.sum(grad_unit * unit, axis=1, keepdims=True) * share
        spread = jnp.concatenate([spread_ref[at, :]] * (channels // lanes), axis=1)
        value = (grad_unit - mean_grad - unit * mean_cross) * spread
        conv_grad_ref[b * 8 : (b + 1) * 8] = value.reshape(block // side, side, channels)
    for j in range(reach):
        first_ref[j] = conv_grad_ref[:, j, :].astype(bf16)
        last_ref[j] = conv_grad_ref[:, side - reach + j, :].astype(bf16)


def norm_back(turned, other, mine, unit, spread, gain):
    total, channels = unit.shape
    shape = jax.ShapeDtypeStruct((reach, side, channels), bf16)
    found, first, last = pl.pallas_call(
        norm_back_body,
        out_shape=(jax.ShapeDtypeStruct((side, side, channels), f32), shape, shape),
        in_specs=[whole] * 6,
        out_specs=[whole] * 3,
        compiler_params=params(14),
        cost_estimate=cost(0.2),
        name="norm_back",
    )(turned, other, mine, unit, spread, gain)
    return found.reshape(total, channels), first, last


def finish_body(
    counts_ref, conv0_ref, conv1_ref, conv2_ref, kernel_ref, left_ref, right_ref, top_ref, bottom_ref,
    grad_ref, out_ref, rows_sum, cols_sum, done, sems,
):
    conv_refs = (conv0_ref, conv1_ref, conv2_ref)
    add_edges(True, kernel_ref, left_ref, right_ref, top_ref, bottom_ref, rows_sum, cols_sum)
    rows = 8
    copies = []
    for block in range(side // rows):
        for i in range(block * rows, (block + 1) * rows):
            at = slice(i * side, (i + 1) * side)
            value = edged_row(i, conv_rows(conv_refs, at), cols_sum)
            if i < reach:
                value = value + rows_sum[i]
            if i >= side - reach:
                value = value + rows_sum[i - (side - 2 * reach)]
            done[at, :] = value + masked_row(i, grad_ref[at, :], counts_ref)
        part = pl.ds(block * rows * side, rows * side)
        copies.append(pltpu.make_async_copy(done.at[part, :], out_ref.at[part, :], sems.at[block]))
        copies[-1].start()
    for copy in copies:
        copy.wait()


def finish(counts, conv, kernel, left, right, top, bottom, grad):
    total, channels = grad.shape
    return pl.pallas_call(
        finish_body,
        out_shape=jax.ShapeDtypeStruct((total, channels), f32),
        in_specs=[pl.BlockSpec(memory_space=pltpu.SMEM)] + [whole] * 9,
        out_specs=pl.BlockSpec(memory_space=pltpu.HBM),
        scratch_shapes=[pltpu.VMEM((2 * reach, side, channels), f32)] * 2
        + [pltpu.VMEM((total, channels), f32), pltpu.SemaphoreType.DMA((4,))],
        compiler_params=params(12),
        cost_estimate=cost(2.5),
        name="finish",
    )(counts, *conv, kernel, left, right, top, bottom, grad)


def split_four_body(own_ref, first_ref, second_ref, third_ref, kept_ref, *sent_refs):
    size = kept_ref.shape[0]
    place = phase_place(True)
    for step in range(4):
        at = pl.ds(pl.multiple_of(lax.rem(place + step, 4) * size, size), size)
        total = own_ref[at, :]
        for ref in (first_ref, second_ref, third_ref):
            total = total + ref[at, :].astype(f32)
        if step == 0:
            kept_ref[...] = total
        else:
            sent_refs[step - 1][...] = total.astype(bf16)


def split_four(own, parts):
    size, width = own.shape[0] // 4, own.shape[1]
    sent = jax.ShapeDtypeStruct((size, width), bf16)
    return pl.pallas_call(
        split_four_body,
        out_shape=(jax.ShapeDtypeStruct((size, width), f32), sent, sent, sent),
        in_specs=[whole] * 4,
        out_specs=[whole] * 4,
        compiler_params=params(4),
        cost_estimate=cost(0.3),
        name="split_four",
    )(own, *parts)


def split_two_body(own_ref, *refs):
    part_refs, (kept_ref, sent_ref) = refs[:-2], refs[-2:]
    size = kept_ref.shape[0]
    total = own_ref[...]
    for ref in part_refs:
        total = total + ref[...].astype(f32)
    low, high = total[:size], total[size:]
    upper = (own_place()[3] & 1) != 0
    kept_ref[...] = jnp.where(upper, high, low)
    sent_ref[...] = jnp.where(upper, low, high)


def split_two(own, parts):
    shape = jax.ShapeDtypeStruct((own.shape[0] // 2, own.shape[1]), f32)
    return pl.pallas_call(
        split_two_body,
        out_shape=(shape, shape),
        in_specs=[whole] * (1 + len(parts)),
        out_specs=[whole] * 2,
        compiler_params=params(4),
        cost_estimate=cost(0.2),
        name="split_two",
    )(own, *parts)


def split_ring_body(own_ref, first_ref, second_ref, third_ref, kept_ref, *sent_refs):
    size = kept_ref.shape[0]
    total = own_ref[...]
    for ref in (first_ref, second_ref, third_ref):
        total = total + ref[...].astype(f32)
    chunks = [total[c * size : (c + 1) * size] for c in range(4)]
    place = own_place()[3] >> 1
    for step, ref in enumerate((kept_ref, *sent_refs)):
        wanted = (place + step) & 3
        found = chunks[0]
        for c in range(1, 4):
            found = jnp.where(wanted == c, chunks[c], found)
        ref[...] = found


def split_ring(own, parts):
    shape = jax.ShapeDtypeStruct((own.shape[0] // 4, own.shape[1]), f32)
    return pl.pallas_call(
        split_ring_body,
        out_shape=(shape,) * 4,
        in_specs=[whole] * 4,
        out_specs=[whole] * 4,
        compiler_params=params(4),
        cost_estimate=cost(0.2),
        name="split_ring",
    )(own, *parts)


def last_sum_body(scale, own_ref, arrived_ref, expand_ref, reduce_ref):
    channels = expand_ref.shape[2]
    total = (own_ref[...] + arrived_ref[...]) * scale
    for r in range(total.shape[0]):
        expand_ref[r] = total[r : r + 1, :channels]
        reduce_ref[r] = total[r : r + 1, channels:]


def last_sum(own, arrived, scale):
    size, width = own.shape
    shape = jax.ShapeDtypeStruct((size, 1, width // 2), f32)
    expand, reduce = pl.pallas_call(
        functools.partial(last_sum_body, scale),
        out_shape=(shape, shape),
        in_specs=[whole] * 2,
        out_specs=[whole] * 2,
        compiler_params=params(4),
        cost_estimate=cost(0.4),
        name="last_sum",
    )(own, arrived)
    return expand.transpose(1, 0, 2), reduce.transpose(1, 0, 2)


every_axis = ("dp", "lat", "lon")


def device_pairs(move):
    def flat(hi, y, core, z, lo):
        return (hi * 8 + y * 2 + core) * 16 + z * 2 + lo

    found = []
    for hi, y, core, z, lo in itertools.product(range(2), range(4), range(2), range(8), range(2)):
        found.append((flat(hi, y, core, z, lo), flat(*move(hi, y, core, z, lo))))
    return found


def plane_pairs(step, first):
    def move(hi, y, core, z, lo):
        if (core == 0) == first:
            return (hi, (y + step) % 4, core, z, lo)
        x = (2 * hi + lo + step) % 4
        return (x // 2, y, core, z, x % 2)

    return device_pairs(move)


def ring_pairs(step):
    return device_pairs(lambda hi, y, core, z, lo: (hi, y, core, (z + 2 * step) % 8, lo))


def last_pairs():
    return device_pairs(lambda hi, y, core, z, lo: (hi, y, core, z ^ 1, lo))


def shifted(axis, step):
    count = lax.axis_size(axis)
    return [(i, (i + step) % count) for i in range(count)]


def lon_halo(first, last):
    left = lax.ppermute(last, "lon", shifted("lon", 1))
    right = lax.ppermute(first, "lon", shifted("lon", -1))
    return left, right


def lat_halo(up, down):
    top = lax.ppermute(down, "lat", shifted("lat", 1))
    bottom = lax.ppermute(up, "lat", shifted("lat", -1))
    return top, bottom


def after(value, *others):
    return lax.optimization_barrier((value, others))[0]


def local(
    state, cotangent, counts, dw_kernel, dw_bias, norm_gain, norm_bias, w_expand, b_expand, w_reduce
):
    channels = state.shape[-1]
    cells = state.reshape(-1, channels)
    grad = cotangent.reshape(-1, channels)
    total = cells.shape[0]
    kernel = dw_kernel.transpose(1, 0, 2)

    first, last = side_cols(cells)
    left, right = lon_halo(first, last)
    grad, w_expand, w_reduce = after((grad, w_expand, w_reduce), first, last)
    rows = mask_rows(counts, grad)
    expand, reduce, expand_t, bias = arrange(w_expand[0], w_reduce[0], b_expand)
    conv = inner_conv(after(cells, rows), kernel, (0,))
    left, right = after((left, right), rows, bias, conv)
    up, down = side_rows(cells, left, right)
    top, bottom = lat_halo(up, down)
    conv += inner_conv(after(cells, up, down), kernel, (1, 2))
    unit, spread, normed = normalise(
        conv, kernel, left, right, top, bottom, dw_bias, norm_gain, norm_bias
    )

    inputs = (normed, rows, expand, reduce, bias)
    sent, far_pre = hidden_far(*inputs)
    arrived = lax.ppermute(sent, "lat", [(i, i ^ 1) for i in range(8)])
    sums, near_pre = near_first(*inputs)
    two, one = near_sends(sums, arrived)
    part_two = lax.ppermute(two, every_axis, plane_pairs(2, True))
    part_one = lax.ppermute(one, every_axis, plane_pairs(1, True))
    own, three, near_pre = near_last(*inputs, arrived, after(near_pre, one, two))
    part_three = lax.ppermute(three, every_axis, plane_pairs(3, True))

    far_pre, part_one = after((far_pre, part_one), three)
    conv_grad, first, last = norm_back(expand_t, far_pre, near_pre, unit, spread, norm_gain)
    first, last, part_two = after((first, last, part_two))
    left, right = lon_halo(first, last)
    own, parts = after((own, (part_one, part_two, part_three)), first, last)
    own, *sent = split_four(own, parts)
    parts = [lax.ppermute(s, every_axis, plane_pairs(i + 1, False)) for i, s in enumerate(sent)]
    back = back_conv(after(conv_grad, sent), kernel, (0, 1))
    up, down = side_rows(*after((conv_grad, left, right), back))

    own, *sent = split_ring(*after((own, parts), up, down))
    parts = [lax.ppermute(s, every_axis, ring_pairs(i + 1)) for i, s in enumerate(sent)]
    top, bottom = lat_halo(up, down)
    back += back_conv(after(conv_grad, sent), kernel, (2,))

    own, sent = split_two(*after((own, parts), back, top, bottom))
    arrived = lax.ppermute(sent, every_axis, last_pairs())
    grad = after(grad, sent)
    gradient = finish(counts, back, kernel, left, right, top, bottom, grad)

    cells_all = lax.axis_size("dp") * lax.axis_size("lat") * lax.axis_size("lon") * total
    kept = last_sum(own, arrived, 1.0 / math.sqrt(cells_all))
    return (gradient.reshape(state.shape), *kept)


def solution(mesh):
    in_specs = (
        P("dp", "lat", "lon", None),
        P("dp", "lat", "lon", None),
        P("lat", "lon"),
        P(),
        P(),
        P(),
        P(),
        P(),
        P(),
        P(),
    )
    out_specs = (
        P("dp", "lat", "lon", None),
        P(None, ("dp", "lat", "lon"), None),
        P(None, ("dp", "lat", "lon"), None),
    )
    return jax.shard_map(local, mesh=mesh, in_specs=in_specs, out_specs=out_specs, check_vma=False)
```

```python
import functools
import itertools
import math

import jax
import jax.numpy as jnp
from jax import lax
from jax.experimental import pallas as pl
from jax.experimental.pallas import tpu as pltpu
from jax.sharding import PartitionSpec as P

norm_eps = 1e-06
inv_root_two_pi = 0.3989422804014327
side = 32
reach = 3
lanes = 128
f32 = jnp.float32
bf16 = jnp.bfloat16
whole = pl.BlockSpec(memory_space=pltpu.VMEM)


def params(mib):
    return pltpu.CompilerParams(vmem_limit_bytes=mib * 1024 * 1024)


def cost(microseconds):
    return pl.CostEstimate(
        flops=int(microseconds * 1.15e9), bytes_accessed=2**20, transcendentals=0
    )


def tap_row(kernel_ref, flipped, p, q, cols):
    index = 7 * p + q
    if flipped:
        index = 48 - index
    return kernel_ref[index, :, cols]


def shift_cols(rows, offset):
    if offset == 0:
        return rows
    count = rows.shape[0]
    turned = pltpu.roll(rows, (-offset) % count, 0)
    place = lax.broadcasted_iota(jnp.int32, (8, rows.shape[1]), 0)
    if offset > 0:
        last = jnp.where(place < 8 - offset, turned[count - 8 :], 0.0)
        return jnp.concatenate([turned[: count - 8], last], axis=0)
    first = jnp.where(place >= -offset, turned[:8], 0.0)
    return jnp.concatenate([first, turned[8:]], axis=0)


def inner_conv_body(parts, cells_ref, kernel_ref, *refs):
    outs, padded = refs[:-1], refs[-1]
    edge = reach * side
    total = side * side
    group = 4
    padded[0:edge] = jnp.zeros((edge, lanes), f32)
    padded[edge + total : 2 * edge + total] = jnp.zeros((edge, lanes), f32)
    for part, out_ref in zip(parts, outs):
        cols = slice(part * lanes, (part + 1) * lanes)
        padded[edge : edge + total] = cells_ref[:, cols]

        def some_rows(i, carry):
            base = pl.multiple_of(i * (group * side), group * side)
            rows = [padded[pl.ds(base + p * side, side), :] for p in range(6 + group)]
            results = [None] * group
            for q in range(7):
                sums = [None] * group
                for p in range(7):
                    tap = tap_row(kernel_ref, False, p, q, cols)
                    for g in range(group):
                        term = tap * rows[p + g]
                        sums[g] = term if sums[g] is None else sums[g] + term
                for g in range(group):
                    moved = shift_cols(sums[g], q - reach)
                    results[g] = moved if results[g] is None else results[g] + moved
            for g in range(group):
                out_ref[pl.ds(base + g * side, side), :] = results[g]
            return carry

        lax.fori_loop(0, side // group, some_rows, 0)


def inner_conv(cells, kernel, parts):
    total = cells.shape[0]
    shape = jax.ShapeDtypeStruct((total, lanes), f32)
    return pl.pallas_call(
        functools.partial(inner_conv_body, parts),
        out_shape=(shape,) * len(parts),
        in_specs=[whole] * 2,
        out_specs=[whole] * len(parts),
        scratch_shapes=[pltpu.VMEM((total + 2 * reach * side, lanes), f32)],
        compiler_params=params(6),
        cost_estimate=cost(2.2 * len(parts)),
        name="inner_conv",
    )(cells, kernel)


def back_conv_body(parts, cells_ref, kernel_ref, *refs):
    outs, (padded, taps) = refs[:-2], refs[-2:]
    edge = reach * side
    total = side * side
    group = 4
    padded[0:edge] = jnp.zeros((edge, lanes), bf16)
    padded[edge + total : 2 * edge + total] = jnp.zeros((edge, lanes), bf16)
    for part, out_ref in zip(parts, outs):
        cols = slice(part * lanes, (part + 1) * lanes)
        padded[edge : edge + total] = cells_ref[:, cols].astype(bf16)
        for p, q in itertools.product(range(7), range(7)):
            tap = jnp.broadcast_to(tap_row(kernel_ref, True, p, q, cols), (16, lanes))
            taps[7 * p + q] = tap.astype(bf16)

        def some_rows(i, carry):
            base = pl.multiple_of(i * (group * side), group * side)
            rows = [padded[pl.ds(base + p * side, side), :] for p in range(6 + group)]
            results = [None] * group
            for q in range(7):
                sums = [None] * group
                for p in range(7):
                    tap = jnp.concatenate([taps[7 * p + q]] * (side // 16), axis=0)
                    for g in range(group):
                        term = tap * rows[p + g]
                        sums[g] = term if sums[g] is None else sums[g] + term
                for g in range(group):
                    moved = shift_cols(sums[g].astype(f32), q - reach)
                    results[g] = moved if results[g] is None else results[g] + moved
            for g in range(group):
                out_ref[pl.ds(base + g * side, side), :] = results[g]
            return carry

        lax.fori_loop(0, side // group, some_rows, 0)


def back_conv(cells, kernel, parts):
    total = cells.shape[0]
    shape = jax.ShapeDtypeStruct((total, lanes), f32)
    return pl.pallas_call(
        functools.partial(back_conv_body, parts),
        out_shape=(shape,) * len(parts),
        in_specs=[whole] * 2,
        out_specs=[whole] * len(parts),
        scratch_shapes=[
            pltpu.VMEM((total + 2 * reach * side, lanes), bf16),
            pltpu.VMEM((49, 16, lanes), bf16),
        ],
        compiler_params=params(6),
        cost_estimate=cost(1.5 * len(parts)),
        name="back_conv",
    )(cells, kernel)


def side_cols_body(cells_ref, first_ref, last_ref, low, high, sems):
    copies = [
        pltpu.make_async_copy(cells_ref.at[:, pl.ds(0, 8), :], low, sems.at[0]),
        pltpu.make_async_copy(cells_ref.at[:, pl.ds(side - 8, 8), :], high, sems.at[1]),
    ]
    for copy in copies:
        copy.start()
    copies[0].wait()
    for j in range(reach):
        first_ref[j] = low[:, j, :].astype(bf16)
    copies[1].wait()
    for j in range(reach):
        last_ref[j] = high[:, 8 - reach + j, :].astype(bf16)


def side_cols(cells):
    channels = cells.shape[1]
    shape = jax.ShapeDtypeStruct((reach, side, channels), bf16)
    return pl.pallas_call(
        side_cols_body,
        out_shape=(shape, shape),
        in_specs=[pl.BlockSpec(memory_space=pltpu.HBM)],
        out_specs=[whole] * 2,
        scratch_shapes=[pltpu.VMEM((side, 8, channels), f32)] * 2 + [pltpu.SemaphoreType.DMA((2,))],
        compiler_params=params(58),
        cost_estimate=cost(1.0),
        name="side_cols",
    )(cells.reshape(side, side, channels))


def side_rows_body(cells_ref, left_ref, right_ref, up_ref, down_ref):
    channels = cells_ref.shape[1]
    place = lax.broadcasted_iota(jnp.int32, (8, channels), 0)
    blank = jnp.zeros((8, channels), f32)
    left = [left_ref[h].astype(f32) for h in range(reach)]
    right = [right_ref[h].astype(f32) for h in range(reach)]
    for r in range(reach):
        for row, ref in ((r, up_ref), (side - reach + r, down_ref)):
            corner = blank
            for h in range(reach):
                corner = jnp.where(place == h, right[h][row : row + 1], corner)
                corner = jnp.where(place == 8 - reach + h, left[h][row : row + 1], corner)
            body = cells_ref[row * side : (row + 1) * side]
            ref[r] = jnp.concatenate([body, corner, blank], axis=0).astype(bf16)


def side_rows(cells, left, right):
    channels = cells.shape[1]
    shape = jax.ShapeDtypeStruct((reach, side + 16, channels), bf16)
    return pl.pallas_call(
        side_rows_body,
        out_shape=(shape, shape),
        in_specs=[whole] * 3,
        out_specs=[whole] * 2,
        compiler_params=params(6),
        cost_estimate=cost(0.5),
        name="side_rows",
    )(cells, left, right)


def add_edges(flipped, kernel_ref, left_ref, right_ref, top_ref, bottom_ref, rows_sum, cols_sum):
    lat = lax.axis_index("lat")
    channels = kernel_ref.shape[2]
    for c in range(channels // lanes):
        cols = slice(c * lanes, (c + 1) * lanes)
        for low, ref in ((True, top_ref), (False, bottom_ref)):
            outside = lat == (0 if low else lax.axis_size("lat") - 1)
            beyond = [
                jnp.where(outside, 0.0, ref[h, :, cols].astype(f32)[: side + 8]) for h in range(reach)
            ]
            for r in range(reach):
                result = None
                steps = [(h, h - r) for h in range(r, reach)] if low else [
                    (h, 6 + h - r) for h in range(0, r + 1)
                ]
                for q in range(7):
                    summed = None
                    for h, p in steps:
                        term = tap_row(kernel_ref, flipped, p, q, cols) * beyond[h]
                        summed = term if summed is None else summed + term
                    summed = pltpu.roll(summed, (reach - q) % (side + 8), 0) if q != reach else summed
                    result = summed if result is None else result + summed
                rows_sum[r if low else reach + r, :, cols] = result[:side]
        for low, ref in ((True, left_ref), (False, right_ref)):
            beyond = [ref[h, :, cols].astype(f32) for h in range(reach)]
            for r in range(reach):
                steps = [(h, h - r) for h in range(r, reach)] if low else [
                    (h, 6 + h - r) for h in range(0, r + 1)
                ]
                result = None
                for p in range(7):
                    summed = None
                    for h, q in steps:
                        term = tap_row(kernel_ref, flipped, p, q, cols) * beyond[h]
                        summed = term if summed is None else summed + term
                    summed = shift_cols(summed, p - reach)
                    result = summed if result is None else result + summed
                cols_sum[r if low else reach + r, :, cols] = result


def edged_row(i, conv_row, cols_sum):
    channels = conv_row.shape[1]
    place = lax.broadcasted_iota(jnp.int32, (8, channels), 0)
    first, last = conv_row[:8], conv_row[side - 8 :]
    for r in range(reach):
        first = first + jnp.where(place == r, cols_sum[r, pl.ds(i, 1), :], 0.0)
        last = last + jnp.where(place == 8 - reach + r, cols_sum[reach + r, pl.ds(i, 1), :], 0.0)
    return jnp.concatenate([first, conv_row[8 : side - 8], last], axis=0)


def each_row(step):
    def low(i, carry):
        step(i, i)
        return carry

    def middle(i, carry):
        step(i, None)
        return carry

    def high(i, carry):
        step(i, i - (side - 2 * reach))
        return carry

    lax.fori_loop(0, reach, low, 0, unroll=reach)
    lax.fori_loop(reach, side - reach, middle, 0, unroll=side // 2 - reach)
    lax.fori_loop(side - reach, side, high, 0, unroll=reach)


def conv_rows(refs, at):
    return jnp.concatenate([ref[at, :] for ref in refs], axis=1)


def normalise_body(
    conv0_ref, conv1_ref, conv2_ref, kernel_ref, left_ref, right_ref, top_ref, bottom_ref, bias_ref, gain_ref, shift_ref,
    unit_ref, spread_ref, normed_ref, rows_sum, cols_sum,
):
    channels = kernel_ref.shape[2]
    conv_refs = (conv0_ref, conv1_ref, conv2_ref)
    add_edges(False, kernel_ref, left_ref, right_ref, top_ref, bottom_ref, rows_sum, cols_sum)
    share = 1.0 / channels

    def step(i, outer):
        at = pl.ds(pl.multiple_of(i * side, side), side)
        value = edged_row(i, conv_rows(conv_refs, at), cols_sum)
        if outer is not None:
            value = value + rows_sum[outer]
        value = value + bias_ref[...]
        mean = jnp.sum(value, axis=1, keepdims=True) * share
        centred = value - mean
        spread = lax.rsqrt(jnp.sum(centred * centred, axis=1, keepdims=True) * share + norm_eps)
        unit = centred * spread
        unit_ref[at, :] = unit
        spread_ref[at, :] = jnp.broadcast_to(spread, (side, lanes))
        normed_ref[at, :] = (unit * gain_ref[...] + shift_ref[...]).astype(bf16)

    each_row(step)


def turn(source_ref, target_ref):
    for b in range(source_ref.shape[0] // 256):
        at = slice(b * 256, (b + 1) * 256)
        target_ref[:, at] = source_ref[at, :].T


def normalise(conv, kernel, left, right, top, bottom, bias, gain, shift):
    total, channels = conv[0].shape[0], kernel.shape[2]
    return pl.pallas_call(
        normalise_body,
        out_shape=(
            jax.ShapeDtypeStruct((total, channels), f32),
            jax.ShapeDtypeStruct((total, lanes), f32),
            jax.ShapeDtypeStruct((total, channels), bf16),
        ),
        in_specs=[whole] * 11,
        out_specs=[whole] * 3,
        scratch_shapes=[pltpu.VMEM((2 * reach, side, channels), f32)] * 2,
        compiler_params=params(12),
        cost_estimate=cost(2.8),
        name="normalise",
    )(*conv, kernel, left, right, top, bottom, bias, gain, shift)


def wet_row(i, counts_ref):
    place = lax.broadcasted_iota(jnp.int32, (8, lanes), 0) + (i % 8) * 8
    pieces = []
    for t in range(side // 8):
        pieces.append(place < counts_ref[i // 8, t])
    return pieces


def masked_row(i, grad_row, counts_ref):
    channels = grad_row.shape[1]
    parts = []
    for t, wet in enumerate(wet_row(i, counts_ref)):
        piece = grad_row[t * 8 : (t + 1) * 8]
        parts.append(
            jnp.concatenate(
                [
                    jnp.where(wet, piece[:, c * lanes : (c + 1) * lanes], 0.0)
                    for c in range(channels // lanes)
                ],
                axis=1,
            )
        )
    return jnp.concatenate(parts, axis=0)


def mask_rows_body(counts_ref, grad_ref, rows_ref):
    def step(i, carry):
        at = pl.ds(pl.multiple_of(i * side, side), side)
        rows_ref[at, :] = masked_row(i, grad_ref[at, :], counts_ref).astype(bf16)
        return carry

    lax.fori_loop(0, side, step, 0, unroll=side)


def mask_rows(counts, grad):
    total, channels = grad.shape
    return pl.pallas_call(
        mask_rows_body,
        out_shape=jax.ShapeDtypeStruct((total, channels), bf16),
        in_specs=[pl.BlockSpec(memory_space=pltpu.SMEM), whole],
        out_specs=whole,
        compiler_params=params(8),
        cost_estimate=cost(0.9),
        name="mask_rows",
    )(counts, grad)


def arrange_body(expand_ref, reduce_ref, bias_ref, expand_out, reduce_out, turned_out, bias_out):
    channels = expand_ref.shape[1]
    new = lax.broadcasted_iota(jnp.int32, (96, 96), 0)
    old = lax.broadcasted_iota(jnp.int32, (96, 96), 1)
    lo, rest = new // 48, new % 48
    pick = old == (rest // 6) * 12 + lo * 6 + rest % 6
    chosen = pick.astype(f32).astype(bf16)
    for hi, y, core in itertools.product(range(2), range(4), range(2)):
        unit = (hi * 4 + y) * 2 + core
        at = slice(unit * 96, (unit + 1) * 96)
        both = jnp.concatenate([expand_ref[at, :], reduce_ref[at, :]], axis=1)
        moved = jnp.dot(chosen, both, preferred_element_type=f32).astype(bf16)
        column = jnp.sum(jnp.where(pick, bias_ref[:, at], 0.0), axis=1, keepdims=True)
        column = jnp.broadcast_to(column, (96, lanes))
        for lo_place in range(2):
            x = 2 * hi + lo_place
            place = core * 16 + (y * 4 + x if core == 0 else x * 4 + y)
            to = slice(place * 48, (place + 1) * 48)
            half = slice(lo_place * 48, (lo_place + 1) * 48)
            expand_out[to, :] = moved[half, :channels]
            reduce_out[to, :] = moved[half, channels:]
            bias_out[to, :] = column[half]
    turn(expand_out, turned_out)


def arrange(expand, reduce, bias):
    units, channels = expand.shape
    shape = jax.ShapeDtypeStruct((units, channels), bf16)
    return pl.pallas_call(
        arrange_body,
        out_shape=(
            shape,
            shape,
            jax.ShapeDtypeStruct((channels, units), bf16),
            jax.ShapeDtypeStruct((units, lanes), f32),
        ),
        in_specs=[whole] * 3,
        out_specs=[whole] * 4,
        compiler_params=params(12),
        cost_estimate=cost(1.5),
        name="arrange",
    )(expand, reduce, bias)


tail_slope = 0.3275911 * 0.7071067811865476
tail_terms = [
    0.5 * a for a in (0.254829592, -0.284496736, 1.421413741, -1.453152027, 1.061405429)
]
exp_scale = -0.5 * 1.4426950408889634


def gelu_pair(v):
    d = 1.0 + tail_slope * jnp.abs(v)
    t = pltpu.reciprocal(d, approx=True)
    poly = tail_terms[4]
    for a in reversed(tail_terms[:4]):
        poly = poly * t + a
    bell = jnp.exp2(v * v * exp_scale)
    tail = poly * t * bell
    below = jnp.where(v >= 0.0, 1.0 - tail, tail)
    return v * below, below + v * bell * inv_root_two_pi


def own_place():
    lat, lon = lax.axis_index("lat"), lax.axis_index("lon")
    x = 2 * lax.axis_index("dp") + (lon & 1)
    return lat & 1, x, lat >> 1, lon >> 1


def phase_place(second):
    core, x, y, _ = own_place()
    along_y = core == (1 if second else 0)
    return jnp.where(along_y, y, x)


def dot_rows(left, right):
    return lax.dot_general(left, right, (((1,), (1,)), ((), ())), preferred_element_type=f32)


class HiddenBlock:

    def __init__(self, cells, sources, rows, grad_pre_ref, places, scratch):
        self.normed, self.grad, self.expand, self.reduce, self.bias = cells
        self.sources, self.rows, self.places = sources, rows, places
        self.grad_pre = grad_pre_ref
        self.preact, self.grad_hidden, self.hidden, self.terms = scratch
        self.total = self.normed.shape[0]

    def gather(self, ref):
        return jnp.concatenate([ref[pl.ds(s, self.rows), :] for s in self.sources], axis=0)

    def dots(self, at):
        self.preact[:, at] = dot_rows(self.gather(self.expand), self.normed[at, :])
        self.grad_hidden[:, at] = dot_rows(self.gather(self.reduce), self.grad[at, :])

    def activate(self, at):
        bias = jnp.concatenate([self.gather(self.bias)] * ((at.stop - at.start) // lanes), axis=1)
        value, slope = gelu_pair(self.preact[:, at] + bias)
        self.hidden[:, at] = value.astype(bf16)
        grad_pre = (self.grad_hidden[:, at] * slope).astype(bf16)
        self.terms[:, at] = grad_pre
        for n, place in enumerate(self.places):
            self.grad_pre[pl.ds(place, self.rows), at] = grad_pre[n * self.rows : (n + 1) * self.rows]

    def expand_sum(self):
        return jnp.dot(self.terms[...], self.normed[...], preferred_element_type=f32)

    def reduce_sum(self):
        return jnp.dot(self.hidden[...], self.grad[...], preferred_element_type=f32)


def hidden_scratch(rows, total):
    return [
        pltpu.VMEM((rows, total), f32),
        pltpu.VMEM((rows, total), f32),
        pltpu.VMEM((rows, total), bf16),
        pltpu.VMEM((rows, total), bf16),
    ]


def far_body(*refs):
    cells, (sent_ref, grad_pre_ref), scratch = refs[:5], refs[5:7], refs[7:]
    half, total = grad_pre_ref.shape
    channels = refs[0].shape[1]
    base = (1 - own_place()[0]) * half
    rows = half // 2
    blocks = [
        HiddenBlock(
            cells, [pl.multiple_of(base + b * rows, rows)], rows, grad_pre_ref, [b * rows],
            scratch[4 * b : 4 * b + 4],
        )
        for b in range(2)
    ]
    first, second = blocks
    pieces = [slice(c, c + 256) for c in range(0, total, 256)]
    for at in pieces:
        first.dots(at)
    for at in pieces:
        first.activate(at)
        second.dots(at)
    second.activate(pieces[0])
    sent_ref[:rows, :channels] = first.expand_sum().astype(bf16)
    second.activate(pieces[1])
    sent_ref[:rows, channels:] = first.reduce_sum().astype(bf16)
    for at in pieces[2:]:
        second.activate(at)
    sent_ref[rows:, :channels] = second.expand_sum().astype(bf16)
    sent_ref[rows:, channels:] = second.reduce_sum().astype(bf16)


def hidden_far(*cells):
    total, channels = cells[0].shape
    half = cells[2].shape[0] // 2
    return pl.pallas_call(
        far_body,
        out_shape=(
            jax.ShapeDtypeStruct((half, 2 * channels), bf16),
            jax.ShapeDtypeStruct((half, total), bf16),
        ),
        in_specs=[whole] * 5,
        out_specs=[whole] * 2,
        scratch_shapes=hidden_scratch(half // 2, total) * 2,
        compiler_params=params(20),
        cost_estimate=cost(5.0),
        name="hidden_far",
    )(*cells)


def near_first_body(*refs):
    cells, (sums_ref, grad_pre_ref), scratch = refs[:5], refs[5:7], refs[7:]
    half = grad_pre_ref.shape[0]
    channels = refs[0].shape[1]
    size = half // 4
    core, place = own_place()[0], phase_place(False)
    chunks = [pl.multiple_of(lax.rem(place + step, 4) * size, size) for step in (2, 1)]
    sources = [pl.multiple_of(core * half + chunk, size) for chunk in chunks]
    block = HiddenBlock(cells, sources, size, grad_pre_ref, chunks, scratch)
    block.dots(slice(0, block.total))
    block.activate(slice(0, block.total))
    sums_ref[:, :channels] = block.expand_sum()
    sums_ref[:, channels:] = block.reduce_sum()


def near_first(*cells):
    total, channels = cells[0].shape
    half = cells[2].shape[0] // 2
    return pl.pallas_call(
        near_first_body,
        out_shape=(
            jax.ShapeDtypeStruct((half // 2, 2 * channels), f32),
            jax.ShapeDtypeStruct((half, total), bf16),
        ),
        in_specs=[whole] * 5,
        out_specs=[whole] * 2,
        scratch_shapes=hidden_scratch(half // 2, total),
        compiler_params=params(16),
        cost_estimate=cost(3.0),
        name="near_first",
    )(*cells)


def near_sends_body(sums_ref, arrived_ref, *sent_refs):
    size = sent_refs[0].shape[0]
    place = phase_place(False)
    for n, step in enumerate((2, 1)):
        chunk = pl.multiple_of(lax.rem(place + step, 4) * size, size)
        total = sums_ref[n * size : (n + 1) * size] + arrived_ref[pl.ds(chunk, size), :].astype(f32)
        sent_refs[n][...] = total.astype(bf16)


def near_sends(sums, arrived):
    size, width = sums.shape[0] // 2, sums.shape[1]
    sent = jax.ShapeDtypeStruct((size, width), bf16)
    return pl.pallas_call(
        near_sends_body,
        out_shape=(sent, sent),
        in_specs=[whole] * 2,
        out_specs=[whole] * 2,
        compiler_params=params(6),
        cost_estimate=cost(0.3),
        name="near_sends",
    )(sums, arrived)


def near_last_body(*refs):
    cells, (arrived_ref, _, own_ref, sent_ref, grad_pre_ref) = refs[:5], refs[5:10]
    half = grad_pre_ref.shape[0]
    channels = refs[0].shape[1]
    size = half // 4
    core, place = own_place()[0], phase_place(False)
    chunks = [pl.multiple_of(lax.rem(place + step, 4) * size, size) for step in (3, 0)]
    sources = [pl.multiple_of(core * half + chunk, size) for chunk in chunks]
    block = HiddenBlock(cells, sources, size, grad_pre_ref, chunks, refs[10:])
    block.dots(slice(0, block.total))
    block.activate(slice(0, block.total))
    expand, reduce = block.expand_sum(), block.reduce_sum()
    for n, (chunk, ref) in enumerate(zip(chunks, (sent_ref, own_ref))):
        at = slice(n * size, (n + 1) * size)
        other = arrived_ref[pl.ds(chunk, size), :].astype(f32)
        ref[:, :channels] = (expand[at] + other[:, :channels]).astype(ref.dtype)
        ref[:, channels:] = (reduce[at] + other[:, channels:]).astype(ref.dtype)


def near_last(*inputs):
    cells, grad_pre = inputs[:5], inputs[6]
    channels = cells[0].shape[1]
    size = cells[2].shape[0] // 8
    return pl.pallas_call(
        near_last_body,
        out_shape=(
            jax.ShapeDtypeStruct((size, 2 * channels), f32),
            jax.ShapeDtypeStruct((size, 2 * channels), bf16),
            jax.ShapeDtypeStruct(grad_pre.shape, bf16),
        ),
        in_specs=[whole] * 7,
        out_specs=[whole] * 3,
        input_output_aliases={6: 2},
        scratch_shapes=hidden_scratch(2 * size, cells[0].shape[0]),
        compiler_params=params(16),
        cost_estimate=cost(3.0),
        name="near_last",
    )(*inputs)


def norm_back_body(
    turned_ref, other_ref, mine_ref, unit_ref, spread_ref, gain_ref,
    conv_grad_ref, first_ref, last_ref,
):
    total, channels = unit_ref.shape
    half = turned_ref.shape[1] // 2
    core = own_place()[0]
    block = 256
    share = 1.0 / channels
    mine_weight = turned_ref[:, pl.ds(pl.multiple_of(core * half, half), half)]
    other_weight = turned_ref[:, pl.ds(pl.multiple_of((1 - core) * half, half), half)]
    for b in range(total // block):
        at = slice(b * block, (b + 1) * block)
        summed = jnp.dot(mine_weight, mine_ref[:, at], preferred_element_type=f32)
        summed = summed + jnp.dot(other_weight, other_ref[:, at], preferred_element_type=f32)
        grad_normed = summed.astype(bf16).T.astype(f32)
        unit = unit_ref[at, :]
        grad_unit = grad_normed * gain_ref[...]
        mean_grad = jnp.sum(grad_unit, axis=1, keepdims=True) * share
        mean_cross = jnp.sum(grad_unit * unit, axis=1, keepdims=True) * share
        spread = jnp.concatenate([spread_ref[at, :]] * (channels // lanes), axis=1)
        value = (grad_unit - mean_grad - unit * mean_cross) * spread
        conv_grad_ref[b * 8 : (b + 1) * 8] = value.reshape(block // side, side, channels)
    for j in range(reach):
        first_ref[j] = conv_grad_ref[:, j, :].astype(bf16)
        last_ref[j] = conv_grad_ref[:, side - reach + j, :].astype(bf16)


def norm_back(turned, other, mine, unit, spread, gain):
    total, channels = unit.shape
    shape = jax.ShapeDtypeStruct((reach, side, channels), bf16)
    found, first, last = pl.pallas_call(
        norm_back_body,
        out_shape=(jax.ShapeDtypeStruct((side, side, channels), f32), shape, shape),
        in_specs=[whole] * 6,
        out_specs=[whole] * 3,
        compiler_params=params(14),
        cost_estimate=cost(0.2),
        name="norm_back",
    )(turned, other, mine, unit, spread, gain)
    return found.reshape(total, channels), first, last


def finish_body(
    counts_ref, conv0_ref, conv1_ref, conv2_ref, kernel_ref, left_ref, right_ref, top_ref, bottom_ref,
    grad_ref, out_ref, rows_sum, cols_sum, done, sems,
):
    conv_refs = (conv0_ref, conv1_ref, conv2_ref)
    add_edges(True, kernel_ref, left_ref, right_ref, top_ref, bottom_ref, rows_sum, cols_sum)
    rows = 8
    copies = []
    for block in range(side // rows):
        for i in range(block * rows, (block + 1) * rows):
            at = slice(i * side, (i + 1) * side)
            value = edged_row(i, conv_rows(conv_refs, at), cols_sum)
            if i < reach:
                value = value + rows_sum[i]
            if i >= side - reach:
                value = value + rows_sum[i - (side - 2 * reach)]
            done[at, :] = value + masked_row(i, grad_ref[at, :], counts_ref)
        part = pl.ds(block * rows * side, rows * side)
        copies.append(pltpu.make_async_copy(done.at[part, :], out_ref.at[part, :], sems.at[block]))
        copies[-1].start()
    for copy in copies:
        copy.wait()


def finish(counts, conv, kernel, left, right, top, bottom, grad):
    total, channels = grad.shape
    return pl.pallas_call(
        finish_body,
        out_shape=jax.ShapeDtypeStruct((total, channels), f32),
        in_specs=[pl.BlockSpec(memory_space=pltpu.SMEM)] + [whole] * 9,
        out_specs=pl.BlockSpec(memory_space=pltpu.HBM),
        scratch_shapes=[pltpu.VMEM((2 * reach, side, channels), f32)] * 2
        + [pltpu.VMEM((total, channels), f32), pltpu.SemaphoreType.DMA((4,))],
        compiler_params=params(12),
        cost_estimate=cost(2.5),
        name="finish",
    )(counts, *conv, kernel, left, right, top, bottom, grad)


def split_four_body(own_ref, first_ref, second_ref, third_ref, kept_ref, *sent_refs):
    size = kept_ref.shape[0]
    place = phase_place(True)
    for step in range(4):
        at = pl.ds(pl.multiple_of(lax.rem(place + step, 4) * size, size), size)
        total = own_ref[at, :]
        for ref in (first_ref, second_ref, third_ref):
            total = total + ref[at, :].astype(f32)
        if step == 0:
            kept_ref[...] = total
        else:
            sent_refs[step - 1][...] = total.astype(bf16)


def split_four(own, parts):
    size, width = own.shape[0] // 4, own.shape[1]
    sent = jax.ShapeDtypeStruct((size, width), bf16)
    return pl.pallas_call(
        split_four_body,
        out_shape=(jax.ShapeDtypeStruct((size, width), f32), sent, sent, sent),
        in_specs=[whole] * 4,
        out_specs=[whole] * 4,
        compiler_params=params(4),
        cost_estimate=cost(0.3),
        name="split_four",
    )(own, *parts)


def split_two_body(own_ref, *refs):
    part_refs, (kept_ref, sent_ref) = refs[:-2], refs[-2:]
    size = kept_ref.shape[0]
    total = own_ref[...]
    for ref in part_refs:
        total = total + ref[...].astype(f32)
    low, high = total[:size], total[size:]
    upper = (own_place()[3] & 1) != 0
    kept_ref[...] = jnp.where(upper, high, low)
    sent_ref[...] = jnp.where(upper, low, high)


def split_two(own, parts):
    shape = jax.ShapeDtypeStruct((own.shape[0] // 2, own.shape[1]), f32)
    return pl.pallas_call(
        split_two_body,
        out_shape=(shape, shape),
        in_specs=[whole] * (1 + len(parts)),
        out_specs=[whole] * 2,
        compiler_params=params(4),
        cost_estimate=cost(0.2),
        name="split_two",
    )(own, *parts)


def split_ring_body(own_ref, first_ref, second_ref, third_ref, kept_ref, *sent_refs):
    size = kept_ref.shape[0]
    total = own_ref[...]
    for ref in (first_ref, second_ref, third_ref):
        total = total + ref[...].astype(f32)
    chunks = [total[c * size : (c + 1) * size] for c in range(4)]
    place = own_place()[3] >> 1
    for step, ref in enumerate((kept_ref, *sent_refs)):
        wanted = (place + step) & 3
        found = chunks[0]
        for c in range(1, 4):
            found = jnp.where(wanted == c, chunks[c], found)
        ref[...] = found


def split_ring(own, parts):
    shape = jax.ShapeDtypeStruct((own.shape[0] // 4, own.shape[1]), f32)
    return pl.pallas_call(
        split_ring_body,
        out_shape=(shape,) * 4,
        in_specs=[whole] * 4,
        out_specs=[whole] * 4,
        compiler_params=params(4),
        cost_estimate=cost(0.2),
        name="split_ring",
    )(own, *parts)


def last_sum_body(scale, own_ref, arrived_ref, expand_ref, reduce_ref):
    channels = expand_ref.shape[2]
    total = (own_ref[...] + arrived_ref[...]) * scale
    for r in range(total.shape[0]):
        expand_ref[r] = total[r : r + 1, :channels]
        reduce_ref[r] = total[r : r + 1, channels:]


def last_sum(own, arrived, scale):
    size, width = own.shape
    shape = jax.ShapeDtypeStruct((size, 1, width // 2), f32)
    expand, reduce = pl.pallas_call(
        functools.partial(last_sum_body, scale),
        out_shape=(shape, shape),
        in_specs=[whole] * 2,
        out_specs=[whole] * 2,
        compiler_params=params(4),
        cost_estimate=cost(0.4),
        name="last_sum",
    )(own, arrived)
    return expand.transpose(1, 0, 2), reduce.transpose(1, 0, 2)


every_axis = ("dp", "lat", "lon")


def device_pairs(move):
    def flat(hi, y, core, z, lo):
        return (hi * 8 + y * 2 + core) * 16 + z * 2 + lo

    found = []
    for hi, y, core, z, lo in itertools.product(range(2), range(4), range(2), range(8), range(2)):
        found.append((flat(hi, y, core, z, lo), flat(*move(hi, y, core, z, lo))))
    return found


def plane_pairs(step, first):
    def move(hi, y, core, z, lo):
        if (core == 0) == first:
            return (hi, (y + step) % 4, core, z, lo)
        x = (2 * hi + lo + step) % 4
        return (x // 2, y, core, z, x % 2)

    return device_pairs(move)


def ring_pairs(step):
    return device_pairs(lambda hi, y, core, z, lo: (hi, y, core, (z + 2 * step) % 8, lo))


def last_pairs():
    return device_pairs(lambda hi, y, core, z, lo: (hi, y, core, z ^ 1, lo))


def shifted(axis, step):
    count = lax.axis_size(axis)
    return [(i, (i + step) % count) for i in range(count)]


def lon_halo(first, last):
    left = lax.ppermute(last, "lon", shifted("lon", 1))
    right = lax.ppermute(first, "lon", shifted("lon", -1))
    return left, right


def lat_halo(up, down):
    top = lax.ppermute(down, "lat", shifted("lat", 1))
    bottom = lax.ppermute(up, "lat", shifted("lat", -1))
    return top, bottom


def after(value, *others):
    return lax.optimization_barrier((value, others))[0]


def local(
    state, cotangent, counts, dw_kernel, dw_bias, norm_gain, norm_bias, w_expand, b_expand, w_reduce
):
    channels = state.shape[-1]
    cells = state.reshape(-1, channels)
    grad = cotangent.reshape(-1, channels)
    total = cells.shape[0]
    kernel = dw_kernel.transpose(1, 0, 2)

    first, last = side_cols(cells)
    left, right = lon_halo(first, last)
    conv = inner_conv(cells, kernel, (0,))
    grad, w_expand, w_reduce = after((grad, w_expand, w_reduce), first, last)
    rows = mask_rows(counts, grad)
    expand, reduce, expand_t, bias = arrange(w_expand[0], w_reduce[0], b_expand)
    left, right = after((left, right), rows, bias, conv)
    up, down = side_rows(cells, left, right)
    top, bottom = lat_halo(up, down)
    conv += inner_conv(after(cells, up, down), kernel, (1, 2))
    unit, spread, normed = normalise(
        conv, kernel, left, right, top, bottom, dw_bias, norm_gain, norm_bias
    )

    inputs = (normed, rows, expand, reduce, bias)
    sent, far_pre = hidden_far(*inputs)
    arrived = lax.ppermute(sent, "lat", [(i, i ^ 1) for i in range(8)])
    sums, near_pre = near_first(*inputs)
    two, one = near_sends(sums, arrived)
    part_two = lax.ppermute(two, every_axis, plane_pairs(2, True))
    part_one = lax.ppermute(one, every_axis, plane_pairs(1, True))
    own, three, near_pre = near_last(*inputs, arrived, after(near_pre, one, two))
    part_three = lax.ppermute(three, every_axis, plane_pairs(3, True))

    far_pre, part_one = after((far_pre, part_one), three)
    conv_grad, first, last = norm_back(expand_t, far_pre, near_pre, unit, spread, norm_gain)
    first, last, part_two = after((first, last, part_two))
    left, right = lon_halo(first, last)
    own, parts = after((own, (part_one, part_two, part_three)), first, last)
    own, *sent = split_four(own, parts)
    parts = [lax.ppermute(sent[i], every_axis, plane_pairs(i + 1, False)) for i in (1, 0, 2)]
    back = back_conv(after(conv_grad, sent), kernel, (0, 1))
    up, down = side_rows(*after((conv_grad, left, right), back))

    own, *sent = split_ring(*after((own, parts), up, down))
    parts = [lax.ppermute(sent[i], every_axis, ring_pairs(i + 1)) for i in (1, 0, 2)]
    top, bottom = lat_halo(up, down)
    back += back_conv(after(conv_grad, sent), kernel, (2,))

    own, sent = split_two(*after((own, parts), back, top, bottom))
    arrived = lax.ppermute(sent, every_axis, last_pairs())
    grad = after(grad, sent)
    gradient = finish(counts, back, kernel, left, right, top, bottom, grad)

    cells_all = lax.axis_size("dp") * lax.axis_size("lat") * lax.axis_size("lon") * total
    kept = last_sum(own, arrived, 1.0 / math.sqrt(cells_all))
    return (gradient.reshape(state.shape), *kept)


def solution(mesh):
    in_specs = (
        P("dp", "lat", "lon", None),
        P("dp", "lat", "lon", None),
        P("lat", "lon"),
        P(),
        P(),
        P(),
        P(),
        P(),
        P(),
        P(),
    )
    out_specs = (
        P("dp", "lat", "lon", None),
        P(None, ("dp", "lat", "lon"), None),
        P(None, ("dp", "lat", "lon"), None),
    )
    return jax.shard_map(local, mesh=mesh, in_specs=in_specs, out_specs=out_specs, check_vma=False)
```

```python
import functools
import itertools
import math

import jax
import jax.numpy as jnp
from jax import lax
from jax.experimental import pallas as pl
from jax.experimental.pallas import tpu as pltpu
from jax.sharding import PartitionSpec as P

norm_eps = 1e-06
inv_root_two_pi = 0.3989422804014327
side = 32
reach = 3
lanes = 128
f32 = jnp.float32
bf16 = jnp.bfloat16
whole = pl.BlockSpec(memory_space=pltpu.VMEM)


def params(mib):
    return pltpu.CompilerParams(vmem_limit_bytes=mib * 1024 * 1024)


def cost(microseconds):
    return pl.CostEstimate(
        flops=int(microseconds * 1.15e9), bytes_accessed=2**20, transcendentals=0
    )


def tap_row(kernel_ref, flipped, p, q, cols):
    index = 7 * p + q
    if flipped:
        index = 48 - index
    return kernel_ref[index, :, cols]


def shift_cols(rows, offset):
    if offset == 0:
        return rows
    count = rows.shape[0]
    turned = pltpu.roll(rows, (-offset) % count, 0)
    place = lax.broadcasted_iota(jnp.int32, (8, rows.shape[1]), 0)
    if offset > 0:
        last = jnp.where(place < 8 - offset, turned[count - 8 :], 0.0)
        return jnp.concatenate([turned[: count - 8], last], axis=0)
    first = jnp.where(place >= -offset, turned[:8], 0.0)
    return jnp.concatenate([first, turned[8:]], axis=0)


def inner_conv_body(parts, cells_ref, kernel_ref, *refs):
    outs, padded = refs[:-1], refs[-1]
    edge = reach * side
    total = side * side
    group = 4
    padded[0:edge] = jnp.zeros((edge, lanes), f32)
    padded[edge + total : 2 * edge + total] = jnp.zeros((edge, lanes), f32)
    for part, out_ref in zip(parts, outs):
        cols = slice(part * lanes, (part + 1) * lanes)
        padded[edge : edge + total] = cells_ref[:, cols]

        def some_rows(i, carry):
            base = pl.multiple_of(i * (group * side), group * side)
            rows = [padded[pl.ds(base + p * side, side), :] for p in range(6 + group)]
            results = [None] * group
            for q in range(7):
                sums = [None] * group
                for p in range(7):
                    tap = tap_row(kernel_ref, False, p, q, cols)
                    for g in range(group):
                        term = tap * rows[p + g]
                        sums[g] = term if sums[g] is None else sums[g] + term
                for g in range(group):
                    moved = shift_cols(sums[g], q - reach)
                    results[g] = moved if results[g] is None else results[g] + moved
            for g in range(group):
                out_ref[pl.ds(base + g * side, side), :] = results[g]
            return carry

        lax.fori_loop(0, side // group, some_rows, 0)


def inner_conv(cells, kernel, parts):
    total = cells.shape[0]
    shape = jax.ShapeDtypeStruct((total, lanes), f32)
    return pl.pallas_call(
        functools.partial(inner_conv_body, parts),
        out_shape=(shape,) * len(parts),
        in_specs=[whole] * 2,
        out_specs=[whole] * len(parts),
        scratch_shapes=[pltpu.VMEM((total + 2 * reach * side, lanes), f32)],
        compiler_params=params(6),
        cost_estimate=cost(2.2 * len(parts)),
        name="inner_conv",
    )(cells, kernel)


def back_conv_body(parts, cells_ref, kernel_ref, *refs):
    outs, (padded, taps) = refs[:-2], refs[-2:]
    edge = reach * side
    total = side * side
    group = 4
    padded[0:edge] = jnp.zeros((edge, lanes), bf16)
    padded[edge + total : 2 * edge + total] = jnp.zeros((edge, lanes), bf16)
    for part, out_ref in zip(parts, outs):
        cols = slice(part * lanes, (part + 1) * lanes)
        padded[edge : edge + total] = cells_ref[:, cols].astype(bf16)
        for p, q in itertools.product(range(7), range(7)):
            tap = jnp.broadcast_to(tap_row(kernel_ref, True, p, q, cols), (16, lanes))
            taps[7 * p + q] = tap.astype(bf16)

        def some_rows(i, carry):
            base = pl.multiple_of(i * (group * side), group * side)
            rows = [padded[pl.ds(base + p * side, side), :] for p in range(6 + group)]
            results = [None] * group
            for q in range(7):
                sums = [None] * group
                for p in range(7):
                    tap = jnp.concatenate([taps[7 * p + q]] * (side // 16), axis=0)
                    for g in range(group):
                        term = tap * rows[p + g]
                        sums[g] = term if sums[g] is None else sums[g] + term
                for g in range(group):
                    moved = shift_cols(sums[g].astype(f32), q - reach)
                    results[g] = moved if results[g] is None else results[g] + moved
            for g in range(group):
                out_ref[pl.ds(base + g * side, side), :] = results[g]
            return carry

        lax.fori_loop(0, side // group, some_rows, 0)


def back_conv(cells, kernel, parts):
    total = cells.shape[0]
    shape = jax.ShapeDtypeStruct((total, lanes), f32)
    return pl.pallas_call(
        functools.partial(back_conv_body, parts),
        out_shape=(shape,) * len(parts),
        in_specs=[whole] * 2,
        out_specs=[whole] * len(parts),
        scratch_shapes=[
            pltpu.VMEM((total + 2 * reach * side, lanes), bf16),
            pltpu.VMEM((49, 16, lanes), bf16),
        ],
        compiler_params=params(6),
        cost_estimate=cost(1.5 * len(parts)),
        name="back_conv",
    )(cells, kernel)


def side_cols_body(cells_ref, first_ref, last_ref, low, high, sems):
    copies = [
        pltpu.make_async_copy(cells_ref.at[:, pl.ds(0, 8), :], low, sems.at[0]),
        pltpu.make_async_copy(cells_ref.at[:, pl.ds(side - 8, 8), :], high, sems.at[1]),
    ]
    for copy in copies:
        copy.start()
    copies[0].wait()
    for j in range(reach):
        first_ref[j] = low[:, j, :].astype(bf16)
    copies[1].wait()
    for j in range(reach):
        last_ref[j] = high[:, 8 - reach + j, :].astype(bf16)


def side_cols(cells):
    channels = cells.shape[1]
    shape = jax.ShapeDtypeStruct((reach, side, channels), bf16)
    return pl.pallas_call(
        side_cols_body,
        out_shape=(shape, shape),
        in_specs=[pl.BlockSpec(memory_space=pltpu.HBM)],
        out_specs=[whole] * 2,
        scratch_shapes=[pltpu.VMEM((side, 8, channels), f32)] * 2 + [pltpu.SemaphoreType.DMA((2,))],
        compiler_params=params(58),
        cost_estimate=cost(1.0),
        name="side_cols",
    )(cells.reshape(side, side, channels))


def side_rows_body(cells_ref, left_ref, right_ref, up_ref, down_ref):
    channels = cells_ref.shape[1]
    place = lax.broadcasted_iota(jnp.int32, (8, channels), 0)
    blank = jnp.zeros((8, channels), f32)
    left = [left_ref[h].astype(f32) for h in range(reach)]
    right = [right_ref[h].astype(f32) for h in range(reach)]
    for r in range(reach):
        for row, ref in ((r, up_ref), (side - reach + r, down_ref)):
            corner = blank
            for h in range(reach):
                corner = jnp.where(place == h, right[h][row : row + 1], corner)
                corner = jnp.where(place == 8 - reach + h, left[h][row : row + 1], corner)
            body = cells_ref[row * side : (row + 1) * side]
            ref[r] = jnp.concatenate([body, corner, blank], axis=0).astype(bf16)


def side_rows(cells, left, right):
    channels = cells.shape[1]
    shape = jax.ShapeDtypeStruct((reach, side + 16, channels), bf16)
    return pl.pallas_call(
        side_rows_body,
        out_shape=(shape, shape),
        in_specs=[whole] * 3,
        out_specs=[whole] * 2,
        compiler_params=params(6),
        cost_estimate=cost(0.5),
        name="side_rows",
    )(cells, left, right)


def beyond_steps(low, r):
    if low:
        return [(h, h - r) for h in range(r, reach)]
    return [(h, 6 + h - r) for h in range(0, r + 1)]


def add_rows(flipped, kernel_ref, top_ref, bottom_ref, rows_sum):
    lat = lax.axis_index("lat")
    channels = kernel_ref.shape[2]
    for c in range(channels // lanes):
        cols = slice(c * lanes, (c + 1) * lanes)
        for low, ref in ((True, top_ref), (False, bottom_ref)):
            outside = lat == (0 if low else lax.axis_size("lat") - 1)
            beyond = [
                jnp.where(outside, 0.0, ref[h, :, cols].astype(f32)[: side + 8]) for h in range(reach)
            ]
            for r in range(reach):
                result = None
                for q in range(7):
                    summed = None
                    for h, p in beyond_steps(low, r):
                        term = tap_row(kernel_ref, flipped, p, q, cols) * beyond[h]
                        summed = term if summed is None else summed + term
                    summed = pltpu.roll(summed, (reach - q) % (side + 8), 0) if q != reach else summed
                    result = summed if result is None else result + summed
                rows_sum[r if low else reach + r, :, cols] = result[:side]


def add_cols(flipped, kernel_ref, left_ref, right_ref, cols_sum):
    channels = kernel_ref.shape[2]
    for c in range(channels // lanes):
        cols = slice(c * lanes, (c + 1) * lanes)
        for low, ref in ((True, left_ref), (False, right_ref)):
            beyond = [ref[h, :, cols].astype(f32) for h in range(reach)]
            for r in range(reach):
                result = None
                for p in range(7):
                    summed = None
                    for h, q in beyond_steps(low, r):
                        term = tap_row(kernel_ref, flipped, p, q, cols) * beyond[h]
                        summed = term if summed is None else summed + term
                    summed = shift_cols(summed, p - reach)
                    result = summed if result is None else result + summed
                cols_sum[r if low else reach + r, :, cols] = result


def edged_row(i, conv_row, cols_sum):
    channels = conv_row.shape[1]
    place = lax.broadcasted_iota(jnp.int32, (8, channels), 0)
    first, last = conv_row[:8], conv_row[side - 8 :]
    for r in range(reach):
        first = first + jnp.where(place == r, cols_sum[r, pl.ds(i, 1), :], 0.0)
        last = last + jnp.where(place == 8 - reach + r, cols_sum[reach + r, pl.ds(i, 1), :], 0.0)
    return jnp.concatenate([first, conv_row[8 : side - 8], last], axis=0)


def each_row(step):
    def low(i, carry):
        step(i, i)
        return carry

    def middle(i, carry):
        step(i, None)
        return carry

    def high(i, carry):
        step(i, i - (side - 2 * reach))
        return carry

    lax.fori_loop(0, reach, low, 0, unroll=reach)
    lax.fori_loop(reach, side - reach, middle, 0, unroll=side // 2 - reach)
    lax.fori_loop(side - reach, side, high, 0, unroll=reach)


def conv_rows(refs, at):
    return jnp.concatenate([ref[at, :] for ref in refs], axis=1)


def normalise_body(
    conv0_ref, conv1_ref, conv2_ref, kernel_ref, left_ref, right_ref, top_ref, bottom_ref, bias_ref, gain_ref, shift_ref,
    unit_ref, spread_ref, normed_ref, rows_sum, cols_sum,
):
    channels = kernel_ref.shape[2]
    conv_refs = (conv0_ref, conv1_ref, conv2_ref)
    add_rows(False, kernel_ref, top_ref, bottom_ref, rows_sum)
    add_cols(False, kernel_ref, left_ref, right_ref, cols_sum)
    share = 1.0 / channels

    def step(i, outer):
        at = pl.ds(pl.multiple_of(i * side, side), side)
        value = edged_row(i, conv_rows(conv_refs, at), cols_sum)
        if outer is not None:
            value = value + rows_sum[outer]
        value = value + bias_ref[...]
        mean = jnp.sum(value, axis=1, keepdims=True) * share
        centred = value - mean
        spread = lax.rsqrt(jnp.sum(centred * centred, axis=1, keepdims=True) * share + norm_eps)
        unit = centred * spread
        unit_ref[at, :] = unit
        spread_ref[at, :] = jnp.broadcast_to(spread, (side, lanes))
        normed_ref[at, :] = (unit * gain_ref[...] + shift_ref[...]).astype(bf16)

    each_row(step)


def turn(source_ref, target_ref):
    for b in range(source_ref.shape[0] // 256):
        at = slice(b * 256, (b + 1) * 256)
        target_ref[:, at] = source_ref[at, :].T


def normalise(conv, kernel, left, right, top, bottom, bias, gain, shift):
    total, channels = conv[0].shape[0], kernel.shape[2]
    return pl.pallas_call(
        normalise_body,
        out_shape=(
            jax.ShapeDtypeStruct((total, channels), f32),
            jax.ShapeDtypeStruct((total, lanes), f32),
            jax.ShapeDtypeStruct((total, channels), bf16),
        ),
        in_specs=[whole] * 11,
        out_specs=[whole] * 3,
        scratch_shapes=[pltpu.VMEM((2 * reach, side, channels), f32)] * 2,
        compiler_params=params(12),
        cost_estimate=cost(2.8),
        name="normalise",
    )(*conv, kernel, left, right, top, bottom, bias, gain, shift)


def wet_row(i, counts_ref):
    place = lax.broadcasted_iota(jnp.int32, (8, lanes), 0) + (i % 8) * 8
    pieces = []
    for t in range(side // 8):
        pieces.append(place < counts_ref[i // 8, t])
    return pieces


def masked_row(i, grad_row, counts_ref):
    channels = grad_row.shape[1]
    parts = []
    for t, wet in enumerate(wet_row(i, counts_ref)):
        piece = grad_row[t * 8 : (t + 1) * 8]
        parts.append(
            jnp.concatenate(
                [
                    jnp.where(wet, piece[:, c * lanes : (c + 1) * lanes], 0.0)
                    for c in range(channels // lanes)
                ],
                axis=1,
            )
        )
    return jnp.concatenate(parts, axis=0)


def mask_rows_body(counts_ref, grad_ref, rows_ref):
    def step(i, carry):
        at = pl.ds(pl.multiple_of(i * side, side), side)
        rows_ref[at, :] = masked_row(i, grad_ref[at, :], counts_ref).astype(bf16)
        return carry

    lax.fori_loop(0, side, step, 0, unroll=side)


def mask_rows(counts, grad):
    total, channels = grad.shape
    return pl.pallas_call(
        mask_rows_body,
        out_shape=jax.ShapeDtypeStruct((total, channels), bf16),
        in_specs=[pl.BlockSpec(memory_space=pltpu.SMEM), whole],
        out_specs=whole,
        compiler_params=params(8),
        cost_estimate=cost(0.9),
        name="mask_rows",
    )(counts, grad)


def arrange_body(expand_ref, reduce_ref, bias_ref, expand_out, reduce_out, turned_out, bias_out):
    channels = expand_ref.shape[1]
    new = lax.broadcasted_iota(jnp.int32, (96, 96), 0)
    old = lax.broadcasted_iota(jnp.int32, (96, 96), 1)
    lo, rest = new // 48, new % 48
    pick = old == (rest // 6) * 12 + lo * 6 + rest % 6
    chosen = pick.astype(f32).astype(bf16)
    for hi, y, core in itertools.product(range(2), range(4), range(2)):
        unit = (hi * 4 + y) * 2 + core
        at = slice(unit * 96, (unit + 1) * 96)
        both = jnp.concatenate([expand_ref[at, :], reduce_ref[at, :]], axis=1)
        moved = jnp.dot(chosen, both, preferred_element_type=f32).astype(bf16)
        column = jnp.sum(jnp.where(pick, bias_ref[:, at], 0.0), axis=1, keepdims=True)
        column = jnp.broadcast_to(column, (96, lanes))
        for lo_place in range(2):
            x = 2 * hi + lo_place
            place = core * 16 + (y * 4 + x if core == 0 else x * 4 + y)
            to = slice(place * 48, (place + 1) * 48)
            half = slice(lo_place * 48, (lo_place + 1) * 48)
            expand_out[to, :] = moved[half, :channels]
            reduce_out[to, :] = moved[half, channels:]
            bias_out[to, :] = column[half]
    turn(expand_out, turned_out)


def arrange(expand, reduce, bias):
    units, channels = expand.shape
    shape = jax.ShapeDtypeStruct((units, channels), bf16)
    return pl.pallas_call(
        arrange_body,
        out_shape=(
            shape,
            shape,
            jax.ShapeDtypeStruct((channels, units), bf16),
            jax.ShapeDtypeStruct((units, lanes), f32),
        ),
        in_specs=[whole] * 3,
        out_specs=[whole] * 4,
        compiler_params=params(12),
        cost_estimate=cost(1.5),
        name="arrange",
    )(expand, reduce, bias)


tail_slope = 0.3275911 * 0.7071067811865476
tail_terms = [
    0.5 * a for a in (0.254829592, -0.284496736, 1.421413741, -1.453152027, 1.061405429)
]
exp_scale = -0.5 * 1.4426950408889634


def gelu_pair(v):
    d = 1.0 + tail_slope * jnp.abs(v)
    t = pltpu.reciprocal(d, approx=True)
    poly = tail_terms[4]
    for a in reversed(tail_terms[:4]):
        poly = poly * t + a
    bell = jnp.exp2(v * v * exp_scale)
    tail = poly * t * bell
    below = jnp.where(v >= 0.0, 1.0 - tail, tail)
    return v * below, below + v * bell * inv_root_two_pi


def own_place():
    lat, lon = lax.axis_index("lat"), lax.axis_index("lon")
    x = 2 * lax.axis_index("dp") + (lon & 1)
    return lat & 1, x, lat >> 1, lon >> 1


def phase_place(second):
    core, x, y, _ = own_place()
    along_y = core == (1 if second else 0)
    return jnp.where(along_y, y, x)


def dot_rows(left, right):
    return lax.dot_general(left, right, (((1,), (1,)), ((), ())), preferred_element_type=f32)


class HiddenBlock:

    def __init__(self, cells, sources, rows, grad_pre_ref, places, scratch):
        self.normed, self.grad, self.expand, self.reduce, self.bias = cells
        self.sources, self.rows, self.places = sources, rows, places
        self.grad_pre = grad_pre_ref
        self.preact, self.grad_hidden, self.hidden, self.terms = scratch
        self.total = self.normed.shape[0]

    def gather(self, ref):
        return jnp.concatenate([ref[pl.ds(s, self.rows), :] for s in self.sources], axis=0)

    def dots(self, at):
        self.preact[:, at] = dot_rows(self.gather(self.expand), self.normed[at, :])
        self.grad_hidden[:, at] = dot_rows(self.gather(self.reduce), self.grad[at, :])

    def activate(self, at):
        bias = jnp.concatenate([self.gather(self.bias)] * ((at.stop - at.start) // lanes), axis=1)
        value, slope = gelu_pair(self.preact[:, at] + bias)
        self.hidden[:, at] = value.astype(bf16)
        grad_pre = (self.grad_hidden[:, at] * slope).astype(bf16)
        self.terms[:, at] = grad_pre
        for n, place in enumerate(self.places):
            self.grad_pre[pl.ds(place, self.rows), at] = grad_pre[n * self.rows : (n + 1) * self.rows]

    def expand_sum(self):
        return jnp.dot(self.terms[...], self.normed[...], preferred_element_type=f32)

    def reduce_sum(self):
        return jnp.dot(self.hidden[...], self.grad[...], preferred_element_type=f32)


def hidden_scratch(rows, total):
    return [
        pltpu.VMEM((rows, total), f32),
        pltpu.VMEM((rows, total), f32),
        pltpu.VMEM((rows, total), bf16),
        pltpu.VMEM((rows, total), bf16),
    ]


def far_body(*refs):
    cells, (sent_ref, grad_pre_ref), scratch = refs[:5], refs[5:7], refs[7:]
    half, total = grad_pre_ref.shape
    channels = refs[0].shape[1]
    base = (1 - own_place()[0]) * half
    rows = half // 2
    blocks = [
        HiddenBlock(
            cells, [pl.multiple_of(base + b * rows, rows)], rows, grad_pre_ref, [b * rows],
            scratch[4 * b : 4 * b + 4],
        )
        for b in range(2)
    ]
    first, second = blocks
    pieces = [slice(c, c + 256) for c in range(0, total, 256)]
    for at in pieces:
        first.dots(at)
    for at in pieces:
        first.activate(at)
        second.dots(at)
    second.activate(pieces[0])
    sent_ref[:rows, :channels] = first.expand_sum().astype(bf16)
    second.activate(pieces[1])
    sent_ref[:rows, channels:] = first.reduce_sum().astype(bf16)
    for at in pieces[2:]:
        second.activate(at)
    sent_ref[rows:, :channels] = second.expand_sum().astype(bf16)
    sent_ref[rows:, channels:] = second.reduce_sum().astype(bf16)


def hidden_far(*cells):
    total, channels = cells[0].shape
    half = cells[2].shape[0] // 2
    return pl.pallas_call(
        far_body,
        out_shape=(
            jax.ShapeDtypeStruct((half, 2 * channels), bf16),
            jax.ShapeDtypeStruct((half, total), bf16),
        ),
        in_specs=[whole] * 5,
        out_specs=[whole] * 2,
        scratch_shapes=hidden_scratch(half // 2, total) * 2,
        compiler_params=params(20),
        cost_estimate=cost(5.0),
        name="hidden_far",
    )(*cells)


def near_first_body(*refs):
    cells, (sums_ref, grad_pre_ref), scratch = refs[:5], refs[5:7], refs[7:]
    half = grad_pre_ref.shape[0]
    channels = refs[0].shape[1]
    size = half // 4
    core, place = own_place()[0], phase_place(False)
    chunks = [pl.multiple_of(lax.rem(place + step, 4) * size, size) for step in (3, 2)]
    sources = [pl.multiple_of(core * half + chunk, size) for chunk in chunks]
    block = HiddenBlock(cells, sources, size, grad_pre_ref, chunks, scratch)
    block.dots(slice(0, block.total))
    block.activate(slice(0, block.total))
    sums_ref[:, :channels] = block.expand_sum()
    sums_ref[:, channels:] = block.reduce_sum()


def near_first(*cells):
    total, channels = cells[0].shape
    half = cells[2].shape[0] // 2
    return pl.pallas_call(
        near_first_body,
        out_shape=(
            jax.ShapeDtypeStruct((half // 2, 2 * channels), f32),
            jax.ShapeDtypeStruct((half, total), bf16),
        ),
        in_specs=[whole] * 5,
        out_specs=[whole] * 2,
        scratch_shapes=hidden_scratch(half // 2, total),
        compiler_params=params(16),
        cost_estimate=cost(3.0),
        name="near_first",
    )(*cells)


def near_sends_body(sums_ref, arrived_ref, *sent_refs):
    size = sent_refs[0].shape[0]
    place = phase_place(False)
    for n, step in enumerate((3, 2)):
        chunk = pl.multiple_of(lax.rem(place + step, 4) * size, size)
        total = sums_ref[n * size : (n + 1) * size] + arrived_ref[pl.ds(chunk, size), :].astype(f32)
        sent_refs[n][...] = total.astype(bf16)


def near_sends(sums, arrived):
    size, width = sums.shape[0] // 2, sums.shape[1]
    sent = jax.ShapeDtypeStruct((size, width), bf16)
    return pl.pallas_call(
        near_sends_body,
        out_shape=(sent, sent),
        in_specs=[whole] * 2,
        out_specs=[whole] * 2,
        compiler_params=params(6),
        cost_estimate=cost(0.3),
        name="near_sends",
    )(sums, arrived)


def near_last_body(*refs):
    cells, (arrived_ref, _, own_ref, sent_ref, grad_pre_ref) = refs[:5], refs[5:10]
    half = grad_pre_ref.shape[0]
    channels = refs[0].shape[1]
    size = half // 4
    core, place = own_place()[0], phase_place(False)
    chunks = [pl.multiple_of(lax.rem(place + step, 4) * size, size) for step in (1, 0)]
    sources = [pl.multiple_of(core * half + chunk, size) for chunk in chunks]
    block = HiddenBlock(cells, sources, size, grad_pre_ref, chunks, refs[10:])
    block.dots(slice(0, block.total))
    block.activate(slice(0, block.total))
    expand, reduce = block.expand_sum(), block.reduce_sum()
    for n, (chunk, ref) in enumerate(zip(chunks, (sent_ref, own_ref))):
        at = slice(n * size, (n + 1) * size)
        other = arrived_ref[pl.ds(chunk, size), :].astype(f32)
        ref[:, :channels] = (expand[at] + other[:, :channels]).astype(ref.dtype)
        ref[:, channels:] = (reduce[at] + other[:, channels:]).astype(ref.dtype)


def near_last(*inputs):
    cells, grad_pre = inputs[:5], inputs[6]
    channels = cells[0].shape[1]
    size = cells[2].shape[0] // 8
    return pl.pallas_call(
        near_last_body,
        out_shape=(
            jax.ShapeDtypeStruct((size, 2 * channels), f32),
            jax.ShapeDtypeStruct((size, 2 * channels), bf16),
            jax.ShapeDtypeStruct(grad_pre.shape, bf16),
        ),
        in_specs=[whole] * 7,
        out_specs=[whole] * 3,
        input_output_aliases={6: 2},
        scratch_shapes=hidden_scratch(2 * size, cells[0].shape[0]),
        compiler_params=params(16),
        cost_estimate=cost(3.0),
        name="near_last",
    )(*inputs)


def norm_back_body(
    turned_ref, other_ref, mine_ref, unit_ref, spread_ref, gain_ref,
    conv_grad_ref, first_ref, last_ref,
):
    total, channels = unit_ref.shape
    half = turned_ref.shape[1] // 2
    core = own_place()[0]
    block = 256
    share = 1.0 / channels
    mine_weight = turned_ref[:, pl.ds(pl.multiple_of(core * half, half), half)]
    other_weight = turned_ref[:, pl.ds(pl.multiple_of((1 - core) * half, half), half)]
    for b in range(total // block):
        at = slice(b * block, (b + 1) * block)
        summed = jnp.dot(mine_weight, mine_ref[:, at], preferred_element_type=f32)
        summed = summed + jnp.dot(other_weight, other_ref[:, at], preferred_element_type=f32)
        grad_normed = summed.astype(bf16).T.astype(f32)
        unit = unit_ref[at, :]
        grad_unit = grad_normed * gain_ref[...]
        mean_grad = jnp.sum(grad_unit, axis=1, keepdims=True) * share
        mean_cross = jnp.sum(grad_unit * unit, axis=1, keepdims=True) * share
        spread = jnp.concatenate([spread_ref[at, :]] * (channels // lanes), axis=1)
        value = (grad_unit - mean_grad - unit * mean_cross) * spread
        conv_grad_ref[b * 8 : (b + 1) * 8] = value.reshape(block // side, side, channels)
    for j in range(reach):
        first_ref[j] = conv_grad_ref[:, j, :].astype(bf16)
        last_ref[j] = conv_grad_ref[:, side - reach + j, :].astype(bf16)


def norm_back(turned, other, mine, unit, spread, gain):
    total, channels = unit.shape
    shape = jax.ShapeDtypeStruct((reach, side, channels), bf16)
    found, first, last = pl.pallas_call(
        norm_back_body,
        out_shape=(jax.ShapeDtypeStruct((side, side, channels), f32), shape, shape),
        in_specs=[whole] * 6,
        out_specs=[whole] * 3,
        compiler_params=params(14),
        cost_estimate=cost(0.2),
        name="norm_back",
    )(turned, other, mine, unit, spread, gain)
    return found.reshape(total, channels), first, last


def finish_inner_body(
    counts_ref, conv0_ref, conv1_ref, conv2_ref, kernel_ref, left_ref, right_ref, grad_ref,
    out_ref, cols_sum, done, sems,
):
    conv_refs = (conv0_ref, conv1_ref, conv2_ref)
    add_cols(True, kernel_ref, left_ref, right_ref, cols_sum)
    bounds = [reach, 9, 16, 23, side - reach]
    copies = []
    for n, (low, high) in enumerate(zip(bounds[:-1], bounds[1:])):
        for i in range(low, high):
            at = slice(i * side, (i + 1) * side)
            value = edged_row(i, conv_rows(conv_refs, at), cols_sum)
            done[at, :] = value + masked_row(i, grad_ref[at, :], counts_ref)
        part = pl.ds(low * side, (high - low) * side)
        copies.append(pltpu.make_async_copy(done.at[part, :], out_ref.at[part, :], sems.at[n]))
        copies[-1].start()
    for copy in copies:
        copy.wait()


def finish_inner(counts, conv, kernel, left, right, grad):
    total, channels = grad.shape
    return pl.pallas_call(
        finish_inner_body,
        out_shape=(
            jax.ShapeDtypeStruct((total, channels), f32),
            jax.ShapeDtypeStruct((2 * reach, side, channels), f32),
        ),
        in_specs=[pl.BlockSpec(memory_space=pltpu.SMEM)] + [whole] * 7,
        out_specs=[pl.BlockSpec(memory_space=pltpu.HBM), whole],
        scratch_shapes=[pltpu.VMEM((total, channels), f32), pltpu.SemaphoreType.DMA((4,))],
        compiler_params=params(12),
        cost_estimate=cost(2.2),
        name="finish_inner",
    )(counts, *conv, kernel, left, right, grad)


def finish_outer_body(
    counts_ref, conv0_ref, conv1_ref, conv2_ref, kernel_ref, top_ref, bottom_ref, cols_ref,
    grad_ref, _, out_ref, rows_sum, done, sems,
):
    conv_refs = (conv0_ref, conv1_ref, conv2_ref)
    add_rows(True, kernel_ref, top_ref, bottom_ref, rows_sum)
    copies = []
    for n, start in enumerate((0, side - reach)):
        for r in range(reach):
            i = start + r
            at = slice(i * side, (i + 1) * side)
            value = edged_row(i, conv_rows(conv_refs, at), cols_ref) + rows_sum[n * reach + r]
            done[n, r * side : (r + 1) * side, :] = value + masked_row(i, grad_ref[at, :], counts_ref)
        part = pl.ds(start * side, reach * side)
        copies.append(pltpu.make_async_copy(done.at[n], out_ref.at[part, :], sems.at[n]))
        copies[-1].start()
    for copy in copies:
        copy.wait()


def finish_outer(counts, conv, kernel, top, bottom, cols_sum, grad, inner):
    channels = grad.shape[1]
    return pl.pallas_call(
        finish_outer_body,
        out_shape=jax.ShapeDtypeStruct(inner.shape, f32),
        in_specs=[pl.BlockSpec(memory_space=pltpu.SMEM)]
        + [whole] * 8
        + [pl.BlockSpec(memory_space=pltpu.HBM)],
        out_specs=pl.BlockSpec(memory_space=pltpu.HBM),
        input_output_aliases={9: 0},
        scratch_shapes=[
            pltpu.VMEM((2 * reach, side, channels), f32),
            pltpu.VMEM((2, reach * side, channels), f32),
            pltpu.SemaphoreType.DMA((2,)),
        ],
        compiler_params=params(12),
        cost_estimate=cost(1.0),
        name="finish_outer",
    )(counts, *conv, kernel, top, bottom, cols_sum, grad, inner)


def split_four_body(own_ref, first_ref, second_ref, third_ref, kept_ref, *sent_refs):
    size = kept_ref.shape[0]
    place = phase_place(True)
    for step in range(4):
        at = pl.ds(pl.multiple_of(lax.rem(place + step, 4) * size, size), size)
        total = own_ref[at, :]
        for ref in (first_ref, second_ref, third_ref):
            total = total + ref[at, :].astype(f32)
        if step == 0:
            kept_ref[...] = total
        else:
            sent_refs[step - 1][...] = total.astype(bf16)


def split_four(own, parts):
    size, width = own.shape[0] // 4, own.shape[1]
    sent = jax.ShapeDtypeStruct((size, width), bf16)
    return pl.pallas_call(
        split_four_body,
        out_shape=(jax.ShapeDtypeStruct((size, width), f32), sent, sent, sent),
        in_specs=[whole] * 4,
        out_specs=[whole] * 4,
        compiler_params=params(4),
        cost_estimate=cost(0.3),
        name="split_four",
    )(own, *parts)


def split_two_body(own_ref, *refs):
    part_refs, (kept_ref, sent_ref) = refs[:-2], refs[-2:]
    size = kept_ref.shape[0]
    total = own_ref[...]
    for ref in part_refs:
        total = total + ref[...].astype(f32)
    low, high = total[:size], total[size:]
    upper = (own_place()[3] & 1) != 0
    kept_ref[...] = jnp.where(upper, high, low)
    sent_ref[...] = jnp.where(upper, low, high)


def split_two(own, parts):
    shape = jax.ShapeDtypeStruct((own.shape[0] // 2, own.shape[1]), f32)
    return pl.pallas_call(
        split_two_body,
        out_shape=(shape, shape),
        in_specs=[whole] * (1 + len(parts)),
        out_specs=[whole] * 2,
        compiler_params=params(4),
        cost_estimate=cost(0.2),
        name="split_two",
    )(own, *parts)


def split_ring_body(own_ref, first_ref, second_ref, third_ref, kept_ref, *sent_refs):
    size = kept_ref.shape[0]
    total = own_ref[...]
    for ref in (first_ref, second_ref, third_ref):
        total = total + ref[...].astype(f32)
    chunks = [total[c * size : (c + 1) * size] for c in range(4)]
    place = own_place()[3] >> 1
    for step, ref in enumerate((kept_ref, *sent_refs)):
        wanted = (place + step) & 3
        found = chunks[0]
        for c in range(1, 4):
            found = jnp.where(wanted == c, chunks[c], found)
        ref[...] = found


def split_ring(own, parts):
    shape = jax.ShapeDtypeStruct((own.shape[0] // 4, own.shape[1]), f32)
    return pl.pallas_call(
        split_ring_body,
        out_shape=(shape,) * 4,
        in_specs=[whole] * 4,
        out_specs=[whole] * 4,
        compiler_params=params(4),
        cost_estimate=cost(0.2),
        name="split_ring",
    )(own, *parts)


def last_sum_body(scale, own_ref, arrived_ref, expand_ref, reduce_ref):
    channels = expand_ref.shape[2]
    total = (own_ref[...] + arrived_ref[...]) * scale
    for r in range(total.shape[0]):
        expand_ref[r] = total[r : r + 1, :channels]
        reduce_ref[r] = total[r : r + 1, channels:]


def last_sum(own, arrived, scale):
    size, width = own.shape
    shape = jax.ShapeDtypeStruct((size, 1, width // 2), f32)
    expand, reduce = pl.pallas_call(
        functools.partial(last_sum_body, scale),
        out_shape=(shape, shape),
        in_specs=[whole] * 2,
        out_specs=[whole] * 2,
        compiler_params=params(4),
        cost_estimate=cost(0.4),
        name="last_sum",
    )(own, arrived)
    return expand.transpose(1, 0, 2), reduce.transpose(1, 0, 2)


every_axis = ("dp", "lat", "lon")


def device_pairs(move):
    def flat(hi, y, core, z, lo):
        return (hi * 8 + y * 2 + core) * 16 + z * 2 + lo

    found = []
    for hi, y, core, z, lo in itertools.product(range(2), range(4), range(2), range(8), range(2)):
        found.append((flat(hi, y, core, z, lo), flat(*move(hi, y, core, z, lo))))
    return found


def plane_pairs(step, first):
    def move(hi, y, core, z, lo):
        if (core == 0) == first:
            return (hi, (y + step) % 4, core, z, lo)
        x = (2 * hi + lo + step) % 4
        return (x // 2, y, core, z, x % 2)

    return device_pairs(move)


def ring_pairs(step):
    return device_pairs(lambda hi, y, core, z, lo: (hi, y, core, (z + 2 * step) % 8, lo))


def last_pairs():
    return device_pairs(lambda hi, y, core, z, lo: (hi, y, core, z ^ 1, lo))


def shifted(axis, step):
    count = lax.axis_size(axis)
    return [(i, (i + step) % count) for i in range(count)]


def lon_halo(first, last):
    left = lax.ppermute(last, "lon", shifted("lon", 1))
    right = lax.ppermute(first, "lon", shifted("lon", -1))
    return left, right


def lat_halo(up, down):
    top = lax.ppermute(down, "lat", shifted("lat", 1))
    bottom = lax.ppermute(up, "lat", shifted("lat", -1))
    return top, bottom


def after(value, *others):
    return lax.optimization_barrier((value, others))[0]


def local(
    state, cotangent, counts, dw_kernel, dw_bias, norm_gain, norm_bias, w_expand, b_expand, w_reduce
):
    channels = state.shape[-1]
    cells = state.reshape(-1, channels)
    grad = cotangent.reshape(-1, channels)
    total = cells.shape[0]
    kernel = dw_kernel.transpose(1, 0, 2)

    first, last = side_cols(cells)
    left, right = lon_halo(first, last)
    conv = inner_conv(cells, kernel, (0,))
    grad, w_expand, w_reduce = after((grad, w_expand, w_reduce), first, last)
    rows = mask_rows(counts, grad)
    expand, reduce, expand_t, bias = arrange(w_expand[0], w_reduce[0], b_expand)
    left, right = after((left, right), rows, bias, conv)
    up, down = side_rows(cells, left, right)
    top, bottom = lat_halo(up, down)
    conv += inner_conv(after(cells, up, down), kernel, (1, 2))
    unit, spread, normed = normalise(
        conv, kernel, left, right, top, bottom, dw_bias, norm_gain, norm_bias
    )

    inputs = (normed, rows, expand, reduce, bias)
    sent, far_pre = hidden_far(*inputs)
    arrived = lax.ppermute(sent, "lat", [(i, i ^ 1) for i in range(8)])
    sums, near_pre = near_first(*inputs)
    three, two = near_sends(sums, arrived)
    part_three = lax.ppermute(three, every_axis, plane_pairs(3, True))
    part_two = lax.ppermute(two, every_axis, plane_pairs(2, True))
    own, one, near_pre = near_last(*inputs, arrived, after(near_pre, three, two))
    part_one = lax.ppermute(one, every_axis, plane_pairs(1, True))

    far_pre, part_three = after((far_pre, part_three), one)
    conv_grad, first, last = norm_back(expand_t, far_pre, near_pre, unit, spread, norm_gain)
    last, part_two = after((last, part_two))
    left, right = lon_halo(first, last)
    own, parts = after((own, (part_one, part_two, part_three)), first, last)
    own, *sent = split_four(own, parts)
    parts = [lax.ppermute(sent[i], every_axis, plane_pairs(i + 1, False)) for i in (1, 0, 2)]
    back = back_conv(after(conv_grad, sent), kernel, (0, 1))
    (conv_grad, left, right), parts = after(((conv_grad, left, right), parts), back)
    up, down = side_rows(conv_grad, left, right)

    own, *sent = split_ring(*after((own, parts), up, down))
    parts = [lax.ppermute(sent[i], every_axis, ring_pairs(i + 1)) for i in (1, 0, 2)]
    top, bottom = lat_halo(up, down)
    back += back_conv(after(conv_grad, sent, top, bottom), kernel, (2,))

    inner, cols_sum = finish_inner(counts, back, kernel, left, right, grad)

    own, sent = split_two(*after((own, parts), inner))
    arrived = lax.ppermute(sent, every_axis, last_pairs())
    inner = after(inner, sent)
    gradient = finish_outer(counts, back, kernel, top, bottom, cols_sum, grad, inner)

    cells_all = lax.axis_size("dp") * lax.axis_size("lat") * lax.axis_size("lon") * total
    kept = last_sum(own, arrived, 1.0 / math.sqrt(cells_all))
    return (gradient.reshape(state.shape), *kept)


def solution(mesh):
    in_specs = (
        P("dp", "lat", "lon", None),
        P("dp", "lat", "lon", None),
        P("lat", "lon"),
        P(),
        P(),
        P(),
        P(),
        P(),
        P(),
        P(),
    )
    out_specs = (
        P("dp", "lat", "lon", None),
        P(None, ("dp", "lat", "lon"), None),
        P(None, ("dp", "lat", "lon"), None),
    )
    return jax.shard_map(local, mesh=mesh, in_specs=in_specs, out_specs=out_specs, check_vma=False)
```

```python
import functools
import itertools
import math

import jax
import jax.numpy as jnp
from jax import lax
from jax.experimental import pallas as pl
from jax.experimental.pallas import tpu as pltpu
from jax.sharding import PartitionSpec as P

norm_eps = 1e-06
inv_root_two_pi = 0.3989422804014327
side = 32
reach = 3
lanes = 128
f32 = jnp.float32
bf16 = jnp.bfloat16
whole = pl.BlockSpec(memory_space=pltpu.VMEM)


def params(mib):
    return pltpu.CompilerParams(vmem_limit_bytes=mib * 1024 * 1024)


def cost(microseconds):
    return pl.CostEstimate(
        flops=int(microseconds * 1.15e9), bytes_accessed=2**20, transcendentals=0
    )


def tap_row(kernel_ref, flipped, p, q, cols):
    index = 7 * p + q
    if flipped:
        index = 48 - index
    return kernel_ref[index, :, cols]


def shift_cols(rows, offset):
    if offset == 0:
        return rows
    count = rows.shape[0]
    turned = pltpu.roll(rows, (-offset) % count, 0)
    place = lax.broadcasted_iota(jnp.int32, (8, rows.shape[1]), 0)
    if offset > 0:
        last = jnp.where(place < 8 - offset, turned[count - 8 :], 0.0)
        return jnp.concatenate([turned[: count - 8], last], axis=0)
    first = jnp.where(place >= -offset, turned[:8], 0.0)
    return jnp.concatenate([first, turned[8:]], axis=0)


def inner_conv_body(parts, cells_ref, kernel_ref, *refs):
    outs, padded = refs[:-1], refs[-1]
    edge = reach * side
    total = side * side
    group = 4
    padded[0:edge] = jnp.zeros((edge, lanes), f32)
    padded[edge + total : 2 * edge + total] = jnp.zeros((edge, lanes), f32)
    for part, out_ref in zip(parts, outs):
        cols = slice(part * lanes, (part + 1) * lanes)
        padded[edge : edge + total] = cells_ref[:, cols]

        def some_rows(i, carry):
            base = pl.multiple_of(i * (group * side), group * side)
            rows = [padded[pl.ds(base + p * side, side), :] for p in range(6 + group)]
            results = [None] * group
            for q in range(7):
                sums = [None] * group
                for p in range(7):
                    tap = tap_row(kernel_ref, False, p, q, cols)
                    for g in range(group):
                        term = tap * rows[p + g]
                        sums[g] = term if sums[g] is None else sums[g] + term
                for g in range(group):
                    moved = shift_cols(sums[g], q - reach)
                    results[g] = moved if results[g] is None else results[g] + moved
            for g in range(group):
                out_ref[pl.ds(base + g * side, side), :] = results[g]
            return carry

        lax.fori_loop(0, side // group, some_rows, 0)


def inner_conv(cells, kernel, parts):
    total = cells.shape[0]
    shape = jax.ShapeDtypeStruct((total, lanes), f32)
    return pl.pallas_call(
        functools.partial(inner_conv_body, parts),
        out_shape=(shape,) * len(parts),
        in_specs=[whole] * 2,
        out_specs=[whole] * len(parts),
        scratch_shapes=[pltpu.VMEM((total + 2 * reach * side, lanes), f32)],
        compiler_params=params(6),
        cost_estimate=cost(2.2 * len(parts)),
        name="inner_conv",
    )(cells, kernel)


def back_conv_body(parts, cells_ref, kernel_ref, *refs):
    outs, (padded, taps) = refs[:-2], refs[-2:]
    edge = reach * side
    total = side * side
    group = 4
    padded[0:edge] = jnp.zeros((edge, lanes), bf16)
    padded[edge + total : 2 * edge + total] = jnp.zeros((edge, lanes), bf16)
    for part, out_ref in zip(parts, outs):
        cols = slice(part * lanes, (part + 1) * lanes)
        padded[edge : edge + total] = cells_ref[:, cols].astype(bf16)
        for p, q in itertools.product(range(7), range(7)):
            tap = jnp.broadcast_to(tap_row(kernel_ref, True, p, q, cols), (16, lanes))
            taps[7 * p + q] = tap.astype(bf16)

        def some_rows(i, carry):
            base = pl.multiple_of(i * (group * side), group * side)
            rows = [padded[pl.ds(base + p * side, side), :] for p in range(6 + group)]
            results = [None] * group
            for q in range(7):
                sums = [None] * group
                for p in range(7):
                    tap = jnp.concatenate([taps[7 * p + q]] * (side // 16), axis=0)
                    for g in range(group):
                        term = tap * rows[p + g]
                        sums[g] = term if sums[g] is None else sums[g] + term
                for g in range(group):
                    moved = shift_cols(sums[g].astype(f32), q - reach)
                    results[g] = moved if results[g] is None else results[g] + moved
            for g in range(group):
                out_ref[pl.ds(base + g * side, side), :] = results[g]
            return carry

        lax.fori_loop(0, side // group, some_rows, 0)


def back_conv(cells, kernel, parts):
    total = cells.shape[0]
    shape = jax.ShapeDtypeStruct((total, lanes), f32)
    return pl.pallas_call(
        functools.partial(back_conv_body, parts),
        out_shape=(shape,) * len(parts),
        in_specs=[whole] * 2,
        out_specs=[whole] * len(parts),
        scratch_shapes=[
            pltpu.VMEM((total + 2 * reach * side, lanes), bf16),
            pltpu.VMEM((49, 16, lanes), bf16),
        ],
        compiler_params=params(6),
        cost_estimate=cost(1.5 * len(parts)),
        name="back_conv",
    )(cells, kernel)


def side_cols_body(cells_ref, first_ref, last_ref, low, high, sems):
    copies = [
        pltpu.make_async_copy(cells_ref.at[:, pl.ds(0, 8), :], low, sems.at[0]),
        pltpu.make_async_copy(cells_ref.at[:, pl.ds(side - 8, 8), :], high, sems.at[1]),
    ]
    for copy in copies:
        copy.start()
    copies[0].wait()
    for j in range(reach):
        first_ref[j] = low[:, j, :].astype(bf16)
    copies[1].wait()
    for j in range(reach):
        last_ref[j] = high[:, 8 - reach + j, :].astype(bf16)


def side_cols(cells):
    channels = cells.shape[1]
    shape = jax.ShapeDtypeStruct((reach, side, channels), bf16)
    return pl.pallas_call(
        side_cols_body,
        out_shape=(shape, shape),
        in_specs=[pl.BlockSpec(memory_space=pltpu.HBM)],
        out_specs=[whole] * 2,
        scratch_shapes=[pltpu.VMEM((side, 8, channels), f32)] * 2 + [pltpu.SemaphoreType.DMA((2,))],
        compiler_params=params(58),
        cost_estimate=cost(1.0),
        name="side_cols",
    )(cells.reshape(side, side, channels))


def side_rows_body(cells_ref, left_ref, right_ref, up_ref, down_ref):
    channels = cells_ref.shape[1]
    place = lax.broadcasted_iota(jnp.int32, (8, channels), 0)
    blank = jnp.zeros((8, channels), f32)
    left = [left_ref[h].astype(f32) for h in range(reach)]
    right = [right_ref[h].astype(f32) for h in range(reach)]
    for r in range(reach):
        for row, ref in ((r, up_ref), (side - reach + r, down_ref)):
            corner = blank
            for h in range(reach):
                corner = jnp.where(place == h, right[h][row : row + 1], corner)
                corner = jnp.where(place == 8 - reach + h, left[h][row : row + 1], corner)
            body = cells_ref[row * side : (row + 1) * side]
            ref[r] = jnp.concatenate([body, corner, blank], axis=0).astype(bf16)


def side_rows(cells, left, right):
    channels = cells.shape[1]
    shape = jax.ShapeDtypeStruct((reach, side + 16, channels), bf16)
    return pl.pallas_call(
        side_rows_body,
        out_shape=(shape, shape),
        in_specs=[whole] * 3,
        out_specs=[whole] * 2,
        compiler_params=params(6),
        cost_estimate=cost(0.5),
        name="side_rows",
    )(cells, left, right)


def beyond_steps(low, r):
    if low:
        return [(h, h - r) for h in range(r, reach)]
    return [(h, 6 + h - r) for h in range(0, r + 1)]


def add_rows(flipped, kernel_ref, top_ref, bottom_ref, rows_sum):
    lat = lax.axis_index("lat")
    channels = kernel_ref.shape[2]
    for c in range(channels // lanes):
        cols = slice(c * lanes, (c + 1) * lanes)
        for low, ref in ((True, top_ref), (False, bottom_ref)):
            outside = lat == (0 if low else lax.axis_size("lat") - 1)
            beyond = [
                jnp.where(outside, 0.0, ref[h, :, cols].astype(f32)[: side + 8]) for h in range(reach)
            ]
            for r in range(reach):
                result = None
                for q in range(7):
                    summed = None
                    for h, p in beyond_steps(low, r):
                        term = tap_row(kernel_ref, flipped, p, q, cols) * beyond[h]
                        summed = term if summed is None else summed + term
                    summed = pltpu.roll(summed, (reach - q) % (side + 8), 0) if q != reach else summed
                    result = summed if result is None else result + summed
                rows_sum[r if low else reach + r, :, cols] = result[:side]


def add_cols(flipped, kernel_ref, left_ref, right_ref, cols_sum):
    channels = kernel_ref.shape[2]
    for c in range(channels // lanes):
        cols = slice(c * lanes, (c + 1) * lanes)
        for low, ref in ((True, left_ref), (False, right_ref)):
            beyond = [ref[h, :, cols].astype(f32) for h in range(reach)]
            for r in range(reach):
                result = None
                for p in range(7):
                    summed = None
                    for h, q in beyond_steps(low, r):
                        term = tap_row(kernel_ref, flipped, p, q, cols) * beyond[h]
                        summed = term if summed is None else summed + term
                    summed = shift_cols(summed, p - reach)
                    result = summed if result is None else result + summed
                cols_sum[r if low else reach + r, :, cols] = result


def edged_row(i, conv_row, cols_sum):
    channels = conv_row.shape[1]
    place = lax.broadcasted_iota(jnp.int32, (8, channels), 0)
    first, last = conv_row[:8], conv_row[side - 8 :]
    for r in range(reach):
        first = first + jnp.where(place == r, cols_sum[r, pl.ds(i, 1), :], 0.0)
        last = last + jnp.where(place == 8 - reach + r, cols_sum[reach + r, pl.ds(i, 1), :], 0.0)
    return jnp.concatenate([first, conv_row[8 : side - 8], last], axis=0)


def each_row(step):
    def low(i, carry):
        step(i, i)
        return carry

    def middle(i, carry):
        step(i, None)
        return carry

    def high(i, carry):
        step(i, i - (side - 2 * reach))
        return carry

    lax.fori_loop(0, reach, low, 0, unroll=reach)
    lax.fori_loop(reach, side - reach, middle, 0, unroll=side // 2 - reach)
    lax.fori_loop(side - reach, side, high, 0, unroll=reach)


def conv_rows(refs, at):
    return jnp.concatenate([ref[at, :] for ref in refs], axis=1)


def normalise_body(
    conv0_ref, conv1_ref, conv2_ref, kernel_ref, left_ref, right_ref, top_ref, bottom_ref, bias_ref, gain_ref, shift_ref,
    unit_ref, spread_ref, normed_ref, rows_sum, cols_sum,
):
    channels = kernel_ref.shape[2]
    conv_refs = (conv0_ref, conv1_ref, conv2_ref)
    add_rows(False, kernel_ref, top_ref, bottom_ref, rows_sum)
    add_cols(False, kernel_ref, left_ref, right_ref, cols_sum)
    share = 1.0 / channels

    def step(i, outer):
        at = pl.ds(pl.multiple_of(i * side, side), side)
        value = edged_row(i, conv_rows(conv_refs, at), cols_sum)
        if outer is not None:
            value = value + rows_sum[outer]
        value = value + bias_ref[...]
        mean = jnp.sum(value, axis=1, keepdims=True) * share
        centred = value - mean
        spread = lax.rsqrt(jnp.sum(centred * centred, axis=1, keepdims=True) * share + norm_eps)
        unit = centred * spread
        unit_ref[at, :] = unit
        spread_ref[at, :] = jnp.broadcast_to(spread, (side, lanes))
        normed_ref[at, :] = (unit * gain_ref[...] + shift_ref[...]).astype(bf16)

    each_row(step)


def turn(source_ref, target_ref):
    for b in range(source_ref.shape[0] // 256):
        at = slice(b * 256, (b + 1) * 256)
        target_ref[:, at] = source_ref[at, :].T


def normalise(conv, kernel, left, right, top, bottom, bias, gain, shift):
    total, channels = conv[0].shape[0], kernel.shape[2]
    return pl.pallas_call(
        normalise_body,
        out_shape=(
            jax.ShapeDtypeStruct((total, channels), f32),
            jax.ShapeDtypeStruct((total, lanes), f32),
            jax.ShapeDtypeStruct((total, channels), bf16),
        ),
        in_specs=[whole] * 11,
        out_specs=[whole] * 3,
        scratch_shapes=[pltpu.VMEM((2 * reach, side, channels), f32)] * 2,
        compiler_params=params(12),
        cost_estimate=cost(2.8),
        name="normalise",
    )(*conv, kernel, left, right, top, bottom, bias, gain, shift)


def wet_row(i, counts_ref):
    place = lax.broadcasted_iota(jnp.int32, (8, lanes), 0) + (i % 8) * 8
    pieces = []
    for t in range(side // 8):
        pieces.append(place < counts_ref[i // 8, t])
    return pieces


def masked_row(i, grad_row, counts_ref):
    channels = grad_row.shape[1]
    parts = []
    for t, wet in enumerate(wet_row(i, counts_ref)):
        piece = grad_row[t * 8 : (t + 1) * 8]
        parts.append(
            jnp.concatenate(
                [
                    jnp.where(wet, piece[:, c * lanes : (c + 1) * lanes], 0.0)
                    for c in range(channels // lanes)
                ],
                axis=1,
            )
        )
    return jnp.concatenate(parts, axis=0)


def mask_rows_body(counts_ref, grad_ref, rows_ref):
    def step(i, carry):
        at = pl.ds(pl.multiple_of(i * side, side), side)
        rows_ref[at, :] = masked_row(i, grad_ref[at, :], counts_ref).astype(bf16)
        return carry

    lax.fori_loop(0, side, step, 0, unroll=side)


def mask_rows(counts, grad):
    total, channels = grad.shape
    return pl.pallas_call(
        mask_rows_body,
        out_shape=jax.ShapeDtypeStruct((total, channels), bf16),
        in_specs=[pl.BlockSpec(memory_space=pltpu.SMEM), whole],
        out_specs=whole,
        compiler_params=params(8),
        cost_estimate=cost(0.9),
        name="mask_rows",
    )(counts, grad)


def arrange_body(expand_ref, reduce_ref, bias_ref, expand_out, reduce_out, turned_out, bias_out):
    channels = expand_ref.shape[1]
    new = lax.broadcasted_iota(jnp.int32, (96, 96), 0)
    old = lax.broadcasted_iota(jnp.int32, (96, 96), 1)
    lo, rest = new // 48, new % 48
    pick = old == (rest // 6) * 12 + lo * 6 + rest % 6
    chosen = pick.astype(f32).astype(bf16)
    for hi, y, core in itertools.product(range(2), range(4), range(2)):
        unit = (hi * 4 + y) * 2 + core
        at = slice(unit * 96, (unit + 1) * 96)
        both = jnp.concatenate([expand_ref[at, :], reduce_ref[at, :]], axis=1)
        moved = jnp.dot(chosen, both, preferred_element_type=f32).astype(bf16)
        column = jnp.sum(jnp.where(pick, bias_ref[:, at], 0.0), axis=1, keepdims=True)
        column = jnp.broadcast_to(column, (96, lanes))
        for lo_place in range(2):
            x = 2 * hi + lo_place
            place = core * 16 + (y * 4 + x if core == 0 else x * 4 + y)
            to = slice(place * 48, (place + 1) * 48)
            half = slice(lo_place * 48, (lo_place + 1) * 48)
            expand_out[to, :] = moved[half, :channels]
            reduce_out[to, :] = moved[half, channels:]
            bias_out[to, :] = column[half]
    turn(expand_out, turned_out)


def arrange(expand, reduce, bias):
    units, channels = expand.shape
    shape = jax.ShapeDtypeStruct((units, channels), bf16)
    return pl.pallas_call(
        arrange_body,
        out_shape=(
            shape,
            shape,
            jax.ShapeDtypeStruct((channels, units), bf16),
            jax.ShapeDtypeStruct((units, lanes), f32),
        ),
        in_specs=[whole] * 3,
        out_specs=[whole] * 4,
        compiler_params=params(12),
        cost_estimate=cost(1.5),
        name="arrange",
    )(expand, reduce, bias)


tail_slope = 0.3275911 * 0.7071067811865476
tail_terms = [
    0.5 * a for a in (0.254829592, -0.284496736, 1.421413741, -1.453152027, 1.061405429)
]
exp_scale = -0.5 * 1.4426950408889634


def gelu_pair(v):
    d = 1.0 + tail_slope * jnp.abs(v)
    t = pltpu.reciprocal(d, approx=True)
    poly = tail_terms[4]
    for a in reversed(tail_terms[:4]):
        poly = poly * t + a
    bell = jnp.exp2(v * v * exp_scale)
    tail = poly * t * bell
    below = jnp.where(v >= 0.0, 1.0 - tail, tail)
    return v * below, below + v * bell * inv_root_two_pi


def own_place():
    lat, lon = lax.axis_index("lat"), lax.axis_index("lon")
    x = 2 * lax.axis_index("dp") + (lon & 1)
    return lat & 1, x, lat >> 1, lon >> 1


def phase_place(second):
    core, x, y, _ = own_place()
    along_y = core == (1 if second else 0)
    return jnp.where(along_y, y, x)


def dot_rows(left, right):
    return lax.dot_general(left, right, (((1,), (1,)), ((), ())), preferred_element_type=f32)


class HiddenBlock:

    def __init__(self, cells, sources, rows, grad_pre_ref, places, scratch):
        self.normed, self.grad, self.expand, self.reduce, self.bias = cells
        self.sources, self.rows, self.places = sources, rows, places
        self.grad_pre = grad_pre_ref
        self.preact, self.grad_hidden, self.hidden, self.terms = scratch
        self.total = self.normed.shape[0]

    def gather(self, ref):
        return jnp.concatenate([ref[pl.ds(s, self.rows), :] for s in self.sources], axis=0)

    def dots(self, at):
        self.preact[:, at] = dot_rows(self.gather(self.expand), self.normed[at, :])
        self.grad_hidden[:, at] = dot_rows(self.gather(self.reduce), self.grad[at, :])

    def activate(self, at):
        bias = jnp.concatenate([self.gather(self.bias)] * ((at.stop - at.start) // lanes), axis=1)
        value, slope = gelu_pair(self.preact[:, at] + bias)
        self.hidden[:, at] = value.astype(bf16)
        grad_pre = (self.grad_hidden[:, at] * slope).astype(bf16)
        self.terms[:, at] = grad_pre
        for n, place in enumerate(self.places):
            self.grad_pre[pl.ds(place, self.rows), at] = grad_pre[n * self.rows : (n + 1) * self.rows]

    def expand_sum(self):
        return jnp.dot(self.terms[...], self.normed[...], preferred_element_type=f32)

    def reduce_sum(self):
        return jnp.dot(self.hidden[...], self.grad[...], preferred_element_type=f32)


def hidden_scratch(rows, total):
    return [
        pltpu.VMEM((rows, total), f32),
        pltpu.VMEM((rows, total), f32),
        pltpu.VMEM((rows, total), bf16),
        pltpu.VMEM((rows, total), bf16),
    ]


def far_body(*refs):
    cells, (sent_ref, grad_pre_ref), scratch = refs[:5], refs[5:7], refs[7:]
    half, total = grad_pre_ref.shape
    channels = refs[0].shape[1]
    base = (1 - own_place()[0]) * half
    rows = half // 2
    blocks = [
        HiddenBlock(
            cells, [pl.multiple_of(base + b * rows, rows)], rows, grad_pre_ref, [b * rows],
            scratch[4 * b : 4 * b + 4],
        )
        for b in range(2)
    ]
    first, second = blocks
    pieces = [slice(c, c + 256) for c in range(0, total, 256)]
    for at in pieces:
        first.dots(at)
    for at in pieces:
        first.activate(at)
        second.dots(at)
    second.activate(pieces[0])
    sent_ref[:rows, :channels] = first.expand_sum().astype(bf16)
    second.activate(pieces[1])
    sent_ref[:rows, channels:] = first.reduce_sum().astype(bf16)
    for at in pieces[2:]:
        second.activate(at)
    sent_ref[rows:, :channels] = second.expand_sum().astype(bf16)
    sent_ref[rows:, channels:] = second.reduce_sum().astype(bf16)


def hidden_far(*cells):
    total, channels = cells[0].shape
    half = cells[2].shape[0] // 2
    return pl.pallas_call(
        far_body,
        out_shape=(
            jax.ShapeDtypeStruct((half, 2 * channels), bf16),
            jax.ShapeDtypeStruct((half, total), bf16),
        ),
        in_specs=[whole] * 5,
        out_specs=[whole] * 2,
        scratch_shapes=hidden_scratch(half // 2, total) * 2,
        compiler_params=params(20),
        cost_estimate=cost(5.0),
        name="hidden_far",
    )(*cells)


def near_first_body(*refs):
    cells, (sums_ref, grad_pre_ref), scratch = refs[:5], refs[5:7], refs[7:]
    half = grad_pre_ref.shape[0]
    channels = refs[0].shape[1]
    size = half // 4
    core, place = own_place()[0], phase_place(False)
    chunks = [pl.multiple_of(lax.rem(place + step, 4) * size, size) for step in (1, 2)]
    sources = [pl.multiple_of(core * half + chunk, size) for chunk in chunks]
    block = HiddenBlock(cells, sources, size, grad_pre_ref, chunks, scratch)
    block.dots(slice(0, block.total))
    block.activate(slice(0, block.total))
    sums_ref[:, :channels] = block.expand_sum()
    sums_ref[:, channels:] = block.reduce_sum()


def near_first(*cells):
    total, channels = cells[0].shape
    half = cells[2].shape[0] // 2
    return pl.pallas_call(
        near_first_body,
        out_shape=(
            jax.ShapeDtypeStruct((half // 2, 2 * channels), f32),
            jax.ShapeDtypeStruct((half, total), bf16),
        ),
        in_specs=[whole] * 5,
        out_specs=[whole] * 2,
        scratch_shapes=hidden_scratch(half // 2, total),
        compiler_params=params(16),
        cost_estimate=cost(3.0),
        name="near_first",
    )(*cells)


def near_sends_body(sums_ref, arrived_ref, *sent_refs):
    size = sent_refs[0].shape[0]
    place = phase_place(False)
    for n, step in enumerate((1, 2)):
        chunk = pl.multiple_of(lax.rem(place + step, 4) * size, size)
        total = sums_ref[n * size : (n + 1) * size] + arrived_ref[pl.ds(chunk, size), :].astype(f32)
        sent_refs[n][...] = total.astype(bf16)


def near_sends(sums, arrived):
    size, width = sums.shape[0] // 2, sums.shape[1]
    sent = jax.ShapeDtypeStruct((size, width), bf16)
    return pl.pallas_call(
        near_sends_body,
        out_shape=(sent, sent),
        in_specs=[whole] * 2,
        out_specs=[whole] * 2,
        compiler_params=params(6),
        cost_estimate=cost(0.3),
        name="near_sends",
    )(sums, arrived)


def near_last_body(*refs):
    cells, (arrived_ref, _, own_ref, sent_ref, grad_pre_ref) = refs[:5], refs[5:10]
    half = grad_pre_ref.shape[0]
    channels = refs[0].shape[1]
    size = half // 4
    core, place = own_place()[0], phase_place(False)
    chunks = [pl.multiple_of(lax.rem(place + step, 4) * size, size) for step in (3, 0)]
    sources = [pl.multiple_of(core * half + chunk, size) for chunk in chunks]
    block = HiddenBlock(cells, sources, size, grad_pre_ref, chunks, refs[10:])
    block.dots(slice(0, block.total))
    block.activate(slice(0, block.total))
    expand, reduce = block.expand_sum(), block.reduce_sum()
    for n, (chunk, ref) in enumerate(zip(chunks, (sent_ref, own_ref))):
        at = slice(n * size, (n + 1) * size)
        other = arrived_ref[pl.ds(chunk, size), :].astype(f32)
        ref[:, :channels] = (expand[at] + other[:, :channels]).astype(ref.dtype)
        ref[:, channels:] = (reduce[at] + other[:, channels:]).astype(ref.dtype)


def near_last(*inputs):
    cells, grad_pre = inputs[:5], inputs[6]
    channels = cells[0].shape[1]
    size = cells[2].shape[0] // 8
    return pl.pallas_call(
        near_last_body,
        out_shape=(
            jax.ShapeDtypeStruct((size, 2 * channels), f32),
            jax.ShapeDtypeStruct((size, 2 * channels), bf16),
            jax.ShapeDtypeStruct(grad_pre.shape, bf16),
        ),
        in_specs=[whole] * 7,
        out_specs=[whole] * 3,
        input_output_aliases={6: 2},
        scratch_shapes=hidden_scratch(2 * size, cells[0].shape[0]),
        compiler_params=params(16),
        cost_estimate=cost(3.0),
        name="near_last",
    )(*inputs)


def norm_back_body(
    turned_ref, other_ref, mine_ref, unit_ref, spread_ref, gain_ref,
    conv_grad_ref, first_ref, last_ref,
):
    total, channels = unit_ref.shape
    half = turned_ref.shape[1] // 2
    core = own_place()[0]
    block = 256
    share = 1.0 / channels
    mine_weight = turned_ref[:, pl.ds(pl.multiple_of(core * half, half), half)]
    other_weight = turned_ref[:, pl.ds(pl.multiple_of((1 - core) * half, half), half)]
    for b in range(total // block):
        at = slice(b * block, (b + 1) * block)
        summed = jnp.dot(mine_weight, mine_ref[:, at], preferred_element_type=f32)
        summed = summed + jnp.dot(other_weight, other_ref[:, at], preferred_element_type=f32)
        grad_normed = summed.astype(bf16).T.astype(f32)
        unit = unit_ref[at, :]
        grad_unit = grad_normed * gain_ref[...]
        mean_grad = jnp.sum(grad_unit, axis=1, keepdims=True) * share
        mean_cross = jnp.sum(grad_unit * unit, axis=1, keepdims=True) * share
        spread = jnp.concatenate([spread_ref[at, :]] * (channels // lanes), axis=1)
        value = (grad_unit - mean_grad - unit * mean_cross) * spread
        conv_grad_ref[b * 8 : (b + 1) * 8] = value.reshape(block // side, side, channels)
    for j in range(reach):
        first_ref[j] = conv_grad_ref[:, j, :].astype(bf16)
        last_ref[j] = conv_grad_ref[:, side - reach + j, :].astype(bf16)


def norm_back(turned, other, mine, unit, spread, gain):
    total, channels = unit.shape
    shape = jax.ShapeDtypeStruct((reach, side, channels), bf16)
    found, first, last = pl.pallas_call(
        norm_back_body,
        out_shape=(jax.ShapeDtypeStruct((side, side, channels), f32), shape, shape),
        in_specs=[whole] * 6,
        out_specs=[whole] * 3,
        compiler_params=params(14),
        cost_estimate=cost(0.2),
        name="norm_back",
    )(turned, other, mine, unit, spread, gain)
    return found.reshape(total, channels), first, last


def finish_inner_body(
    counts_ref, conv0_ref, conv1_ref, conv2_ref, kernel_ref, left_ref, right_ref, grad_ref,
    out_ref, cols_sum, done, sems,
):
    conv_refs = (conv0_ref, conv1_ref, conv2_ref)
    add_cols(True, kernel_ref, left_ref, right_ref, cols_sum)
    bounds = [reach, 9, 16, 23, side - reach]
    copies = []
    for n, (low, high) in enumerate(zip(bounds[:-1], bounds[1:])):
        for i in range(low, high):
            at = slice(i * side, (i + 1) * side)
            value = edged_row(i, conv_rows(conv_refs, at), cols_sum)
            done[at, :] = value + masked_row(i, grad_ref[at, :], counts_ref)
        part = pl.ds(low * side, (high - low) * side)
        copies.append(pltpu.make_async_copy(done.at[part, :], out_ref.at[part, :], sems.at[n]))
        copies[-1].start()
    for copy in copies:
        copy.wait()


def finish_inner(counts, conv, kernel, left, right, grad):
    total, channels = grad.shape
    return pl.pallas_call(
        finish_inner_body,
        out_shape=(
            jax.ShapeDtypeStruct((total, channels), f32),
            jax.ShapeDtypeStruct((2 * reach, side, channels), f32),
        ),
        in_specs=[pl.BlockSpec(memory_space=pltpu.SMEM)] + [whole] * 7,
        out_specs=[pl.BlockSpec(memory_space=pltpu.HBM), whole],
        scratch_shapes=[pltpu.VMEM((total, channels), f32), pltpu.SemaphoreType.DMA((4,))],
        compiler_params=params(12),
        cost_estimate=cost(2.2),
        name="finish_inner",
    )(counts, *conv, kernel, left, right, grad)


def finish_outer_body(
    counts_ref, conv0_ref, conv1_ref, conv2_ref, kernel_ref, top_ref, bottom_ref, cols_ref,
    grad_ref, _, out_ref, rows_sum, done, sems,
):
    conv_refs = (conv0_ref, conv1_ref, conv2_ref)
    add_rows(True, kernel_ref, top_ref, bottom_ref, rows_sum)
    copies = []
    for n, start in enumerate((0, side - reach)):
        for r in range(reach):
            i = start + r
            at = slice(i * side, (i + 1) * side)
            value = edged_row(i, conv_rows(conv_refs, at), cols_ref) + rows_sum[n * reach + r]
            done[n, r * side : (r + 1) * side, :] = value + masked_row(i, grad_ref[at, :], counts_ref)
        part = pl.ds(start * side, reach * side)
        copies.append(pltpu.make_async_copy(done.at[n], out_ref.at[part, :], sems.at[n]))
        copies[-1].start()
    for copy in copies:
        copy.wait()


def finish_outer(counts, conv, kernel, top, bottom, cols_sum, grad, inner):
    channels = grad.shape[1]
    return pl.pallas_call(
        finish_outer_body,
        out_shape=jax.ShapeDtypeStruct(inner.shape, f32),
        in_specs=[pl.BlockSpec(memory_space=pltpu.SMEM)]
        + [whole] * 8
        + [pl.BlockSpec(memory_space=pltpu.HBM)],
        out_specs=pl.BlockSpec(memory_space=pltpu.HBM),
        input_output_aliases={9: 0},
        scratch_shapes=[
            pltpu.VMEM((2 * reach, side, channels), f32),
            pltpu.VMEM((2, reach * side, channels), f32),
            pltpu.SemaphoreType.DMA((2,)),
        ],
        compiler_params=params(12),
        cost_estimate=cost(1.0),
        name="finish_outer",
    )(counts, *conv, kernel, top, bottom, cols_sum, grad, inner)


def split_four_body(own_ref, first_ref, second_ref, third_ref, kept_ref, *sent_refs):
    size = kept_ref.shape[0]
    place = phase_place(True)
    for step in range(4):
        at = pl.ds(pl.multiple_of(lax.rem(place + step, 4) * size, size), size)
        total = own_ref[at, :]
        for ref in (first_ref, second_ref, third_ref):
            total = total + ref[at, :].astype(f32)
        if step == 0:
            kept_ref[...] = total
        else:
            sent_refs[step - 1][...] = total.astype(bf16)


def split_four(own, parts):
    size, width = own.shape[0] // 4, own.shape[1]
    sent = jax.ShapeDtypeStruct((size, width), bf16)
    return pl.pallas_call(
        split_four_body,
        out_shape=(jax.ShapeDtypeStruct((size, width), f32), sent, sent, sent),
        in_specs=[whole] * 4,
        out_specs=[whole] * 4,
        compiler_params=params(4),
        cost_estimate=cost(0.3),
        name="split_four",
    )(own, *parts)


def split_two_body(own_ref, *refs):
    part_refs, (kept_ref, sent_ref) = refs[:-2], refs[-2:]
    size = kept_ref.shape[0]
    total = own_ref[...]
    for ref in part_refs:
        total = total + ref[...].astype(f32)
    low, high = total[:size], total[size:]
    upper = (own_place()[3] & 1) != 0
    kept_ref[...] = jnp.where(upper, high, low)
    sent_ref[...] = jnp.where(upper, low, high)


def split_two(own, parts):
    shape = jax.ShapeDtypeStruct((own.shape[0] // 2, own.shape[1]), f32)
    return pl.pallas_call(
        split_two_body,
        out_shape=(shape, shape),
        in_specs=[whole] * (1 + len(parts)),
        out_specs=[whole] * 2,
        compiler_params=params(4),
        cost_estimate=cost(0.2),
        name="split_two",
    )(own, *parts)


def split_ring_body(own_ref, first_ref, second_ref, third_ref, kept_ref, *sent_refs):
    size = kept_ref.shape[0]
    total = own_ref[...]
    for ref in (first_ref, second_ref, third_ref):
        total = total + ref[...].astype(f32)
    chunks = [total[c * size : (c + 1) * size] for c in range(4)]
    place = own_place()[3] >> 1
    for step, ref in enumerate((kept_ref, *sent_refs)):
        wanted = (place + step) & 3
        found = chunks[0]
        for c in range(1, 4):
            found = jnp.where(wanted == c, chunks[c], found)
        ref[...] = found.astype(ref.dtype)


def split_ring(own, parts):
    size, width = own.shape[0] // 4, own.shape[1]
    sent = jax.ShapeDtypeStruct((size, width), bf16)
    return pl.pallas_call(
        split_ring_body,
        out_shape=(jax.ShapeDtypeStruct((size, width), f32), sent, sent, sent),
        in_specs=[whole] * 4,
        out_specs=[whole] * 4,
        compiler_params=params(4),
        cost_estimate=cost(0.2),
        name="split_ring",
    )(own, *parts)


def last_sum_body(scale, own_ref, arrived_ref, expand_ref, reduce_ref):
    channels = expand_ref.shape[2]
    total = (own_ref[...] + arrived_ref[...]) * scale
    for r in range(total.shape[0]):
        expand_ref[r] = total[r : r + 1, :channels]
        reduce_ref[r] = total[r : r + 1, channels:]


def last_sum(own, arrived, scale):
    size, width = own.shape
    shape = jax.ShapeDtypeStruct((size, 1, width // 2), f32)
    expand, reduce = pl.pallas_call(
        functools.partial(last_sum_body, scale),
        out_shape=(shape, shape),
        in_specs=[whole] * 2,
        out_specs=[whole] * 2,
        compiler_params=params(4),
        cost_estimate=cost(0.4),
        name="last_sum",
    )(own, arrived)
    return expand.transpose(1, 0, 2), reduce.transpose(1, 0, 2)


every_axis = ("dp", "lat", "lon")


def device_pairs(move):
    def flat(hi, y, core, z, lo):
        return (hi * 8 + y * 2 + core) * 16 + z * 2 + lo

    found = []
    for hi, y, core, z, lo in itertools.product(range(2), range(4), range(2), range(8), range(2)):
        found.append((flat(hi, y, core, z, lo), flat(*move(hi, y, core, z, lo))))
    return found


def plane_pairs(step, first):
    def move(hi, y, core, z, lo):
        if (core == 0) == first:
            return (hi, (y + step) % 4, core, z, lo)
        x = (2 * hi + lo + step) % 4
        return (x // 2, y, core, z, x % 2)

    return device_pairs(move)


def ring_pairs(step):
    return device_pairs(lambda hi, y, core, z, lo: (hi, y, core, (z + 2 * step) % 8, lo))


def last_pairs():
    return device_pairs(lambda hi, y, core, z, lo: (hi, y, core, z ^ 1, lo))


def shifted(axis, step):
    count = lax.axis_size(axis)
    return [(i, (i + step) % count) for i in range(count)]


def lon_halo(first, last):
    left = lax.ppermute(last, "lon", shifted("lon", 1))
    right = lax.ppermute(first, "lon", shifted("lon", -1))
    return left, right


def lat_halo(up, down):
    top = lax.ppermute(down, "lat", shifted("lat", 1))
    bottom = lax.ppermute(up, "lat", shifted("lat", -1))
    return top, bottom


def after(value, *others):
    return lax.optimization_barrier((value, others))[0]


def local(
    state, cotangent, counts, dw_kernel, dw_bias, norm_gain, norm_bias, w_expand, b_expand, w_reduce
):
    channels = state.shape[-1]
    cells = state.reshape(-1, channels)
    grad = cotangent.reshape(-1, channels)
    total = cells.shape[0]
    kernel = dw_kernel.transpose(1, 0, 2)

    first, last = side_cols(cells)
    left, right = lon_halo(first, last)
    conv = inner_conv(cells, kernel, (0,))
    grad, w_expand, w_reduce = after((grad, w_expand, w_reduce), first, last)
    rows = mask_rows(counts, grad)
    expand, reduce, expand_t, bias = arrange(w_expand[0], w_reduce[0], b_expand)
    left, right = after((left, right), rows, bias, conv)
    up, down = side_rows(cells, left, right)
    top, bottom = lat_halo(up, down)
    conv += inner_conv(after(cells, up, down), kernel, (1, 2))
    unit, spread, normed = normalise(
        conv, kernel, left, right, top, bottom, dw_bias, norm_gain, norm_bias
    )

    inputs = (normed, rows, expand, reduce, bias)
    sent, far_pre = hidden_far(*inputs)
    arrived = lax.ppermute(sent, "lat", [(i, i ^ 1) for i in range(8)])
    sums, near_pre = near_first(*inputs)
    one, two = near_sends(sums, arrived)
    part_one = lax.ppermute(one, every_axis, plane_pairs(1, True))
    part_two = lax.ppermute(two, every_axis, plane_pairs(2, True))
    own, three, near_pre = near_last(*inputs, arrived, after(near_pre, one, two))
    part_three = lax.ppermute(three, every_axis, plane_pairs(3, True))

    far_pre, part_one = after((far_pre, part_one), three)
    conv_grad, first, last = norm_back(expand_t, far_pre, near_pre, unit, spread, norm_gain)
    last, part_two = after((last, part_two))
    left, right = lon_halo(first, last)
    own, parts = after((own, (part_one, part_two, part_three)), first, last)
    own, *sent = split_four(own, parts)
    parts = [lax.ppermute(sent[i], every_axis, plane_pairs(i + 1, False)) for i in (1, 0, 2)]
    back = back_conv(after(conv_grad, sent), kernel, (0, 1))
    (conv_grad, left, right), parts = after(((conv_grad, left, right), parts), back)
    up, down = side_rows(conv_grad, left, right)

    own, *sent = split_ring(*after((own, parts), up, down))
    parts = [lax.ppermute(sent[i], every_axis, ring_pairs(i + 1)) for i in (1, 0, 2)]
    top, bottom = lat_halo(up, down)
    back += back_conv(after(conv_grad, sent, top, bottom), kernel, (2,))

    inner, cols_sum = finish_inner(counts, back, kernel, left, right, grad)

    own, sent = split_two(*after((own, parts), inner))
    arrived = lax.ppermute(sent, every_axis, last_pairs())
    inner = after(inner, sent)
    gradient = finish_outer(counts, back, kernel, top, bottom, cols_sum, grad, inner)

    cells_all = lax.axis_size("dp") * lax.axis_size("lat") * lax.axis_size("lon") * total
    kept = last_sum(own, arrived, 1.0 / math.sqrt(cells_all))
    return (gradient.reshape(state.shape), *kept)


def solution(mesh):
    in_specs = (
        P("dp", "lat", "lon", None),
        P("dp", "lat", "lon", None),
        P("lat", "lon"),
        P(),
        P(),
        P(),
        P(),
        P(),
        P(),
        P(),
    )
    out_specs = (
        P("dp", "lat", "lon", None),
        P(None, ("dp", "lat", "lon"), None),
        P(None, ("dp", "lat", "lon"), None),
    )
    return jax.shard_map(local, mesh=mesh, in_specs=in_specs, out_specs=out_specs, check_vma=False)
```

```python
import functools
import itertools
import math

import jax
import jax.numpy as jnp
from jax import lax
from jax.experimental import pallas as pl
from jax.experimental.pallas import tpu as pltpu
from jax.sharding import PartitionSpec as P

norm_eps = 1e-06
inv_root_two_pi = 0.3989422804014327
side = 32
reach = 3
lanes = 128
f32 = jnp.float32
bf16 = jnp.bfloat16
whole = pl.BlockSpec(memory_space=pltpu.VMEM)


def params(mib):
    return pltpu.CompilerParams(vmem_limit_bytes=mib * 1024 * 1024)


def cost(microseconds):
    return pl.CostEstimate(
        flops=int(microseconds * 1.15e9), bytes_accessed=2**20, transcendentals=0
    )


def tap_row(kernel_ref, flipped, p, q, cols):
    index = 7 * p + q
    if flipped:
        index = 48 - index
    return kernel_ref[index, :, cols]


def shift_cols(rows, offset):
    if offset == 0:
        return rows
    count = rows.shape[0]
    turned = pltpu.roll(rows, (-offset) % count, 0)
    place = lax.broadcasted_iota(jnp.int32, (8, rows.shape[1]), 0)
    if offset > 0:
        last = jnp.where(place < 8 - offset, turned[count - 8 :], 0.0)
        return jnp.concatenate([turned[: count - 8], last], axis=0)
    first = jnp.where(place >= -offset, turned[:8], 0.0)
    return jnp.concatenate([first, turned[8:]], axis=0)


def inner_conv_body(parts, cells_ref, kernel_ref, *refs):
    outs, padded = refs[:-1], refs[-1]
    edge = reach * side
    total = side * side
    group = 4
    padded[0:edge] = jnp.zeros((edge, lanes), f32)
    padded[edge + total : 2 * edge + total] = jnp.zeros((edge, lanes), f32)
    for part, out_ref in zip(parts, outs):
        cols = slice(part * lanes, (part + 1) * lanes)
        padded[edge : edge + total] = cells_ref[:, cols]

        def some_rows(i, carry):
            base = pl.multiple_of(i * (group * side), group * side)
            rows = [padded[pl.ds(base + p * side, side), :] for p in range(6 + group)]
            results = [None] * group
            for q in range(7):
                sums = [None] * group
                for p in range(7):
                    tap = tap_row(kernel_ref, False, p, q, cols)
                    for g in range(group):
                        term = tap * rows[p + g]
                        sums[g] = term if sums[g] is None else sums[g] + term
                for g in range(group):
                    moved = shift_cols(sums[g], q - reach)
                    results[g] = moved if results[g] is None else results[g] + moved
            for g in range(group):
                out_ref[pl.ds(base + g * side, side), :] = results[g]
            return carry

        lax.fori_loop(0, side // group, some_rows, 0)


def inner_conv(cells, kernel, parts):
    total = cells.shape[0]
    shape = jax.ShapeDtypeStruct((total, lanes), f32)
    return pl.pallas_call(
        functools.partial(inner_conv_body, parts),
        out_shape=(shape,) * len(parts),
        in_specs=[whole] * 2,
        out_specs=[whole] * len(parts),
        scratch_shapes=[pltpu.VMEM((total + 2 * reach * side, lanes), f32)],
        compiler_params=params(6),
        cost_estimate=cost(2.2 * len(parts)),
        name="inner_conv",
    )(cells, kernel)


def back_conv_body(parts, cells_ref, kernel_ref, *refs):
    outs, (padded, taps) = refs[:-2], refs[-2:]
    edge = reach * side
    total = side * side
    group = 4
    padded[0:edge] = jnp.zeros((edge, lanes), bf16)
    padded[edge + total : 2 * edge + total] = jnp.zeros((edge, lanes), bf16)
    for part, out_ref in zip(parts, outs):
        cols = slice(part * lanes, (part + 1) * lanes)
        padded[edge : edge + total] = cells_ref[:, cols].astype(bf16)
        for p, q in itertools.product(range(7), range(7)):
            tap = jnp.broadcast_to(tap_row(kernel_ref, True, p, q, cols), (16, lanes))
            taps[7 * p + q] = tap.astype(bf16)

        def some_rows(i, carry):
            base = pl.multiple_of(i * (group * side), group * side)
            rows = [padded[pl.ds(base + p * side, side), :] for p in range(6 + group)]
            results = [None] * group
            for q in range(7):
                sums = [None] * group
                for p in range(7):
                    tap = jnp.concatenate([taps[7 * p + q]] * (side // 16), axis=0)
                    for g in range(group):
                        term = tap * rows[p + g]
                        sums[g] = term if sums[g] is None else sums[g] + term
                for g in range(group):
                    moved = shift_cols(sums[g].astype(f32), q - reach)
                    results[g] = moved if results[g] is None else results[g] + moved
            for g in range(group):
                out_ref[pl.ds(base + g * side, side), :] = results[g]
            return carry

        lax.fori_loop(0, side // group, some_rows, 0)


def back_conv(cells, kernel, parts):
    total = cells.shape[0]
    shape = jax.ShapeDtypeStruct((total, lanes), f32)
    return pl.pallas_call(
        functools.partial(back_conv_body, parts),
        out_shape=(shape,) * len(parts),
        in_specs=[whole] * 2,
        out_specs=[whole] * len(parts),
        scratch_shapes=[
            pltpu.VMEM((total + 2 * reach * side, lanes), bf16),
            pltpu.VMEM((49, 16, lanes), bf16),
        ],
        compiler_params=params(6),
        cost_estimate=cost(1.5 * len(parts)),
        name="back_conv",
    )(cells, kernel)


def side_cols_body(cells_ref, first_ref, last_ref, low, high, sems):
    copies = [
        pltpu.make_async_copy(cells_ref.at[:, pl.ds(0, 8), :], low, sems.at[0]),
        pltpu.make_async_copy(cells_ref.at[:, pl.ds(side - 8, 8), :], high, sems.at[1]),
    ]
    for copy in copies:
        copy.start()
    copies[0].wait()
    for j in range(reach):
        first_ref[j] = low[:, j, :].astype(bf16)
    copies[1].wait()
    for j in range(reach):
        last_ref[j] = high[:, 8 - reach + j, :].astype(bf16)


def side_cols(cells):
    channels = cells.shape[1]
    shape = jax.ShapeDtypeStruct((reach, side, channels), bf16)
    return pl.pallas_call(
        side_cols_body,
        out_shape=(shape, shape),
        in_specs=[pl.BlockSpec(memory_space=pltpu.HBM)],
        out_specs=[whole] * 2,
        scratch_shapes=[pltpu.VMEM((side, 8, channels), f32)] * 2 + [pltpu.SemaphoreType.DMA((2,))],
        compiler_params=params(58),
        cost_estimate=cost(1.0),
        name="side_cols",
    )(cells.reshape(side, side, channels))


def side_rows_body(cells_ref, left_ref, right_ref, up_ref, down_ref):
    channels = cells_ref.shape[1]
    place = lax.broadcasted_iota(jnp.int32, (8, channels), 0)
    blank = jnp.zeros((8, channels), f32)
    left = [left_ref[h].astype(f32) for h in range(reach)]
    right = [right_ref[h].astype(f32) for h in range(reach)]
    for r in range(reach):
        for row, ref in ((r, up_ref), (side - reach + r, down_ref)):
            corner = blank
            for h in range(reach):
                corner = jnp.where(place == h, right[h][row : row + 1], corner)
                corner = jnp.where(place == 8 - reach + h, left[h][row : row + 1], corner)
            body = cells_ref[row * side : (row + 1) * side]
            ref[r] = jnp.concatenate([body, corner, blank], axis=0).astype(bf16)


def side_rows(cells, left, right):
    channels = cells.shape[1]
    shape = jax.ShapeDtypeStruct((reach, side + 16, channels), bf16)
    return pl.pallas_call(
        side_rows_body,
        out_shape=(shape, shape),
        in_specs=[whole] * 3,
        out_specs=[whole] * 2,
        compiler_params=params(6),
        cost_estimate=cost(0.5),
        name="side_rows",
    )(cells, left, right)


def beyond_steps(low, r):
    if low:
        return [(h, h - r) for h in range(r, reach)]
    return [(h, 6 + h - r) for h in range(0, r + 1)]


def add_rows(flipped, kernel_ref, top_ref, bottom_ref, rows_sum):
    lat = lax.axis_index("lat")
    channels = kernel_ref.shape[2]
    for c in range(channels // lanes):
        cols = slice(c * lanes, (c + 1) * lanes)
        for low, ref in ((True, top_ref), (False, bottom_ref)):
            outside = lat == (0 if low else lax.axis_size("lat") - 1)
            beyond = [
                jnp.where(outside, 0.0, ref[h, :, cols].astype(f32)[: side + 8]) for h in range(reach)
            ]
            for r in range(reach):
                result = None
                for q in range(7):
                    summed = None
                    for h, p in beyond_steps(low, r):
                        term = tap_row(kernel_ref, flipped, p, q, cols) * beyond[h]
                        summed = term if summed is None else summed + term
                    summed = pltpu.roll(summed, (reach - q) % (side + 8), 0) if q != reach else summed
                    result = summed if result is None else result + summed
                rows_sum[r if low else reach + r, :, cols] = result[:side]


def add_cols(flipped, kernel_ref, left_ref, right_ref, cols_sum):
    channels = kernel_ref.shape[2]
    for c in range(channels // lanes):
        cols = slice(c * lanes, (c + 1) * lanes)
        for low, ref in ((True, left_ref), (False, right_ref)):
            beyond = [ref[h, :, cols].astype(f32) for h in range(reach)]
            for r in range(reach):
                result = None
                for p in range(7):
                    summed = None
                    for h, q in beyond_steps(low, r):
                        term = tap_row(kernel_ref, flipped, p, q, cols) * beyond[h]
                        summed = term if summed is None else summed + term
                    summed = shift_cols(summed, p - reach)
                    result = summed if result is None else result + summed
                cols_sum[r if low else reach + r, :, cols] = result


def edged_row(i, conv_row, cols_sum):
    channels = conv_row.shape[1]
    place = lax.broadcasted_iota(jnp.int32, (8, channels), 0)
    first, last = conv_row[:8], conv_row[side - 8 :]
    for r in range(reach):
        first = first + jnp.where(place == r, cols_sum[r, pl.ds(i, 1), :], 0.0)
        last = last + jnp.where(place == 8 - reach + r, cols_sum[reach + r, pl.ds(i, 1), :], 0.0)
    return jnp.concatenate([first, conv_row[8 : side - 8], last], axis=0)


def each_row(step):
    def low(i, carry):
        step(i, i)
        return carry

    def middle(i, carry):
        step(i, None)
        return carry

    def high(i, carry):
        step(i, i - (side - 2 * reach))
        return carry

    lax.fori_loop(0, reach, low, 0, unroll=reach)
    lax.fori_loop(reach, side - reach, middle, 0, unroll=side // 2 - reach)
    lax.fori_loop(side - reach, side, high, 0, unroll=reach)


def conv_rows(refs, at):
    return jnp.concatenate([ref[at, :] for ref in refs], axis=1)


def normalise_body(
    conv0_ref, conv1_ref, conv2_ref, kernel_ref, left_ref, right_ref, top_ref, bottom_ref, bias_ref, gain_ref, shift_ref,
    unit_ref, spread_ref, normed_ref, rows_sum, cols_sum,
):
    channels = kernel_ref.shape[2]
    conv_refs = (conv0_ref, conv1_ref, conv2_ref)
    add_rows(False, kernel_ref, top_ref, bottom_ref, rows_sum)
    add_cols(False, kernel_ref, left_ref, right_ref, cols_sum)
    share = 1.0 / channels

    def step(i, outer):
        at = pl.ds(pl.multiple_of(i * side, side), side)
        value = edged_row(i, conv_rows(conv_refs, at), cols_sum)
        if outer is not None:
            value = value + rows_sum[outer]
        value = value + bias_ref[...]
        mean = jnp.sum(value, axis=1, keepdims=True) * share
        centred = value - mean
        spread = lax.rsqrt(jnp.sum(centred * centred, axis=1, keepdims=True) * share + norm_eps)
        unit = centred * spread
        unit_ref[at, :] = unit
        spread_ref[at, :] = jnp.broadcast_to(spread, (side, lanes))
        normed_ref[at, :] = (unit * gain_ref[...] + shift_ref[...]).astype(bf16)

    each_row(step)


def turn(source_ref, target_ref):
    for b in range(source_ref.shape[0] // 256):
        at = slice(b * 256, (b + 1) * 256)
        target_ref[:, at] = source_ref[at, :].T


def normalise(conv, kernel, left, right, top, bottom, bias, gain, shift):
    total, channels = conv[0].shape[0], kernel.shape[2]
    return pl.pallas_call(
        normalise_body,
        out_shape=(
            jax.ShapeDtypeStruct((total, channels), f32),
            jax.ShapeDtypeStruct((total, lanes), f32),
            jax.ShapeDtypeStruct((total, channels), bf16),
        ),
        in_specs=[whole] * 11,
        out_specs=[whole] * 3,
        scratch_shapes=[pltpu.VMEM((2 * reach, side, channels), f32)] * 2,
        compiler_params=params(12),
        cost_estimate=cost(2.8),
        name="normalise",
    )(*conv, kernel, left, right, top, bottom, bias, gain, shift)


def wet_row(i, counts_ref):
    place = lax.broadcasted_iota(jnp.int32, (8, lanes), 0) + (i % 8) * 8
    pieces = []
    for t in range(side // 8):
        pieces.append(place < counts_ref[i // 8, t])
    return pieces


def masked_row(i, grad_row, counts_ref):
    channels = grad_row.shape[1]
    parts = []
    for t, wet in enumerate(wet_row(i, counts_ref)):
        piece = grad_row[t * 8 : (t + 1) * 8]
        parts.append(
            jnp.concatenate(
                [
                    jnp.where(wet, piece[:, c * lanes : (c + 1) * lanes], 0.0)
                    for c in range(channels // lanes)
                ],
                axis=1,
            )
        )
    return jnp.concatenate(parts, axis=0)


def mask_rows_body(counts_ref, grad_ref, rows_ref):
    def step(i, carry):
        at = pl.ds(pl.multiple_of(i * side, side), side)
        rows_ref[at, :] = masked_row(i, grad_ref[at, :], counts_ref).astype(bf16)
        return carry

    lax.fori_loop(0, side, step, 0, unroll=side)


def mask_rows(counts, grad):
    total, channels = grad.shape
    return pl.pallas_call(
        mask_rows_body,
        out_shape=jax.ShapeDtypeStruct((total, channels), bf16),
        in_specs=[pl.BlockSpec(memory_space=pltpu.SMEM), whole],
        out_specs=whole,
        compiler_params=params(8),
        cost_estimate=cost(0.9),
        name="mask_rows",
    )(counts, grad)


def arrange_body(expand_ref, reduce_ref, bias_ref, expand_out, reduce_out, turned_out, bias_out):
    channels = expand_ref.shape[1]
    new = lax.broadcasted_iota(jnp.int32, (96, 96), 0)
    old = lax.broadcasted_iota(jnp.int32, (96, 96), 1)
    lo, rest = new // 48, new % 48
    pick = old == (rest // 6) * 12 + lo * 6 + rest % 6
    chosen = pick.astype(f32).astype(bf16)
    for hi, y, core in itertools.product(range(2), range(4), range(2)):
        unit = (hi * 4 + y) * 2 + core
        at = slice(unit * 96, (unit + 1) * 96)
        both = jnp.concatenate([expand_ref[at, :], reduce_ref[at, :]], axis=1)
        moved = jnp.dot(chosen, both, preferred_element_type=f32).astype(bf16)
        column = jnp.sum(jnp.where(pick, bias_ref[:, at], 0.0), axis=1, keepdims=True)
        column = jnp.broadcast_to(column, (96, lanes))
        for lo_place in range(2):
            x = 2 * hi + lo_place
            place = core * 16 + (y * 4 + x if core == 0 else x * 4 + y)
            to = slice(place * 48, (place + 1) * 48)
            half = slice(lo_place * 48, (lo_place + 1) * 48)
            expand_out[to, :] = moved[half, :channels]
            reduce_out[to, :] = moved[half, channels:]
            bias_out[to, :] = column[half]
    turn(expand_out, turned_out)


def arrange(expand, reduce, bias):
    units, channels = expand.shape
    shape = jax.ShapeDtypeStruct((units, channels), bf16)
    return pl.pallas_call(
        arrange_body,
        out_shape=(
            shape,
            shape,
            jax.ShapeDtypeStruct((channels, units), bf16),
            jax.ShapeDtypeStruct((units, lanes), f32),
        ),
        in_specs=[whole] * 3,
        out_specs=[whole] * 4,
        compiler_params=params(12),
        cost_estimate=cost(1.5),
        name="arrange",
    )(expand, reduce, bias)


tail_slope = 0.3275911 * 0.7071067811865476
tail_terms = [
    0.5 * a for a in (0.254829592, -0.284496736, 1.421413741, -1.453152027, 1.061405429)
]
exp_scale = -0.5 * 1.4426950408889634


def gelu_pair(v):
    d = 1.0 + tail_slope * jnp.abs(v)
    t = pltpu.reciprocal(d, approx=True)
    poly = tail_terms[4]
    for a in reversed(tail_terms[:4]):
        poly = poly * t + a
    bell = jnp.exp2(v * v * exp_scale)
    tail = poly * t * bell
    below = jnp.where(v >= 0.0, 1.0 - tail, tail)
    return v * below, below + v * bell * inv_root_two_pi


def own_place():
    lat, lon = lax.axis_index("lat"), lax.axis_index("lon")
    x = 2 * lax.axis_index("dp") + (lon & 1)
    return lat & 1, x, lat >> 1, lon >> 1


def phase_place(second):
    core, x, y, _ = own_place()
    along_y = core == (1 if second else 0)
    return jnp.where(along_y, y, x)


def dot_rows(left, right):
    return lax.dot_general(left, right, (((1,), (1,)), ((), ())), preferred_element_type=f32)


class HiddenBlock:

    def __init__(self, cells, sources, rows, grad_pre_ref, places, scratch):
        self.normed, self.grad, self.expand, self.reduce, self.bias = cells
        self.sources, self.rows, self.places = sources, rows, places
        self.grad_pre = grad_pre_ref
        self.preact, self.grad_hidden, self.hidden, self.terms = scratch
        self.total = self.normed.shape[0]

    def gather(self, ref):
        return jnp.concatenate([ref[pl.ds(s, self.rows), :] for s in self.sources], axis=0)

    def dots(self, at):
        self.preact[:, at] = dot_rows(self.gather(self.expand), self.normed[at, :])
        self.grad_hidden[:, at] = dot_rows(self.gather(self.reduce), self.grad[at, :])

    def activate(self, at):
        bias = jnp.concatenate([self.gather(self.bias)] * ((at.stop - at.start) // lanes), axis=1)
        value, slope = gelu_pair(self.preact[:, at] + bias)
        self.hidden[:, at] = value.astype(bf16)
        grad_pre = (self.grad_hidden[:, at] * slope).astype(bf16)
        self.terms[:, at] = grad_pre
        for n, place in enumerate(self.places):
            self.grad_pre[pl.ds(place, self.rows), at] = grad_pre[n * self.rows : (n + 1) * self.rows]

    def expand_sum(self):
        return jnp.dot(self.terms[...], self.normed[...], preferred_element_type=f32)

    def reduce_sum(self):
        return jnp.dot(self.hidden[...], self.grad[...], preferred_element_type=f32)


def hidden_scratch(rows, total):
    return [
        pltpu.VMEM((rows, total), f32),
        pltpu.VMEM((rows, total), f32),
        pltpu.VMEM((rows, total), bf16),
        pltpu.VMEM((rows, total), bf16),
    ]


def far_body(*refs):
    cells, (sent_ref, grad_pre_ref), scratch = refs[:5], refs[5:7], refs[7:]
    half, total = grad_pre_ref.shape
    channels = refs[0].shape[1]
    base = (1 - own_place()[0]) * half
    rows = half // 2
    blocks = [
        HiddenBlock(
            cells, [pl.multiple_of(base + b * rows, rows)], rows, grad_pre_ref, [b * rows],
            scratch[4 * b : 4 * b + 4],
        )
        for b in range(2)
    ]
    first, second = blocks
    pieces = [slice(c, c + 256) for c in range(0, total, 256)]
    for at in pieces:
        first.dots(at)
    for at in pieces:
        first.activate(at)
        second.dots(at)
    second.activate(pieces[0])
    sent_ref[:rows, :channels] = first.expand_sum().astype(bf16)
    second.activate(pieces[1])
    sent_ref[:rows, channels:] = first.reduce_sum().astype(bf16)
    for at in pieces[2:]:
        second.activate(at)
    sent_ref[rows:, :channels] = second.expand_sum().astype(bf16)
    sent_ref[rows:, channels:] = second.reduce_sum().astype(bf16)


def hidden_far(*cells):
    total, channels = cells[0].shape
    half = cells[2].shape[0] // 2
    return pl.pallas_call(
        far_body,
        out_shape=(
            jax.ShapeDtypeStruct((half, 2 * channels), bf16),
            jax.ShapeDtypeStruct((half, total), bf16),
        ),
        in_specs=[whole] * 5,
        out_specs=[whole] * 2,
        scratch_shapes=hidden_scratch(half // 2, total) * 2,
        compiler_params=params(20),
        cost_estimate=cost(5.0),
        name="hidden_far",
    )(*cells)


def near_first_body(*refs):
    cells, (sums_ref, grad_pre_ref), scratch = refs[:5], refs[5:7], refs[7:]
    half = grad_pre_ref.shape[0]
    channels = refs[0].shape[1]
    size = half // 4
    core, place = own_place()[0], phase_place(False)
    chunks = [pl.multiple_of(lax.rem(place + step, 4) * size, size) for step in (2, 3)]
    sources = [pl.multiple_of(core * half + chunk, size) for chunk in chunks]
    block = HiddenBlock(cells, sources, size, grad_pre_ref, chunks, scratch)
    block.dots(slice(0, block.total))
    block.activate(slice(0, block.total))
    sums_ref[:, :channels] = block.expand_sum()
    sums_ref[:, channels:] = block.reduce_sum()


def near_first(*cells):
    total, channels = cells[0].shape
    half = cells[2].shape[0] // 2
    return pl.pallas_call(
        near_first_body,
        out_shape=(
            jax.ShapeDtypeStruct((half // 2, 2 * channels), f32),
            jax.ShapeDtypeStruct((half, total), bf16),
        ),
        in_specs=[whole] * 5,
        out_specs=[whole] * 2,
        scratch_shapes=hidden_scratch(half // 2, total),
        compiler_params=params(16),
        cost_estimate=cost(3.0),
        name="near_first",
    )(*cells)


def near_sends_body(sums_ref, arrived_ref, *sent_refs):
    size = sent_refs[0].shape[0]
    place = phase_place(False)
    for n, step in enumerate((2, 3)):
        chunk = pl.multiple_of(lax.rem(place + step, 4) * size, size)
        total = sums_ref[n * size : (n + 1) * size] + arrived_ref[pl.ds(chunk, size), :].astype(f32)
        sent_refs[n][...] = total.astype(bf16)


def near_sends(sums, arrived):
    size, width = sums.shape[0] // 2, sums.shape[1]
    sent = jax.ShapeDtypeStruct((size, width), bf16)
    return pl.pallas_call(
        near_sends_body,
        out_shape=(sent, sent),
        in_specs=[whole] * 2,
        out_specs=[whole] * 2,
        compiler_params=params(6),
        cost_estimate=cost(0.3),
        name="near_sends",
    )(sums, arrived)


def near_last_body(*refs):
    cells, (arrived_ref, _, own_ref, next_ref, grad_pre_ref) = refs[:5], refs[5:10]
    half = grad_pre_ref.shape[0]
    channels = refs[0].shape[1]
    size = half // 4
    core, place = own_place()[0], phase_place(False)
    chunks = [pl.multiple_of(lax.rem(place + step, 4) * size, size) for step in (1, 0)]
    sources = [pl.multiple_of(core * half + chunk, size) for chunk in chunks]
    block = HiddenBlock(cells, sources, size, grad_pre_ref, chunks, refs[10:])
    block.dots(slice(0, block.total))
    block.activate(slice(0, block.total))
    expand, reduce = block.expand_sum(), block.reduce_sum()
    for n, (chunk, ref) in enumerate(zip(chunks, (next_ref, own_ref))):
        at = slice(n * size, (n + 1) * size)
        other = arrived_ref[pl.ds(chunk, size), :].astype(f32)
        ref[:, :channels] = expand[at] + other[:, :channels]
        ref[:, channels:] = reduce[at] + other[:, channels:]


def near_last(*inputs):
    cells, grad_pre = inputs[:5], inputs[6]
    channels = cells[0].shape[1]
    size = cells[2].shape[0] // 8
    return pl.pallas_call(
        near_last_body,
        out_shape=(
            jax.ShapeDtypeStruct((size, 2 * channels), f32),
            jax.ShapeDtypeStruct((size, 2 * channels), f32),
            jax.ShapeDtypeStruct(grad_pre.shape, bf16),
        ),
        in_specs=[whole] * 7,
        out_specs=[whole] * 3,
        input_output_aliases={6: 2},
        scratch_shapes=hidden_scratch(2 * size, cells[0].shape[0]),
        compiler_params=params(16),
        cost_estimate=cost(3.0),
        name="near_last",
    )(*inputs)


def norm_back_body(
    turned_ref, other_ref, mine_ref, unit_ref, spread_ref, gain_ref,
    conv_grad_ref, first_ref, last_ref,
):
    total, channels = unit_ref.shape
    half = turned_ref.shape[1] // 2
    core = own_place()[0]
    block = 256
    share = 1.0 / channels
    mine_weight = turned_ref[:, pl.ds(pl.multiple_of(core * half, half), half)]
    other_weight = turned_ref[:, pl.ds(pl.multiple_of((1 - core) * half, half), half)]
    for b in range(total // block):
        at = slice(b * block, (b + 1) * block)
        summed = jnp.dot(mine_weight, mine_ref[:, at], preferred_element_type=f32)
        summed = summed + jnp.dot(other_weight, other_ref[:, at], preferred_element_type=f32)
        grad_normed = summed.astype(bf16).T.astype(f32)
        unit = unit_ref[at, :]
        grad_unit = grad_normed * gain_ref[...]
        mean_grad = jnp.sum(grad_unit, axis=1, keepdims=True) * share
        mean_cross = jnp.sum(grad_unit * unit, axis=1, keepdims=True) * share
        spread = jnp.concatenate([spread_ref[at, :]] * (channels // lanes), axis=1)
        value = (grad_unit - mean_grad - unit * mean_cross) * spread
        conv_grad_ref[b * 8 : (b + 1) * 8] = value.reshape(block // side, side, channels)
    for j in range(reach):
        first_ref[j] = conv_grad_ref[:, j, :].astype(bf16)
        last_ref[j] = conv_grad_ref[:, side - reach + j, :].astype(bf16)


def norm_back(turned, other, mine, unit, spread, gain):
    total, channels = unit.shape
    shape = jax.ShapeDtypeStruct((reach, side, channels), bf16)
    found, first, last = pl.pallas_call(
        norm_back_body,
        out_shape=(jax.ShapeDtypeStruct((side, side, channels), f32), shape, shape),
        in_specs=[whole] * 6,
        out_specs=[whole] * 3,
        compiler_params=params(14),
        cost_estimate=cost(0.2),
        name="norm_back",
    )(turned, other, mine, unit, spread, gain)
    return found.reshape(total, channels), first, last


def finish_inner_body(
    counts_ref, conv0_ref, conv1_ref, conv2_ref, kernel_ref, left_ref, right_ref, grad_ref,
    out_ref, cols_sum, done, sems,
):
    conv_refs = (conv0_ref, conv1_ref, conv2_ref)
    add_cols(True, kernel_ref, left_ref, right_ref, cols_sum)
    bounds = [reach, 9, 16, 23, side - reach]
    copies = []
    for n, (low, high) in enumerate(zip(bounds[:-1], bounds[1:])):
        for i in range(low, high):
            at = slice(i * side, (i + 1) * side)
            value = edged_row(i, conv_rows(conv_refs, at), cols_sum)
            done[at, :] = value + masked_row(i, grad_ref[at, :], counts_ref)
        part = pl.ds(low * side, (high - low) * side)
        copies.append(pltpu.make_async_copy(done.at[part, :], out_ref.at[part, :], sems.at[n]))
        copies[-1].start()
    for copy in copies:
        copy.wait()


def finish_inner(counts, conv, kernel, left, right, grad):
    total, channels = grad.shape
    return pl.pallas_call(
        finish_inner_body,
        out_shape=(
            jax.ShapeDtypeStruct((total, channels), f32),
            jax.ShapeDtypeStruct((2 * reach, side, channels), f32),
        ),
        in_specs=[pl.BlockSpec(memory_space=pltpu.SMEM)] + [whole] * 7,
        out_specs=[pl.BlockSpec(memory_space=pltpu.HBM), whole],
        scratch_shapes=[pltpu.VMEM((total, channels), f32), pltpu.SemaphoreType.DMA((4,))],
        compiler_params=params(12),
        cost_estimate=cost(2.2),
        name="finish_inner",
    )(counts, *conv, kernel, left, right, grad)


def finish_outer_body(
    counts_ref, conv0_ref, conv1_ref, conv2_ref, kernel_ref, top_ref, bottom_ref, cols_ref,
    grad_ref, _, out_ref, rows_sum, done, sems,
):
    conv_refs = (conv0_ref, conv1_ref, conv2_ref)
    add_rows(True, kernel_ref, top_ref, bottom_ref, rows_sum)
    copies = []
    for n, start in enumerate((0, side - reach)):
        for r in range(reach):
            i = start + r
            at = slice(i * side, (i + 1) * side)
            value = edged_row(i, conv_rows(conv_refs, at), cols_ref) + rows_sum[n * reach + r]
            done[n, r * side : (r + 1) * side, :] = value + masked_row(i, grad_ref[at, :], counts_ref)
        part = pl.ds(start * side, reach * side)
        copies.append(pltpu.make_async_copy(done.at[n], out_ref.at[part, :], sems.at[n]))
        copies[-1].start()
    for copy in copies:
        copy.wait()


def finish_outer(counts, conv, kernel, top, bottom, cols_sum, grad, inner):
    channels = grad.shape[1]
    return pl.pallas_call(
        finish_outer_body,
        out_shape=jax.ShapeDtypeStruct(inner.shape, f32),
        in_specs=[pl.BlockSpec(memory_space=pltpu.SMEM)]
        + [whole] * 8
        + [pl.BlockSpec(memory_space=pltpu.HBM)],
        out_specs=pl.BlockSpec(memory_space=pltpu.HBM),
        input_output_aliases={9: 0},
        scratch_shapes=[
            pltpu.VMEM((2 * reach, side, channels), f32),
            pltpu.VMEM((2, reach * side, channels), f32),
            pltpu.SemaphoreType.DMA((2,)),
        ],
        compiler_params=params(12),
        cost_estimate=cost(1.0),
        name="finish_outer",
    )(counts, *conv, kernel, top, bottom, cols_sum, grad, inner)


def relay_body(own_ref, passed_ref, sent_ref):
    sent_ref[...] = (own_ref[...] + passed_ref[...].astype(f32)).astype(bf16)


def relay(own, passed):
    return pl.pallas_call(
        relay_body,
        out_shape=jax.ShapeDtypeStruct(own.shape, bf16),
        in_specs=[whole] * 2,
        out_specs=whole,
        compiler_params=params(6),
        cost_estimate=cost(0.2),
        name="relay",
    )(own, passed)


def split_four_body(own_ref, first_ref, second_ref, kept_ref, *sent_refs):
    size = kept_ref.shape[0]
    place = phase_place(True)
    for step in range(4):
        at = pl.ds(pl.multiple_of(lax.rem(place + step, 4) * size, size), size)
        total = own_ref[at, :]
        for ref in (first_ref, second_ref):
            total = total + ref[at, :].astype(f32)
        if step == 0:
            kept_ref[...] = total
        else:
            sent_refs[step - 1][...] = total.astype(bf16)


def split_four(own, parts):
    size, width = own.shape[0] // 4, own.shape[1]
    sent = jax.ShapeDtypeStruct((size, width), bf16)
    return pl.pallas_call(
        split_four_body,
        out_shape=(jax.ShapeDtypeStruct((size, width), f32), sent, sent, sent),
        in_specs=[whole] * 3,
        out_specs=[whole] * 4,
        compiler_params=params(4),
        cost_estimate=cost(0.3),
        name="split_four",
    )(own, *parts)


def split_two_body(own_ref, *refs):
    part_refs, (kept_ref, sent_ref) = refs[:-2], refs[-2:]
    size = kept_ref.shape[0]
    total = own_ref[...]
    for ref in part_refs:
        total = total + ref[...].astype(f32)
    low, high = total[:size], total[size:]
    upper = (own_place()[3] & 1) != 0
    kept_ref[...] = jnp.where(upper, high, low)
    sent_ref[...] = jnp.where(upper, low, high)


def split_two(own, parts):
    shape = jax.ShapeDtypeStruct((own.shape[0] // 2, own.shape[1]), f32)
    return pl.pallas_call(
        split_two_body,
        out_shape=(shape, shape),
        in_specs=[whole] * (1 + len(parts)),
        out_specs=[whole] * 2,
        compiler_params=params(4),
        cost_estimate=cost(0.2),
        name="split_two",
    )(own, *parts)


def split_ring_body(own_ref, first_ref, second_ref, third_ref, kept_ref, *sent_refs):
    size = kept_ref.shape[0]
    total = own_ref[...]
    for ref in (first_ref, second_ref, third_ref):
        total = total + ref[...].astype(f32)
    chunks = [total[c * size : (c + 1) * size] for c in range(4)]
    place = own_place()[3] >> 1
    for step, ref in enumerate((kept_ref, *sent_refs)):
        wanted = (place + step) & 3
        found = chunks[0]
        for c in range(1, 4):
            found = jnp.where(wanted == c, chunks[c], found)
        ref[...] = found.astype(ref.dtype)


def split_ring(own, parts):
    size, width = own.shape[0] // 4, own.shape[1]
    sent = jax.ShapeDtypeStruct((size, width), bf16)
    return pl.pallas_call(
        split_ring_body,
        out_shape=(jax.ShapeDtypeStruct((size, width), f32), sent, sent, sent),
        in_specs=[whole] * 4,
        out_specs=[whole] * 4,
        compiler_params=params(4),
        cost_estimate=cost(0.2),
        name="split_ring",
    )(own, *parts)


def last_sum_body(scale, own_ref, arrived_ref, expand_ref, reduce_ref):
    channels = expand_ref.shape[2]
    total = (own_ref[...] + arrived_ref[...]) * scale
    for r in range(total.shape[0]):
        expand_ref[r] = total[r : r + 1, :channels]
        reduce_ref[r] = total[r : r + 1, channels:]


def last_sum(own, arrived, scale):
    size, width = own.shape
    shape = jax.ShapeDtypeStruct((size, 1, width // 2), f32)
    expand, reduce = pl.pallas_call(
        functools.partial(last_sum_body, scale),
        out_shape=(shape, shape),
        in_specs=[whole] * 2,
        out_specs=[whole] * 2,
        compiler_params=params(4),
        cost_estimate=cost(0.4),
        name="last_sum",
    )(own, arrived)
    return expand.transpose(1, 0, 2), reduce.transpose(1, 0, 2)


every_axis = ("dp", "lat", "lon")


def device_pairs(move):
    def flat(hi, y, core, z, lo):
        return (hi * 8 + y * 2 + core) * 16 + z * 2 + lo

    found = []
    for hi, y, core, z, lo in itertools.product(range(2), range(4), range(2), range(8), range(2)):
        found.append((flat(hi, y, core, z, lo), flat(*move(hi, y, core, z, lo))))
    return found


def plane_pairs(step, first):
    def move(hi, y, core, z, lo):
        if (core == 0) == first:
            return (hi, (y + step) % 4, core, z, lo)
        x = (2 * hi + lo + step) % 4
        return (x // 2, y, core, z, x % 2)

    return device_pairs(move)


def ring_pairs(step):
    return device_pairs(lambda hi, y, core, z, lo: (hi, y, core, (z + 2 * step) % 8, lo))


def last_pairs():
    return device_pairs(lambda hi, y, core, z, lo: (hi, y, core, z ^ 1, lo))


def shifted(axis, step):
    count = lax.axis_size(axis)
    return [(i, (i + step) % count) for i in range(count)]


def lon_halo(first, last):
    left = lax.ppermute(last, "lon", shifted("lon", 1))
    right = lax.ppermute(first, "lon", shifted("lon", -1))
    return left, right


def lat_halo(up, down):
    top = lax.ppermute(down, "lat", shifted("lat", 1))
    bottom = lax.ppermute(up, "lat", shifted("lat", -1))
    return top, bottom


def after(value, *others):
    return lax.optimization_barrier((value, others))[0]


def local(
    state, cotangent, counts, dw_kernel, dw_bias, norm_gain, norm_bias, w_expand, b_expand, w_reduce
):
    channels = state.shape[-1]
    cells = state.reshape(-1, channels)
    grad = cotangent.reshape(-1, channels)
    total = cells.shape[0]
    kernel = dw_kernel.transpose(1, 0, 2)

    first, last = side_cols(cells)
    left, right = lon_halo(first, last)
    conv = inner_conv(cells, kernel, (0,))
    grad, w_expand, w_reduce = after((grad, w_expand, w_reduce), first, last)
    rows = mask_rows(counts, grad)
    expand, reduce, expand_t, bias = arrange(w_expand[0], w_reduce[0], b_expand)
    left, right = after((left, right), rows, bias, conv)
    up, down = side_rows(cells, left, right)
    top, bottom = lat_halo(up, down)
    conv += inner_conv(after(cells, up, down), kernel, (1, 2))
    unit, spread, normed = normalise(
        conv, kernel, left, right, top, bottom, dw_bias, norm_gain, norm_bias
    )

    inputs = (normed, rows, expand, reduce, bias)
    sent, far_pre = hidden_far(*inputs)
    arrived = lax.ppermute(sent, "lat", [(i, i ^ 1) for i in range(8)])
    sums, near_pre = near_first(*inputs)
    two, three = near_sends(sums, arrived)
    passed = lax.ppermute(two, every_axis, plane_pairs(1, True))
    part_before = lax.ppermute(three, every_axis, plane_pairs(3, True))
    own, following, near_pre = near_last(*inputs, arrived, after(near_pre, two, three))
    one = relay(following, passed)
    part_after = lax.ppermute(one, every_axis, plane_pairs(1, True))

    far_pre = after(far_pre, one)
    conv_grad, first, last = norm_back(expand_t, far_pre, near_pre, unit, spread, norm_gain)
    last, part_before = after((last, part_before))
    left, right = lon_halo(first, last)
    own, parts = after((own, (part_before, part_after)), first, last)
    own, *sent = split_four(own, parts)
    parts = [lax.ppermute(sent[i], every_axis, plane_pairs(i + 1, False)) for i in (1, 0, 2)]
    back = back_conv(after(conv_grad, sent), kernel, (0, 1))
    (conv_grad, left, right), parts = after(((conv_grad, left, right), parts), back)
    up, down = side_rows(conv_grad, left, right)

    own, *sent = split_ring(*after((own, parts), up, down))
    parts = [lax.ppermute(sent[i], every_axis, ring_pairs(i + 1)) for i in (1, 0, 2)]
    top, bottom = lat_halo(up, down)
    back += back_conv(after(conv_grad, sent, top, bottom), kernel, (2,))

    inner, cols_sum = finish_inner(counts, back, kernel, left, right, grad)

    own, sent = split_two(*after((own, parts), inner))
    arrived = lax.ppermute(sent, every_axis, last_pairs())
    inner = after(inner, sent)
    gradient = finish_outer(counts, back, kernel, top, bottom, cols_sum, grad, inner)

    cells_all = lax.axis_size("dp") * lax.axis_size("lat") * lax.axis_size("lon") * total
    kept = last_sum(own, arrived, 1.0 / math.sqrt(cells_all))
    return (gradient.reshape(state.shape), *kept)


def solution(mesh):
    in_specs = (
        P("dp", "lat", "lon", None),
        P("dp", "lat", "lon", None),
        P("lat", "lon"),
        P(),
        P(),
        P(),
        P(),
        P(),
        P(),
        P(),
    )
    out_specs = (
        P("dp", "lat", "lon", None),
        P(None, ("dp", "lat", "lon"), None),
        P(None, ("dp", "lat", "lon"), None),
    )
    return jax.shard_map(local, mesh=mesh, in_specs=in_specs, out_specs=out_specs, check_vma=False)
```

```python
import functools
import itertools
import math

import jax
import jax.numpy as jnp
from jax import lax
from jax.experimental import pallas as pl
from jax.experimental.pallas import tpu as pltpu
from jax.sharding import PartitionSpec as P

norm_eps = 1e-06
inv_root_two_pi = 0.3989422804014327
side = 32
reach = 3
lanes = 128
f32 = jnp.float32
bf16 = jnp.bfloat16
whole = pl.BlockSpec(memory_space=pltpu.VMEM)


def params(mib):
    return pltpu.CompilerParams(vmem_limit_bytes=mib * 1024 * 1024)


def cost(microseconds):
    return pl.CostEstimate(
        flops=int(microseconds * 1.15e9), bytes_accessed=2**20, transcendentals=0
    )


def tap_row(kernel_ref, flipped, p, q, cols):
    index = 7 * p + q
    if flipped:
        index = 48 - index
    return kernel_ref[index, :, cols]


def shift_cols(rows, offset):
    if offset == 0:
        return rows
    count = rows.shape[0]
    turned = pltpu.roll(rows, (-offset) % count, 0)
    place = lax.broadcasted_iota(jnp.int32, (8, rows.shape[1]), 0)
    if offset > 0:
        last = jnp.where(place < 8 - offset, turned[count - 8 :], 0.0)
        return jnp.concatenate([turned[: count - 8], last], axis=0)
    first = jnp.where(place >= -offset, turned[:8], 0.0)
    return jnp.concatenate([first, turned[8:]], axis=0)


def inner_conv_body(parts, cells_ref, kernel_ref, *refs):
    outs, padded = refs[:-1], refs[-1]
    edge = reach * side
    total = side * side
    group = 4
    padded[0:edge] = jnp.zeros((edge, lanes), f32)
    padded[edge + total : 2 * edge + total] = jnp.zeros((edge, lanes), f32)
    for part, out_ref in zip(parts, outs):
        cols = slice(part * lanes, (part + 1) * lanes)
        padded[edge : edge + total] = cells_ref[:, cols]

        def some_rows(i, carry):
            base = pl.multiple_of(i * (group * side), group * side)
            rows = [padded[pl.ds(base + p * side, side), :] for p in range(6 + group)]
            results = [None] * group
            for q in range(7):
                sums = [None] * group
                for p in range(7):
                    tap = tap_row(kernel_ref, False, p, q, cols)
                    for g in range(group):
                        term = tap * rows[p + g]
                        sums[g] = term if sums[g] is None else sums[g] + term
                for g in range(group):
                    moved = shift_cols(sums[g], q - reach)
                    results[g] = moved if results[g] is None else results[g] + moved
            for g in range(group):
                out_ref[pl.ds(base + g * side, side), :] = results[g]
            return carry

        lax.fori_loop(0, side // group, some_rows, 0)


def inner_conv(cells, kernel, parts):
    total = cells.shape[0]
    shape = jax.ShapeDtypeStruct((total, lanes), f32)
    return pl.pallas_call(
        functools.partial(inner_conv_body, parts),
        out_shape=(shape,) * len(parts),
        in_specs=[whole] * 2,
        out_specs=[whole] * len(parts),
        scratch_shapes=[pltpu.VMEM((total + 2 * reach * side, lanes), f32)],
        compiler_params=params(6),
        cost_estimate=cost(2.2 * len(parts)),
        name="inner_conv",
    )(cells, kernel)


def back_conv_body(parts, cells_ref, kernel_ref, *refs):
    outs, (padded, taps) = refs[:-2], refs[-2:]
    edge = reach * side
    total = side * side
    group = 4
    padded[0:edge] = jnp.zeros((edge, lanes), bf16)
    padded[edge + total : 2 * edge + total] = jnp.zeros((edge, lanes), bf16)
    for part, out_ref in zip(parts, outs):
        cols = slice(part * lanes, (part + 1) * lanes)
        padded[edge : edge + total] = cells_ref[:, cols].astype(bf16)
        for p, q in itertools.product(range(7), range(7)):
            tap = jnp.broadcast_to(tap_row(kernel_ref, True, p, q, cols), (16, lanes))
            taps[7 * p + q] = tap.astype(bf16)

        def some_rows(i, carry):
            base = pl.multiple_of(i * (group * side), group * side)
            rows = [padded[pl.ds(base + p * side, side), :] for p in range(6 + group)]
            results = [None] * group
            for q in range(7):
                sums = [None] * group
                for p in range(7):
                    tap = jnp.concatenate([taps[7 * p + q]] * (side // 16), axis=0)
                    for g in range(group):
                        term = tap * rows[p + g]
                        sums[g] = term if sums[g] is None else sums[g] + term
                for g in range(group):
                    moved = shift_cols(sums[g].astype(f32), q - reach)
                    results[g] = moved if results[g] is None else results[g] + moved
            for g in range(group):
                out_ref[pl.ds(base + g * side, side), :] = results[g]
            return carry

        lax.fori_loop(0, side // group, some_rows, 0)


def back_conv(cells, kernel, parts):
    total = cells.shape[0]
    shape = jax.ShapeDtypeStruct((total, lanes), f32)
    return pl.pallas_call(
        functools.partial(back_conv_body, parts),
        out_shape=(shape,) * len(parts),
        in_specs=[whole] * 2,
        out_specs=[whole] * len(parts),
        scratch_shapes=[
            pltpu.VMEM((total + 2 * reach * side, lanes), bf16),
            pltpu.VMEM((49, 16, lanes), bf16),
        ],
        compiler_params=params(6),
        cost_estimate=cost(1.5 * len(parts)),
        name="back_conv",
    )(cells, kernel)


def side_cols_body(cells_ref, first_ref, last_ref):
    for j in range(reach):
        first_ref[j] = cells_ref[:, j, :].astype(bf16)
        last_ref[j] = cells_ref[:, side - reach + j, :].astype(bf16)


def side_cols(cells):
    channels = cells.shape[1]
    shape = jax.ShapeDtypeStruct((reach, side, channels), bf16)
    return pl.pallas_call(
        side_cols_body,
        out_shape=(shape, shape),
        in_specs=[whole],
        out_specs=[whole] * 2,
        compiler_params=params(4),
        cost_estimate=cost(0.3),
        name="side_cols",
    )(cells.reshape(side, side, channels))


def side_rows_body(cells_ref, left_ref, right_ref, up_ref, down_ref):
    channels = cells_ref.shape[1]
    place = lax.broadcasted_iota(jnp.int32, (8, channels), 0)
    blank = jnp.zeros((8, channels), f32)
    left = [left_ref[h].astype(f32) for h in range(reach)]
    right = [right_ref[h].astype(f32) for h in range(reach)]
    for r in range(reach):
        for row, ref in ((r, up_ref), (side - reach + r, down_ref)):
            corner = blank
            for h in range(reach):
                corner = jnp.where(place == h, right[h][row : row + 1], corner)
                corner = jnp.where(place == 8 - reach + h, left[h][row : row + 1], corner)
            body = cells_ref[row * side : (row + 1) * side]
            ref[r] = jnp.concatenate([body, corner, blank], axis=0).astype(bf16)


def side_rows(cells, left, right):
    channels = cells.shape[1]
    shape = jax.ShapeDtypeStruct((reach, side + 16, channels), bf16)
    return pl.pallas_call(
        side_rows_body,
        out_shape=(shape, shape),
        in_specs=[whole] * 3,
        out_specs=[whole] * 2,
        compiler_params=params(6),
        cost_estimate=cost(0.5),
        name="side_rows",
    )(cells, left, right)


def beyond_steps(low, r):
    if low:
        return [(h, h - r) for h in range(r, reach)]
    return [(h, 6 + h - r) for h in range(0, r + 1)]


def add_rows(flipped, kernel_ref, top_ref, bottom_ref, rows_sum):
    lat = lax.axis_index("lat")
    channels = kernel_ref.shape[2]
    for c in range(channels // lanes):
        cols = slice(c * lanes, (c + 1) * lanes)
        for low, ref in ((True, top_ref), (False, bottom_ref)):
            outside = lat == (0 if low else lax.axis_size("lat") - 1)
            beyond = [
                jnp.where(outside, 0.0, ref[h, :, cols].astype(f32)[: side + 8]) for h in range(reach)
            ]
            for r in range(reach):
                result = None
                for q in range(7):
                    summed = None
                    for h, p in beyond_steps(low, r):
                        term = tap_row(kernel_ref, flipped, p, q, cols) * beyond[h]
                        summed = term if summed is None else summed + term
                    summed = pltpu.roll(summed, (reach - q) % (side + 8), 0) if q != reach else summed
                    result = summed if result is None else result + summed
                rows_sum[r if low else reach + r, :, cols] = result[:side]


def add_cols(flipped, kernel_ref, left_ref, right_ref, cols_sum):
    channels = kernel_ref.shape[2]
    for c in range(channels // lanes):
        cols = slice(c * lanes, (c + 1) * lanes)
        for low, ref in ((True, left_ref), (False, right_ref)):
            beyond = [ref[h, :, cols].astype(f32) for h in range(reach)]
            for r in range(reach):
                result = None
                for p in range(7):
                    summed = None
                    for h, q in beyond_steps(low, r):
                        term = tap_row(kernel_ref, flipped, p, q, cols) * beyond[h]
                        summed = term if summed is None else summed + term
                    summed = shift_cols(summed, p - reach)
                    result = summed if result is None else result + summed
                cols_sum[r if low else reach + r, :, cols] = result


def edged_row(i, conv_row, cols_sum):
    channels = conv_row.shape[1]
    place = lax.broadcasted_iota(jnp.int32, (8, channels), 0)
    first, last = conv_row[:8], conv_row[side - 8 :]
    for r in range(reach):
        first = first + jnp.where(place == r, cols_sum[r, pl.ds(i, 1), :], 0.0)
        last = last + jnp.where(place == 8 - reach + r, cols_sum[reach + r, pl.ds(i, 1), :], 0.0)
    return jnp.concatenate([first, conv_row[8 : side - 8], last], axis=0)


def each_row(step):
    def low(i, carry):
        step(i, i)
        return carry

    def middle(i, carry):
        step(i, None)
        return carry

    def high(i, carry):
        step(i, i - (side - 2 * reach))
        return carry

    lax.fori_loop(0, reach, low, 0, unroll=reach)
    lax.fori_loop(reach, side - reach, middle, 0, unroll=side // 2 - reach)
    lax.fori_loop(side - reach, side, high, 0, unroll=reach)


def conv_rows(refs, at):
    return jnp.concatenate([ref[at, :] for ref in refs], axis=1)


def normalise_body(
    conv0_ref, conv1_ref, conv2_ref, kernel_ref, left_ref, right_ref, top_ref, bottom_ref, bias_ref, gain_ref, shift_ref,
    unit_ref, spread_ref, normed_ref, rows_sum, cols_sum,
):
    channels = kernel_ref.shape[2]
    conv_refs = (conv0_ref, conv1_ref, conv2_ref)
    add_rows(False, kernel_ref, top_ref, bottom_ref, rows_sum)
    add_cols(False, kernel_ref, left_ref, right_ref, cols_sum)
    share = 1.0 / channels

    def step(i, outer):
        at = pl.ds(pl.multiple_of(i * side, side), side)
        value = edged_row(i, conv_rows(conv_refs, at), cols_sum)
        if outer is not None:
            value = value + rows_sum[outer]
        value = value + bias_ref[...]
        mean = jnp.sum(value, axis=1, keepdims=True) * share
        centred = value - mean
        spread = lax.rsqrt(jnp.sum(centred * centred, axis=1, keepdims=True) * share + norm_eps)
        unit = centred * spread
        unit_ref[at, :] = unit
        spread_ref[at, :] = jnp.broadcast_to(spread, (side, lanes))
        normed_ref[at, :] = (unit * gain_ref[...] + shift_ref[...]).astype(bf16)

    each_row(step)


def turn(source_ref, target_ref):
    for b in range(source_ref.shape[0] // 256):
        at = slice(b * 256, (b + 1) * 256)
        target_ref[:, at] = source_ref[at, :].T


def normalise(conv, kernel, left, right, top, bottom, bias, gain, shift):
    total, channels = conv[0].shape[0], kernel.shape[2]
    return pl.pallas_call(
        normalise_body,
        out_shape=(
            jax.ShapeDtypeStruct((total, channels), f32),
            jax.ShapeDtypeStruct((total, lanes), f32),
            jax.ShapeDtypeStruct((total, channels), bf16),
        ),
        in_specs=[whole] * 11,
        out_specs=[whole] * 3,
        scratch_shapes=[pltpu.VMEM((2 * reach, side, channels), f32)] * 2,
        compiler_params=params(12),
        cost_estimate=cost(2.8),
        name="normalise",
    )(*conv, kernel, left, right, top, bottom, bias, gain, shift)


def wet_row(i, counts_ref):
    place = lax.broadcasted_iota(jnp.int32, (8, lanes), 0) + (i % 8) * 8
    pieces = []
    for t in range(side // 8):
        pieces.append(place < counts_ref[i // 8, t])
    return pieces


def masked_row(i, grad_row, counts_ref):
    channels = grad_row.shape[1]
    parts = []
    for t, wet in enumerate(wet_row(i, counts_ref)):
        piece = grad_row[t * 8 : (t + 1) * 8]
        parts.append(
            jnp.concatenate(
                [
                    jnp.where(wet, piece[:, c * lanes : (c + 1) * lanes], 0.0)
                    for c in range(channels // lanes)
                ],
                axis=1,
            )
        )
    return jnp.concatenate(parts, axis=0)


def mask_rows_body(counts_ref, grad_ref, rows_ref):
    def step(i, carry):
        at = pl.ds(pl.multiple_of(i * side, side), side)
        rows_ref[at, :] = masked_row(i, grad_ref[at, :], counts_ref).astype(bf16)
        return carry

    lax.fori_loop(0, side, step, 0, unroll=side)


def mask_rows(counts, grad):
    total, channels = grad.shape
    return pl.pallas_call(
        mask_rows_body,
        out_shape=jax.ShapeDtypeStruct((total, channels), bf16),
        in_specs=[pl.BlockSpec(memory_space=pltpu.SMEM), whole],
        out_specs=whole,
        compiler_params=params(8),
        cost_estimate=cost(0.9),
        name="mask_rows",
    )(counts, grad)


def arrange_body(expand_ref, reduce_ref, bias_ref, expand_out, reduce_out, turned_out, bias_out):
    channels = expand_ref.shape[1]
    new = lax.broadcasted_iota(jnp.int32, (96, 96), 0)
    old = lax.broadcasted_iota(jnp.int32, (96, 96), 1)
    lo, rest = new // 48, new % 48
    pick = old == (rest // 6) * 12 + lo * 6 + rest % 6
    chosen = pick.astype(f32).astype(bf16)
    for hi, y, core in itertools.product(range(2), range(4), range(2)):
        unit = (hi * 4 + y) * 2 + core
        at = slice(unit * 96, (unit + 1) * 96)
        both = jnp.concatenate([expand_ref[at, :], reduce_ref[at, :]], axis=1)
        moved = jnp.dot(chosen, both, preferred_element_type=f32).astype(bf16)
        column = jnp.sum(jnp.where(pick, bias_ref[:, at], 0.0), axis=1, keepdims=True)
        column = jnp.broadcast_to(column, (96, lanes))
        for lo_place in range(2):
            x = 2 * hi + lo_place
            place = core * 16 + (y * 4 + x if core == 0 else x * 4 + y)
            to = slice(place * 48, (place + 1) * 48)
            half = slice(lo_place * 48, (lo_place + 1) * 48)
            expand_out[to, :] = moved[half, :channels]
            reduce_out[to, :] = moved[half, channels:]
            bias_out[to, :] = column[half]
    turn(expand_out, turned_out)


def arrange(expand, reduce, bias):
    units, channels = expand.shape
    shape = jax.ShapeDtypeStruct((units, channels), bf16)
    return pl.pallas_call(
        arrange_body,
        out_shape=(
            shape,
            shape,
            jax.ShapeDtypeStruct((channels, units), bf16),
            jax.ShapeDtypeStruct((units, lanes), f32),
        ),
        in_specs=[whole] * 3,
        out_specs=[whole] * 4,
        compiler_params=params(12),
        cost_estimate=cost(1.5),
        name="arrange",
    )(expand, reduce, bias)


tail_slope = 0.3275911 * 0.7071067811865476
tail_terms = [
    0.5 * a for a in (0.254829592, -0.284496736, 1.421413741, -1.453152027, 1.061405429)
]
exp_scale = -0.5 * 1.4426950408889634


def gelu_pair(v):
    d = 1.0 + tail_slope * jnp.abs(v)
    t = pltpu.reciprocal(d, approx=True)
    poly = tail_terms[4]
    for a in reversed(tail_terms[:4]):
        poly = poly * t + a
    bell = jnp.exp2(v * v * exp_scale)
    tail = poly * t * bell
    below = jnp.where(v >= 0.0, 1.0 - tail, tail)
    return v * below, below + v * bell * inv_root_two_pi


def own_place():
    lat, lon = lax.axis_index("lat"), lax.axis_index("lon")
    x = 2 * lax.axis_index("dp") + (lon & 1)
    return lat & 1, x, lat >> 1, lon >> 1


def phase_place(second):
    core, x, y, _ = own_place()
    along_y = core == (1 if second else 0)
    return jnp.where(along_y, y, x)


def dot_rows(left, right):
    return lax.dot_general(left, right, (((1,), (1,)), ((), ())), preferred_element_type=f32)


class HiddenBlock:

    def __init__(self, cells, sources, rows, grad_pre_ref, places, scratch):
        self.normed, self.grad, self.expand, self.reduce, self.bias = cells
        self.sources, self.rows, self.places = sources, rows, places
        self.grad_pre = grad_pre_ref
        self.preact, self.grad_hidden, self.hidden, self.terms = scratch
        self.total = self.normed.shape[0]

    def gather(self, ref):
        return jnp.concatenate([ref[pl.ds(s, self.rows), :] for s in self.sources], axis=0)

    def dots(self, at):
        self.preact[:, at] = dot_rows(self.gather(self.expand), self.normed[at, :])
        self.grad_hidden[:, at] = dot_rows(self.gather(self.reduce), self.grad[at, :])

    def activate(self, at):
        bias = jnp.concatenate([self.gather(self.bias)] * ((at.stop - at.start) // lanes), axis=1)
        value, slope = gelu_pair(self.preact[:, at] + bias)
        self.hidden[:, at] = value.astype(bf16)
        grad_pre = (self.grad_hidden[:, at] * slope).astype(bf16)
        self.terms[:, at] = grad_pre
        for n, place in enumerate(self.places):
            self.grad_pre[pl.ds(place, self.rows), at] = grad_pre[n * self.rows : (n + 1) * self.rows]

    def expand_sum(self):
        return jnp.dot(self.terms[...], self.normed[...], preferred_element_type=f32)

    def reduce_sum(self):
        return jnp.dot(self.hidden[...], self.grad[...], preferred_element_type=f32)


def hidden_scratch(rows, total):
    return [
        pltpu.VMEM((rows, total), f32),
        pltpu.VMEM((rows, total), f32),
        pltpu.VMEM((rows, total), bf16),
        pltpu.VMEM((rows, total), bf16),
    ]


def far_body(*refs):
    cells, (sent_ref, grad_pre_ref), scratch = refs[:5], refs[5:7], refs[7:]
    half, total = grad_pre_ref.shape
    channels = refs[0].shape[1]
    base = (1 - own_place()[0]) * half
    rows = half // 2
    blocks = [
        HiddenBlock(
            cells, [pl.multiple_of(base + b * rows, rows)], rows, grad_pre_ref, [b * rows],
            scratch[4 * b : 4 * b + 4],
        )
        for b in range(2)
    ]
    first, second = blocks
    pieces = [slice(c, c + 256) for c in range(0, total, 256)]
    for at in pieces:
        first.dots(at)
    for at in pieces:
        first.activate(at)
        second.dots(at)
    second.activate(pieces[0])
    sent_ref[:rows, :channels] = first.expand_sum().astype(bf16)
    second.activate(pieces[1])
    sent_ref[:rows, channels:] = first.reduce_sum().astype(bf16)
    for at in pieces[2:]:
        second.activate(at)
    sent_ref[rows:, :channels] = second.expand_sum().astype(bf16)
    sent_ref[rows:, channels:] = second.reduce_sum().astype(bf16)


def hidden_far(*cells):
    total, channels = cells[0].shape
    half = cells[2].shape[0] // 2
    return pl.pallas_call(
        far_body,
        out_shape=(
            jax.ShapeDtypeStruct((half, 2 * channels), bf16),
            jax.ShapeDtypeStruct((half, total), bf16),
        ),
        in_specs=[whole] * 5,
        out_specs=[whole] * 2,
        scratch_shapes=hidden_scratch(half // 2, total) * 2,
        compiler_params=params(20),
        cost_estimate=cost(5.0),
        name="hidden_far",
    )(*cells)


def near_first_body(*refs):
    cells, (sums_ref, grad_pre_ref), scratch = refs[:5], refs[5:7], refs[7:]
    half = grad_pre_ref.shape[0]
    channels = refs[0].shape[1]
    size = half // 4
    core, place = own_place()[0], phase_place(False)
    chunks = [pl.multiple_of(lax.rem(place + step, 4) * size, size) for step in (1, 2)]
    sources = [pl.multiple_of(core * half + chunk, size) for chunk in chunks]
    block = HiddenBlock(cells, sources, size, grad_pre_ref, chunks, scratch)
    block.dots(slice(0, block.total))
    block.activate(slice(0, block.total))
    sums_ref[:, :channels] = block.expand_sum()
    sums_ref[:, channels:] = block.reduce_sum()


def near_first(*cells):
    total, channels = cells[0].shape
    half = cells[2].shape[0] // 2
    return pl.pallas_call(
        near_first_body,
        out_shape=(
            jax.ShapeDtypeStruct((half // 2, 2 * channels), f32),
            jax.ShapeDtypeStruct((half, total), bf16),
        ),
        in_specs=[whole] * 5,
        out_specs=[whole] * 2,
        scratch_shapes=hidden_scratch(half // 2, total),
        compiler_params=params(16),
        cost_estimate=cost(3.0),
        name="near_first",
    )(*cells)


def near_sends_body(sums_ref, arrived_ref, *sent_refs):
    size = sent_refs[0].shape[0]
    place = phase_place(False)
    for n, step in enumerate((1, 2)):
        chunk = pl.multiple_of(lax.rem(place + step, 4) * size, size)
        total = sums_ref[n * size : (n + 1) * size] + arrived_ref[pl.ds(chunk, size), :].astype(f32)
        sent_refs[n][...] = total.astype(bf16)


def near_sends(sums, arrived):
    size, width = sums.shape[0] // 2, sums.shape[1]
    sent = jax.ShapeDtypeStruct((size, width), bf16)
    return pl.pallas_call(
        near_sends_body,
        out_shape=(sent, sent),
        in_specs=[whole] * 2,
        out_specs=[whole] * 2,
        compiler_params=params(6),
        cost_estimate=cost(0.3),
        name="near_sends",
    )(sums, arrived)


def near_last_body(*refs):
    cells, (arrived_ref, _, own_ref, sent_ref, grad_pre_ref) = refs[:5], refs[5:10]
    half = grad_pre_ref.shape[0]
    channels = refs[0].shape[1]
    size = half // 4
    core, place = own_place()[0], phase_place(False)
    chunks = [pl.multiple_of(lax.rem(place + step, 4) * size, size) for step in (3, 0)]
    sources = [pl.multiple_of(core * half + chunk, size) for chunk in chunks]
    block = HiddenBlock(cells, sources, size, grad_pre_ref, chunks, refs[10:])
    block.dots(slice(0, block.total))
    block.activate(slice(0, block.total))
    expand, reduce = block.expand_sum(), block.reduce_sum()
    for n, (chunk, ref) in enumerate(zip(chunks, (sent_ref, own_ref))):
        at = slice(n * size, (n + 1) * size)
        other = arrived_ref[pl.ds(chunk, size), :].astype(f32)
        ref[:, :channels] = (expand[at] + other[:, :channels]).astype(ref.dtype)
        ref[:, channels:] = (reduce[at] + other[:, channels:]).astype(ref.dtype)


def near_last(*inputs):
    cells, grad_pre = inputs[:5], inputs[6]
    channels = cells[0].shape[1]
    size = cells[2].shape[0] // 8
    return pl.pallas_call(
        near_last_body,
        out_shape=(
            jax.ShapeDtypeStruct((size, 2 * channels), f32),
            jax.ShapeDtypeStruct((size, 2 * channels), bf16),
            jax.ShapeDtypeStruct(grad_pre.shape, bf16),
        ),
        in_specs=[whole] * 7,
        out_specs=[whole] * 3,
        input_output_aliases={6: 2},
        scratch_shapes=hidden_scratch(2 * size, cells[0].shape[0]),
        compiler_params=params(16),
        cost_estimate=cost(3.0),
        name="near_last",
    )(*inputs)


def norm_back_body(
    turned_ref, other_ref, mine_ref, unit_ref, spread_ref, gain_ref,
    conv_grad_ref, first_ref, last_ref,
):
    total, channels = unit_ref.shape
    half = turned_ref.shape[1] // 2
    core = own_place()[0]
    block = 256
    share = 1.0 / channels
    mine_weight = turned_ref[:, pl.ds(pl.multiple_of(core * half, half), half)]
    other_weight = turned_ref[:, pl.ds(pl.multiple_of((1 - core) * half, half), half)]
    for b in range(total // block):
        at = slice(b * block, (b + 1) * block)
        summed = jnp.dot(mine_weight, mine_ref[:, at], preferred_element_type=f32)
        summed = summed + jnp.dot(other_weight, other_ref[:, at], preferred_element_type=f32)
        grad_normed = summed.astype(bf16).T.astype(f32)
        unit = unit_ref[at, :]
        grad_unit = grad_normed * gain_ref[...]
        mean_grad = jnp.sum(grad_unit, axis=1, keepdims=True) * share
        mean_cross = jnp.sum(grad_unit * unit, axis=1, keepdims=True) * share
        spread = jnp.concatenate([spread_ref[at, :]] * (channels // lanes), axis=1)
        value = (grad_unit - mean_grad - unit * mean_cross) * spread
        conv_grad_ref[b * 8 : (b + 1) * 8] = value.reshape(block // side, side, channels)
    for j in range(reach):
        first_ref[j] = conv_grad_ref[:, j, :].astype(bf16)
        last_ref[j] = conv_grad_ref[:, side - reach + j, :].astype(bf16)


def norm_back(turned, other, mine, unit, spread, gain):
    total, channels = unit.shape
    shape = jax.ShapeDtypeStruct((reach, side, channels), bf16)
    found, first, last = pl.pallas_call(
        norm_back_body,
        out_shape=(jax.ShapeDtypeStruct((side, side, channels), f32), shape, shape),
        in_specs=[whole] * 6,
        out_specs=[whole] * 3,
        compiler_params=params(14),
        cost_estimate=cost(0.2),
        name="norm_back",
    )(turned, other, mine, unit, spread, gain)
    return found.reshape(total, channels), first, last


def finish_inner_body(
    counts_ref, conv0_ref, conv1_ref, conv2_ref, kernel_ref, left_ref, right_ref, grad_ref,
    out_ref, cols_sum, done, sems,
):
    conv_refs = (conv0_ref, conv1_ref, conv2_ref)
    add_cols(True, kernel_ref, left_ref, right_ref, cols_sum)
    bounds = [reach, 9, 16, 23, side - reach]
    copies = []
    for n, (low, high) in enumerate(zip(bounds[:-1], bounds[1:])):
        for i in range(low, high):
            at = slice(i * side, (i + 1) * side)
            value = edged_row(i, conv_rows(conv_refs, at), cols_sum)
            done[at, :] = value + masked_row(i, grad_ref[at, :], counts_ref)
        part = pl.ds(low * side, (high - low) * side)
        copies.append(pltpu.make_async_copy(done.at[part, :], out_ref.at[part, :], sems.at[n]))
        copies[-1].start()
    for copy in copies:
        copy.wait()


def finish_inner(counts, conv, kernel, left, right, grad):
    total, channels = grad.shape
    return pl.pallas_call(
        finish_inner_body,
        out_shape=(
            jax.ShapeDtypeStruct((total, channels), f32),
            jax.ShapeDtypeStruct((2 * reach, side, channels), f32),
        ),
        in_specs=[pl.BlockSpec(memory_space=pltpu.SMEM)] + [whole] * 7,
        out_specs=[pl.BlockSpec(memory_space=pltpu.HBM), whole],
        scratch_shapes=[pltpu.VMEM((total, channels), f32), pltpu.SemaphoreType.DMA((4,))],
        compiler_params=params(12),
        cost_estimate=cost(2.2),
        name="finish_inner",
    )(counts, *conv, kernel, left, right, grad)


def finish_outer_body(
    counts_ref, conv0_ref, conv1_ref, conv2_ref, kernel_ref, top_ref, bottom_ref, cols_ref,
    grad_ref, _, out_ref, rows_sum, done, sems,
):
    conv_refs = (conv0_ref, conv1_ref, conv2_ref)
    add_rows(True, kernel_ref, top_ref, bottom_ref, rows_sum)
    copies = []
    for n, start in enumerate((0, side - reach)):
        for r in range(reach):
            i = start + r
            at = slice(i * side, (i + 1) * side)
            value = edged_row(i, conv_rows(conv_refs, at), cols_ref) + rows_sum[n * reach + r]
            done[n, r * side : (r + 1) * side, :] = value + masked_row(i, grad_ref[at, :], counts_ref)
        part = pl.ds(start * side, reach * side)
        copies.append(pltpu.make_async_copy(done.at[n], out_ref.at[part, :], sems.at[n]))
        copies[-1].start()
    for copy in copies:
        copy.wait()


def finish_outer(counts, conv, kernel, top, bottom, cols_sum, grad, inner):
    channels = grad.shape[1]
    return pl.pallas_call(
        finish_outer_body,
        out_shape=jax.ShapeDtypeStruct(inner.shape, f32),
        in_specs=[pl.BlockSpec(memory_space=pltpu.SMEM)]
        + [whole] * 8
        + [pl.BlockSpec(memory_space=pltpu.HBM)],
        out_specs=pl.BlockSpec(memory_space=pltpu.HBM),
        input_output_aliases={9: 0},
        scratch_shapes=[
            pltpu.VMEM((2 * reach, side, channels), f32),
            pltpu.VMEM((2, reach * side, channels), f32),
            pltpu.SemaphoreType.DMA((2,)),
        ],
        compiler_params=params(12),
        cost_estimate=cost(1.0),
        name="finish_outer",
    )(counts, *conv, kernel, top, bottom, cols_sum, grad, inner)


def split_four_body(own_ref, first_ref, second_ref, third_ref, kept_ref, *sent_refs):
    size = kept_ref.shape[0]
    place = phase_place(True)
    for step in range(4):
        at = pl.ds(pl.multiple_of(lax.rem(place + step, 4) * size, size), size)
        total = own_ref[at, :]
        for ref in (first_ref, second_ref, third_ref):
            total = total + ref[at, :].astype(f32)
        if step == 0:
            kept_ref[...] = total
        else:
            sent_refs[step - 1][...] = total.astype(bf16)


def split_four(own, parts):
    size, width = own.shape[0] // 4, own.shape[1]
    sent = jax.ShapeDtypeStruct((size, width), bf16)
    return pl.pallas_call(
        split_four_body,
        out_shape=(jax.ShapeDtypeStruct((size, width), f32), sent, sent, sent),
        in_specs=[whole] * 4,
        out_specs=[whole] * 4,
        compiler_params=params(4),
        cost_estimate=cost(0.3),
        name="split_four",
    )(own, *parts)


def split_two_body(own_ref, *refs):
    part_refs, (kept_ref, sent_ref) = refs[:-2], refs[-2:]
    size = kept_ref.shape[0]
    total = own_ref[...]
    for ref in part_refs:
        total = total + ref[...].astype(f32)
    low, high = total[:size], total[size:]
    upper = (own_place()[3] & 1) != 0
    kept_ref[...] = jnp.where(upper, high, low)
    sent_ref[...] = jnp.where(upper, low, high)


def split_two(own, parts):
    shape = jax.ShapeDtypeStruct((own.shape[0] // 2, own.shape[1]), f32)
    return pl.pallas_call(
        split_two_body,
        out_shape=(shape, shape),
        in_specs=[whole] * (1 + len(parts)),
        out_specs=[whole] * 2,
        compiler_params=params(4),
        cost_estimate=cost(0.2),
        name="split_two",
    )(own, *parts)


def split_ring_body(own_ref, first_ref, second_ref, third_ref, kept_ref, *sent_refs):
    size = kept_ref.shape[0]
    total = own_ref[...]
    for ref in (first_ref, second_ref, third_ref):
        total = total + ref[...].astype(f32)
    chunks = [total[c * size : (c + 1) * size] for c in range(4)]
    place = own_place()[3] >> 1
    for step, ref in enumerate((kept_ref, *sent_refs)):
        wanted = (place + step) & 3
        found = chunks[0]
        for c in range(1, 4):
            found = jnp.where(wanted == c, chunks[c], found)
        ref[...] = found.astype(ref.dtype)


def split_ring(own, parts):
    size, width = own.shape[0] // 4, own.shape[1]
    sent = jax.ShapeDtypeStruct((size, width), bf16)
    return pl.pallas_call(
        split_ring_body,
        out_shape=(jax.ShapeDtypeStruct((size, width), f32), sent, sent, sent),
        in_specs=[whole] * 4,
        out_specs=[whole] * 4,
        compiler_params=params(4),
        cost_estimate=cost(0.2),
        name="split_ring",
    )(own, *parts)


def last_sum_body(scale, own_ref, arrived_ref, expand_ref, reduce_ref):
    channels = expand_ref.shape[2]
    total = (own_ref[...] + arrived_ref[...]) * scale
    for r in range(total.shape[0]):
        expand_ref[r] = total[r : r + 1, :channels]
        reduce_ref[r] = total[r : r + 1, channels:]


def last_sum(own, arrived, scale):
    size, width = own.shape
    shape = jax.ShapeDtypeStruct((size, 1, width // 2), f32)
    expand, reduce = pl.pallas_call(
        functools.partial(last_sum_body, scale),
        out_shape=(shape, shape),
        in_specs=[whole] * 2,
        out_specs=[whole] * 2,
        compiler_params=params(4),
        cost_estimate=cost(0.4),
        name="last_sum",
    )(own, arrived)
    return expand.transpose(1, 0, 2), reduce.transpose(1, 0, 2)


every_axis = ("dp", "lat", "lon")


def device_pairs(move):
    def flat(hi, y, core, z, lo):
        return (hi * 8 + y * 2 + core) * 16 + z * 2 + lo

    found = []
    for hi, y, core, z, lo in itertools.product(range(2), range(4), range(2), range(8), range(2)):
        found.append((flat(hi, y, core, z, lo), flat(*move(hi, y, core, z, lo))))
    return found


def plane_pairs(step, first):
    def move(hi, y, core, z, lo):
        if (core == 0) == first:
            return (hi, (y + step) % 4, core, z, lo)
        x = (2 * hi + lo + step) % 4
        return (x // 2, y, core, z, x % 2)

    return device_pairs(move)


def ring_pairs(step):
    return device_pairs(lambda hi, y, core, z, lo: (hi, y, core, (z + 2 * step) % 8, lo))


def last_pairs():
    return device_pairs(lambda hi, y, core, z, lo: (hi, y, core, z ^ 1, lo))


def shifted(axis, step):
    count = lax.axis_size(axis)
    return [(i, (i + step) % count) for i in range(count)]


def lon_halo(first, last):
    left = lax.ppermute(last, "lon", shifted("lon", 1))
    right = lax.ppermute(first, "lon", shifted("lon", -1))
    return left, right


def lat_halo(up, down):
    top = lax.ppermute(down, "lat", shifted("lat", 1))
    bottom = lax.ppermute(up, "lat", shifted("lat", -1))
    return top, bottom


def after(value, *others):
    return lax.optimization_barrier((value, others))[0]


def local(
    state, cotangent, counts, dw_kernel, dw_bias, norm_gain, norm_bias, w_expand, b_expand, w_reduce
):
    channels = state.shape[-1]
    cells = state.reshape(-1, channels)
    grad = cotangent.reshape(-1, channels)
    total = cells.shape[0]
    kernel = dw_kernel.transpose(1, 0, 2)

    first, last = side_cols(cells)
    left, right = lon_halo(first, last)
    conv = inner_conv(cells, kernel, (0,))
    grad, w_expand, w_reduce = after((grad, w_expand, w_reduce), first, last)
    rows = mask_rows(counts, grad)
    expand, reduce, expand_t, bias = arrange(w_expand[0], w_reduce[0], b_expand)
    left, right = after((left, right), rows, bias, conv)
    up, down = side_rows(cells, left, right)
    top, bottom = lat_halo(up, down)
    conv += inner_conv(after(cells, up, down), kernel, (1, 2))
    unit, spread, normed = normalise(
        conv, kernel, left, right, top, bottom, dw_bias, norm_gain, norm_bias
    )

    inputs = (normed, rows, expand, reduce, bias)
    sent, far_pre = hidden_far(*inputs)
    arrived = lax.ppermute(sent, "lat", [(i, i ^ 1) for i in range(8)])
    sums, near_pre = near_first(*inputs)
    one, two = near_sends(sums, arrived)
    part_one = lax.ppermute(one, every_axis, plane_pairs(1, True))
    part_two = lax.ppermute(two, every_axis, plane_pairs(2, True))
    own, three, near_pre = near_last(*inputs, arrived, after(near_pre, one, two))
    part_three = lax.ppermute(three, every_axis, plane_pairs(3, True))

    far_pre, part_one = after((far_pre, part_one), three)
    conv_grad, first, last = norm_back(expand_t, far_pre, near_pre, unit, spread, norm_gain)
    last, part_two = after((last, part_two))
    left, right = lon_halo(first, last)
    own, parts = after((own, (part_one, part_two, part_three)), first, last)
    own, *sent = split_four(own, parts)
    parts = [lax.ppermute(sent[i], every_axis, plane_pairs(i + 1, False)) for i in (0, 2, 1)]
    back = back_conv(after(conv_grad, sent), kernel, (0, 1))
    (conv_grad, left, right), parts = after(((conv_grad, left, right), parts), back)
    up, down = side_rows(conv_grad, left, right)

    own, *sent = split_ring(*after((own, parts), up, down))
    parts = [lax.ppermute(sent[i], every_axis, ring_pairs(i + 1)) for i in (0, 2, 1)]
    top, bottom = lat_halo(up, down)
    back += back_conv(after(conv_grad, sent, top, bottom), kernel, (2,))

    inner, cols_sum = finish_inner(counts, back, kernel, left, right, grad)

    own, sent = split_two(*after((own, parts), inner))
    arrived = lax.ppermute(sent, every_axis, last_pairs())
    inner = after(inner, sent)
    gradient = finish_outer(counts, back, kernel, top, bottom, cols_sum, grad, inner)

    cells_all = lax.axis_size("dp") * lax.axis_size("lat") * lax.axis_size("lon") * total
    kept = last_sum(own, arrived, 1.0 / math.sqrt(cells_all))
    return (gradient.reshape(state.shape), *kept)


def solution(mesh):
    in_specs = (
        P("dp", "lat", "lon", None),
        P("dp", "lat", "lon", None),
        P("lat", "lon"),
        P(),
        P(),
        P(),
        P(),
        P(),
        P(),
        P(),
    )
    out_specs = (
        P("dp", "lat", "lon", None),
        P(None, ("dp", "lat", "lon"), None),
        P(None, ("dp", "lat", "lon"), None),
    )
    return jax.shard_map(local, mesh=mesh, in_specs=in_specs, out_specs=out_specs, check_vma=False)
```

```python
import functools
import itertools
import math

import jax
import jax.numpy as jnp
from jax import lax
from jax.experimental import pallas as pl
from jax.experimental.pallas import tpu as pltpu
from jax.sharding import PartitionSpec as P

norm_eps = 1e-06
inv_root_two_pi = 0.3989422804014327
side = 32
reach = 3
lanes = 128
f32 = jnp.float32
bf16 = jnp.bfloat16
whole = pl.BlockSpec(memory_space=pltpu.VMEM)


def params(mib):
    return pltpu.CompilerParams(vmem_limit_bytes=mib * 1024 * 1024)


def cost(microseconds):
    return pl.CostEstimate(
        flops=int(microseconds * 1.15e9), bytes_accessed=2**20, transcendentals=0
    )


def tap_row(kernel_ref, flipped, p, q, cols):
    index = 7 * p + q
    if flipped:
        index = 48 - index
    return kernel_ref[index, :, cols]


def shift_cols(rows, offset):
    if offset == 0:
        return rows
    count = rows.shape[0]
    turned = pltpu.roll(rows, (-offset) % count, 0)
    place = lax.broadcasted_iota(jnp.int32, (8, rows.shape[1]), 0)
    if offset > 0:
        last = jnp.where(place < 8 - offset, turned[count - 8 :], 0.0)
        return jnp.concatenate([turned[: count - 8], last], axis=0)
    first = jnp.where(place >= -offset, turned[:8], 0.0)
    return jnp.concatenate([first, turned[8:]], axis=0)


def inner_conv_body(parts, cells_ref, kernel_ref, *refs):
    outs, padded = refs[:-1], refs[-1]
    edge = reach * side
    total = side * side
    group = 4
    padded[0:edge] = jnp.zeros((edge, lanes), f32)
    padded[edge + total : 2 * edge + total] = jnp.zeros((edge, lanes), f32)
    for part, out_ref in zip(parts, outs):
        cols = slice(part * lanes, (part + 1) * lanes)
        padded[edge : edge + total] = cells_ref[:, cols]

        def some_rows(i, carry):
            base = pl.multiple_of(i * (group * side), group * side)
            rows = [padded[pl.ds(base + p * side, side), :] for p in range(6 + group)]
            results = [None] * group
            for q in range(7):
                sums = [None] * group
                for p in range(7):
                    tap = tap_row(kernel_ref, False, p, q, cols)
                    for g in range(group):
                        term = tap * rows[p + g]
                        sums[g] = term if sums[g] is None else sums[g] + term
                for g in range(group):
                    moved = shift_cols(sums[g], q - reach)
                    results[g] = moved if results[g] is None else results[g] + moved
            for g in range(group):
                out_ref[pl.ds(base + g * side, side), :] = results[g]
            return carry

        lax.fori_loop(0, side // group, some_rows, 0)


def inner_conv(cells, kernel, parts):
    total = cells.shape[0]
    shape = jax.ShapeDtypeStruct((total, lanes), f32)
    return pl.pallas_call(
        functools.partial(inner_conv_body, parts),
        out_shape=(shape,) * len(parts),
        in_specs=[whole] * 2,
        out_specs=[whole] * len(parts),
        scratch_shapes=[pltpu.VMEM((total + 2 * reach * side, lanes), f32)],
        compiler_params=params(6),
        cost_estimate=cost(2.2 * len(parts)),
        name="inner_conv",
    )(cells, kernel)


def back_conv_body(parts, cells_ref, kernel_ref, *refs):
    outs, (padded, taps) = refs[:-2], refs[-2:]
    edge = reach * side
    total = side * side
    group = 4
    padded[0:edge] = jnp.zeros((edge, lanes), bf16)
    padded[edge + total : 2 * edge + total] = jnp.zeros((edge, lanes), bf16)
    for part, out_ref in zip(parts, outs):
        cols = slice(part * lanes, (part + 1) * lanes)
        padded[edge : edge + total] = cells_ref[:, cols].astype(bf16)
        for p, q in itertools.product(range(7), range(7)):
            tap = jnp.broadcast_to(tap_row(kernel_ref, True, p, q, cols), (16, lanes))
            taps[7 * p + q] = tap.astype(bf16)

        def some_rows(i, carry):
            base = pl.multiple_of(i * (group * side), group * side)
            rows = [padded[pl.ds(base + p * side, side), :] for p in range(6 + group)]
            results = [None] * group
            for q in range(7):
                sums = [None] * group
                for p in range(7):
                    tap = jnp.concatenate([taps[7 * p + q]] * (side // 16), axis=0)
                    for g in range(group):
                        term = tap * rows[p + g]
                        sums[g] = term if sums[g] is None else sums[g] + term
                for g in range(group):
                    moved = shift_cols(sums[g].astype(f32), q - reach)
                    results[g] = moved if results[g] is None else results[g] + moved
            for g in range(group):
                out_ref[pl.ds(base + g * side, side), :] = results[g]
            return carry

        lax.fori_loop(0, side // group, some_rows, 0)


def back_conv(cells, kernel, parts):
    total = cells.shape[0]
    shape = jax.ShapeDtypeStruct((total, lanes), f32)
    return pl.pallas_call(
        functools.partial(back_conv_body, parts),
        out_shape=(shape,) * len(parts),
        in_specs=[whole] * 2,
        out_specs=[whole] * len(parts),
        scratch_shapes=[
            pltpu.VMEM((total + 2 * reach * side, lanes), bf16),
            pltpu.VMEM((49, 16, lanes), bf16),
        ],
        compiler_params=params(6),
        cost_estimate=cost(1.5 * len(parts)),
        name="back_conv",
    )(cells, kernel)


def side_cols_body(cells_ref, first_ref, last_ref, low, high, sems):
    copies = [
        pltpu.make_async_copy(cells_ref.at[:, pl.ds(0, 8), :], low, sems.at[0]),
        pltpu.make_async_copy(cells_ref.at[:, pl.ds(side - 8, 8), :], high, sems.at[1]),
    ]
    for copy in copies:
        copy.start()
    copies[0].wait()
    for j in range(reach):
        first_ref[j] = low[:, j, :].astype(bf16)
    copies[1].wait()
    for j in range(reach):
        last_ref[j] = high[:, 8 - reach + j, :].astype(bf16)


def side_cols(cells):
    channels = cells.shape[1]
    shape = jax.ShapeDtypeStruct((reach, side, channels), bf16)
    return pl.pallas_call(
        side_cols_body,
        out_shape=(shape, shape),
        in_specs=[pl.BlockSpec(memory_space=pltpu.HBM)],
        out_specs=[whole] * 2,
        scratch_shapes=[pltpu.VMEM((side, 8, channels), f32)] * 2 + [pltpu.SemaphoreType.DMA((2,))],
        compiler_params=params(58),
        cost_estimate=cost(1.0),
        name="side_cols",
    )(cells.reshape(side, side, channels))


def side_rows_body(cells_ref, left_ref, right_ref, up_ref, down_ref):
    channels = cells_ref.shape[1]
    place = lax.broadcasted_iota(jnp.int32, (8, channels), 0)
    blank = jnp.zeros((8, channels), f32)
    left = [left_ref[h].astype(f32) for h in range(reach)]
    right = [right_ref[h].astype(f32) for h in range(reach)]
    for r in range(reach):
        for row, ref in ((r, up_ref), (side - reach + r, down_ref)):
            corner = blank
            for h in range(reach):
                corner = jnp.where(place == h, right[h][row : row + 1], corner)
                corner = jnp.where(place == 8 - reach + h, left[h][row : row + 1], corner)
            body = cells_ref[row * side : (row + 1) * side]
            ref[r] = jnp.concatenate([body, corner, blank], axis=0).astype(bf16)


def side_rows(cells, left, right):
    channels = cells.shape[1]
    shape = jax.ShapeDtypeStruct((reach, side + 16, channels), bf16)
    return pl.pallas_call(
        side_rows_body,
        out_shape=(shape, shape),
        in_specs=[whole] * 3,
        out_specs=[whole] * 2,
        compiler_params=params(6),
        cost_estimate=cost(0.5),
        name="side_rows",
    )(cells, left, right)


def beyond_steps(low, r):
    if low:
        return [(h, h - r) for h in range(r, reach)]
    return [(h, 6 + h - r) for h in range(0, r + 1)]


def add_rows(flipped, kernel_ref, top_ref, bottom_ref, rows_sum):
    lat = lax.axis_index("lat")
    channels = kernel_ref.shape[2]
    for c in range(channels // lanes):
        cols = slice(c * lanes, (c + 1) * lanes)
        for low, ref in ((True, top_ref), (False, bottom_ref)):
            outside = lat == (0 if low else lax.axis_size("lat") - 1)
            beyond = [
                jnp.where(outside, 0.0, ref[h, :, cols].astype(f32)[: side + 8]) for h in range(reach)
            ]
            for r in range(reach):
                result = None
                for q in range(7):
                    summed = None
                    for h, p in beyond_steps(low, r):
                        term = tap_row(kernel_ref, flipped, p, q, cols) * beyond[h]
                        summed = term if summed is None else summed + term
                    summed = pltpu.roll(summed, (reach - q) % (side + 8), 0) if q != reach else summed
                    result = summed if result is None else result + summed
                rows_sum[r if low else reach + r, :, cols] = result[:side]


def add_cols(flipped, kernel_ref, left_ref, right_ref, cols_sum):
    channels = kernel_ref.shape[2]
    for c in range(channels // lanes):
        cols = slice(c * lanes, (c + 1) * lanes)
        for low, ref in ((True, left_ref), (False, right_ref)):
            beyond = [ref[h, :, cols].astype(f32) for h in range(reach)]
            for r in range(reach):
                result = None
                for p in range(7):
                    summed = None
                    for h, q in beyond_steps(low, r):
                        term = tap_row(kernel_ref, flipped, p, q, cols) * beyond[h]
                        summed = term if summed is None else summed + term
                    summed = shift_cols(summed, p - reach)
                    result = summed if result is None else result + summed
                cols_sum[r if low else reach + r, :, cols] = result


def edged_row(i, conv_row, cols_sum):
    channels = conv_row.shape[1]
    place = lax.broadcasted_iota(jnp.int32, (8, channels), 0)
    first, last = conv_row[:8], conv_row[side - 8 :]
    for r in range(reach):
        first = first + jnp.where(place == r, cols_sum[r, pl.ds(i, 1), :], 0.0)
        last = last + jnp.where(place == 8 - reach + r, cols_sum[reach + r, pl.ds(i, 1), :], 0.0)
    return jnp.concatenate([first, conv_row[8 : side - 8], last], axis=0)


def each_row(step):
    def low(i, carry):
        step(i, i)
        return carry

    def middle(i, carry):
        step(i, None)
        return carry

    def high(i, carry):
        step(i, i - (side - 2 * reach))
        return carry

    lax.fori_loop(0, reach, low, 0, unroll=reach)
    lax.fori_loop(reach, side - reach, middle, 0, unroll=side // 2 - reach)
    lax.fori_loop(side - reach, side, high, 0, unroll=reach)


def conv_rows(refs, at):
    return jnp.concatenate([ref[at, :] for ref in refs], axis=1)


def normalise_body(
    conv0_ref, conv1_ref, conv2_ref, kernel_ref, left_ref, right_ref, top_ref, bottom_ref, bias_ref, gain_ref, shift_ref,
    unit_ref, spread_ref, normed_ref, rows_sum, cols_sum,
):
    channels = kernel_ref.shape[2]
    conv_refs = (conv0_ref, conv1_ref, conv2_ref)
    add_rows(False, kernel_ref, top_ref, bottom_ref, rows_sum)
    add_cols(False, kernel_ref, left_ref, right_ref, cols_sum)
    share = 1.0 / channels

    def step(i, outer):
        at = pl.ds(pl.multiple_of(i * side, side), side)
        value = edged_row(i, conv_rows(conv_refs, at), cols_sum)
        if outer is not None:
            value = value + rows_sum[outer]
        value = value + bias_ref[...]
        mean = jnp.sum(value, axis=1, keepdims=True) * share
        centred = value - mean
        spread = lax.rsqrt(jnp.sum(centred * centred, axis=1, keepdims=True) * share + norm_eps)
        unit = centred * spread
        unit_ref[at, :] = unit
        spread_ref[at, :] = jnp.broadcast_to(spread, (side, lanes))
        normed_ref[at, :] = (unit * gain_ref[...] + shift_ref[...]).astype(bf16)

    each_row(step)


def turn(source_ref, target_ref):
    for b in range(source_ref.shape[0] // 256):
        at = slice(b * 256, (b + 1) * 256)
        target_ref[:, at] = source_ref[at, :].T


def normalise(conv, kernel, left, right, top, bottom, bias, gain, shift):
    total, channels = conv[0].shape[0], kernel.shape[2]
    return pl.pallas_call(
        normalise_body,
        out_shape=(
            jax.ShapeDtypeStruct((total, channels), f32),
            jax.ShapeDtypeStruct((total, lanes), f32),
            jax.ShapeDtypeStruct((total, channels), bf16),
        ),
        in_specs=[whole] * 11,
        out_specs=[whole] * 3,
        scratch_shapes=[pltpu.VMEM((2 * reach, side, channels), f32)] * 2,
        compiler_params=params(12),
        cost_estimate=cost(2.8),
        name="normalise",
    )(*conv, kernel, left, right, top, bottom, bias, gain, shift)


def wet_row(i, counts_ref):
    place = lax.broadcasted_iota(jnp.int32, (8, lanes), 0) + (i % 8) * 8
    pieces = []
    for t in range(side // 8):
        pieces.append(place < counts_ref[i // 8, t])
    return pieces


def masked_row(i, grad_row, counts_ref):
    channels = grad_row.shape[1]
    parts = []
    for t, wet in enumerate(wet_row(i, counts_ref)):
        piece = grad_row[t * 8 : (t + 1) * 8]
        parts.append(
            jnp.concatenate(
                [
                    jnp.where(wet, piece[:, c * lanes : (c + 1) * lanes], 0.0)
                    for c in range(channels // lanes)
                ],
                axis=1,
            )
        )
    return jnp.concatenate(parts, axis=0)


def mask_rows_body(counts_ref, grad_ref, rows_ref):
    def step(i, carry):
        at = pl.ds(pl.multiple_of(i * side, side), side)
        rows_ref[at, :] = masked_row(i, grad_ref[at, :], counts_ref).astype(bf16)
        return carry

    lax.fori_loop(0, side, step, 0, unroll=side)


def mask_rows(counts, grad):
    total, channels = grad.shape
    return pl.pallas_call(
        mask_rows_body,
        out_shape=jax.ShapeDtypeStruct((total, channels), bf16),
        in_specs=[pl.BlockSpec(memory_space=pltpu.SMEM), whole],
        out_specs=whole,
        compiler_params=params(8),
        cost_estimate=cost(0.9),
        name="mask_rows",
    )(counts, grad)


def arrange_body(expand_ref, reduce_ref, bias_ref, expand_out, reduce_out, turned_out, bias_out):
    channels = expand_ref.shape[1]
    new = lax.broadcasted_iota(jnp.int32, (96, 96), 0)
    old = lax.broadcasted_iota(jnp.int32, (96, 96), 1)
    lo, rest = new // 48, new % 48
    pick = old == (rest // 6) * 12 + lo * 6 + rest % 6
    chosen = pick.astype(f32).astype(bf16)
    for hi, y, core in itertools.product(range(2), range(4), range(2)):
        unit = (hi * 4 + y) * 2 + core
        at = slice(unit * 96, (unit + 1) * 96)
        both = jnp.concatenate([expand_ref[at, :], reduce_ref[at, :]], axis=1)
        moved = jnp.dot(chosen, both, preferred_element_type=f32).astype(bf16)
        column = jnp.sum(jnp.where(pick, bias_ref[:, at], 0.0), axis=1, keepdims=True)
        column = jnp.broadcast_to(column, (96, lanes))
        for lo_place in range(2):
            x = 2 * hi + lo_place
            place = core * 16 + (y * 4 + x if core == 0 else x * 4 + y)
            to = slice(place * 48, (place + 1) * 48)
            half = slice(lo_place * 48, (lo_place + 1) * 48)
            expand_out[to, :] = moved[half, :channels]
            reduce_out[to, :] = moved[half, channels:]
            bias_out[to, :] = column[half]
    turn(expand_out, turned_out)


def arrange(expand, reduce, bias):
    units, channels = expand.shape
    shape = jax.ShapeDtypeStruct((units, channels), bf16)
    return pl.pallas_call(
        arrange_body,
        out_shape=(
            shape,
            shape,
            jax.ShapeDtypeStruct((channels, units), bf16),
            jax.ShapeDtypeStruct((units, lanes), f32),
        ),
        in_specs=[whole] * 3,
        out_specs=[whole] * 4,
        compiler_params=params(12),
        cost_estimate=cost(1.5),
        name="arrange",
    )(expand, reduce, bias)


tail_slope = 0.3275911 * 0.7071067811865476
tail_terms = [
    0.5 * a for a in (0.254829592, -0.284496736, 1.421413741, -1.453152027, 1.061405429)
]
exp_scale = -0.5 * 1.4426950408889634


def gelu_pair(v):
    d = 1.0 + tail_slope * jnp.abs(v)
    t = pltpu.reciprocal(d, approx=True)
    poly = tail_terms[4]
    for a in reversed(tail_terms[:4]):
        poly = poly * t + a
    bell = jnp.exp2(v * v * exp_scale)
    tail = poly * t * bell
    below = jnp.where(v >= 0.0, 1.0 - tail, tail)
    return v * below, below + v * bell * inv_root_two_pi


def own_place():
    lat, lon = lax.axis_index("lat"), lax.axis_index("lon")
    x = 2 * lax.axis_index("dp") + (lon & 1)
    return lat & 1, x, lat >> 1, lon >> 1


def phase_place(second):
    core, x, y, _ = own_place()
    along_y = core == (1 if second else 0)
    return jnp.where(along_y, y, x)


def dot_rows(left, right):
    return lax.dot_general(left, right, (((1,), (1,)), ((), ())), preferred_element_type=f32)


class HiddenBlock:

    def __init__(self, cells, sources, rows, grad_pre_ref, places, scratch):
        self.normed, self.grad, self.expand, self.reduce, self.bias = cells
        self.sources, self.rows, self.places = sources, rows, places
        self.grad_pre = grad_pre_ref
        self.preact, self.grad_hidden, self.hidden, self.terms = scratch
        self.total = self.normed.shape[0]

    def gather(self, ref):
        return jnp.concatenate([ref[pl.ds(s, self.rows), :] for s in self.sources], axis=0)

    def dots(self, at):
        self.preact[:, at] = dot_rows(self.gather(self.expand), self.normed[at, :])
        self.grad_hidden[:, at] = dot_rows(self.gather(self.reduce), self.grad[at, :])

    def activate(self, at):
        bias = jnp.concatenate([self.gather(self.bias)] * ((at.stop - at.start) // lanes), axis=1)
        value, slope = gelu_pair(self.preact[:, at] + bias)
        self.hidden[:, at] = value.astype(bf16)
        grad_pre = (self.grad_hidden[:, at] * slope).astype(bf16)
        self.terms[:, at] = grad_pre
        for n, place in enumerate(self.places):
            self.grad_pre[pl.ds(place, self.rows), at] = grad_pre[n * self.rows : (n + 1) * self.rows]

    def expand_sum(self):
        return jnp.dot(self.terms[...], self.normed[...], preferred_element_type=f32)

    def reduce_sum(self):
        return jnp.dot(self.hidden[...], self.grad[...], preferred_element_type=f32)


def hidden_scratch(rows, total):
    return [
        pltpu.VMEM((rows, total), f32),
        pltpu.VMEM((rows, total), f32),
        pltpu.VMEM((rows, total), bf16),
        pltpu.VMEM((rows, total), bf16),
    ]


def far_body(*refs):
    cells, (sent_ref, grad_pre_ref), scratch = refs[:5], refs[5:7], refs[7:]
    half, total = grad_pre_ref.shape
    channels = refs[0].shape[1]
    base = (1 - own_place()[0]) * half
    rows = half // 2
    blocks = [
        HiddenBlock(
            cells, [pl.multiple_of(base + b * rows, rows)], rows, grad_pre_ref, [b * rows],
            scratch[4 * b : 4 * b + 4],
        )
        for b in range(2)
    ]
    first, second = blocks
    pieces = [slice(c, c + 256) for c in range(0, total, 256)]
    for at in pieces:
        first.dots(at)
    for at in pieces:
        first.activate(at)
        second.dots(at)
    second.activate(pieces[0])
    sent_ref[:rows, :channels] = first.expand_sum().astype(bf16)
    second.activate(pieces[1])
    sent_ref[:rows, channels:] = first.reduce_sum().astype(bf16)
    for at in pieces[2:]:
        second.activate(at)
    sent_ref[rows:, :channels] = second.expand_sum().astype(bf16)
    sent_ref[rows:, channels:] = second.reduce_sum().astype(bf16)


def hidden_far(*cells):
    total, channels = cells[0].shape
    half = cells[2].shape[0] // 2
    return pl.pallas_call(
        far_body,
        out_shape=(
            jax.ShapeDtypeStruct((half, 2 * channels), bf16),
            jax.ShapeDtypeStruct((half, total), bf16),
        ),
        in_specs=[whole] * 5,
        out_specs=[whole] * 2,
        scratch_shapes=hidden_scratch(half // 2, total) * 2,
        compiler_params=params(20),
        cost_estimate=cost(5.0),
        name="hidden_far",
    )(*cells)


def near_first_body(*refs):
    cells, (sums_ref, grad_pre_ref), scratch = refs[:5], refs[5:7], refs[7:]
    half = grad_pre_ref.shape[0]
    channels = refs[0].shape[1]
    size = half // 4
    core, place = own_place()[0], phase_place(False)
    chunks = [pl.multiple_of(lax.rem(place + step, 4) * size, size) for step in (1, 2)]
    sources = [pl.multiple_of(core * half + chunk, size) for chunk in chunks]
    block = HiddenBlock(cells, sources, size, grad_pre_ref, chunks, scratch)
    block.dots(slice(0, block.total))
    block.activate(slice(0, block.total))
    sums_ref[:, :channels] = block.expand_sum()
    sums_ref[:, channels:] = block.reduce_sum()


def near_first(*cells):
    total, channels = cells[0].shape
    half = cells[2].shape[0] // 2
    return pl.pallas_call(
        near_first_body,
        out_shape=(
            jax.ShapeDtypeStruct((half // 2, 2 * channels), f32),
            jax.ShapeDtypeStruct((half, total), bf16),
        ),
        in_specs=[whole] * 5,
        out_specs=[whole] * 2,
        scratch_shapes=hidden_scratch(half // 2, total),
        compiler_params=params(16),
        cost_estimate=cost(3.0),
        name="near_first",
    )(*cells)


def near_sends_body(sums_ref, arrived_ref, *sent_refs):
    size = sent_refs[0].shape[0]
    place = phase_place(False)
    for n, step in enumerate((1, 2)):
        chunk = pl.multiple_of(lax.rem(place + step, 4) * size, size)
        total = sums_ref[n * size : (n + 1) * size] + arrived_ref[pl.ds(chunk, size), :].astype(f32)
        sent_refs[n][...] = total.astype(bf16)


def near_sends(sums, arrived):
    size, width = sums.shape[0] // 2, sums.shape[1]
    sent = jax.ShapeDtypeStruct((size, width), bf16)
    return pl.pallas_call(
        near_sends_body,
        out_shape=(sent, sent),
        in_specs=[whole] * 2,
        out_specs=[whole] * 2,
        compiler_params=params(6),
        cost_estimate=cost(0.3),
        name="near_sends",
    )(sums, arrived)


def near_last_body(*refs):
    cells, (arrived_ref, _, own_ref, sent_ref, grad_pre_ref) = refs[:5], refs[5:10]
    half = grad_pre_ref.shape[0]
    channels = refs[0].shape[1]
    size = half // 4
    core, place = own_place()[0], phase_place(False)
    chunks = [pl.multiple_of(lax.rem(place + step, 4) * size, size) for step in (3, 0)]
    sources = [pl.multiple_of(core * half + chunk, size) for chunk in chunks]
    block = HiddenBlock(cells, sources, size, grad_pre_ref, chunks, refs[10:])
    block.dots(slice(0, block.total))
    block.activate(slice(0, block.total))
    expand, reduce = block.expand_sum(), block.reduce_sum()
    for n, (chunk, ref) in enumerate(zip(chunks, (sent_ref, own_ref))):
        at = slice(n * size, (n + 1) * size)
        other = arrived_ref[pl.ds(chunk, size), :].astype(f32)
        ref[:, :channels] = (expand[at] + other[:, :channels]).astype(ref.dtype)
        ref[:, channels:] = (reduce[at] + other[:, channels:]).astype(ref.dtype)


def near_last(*inputs):
    cells, grad_pre = inputs[:5], inputs[6]
    channels = cells[0].shape[1]
    size = cells[2].shape[0] // 8
    return pl.pallas_call(
        near_last_body,
        out_shape=(
            jax.ShapeDtypeStruct((size, 2 * channels), f32),
            jax.ShapeDtypeStruct((size, 2 * channels), bf16),
            jax.ShapeDtypeStruct(grad_pre.shape, bf16),
        ),
        in_specs=[whole] * 7,
        out_specs=[whole] * 3,
        input_output_aliases={6: 2},
        scratch_shapes=hidden_scratch(2 * size, cells[0].shape[0]),
        compiler_params=params(16),
        cost_estimate=cost(3.0),
        name="near_last",
    )(*inputs)


def norm_back_body(
    turned_ref, other_ref, mine_ref, unit_ref, spread_ref, gain_ref,
    conv_grad_ref, first_ref, last_ref,
):
    total, channels = unit_ref.shape
    half = turned_ref.shape[1] // 2
    core = own_place()[0]
    block = 256
    share = 1.0 / channels
    mine_weight = turned_ref[:, pl.ds(pl.multiple_of(core * half, half), half)]
    other_weight = turned_ref[:, pl.ds(pl.multiple_of((1 - core) * half, half), half)]
    for b in range(total // block):
        at = slice(b * block, (b + 1) * block)
        summed = jnp.dot(mine_weight, mine_ref[:, at], preferred_element_type=f32)
        summed = summed + jnp.dot(other_weight, other_ref[:, at], preferred_element_type=f32)
        grad_normed = summed.astype(bf16).T.astype(f32)
        unit = unit_ref[at, :]
        grad_unit = grad_normed * gain_ref[...]
        mean_grad = jnp.sum(grad_unit, axis=1, keepdims=True) * share
        mean_cross = jnp.sum(grad_unit * unit, axis=1, keepdims=True) * share
        spread = jnp.concatenate([spread_ref[at, :]] * (channels // lanes), axis=1)
        value = (grad_unit - mean_grad - unit * mean_cross) * spread
        conv_grad_ref[b * 8 : (b + 1) * 8] = value.reshape(block // side, side, channels)
    for j in range(reach):
        first_ref[j] = conv_grad_ref[:, j, :].astype(bf16)
        last_ref[j] = conv_grad_ref[:, side - reach + j, :].astype(bf16)


def norm_back(turned, other, mine, unit, spread, gain):
    total, channels = unit.shape
    shape = jax.ShapeDtypeStruct((reach, side, channels), bf16)
    found, first, last = pl.pallas_call(
        norm_back_body,
        out_shape=(jax.ShapeDtypeStruct((side, side, channels), f32), shape, shape),
        in_specs=[whole] * 6,
        out_specs=[whole] * 3,
        compiler_params=params(14),
        cost_estimate=cost(0.2),
        name="norm_back",
    )(turned, other, mine, unit, spread, gain)
    return found.reshape(total, channels), first, last


def finish_inner_body(
    counts_ref, conv0_ref, conv1_ref, conv2_ref, kernel_ref, left_ref, right_ref, grad_ref,
    out_ref, cols_sum, done, sems,
):
    conv_refs = (conv0_ref, conv1_ref, conv2_ref)
    add_cols(True, kernel_ref, left_ref, right_ref, cols_sum)
    bounds = [reach, 9, 16, 23, side - reach]
    copies = []
    for n, (low, high) in enumerate(zip(bounds[:-1], bounds[1:])):
        for i in range(low, high):
            at = slice(i * side, (i + 1) * side)
            value = edged_row(i, conv_rows(conv_refs, at), cols_sum)
            done[at, :] = value + masked_row(i, grad_ref[at, :], counts_ref)
        part = pl.ds(low * side, (high - low) * side)
        copies.append(pltpu.make_async_copy(done.at[part, :], out_ref.at[part, :], sems.at[n]))
        copies[-1].start()
    for copy in copies:
        copy.wait()


def finish_inner(counts, conv, kernel, left, right, grad):
    total, channels = grad.shape
    return pl.pallas_call(
        finish_inner_body,
        out_shape=(
            jax.ShapeDtypeStruct((total, channels), f32),
            jax.ShapeDtypeStruct((2 * reach, side, channels), f32),
        ),
        in_specs=[pl.BlockSpec(memory_space=pltpu.SMEM)] + [whole] * 7,
        out_specs=[pl.BlockSpec(memory_space=pltpu.HBM), whole],
        scratch_shapes=[pltpu.VMEM((total, channels), f32), pltpu.SemaphoreType.DMA((4,))],
        compiler_params=params(12),
        cost_estimate=cost(2.2),
        name="finish_inner",
    )(counts, *conv, kernel, left, right, grad)


def finish_outer_body(
    counts_ref, conv0_ref, conv1_ref, conv2_ref, kernel_ref, top_ref, bottom_ref, cols_ref,
    grad_ref, _, out_ref, rows_sum, done, sems,
):
    conv_refs = (conv0_ref, conv1_ref, conv2_ref)
    add_rows(True, kernel_ref, top_ref, bottom_ref, rows_sum)
    copies = []
    for n, start in enumerate((0, side - reach)):
        for r in range(reach):
            i = start + r
            at = slice(i * side, (i + 1) * side)
            value = edged_row(i, conv_rows(conv_refs, at), cols_ref) + rows_sum[n * reach + r]
            done[n, r * side : (r + 1) * side, :] = value + masked_row(i, grad_ref[at, :], counts_ref)
        part = pl.ds(start * side, reach * side)
        copies.append(pltpu.make_async_copy(done.at[n], out_ref.at[part, :], sems.at[n]))
        copies[-1].start()
    for copy in copies:
        copy.wait()


def finish_outer(counts, conv, kernel, top, bottom, cols_sum, grad, inner):
    channels = grad.shape[1]
    return pl.pallas_call(
        finish_outer_body,
        out_shape=jax.ShapeDtypeStruct(inner.shape, f32),
        in_specs=[pl.BlockSpec(memory_space=pltpu.SMEM)]
        + [whole] * 8
        + [pl.BlockSpec(memory_space=pltpu.HBM)],
        out_specs=pl.BlockSpec(memory_space=pltpu.HBM),
        input_output_aliases={9: 0},
        scratch_shapes=[
            pltpu.VMEM((2 * reach, side, channels), f32),
            pltpu.VMEM((2, reach * side, channels), f32),
            pltpu.SemaphoreType.DMA((2,)),
        ],
        compiler_params=params(12),
        cost_estimate=cost(1.0),
        name="finish_outer",
    )(counts, *conv, kernel, top, bottom, cols_sum, grad, inner)


def split_four_body(own_ref, first_ref, second_ref, third_ref, kept_ref, *sent_refs):
    size = kept_ref.shape[0]
    place = phase_place(True)
    for step in range(4):
        at = pl.ds(pl.multiple_of(lax.rem(place + step, 4) * size, size), size)
        total = own_ref[at, :]
        for ref in (first_ref, second_ref, third_ref):
            total = total + ref[at, :].astype(f32)
        if step == 0:
            kept_ref[...] = total
        else:
            sent_refs[step - 1][...] = total.astype(bf16)


def split_four(own, parts):
    size, width = own.shape[0] // 4, own.shape[1]
    sent = jax.ShapeDtypeStruct((size, width), bf16)
    return pl.pallas_call(
        split_four_body,
        out_shape=(jax.ShapeDtypeStruct((size, width), f32), sent, sent, sent),
        in_specs=[whole] * 4,
        out_specs=[whole] * 4,
        compiler_params=params(4),
        cost_estimate=cost(0.3),
        name="split_four",
    )(own, *parts)


def split_two_body(own_ref, *refs):
    part_refs, (kept_ref, sent_ref) = refs[:-2], refs[-2:]
    size = kept_ref.shape[0]
    total = own_ref[...]
    for ref in part_refs:
        total = total + ref[...].astype(f32)
    low, high = total[:size], total[size:]
    upper = (own_place()[3] & 1) != 0
    kept_ref[...] = jnp.where(upper, high, low)
    sent_ref[...] = jnp.where(upper, low, high)


def split_two(own, parts):
    shape = jax.ShapeDtypeStruct((own.shape[0] // 2, own.shape[1]), f32)
    return pl.pallas_call(
        split_two_body,
        out_shape=(shape, shape),
        in_specs=[whole] * (1 + len(parts)),
        out_specs=[whole] * 2,
        compiler_params=params(4),
        cost_estimate=cost(0.2),
        name="split_two",
    )(own, *parts)


def split_ring_body(own_ref, first_ref, second_ref, third_ref, kept_ref, following_ref, *sent_refs):
    size = kept_ref.shape[0]
    total = own_ref[...]
    for ref in (first_ref, second_ref, third_ref):
        total = total + ref[...].astype(f32)
    chunks = [total[c * size : (c + 1) * size] for c in range(4)]
    place = own_place()[3] >> 1
    for step, ref in enumerate((kept_ref, following_ref, *sent_refs)):
        wanted = (place + step) & 3
        found = chunks[0]
        for c in range(1, 4):
            found = jnp.where(wanted == c, chunks[c], found)
        ref[...] = found.astype(ref.dtype)


def split_ring(own, parts):
    size, width = own.shape[0] // 4, own.shape[1]
    kept = jax.ShapeDtypeStruct((size, width), f32)
    sent = jax.ShapeDtypeStruct((size, width), bf16)
    return pl.pallas_call(
        split_ring_body,
        out_shape=(kept, kept, sent, sent),
        in_specs=[whole] * 4,
        out_specs=[whole] * 4,
        compiler_params=params(4),
        cost_estimate=cost(0.2),
        name="split_ring",
    )(own, *parts)


def relay_body(own_ref, passed_ref, sent_ref):
    sent_ref[...] = (own_ref[...] + passed_ref[...].astype(f32)).astype(bf16)


def relay(own, passed):
    return pl.pallas_call(
        relay_body,
        out_shape=jax.ShapeDtypeStruct(own.shape, bf16),
        in_specs=[whole] * 2,
        out_specs=whole,
        compiler_params=params(4),
        cost_estimate=cost(0.1),
        name="relay",
    )(own, passed)


def last_sum_body(scale, own_ref, arrived_ref, expand_ref, reduce_ref):
    channels = expand_ref.shape[2]
    total = (own_ref[...] + arrived_ref[...]) * scale
    for r in range(total.shape[0]):
        expand_ref[r] = total[r : r + 1, :channels]
        reduce_ref[r] = total[r : r + 1, channels:]


def last_sum(own, arrived, scale):
    size, width = own.shape
    shape = jax.ShapeDtypeStruct((size, 1, width // 2), f32)
    expand, reduce = pl.pallas_call(
        functools.partial(last_sum_body, scale),
        out_shape=(shape, shape),
        in_specs=[whole] * 2,
        out_specs=[whole] * 2,
        compiler_params=params(4),
        cost_estimate=cost(0.4),
        name="last_sum",
    )(own, arrived)
    return expand.transpose(1, 0, 2), reduce.transpose(1, 0, 2)


every_axis = ("dp", "lat", "lon")


def device_pairs(move):
    def flat(hi, y, core, z, lo):
        return (hi * 8 + y * 2 + core) * 16 + z * 2 + lo

    found = []
    for hi, y, core, z, lo in itertools.product(range(2), range(4), range(2), range(8), range(2)):
        found.append((flat(hi, y, core, z, lo), flat(*move(hi, y, core, z, lo))))
    return found


def plane_pairs(step, first):
    def move(hi, y, core, z, lo):
        if (core == 0) == first:
            return (hi, (y + step) % 4, core, z, lo)
        x = (2 * hi + lo + step) % 4
        return (x // 2, y, core, z, x % 2)

    return device_pairs(move)


def ring_pairs(step):
    return device_pairs(lambda hi, y, core, z, lo: (hi, y, core, (z + 2 * step) % 8, lo))


def last_pairs():
    return device_pairs(lambda hi, y, core, z, lo: (hi, y, core, z ^ 1, lo))


def shifted(axis, step):
    count = lax.axis_size(axis)
    return [(i, (i + step) % count) for i in range(count)]


def lon_halo(first, last):
    left = lax.ppermute(last, "lon", shifted("lon", 1))
    right = lax.ppermute(first, "lon", shifted("lon", -1))
    return left, right


def lat_halo(up, down):
    top = lax.ppermute(down, "lat", shifted("lat", 1))
    bottom = lax.ppermute(up, "lat", shifted("lat", -1))
    return top, bottom


def after(value, *others):
    return lax.optimization_barrier((value, others))[0]


def local(
    state, cotangent, counts, dw_kernel, dw_bias, norm_gain, norm_bias, w_expand, b_expand, w_reduce
):
    channels = state.shape[-1]
    cells = state.reshape(-1, channels)
    grad = cotangent.reshape(-1, channels)
    total = cells.shape[0]
    kernel = dw_kernel.transpose(1, 0, 2)

    first, last = side_cols(cells)
    left, right = lon_halo(first, last)
    conv = inner_conv(cells, kernel, (0,))
    grad, w_expand, w_reduce = after((grad, w_expand, w_reduce), first, last)
    rows = mask_rows(counts, grad)
    expand, reduce, expand_t, bias = arrange(w_expand[0], w_reduce[0], b_expand)
    left, right = after((left, right), rows, bias, conv)
    up, down = side_rows(cells, left, right)
    top, bottom = lat_halo(up, down)
    conv += inner_conv(after(cells, up, down), kernel, (1, 2))
    unit, spread, normed = normalise(
        conv, kernel, left, right, top, bottom, dw_bias, norm_gain, norm_bias
    )

    inputs = (normed, rows, expand, reduce, bias)
    sent, far_pre = hidden_far(*inputs)
    arrived = lax.ppermute(sent, "lat", [(i, i ^ 1) for i in range(8)])
    sums, near_pre = near_first(*inputs)
    one, two = near_sends(sums, arrived)
    part_one = lax.ppermute(one, every_axis, plane_pairs(1, True))
    part_two = lax.ppermute(two, every_axis, plane_pairs(2, True))
    own, three, near_pre = near_last(*inputs, arrived, after(near_pre, one, two))
    part_three = lax.ppermute(three, every_axis, plane_pairs(3, True))

    far_pre, part_one = after((far_pre, part_one), three)
    conv_grad, first, last = norm_back(expand_t, far_pre, near_pre, unit, spread, norm_gain)
    last, part_two = after((last, part_two))
    left, right = lon_halo(first, last)
    own, parts = after((own, (part_one, part_two, part_three)), first, last)
    own, *sent = split_four(own, parts)
    parts = [lax.ppermute(sent[i], every_axis, plane_pairs(i + 1, False)) for i in (1, 0, 2)]
    back = back_conv(after(conv_grad, sent), kernel, (0, 1))
    (conv_grad, left, right), parts = after(((conv_grad, left, right), parts), back)
    up, down = side_rows(conv_grad, left, right)

    own, following, two, three = split_ring(*after((own, parts), up, down))
    passed = lax.ppermute(two, every_axis, ring_pairs(1))
    part_before = lax.ppermute(three, every_axis, ring_pairs(3))
    top, bottom = lat_halo(up, down)
    back += back_conv(after(conv_grad, two, three, top, bottom), kernel, (2,))
    passed, part_before = after((passed, part_before), back)
    one = relay(following, passed)
    part_after = lax.ppermute(one, every_axis, ring_pairs(1))
    parts = [part_before, part_after]
    inner, cols_sum = finish_inner(counts, back, kernel, left, right, after(grad, one))

    own, sent = split_two(*after((own, parts), inner))
    arrived = lax.ppermute(sent, every_axis, last_pairs())
    inner = after(inner, sent)
    gradient = finish_outer(counts, back, kernel, top, bottom, cols_sum, grad, inner)

    cells_all = lax.axis_size("dp") * lax.axis_size("lat") * lax.axis_size("lon") * total
    kept = last_sum(own, arrived, 1.0 / math.sqrt(cells_all))
    return (gradient.reshape(state.shape), *kept)


def solution(mesh):
    in_specs = (
        P("dp", "lat", "lon", None),
        P("dp", "lat", "lon", None),
        P("lat", "lon"),
        P(),
        P(),
        P(),
        P(),
        P(),
        P(),
        P(),
    )
    out_specs = (
        P("dp", "lat", "lon", None),
        P(None, ("dp", "lat", "lon"), None),
        P(None, ("dp", "lat", "lon"), None),
    )
    return jax.shard_map(local, mesh=mesh, in_specs=in_specs, out_specs=out_specs, check_vma=False)
```

```python
import functools
import itertools
import math

import jax
import jax.numpy as jnp
from jax import lax
from jax.experimental import pallas as pl
from jax.experimental.pallas import tpu as pltpu
from jax.sharding import PartitionSpec as P

norm_eps = 1e-06
inv_root_two_pi = 0.3989422804014327
side = 32
reach = 3
lanes = 128
f32 = jnp.float32
bf16 = jnp.bfloat16
whole = pl.BlockSpec(memory_space=pltpu.VMEM)


def params(mib):
    return pltpu.CompilerParams(vmem_limit_bytes=mib * 1024 * 1024)


def cost(microseconds):
    return pl.CostEstimate(
        flops=int(microseconds * 1.15e9), bytes_accessed=2**20, transcendentals=0
    )


def tap_row(kernel_ref, flipped, p, q, cols):
    index = 7 * p + q
    if flipped:
        index = 48 - index
    return kernel_ref[index, :, cols]


def shift_cols(rows, offset):
    if offset == 0:
        return rows
    count = rows.shape[0]
    turned = pltpu.roll(rows, (-offset) % count, 0)
    place = lax.broadcasted_iota(jnp.int32, (8, rows.shape[1]), 0)
    if offset > 0:
        last = jnp.where(place < 8 - offset, turned[count - 8 :], 0.0)
        return jnp.concatenate([turned[: count - 8], last], axis=0)
    first = jnp.where(place >= -offset, turned[:8], 0.0)
    return jnp.concatenate([first, turned[8:]], axis=0)


def inner_conv_body(parts, cells_ref, kernel_ref, *refs):
    outs, padded = refs[:-1], refs[-1]
    edge = reach * side
    total = side * side
    group = 4
    padded[0:edge] = jnp.zeros((edge, lanes), f32)
    padded[edge + total : 2 * edge + total] = jnp.zeros((edge, lanes), f32)
    for part, out_ref in zip(parts, outs):
        cols = slice(part * lanes, (part + 1) * lanes)
        padded[edge : edge + total] = cells_ref[:, cols]

        def some_rows(i, carry):
            base = pl.multiple_of(i * (group * side), group * side)
            rows = [padded[pl.ds(base + p * side, side), :] for p in range(6 + group)]
            results = [None] * group
            for q in range(7):
                sums = [None] * group
                for p in range(7):
                    tap = tap_row(kernel_ref, False, p, q, cols)
                    for g in range(group):
                        term = tap * rows[p + g]
                        sums[g] = term if sums[g] is None else sums[g] + term
                for g in range(group):
                    moved = shift_cols(sums[g], q - reach)
                    results[g] = moved if results[g] is None else results[g] + moved
            for g in range(group):
                out_ref[pl.ds(base + g * side, side), :] = results[g]
            return carry

        lax.fori_loop(0, side // group, some_rows, 0)


def inner_conv(cells, kernel, parts):
    total = cells.shape[0]
    shape = jax.ShapeDtypeStruct((total, lanes), f32)
    return pl.pallas_call(
        functools.partial(inner_conv_body, parts),
        out_shape=(shape,) * len(parts),
        in_specs=[whole] * 2,
        out_specs=[whole] * len(parts),
        scratch_shapes=[pltpu.VMEM((total + 2 * reach * side, lanes), f32)],
        compiler_params=params(6),
        cost_estimate=cost(2.2 * len(parts)),
        name="inner_conv",
    )(cells, kernel)


def back_conv_body(parts, cells_ref, kernel_ref, *refs):
    outs, (padded, taps) = refs[:-2], refs[-2:]
    edge = reach * side
    total = side * side
    group = 4
    padded[0:edge] = jnp.zeros((edge, lanes), bf16)
    padded[edge + total : 2 * edge + total] = jnp.zeros((edge, lanes), bf16)
    for part, out_ref in zip(parts, outs):
        cols = slice(part * lanes, (part + 1) * lanes)
        padded[edge : edge + total] = cells_ref[:, cols].astype(bf16)
        for p, q in itertools.product(range(7), range(7)):
            tap = jnp.broadcast_to(tap_row(kernel_ref, True, p, q, cols), (16, lanes))
            taps[7 * p + q] = tap.astype(bf16)

        def some_rows(i, carry):
            base = pl.multiple_of(i * (group * side), group * side)
            rows = [padded[pl.ds(base + p * side, side), :] for p in range(6 + group)]
            results = [None] * group
            for q in range(7):
                sums = [None] * group
                for p in range(7):
                    tap = jnp.concatenate([taps[7 * p + q]] * (side // 16), axis=0)
                    for g in range(group):
                        term = tap * rows[p + g]
                        sums[g] = term if sums[g] is None else sums[g] + term
                for g in range(group):
                    moved = shift_cols(sums[g].astype(f32), q - reach)
                    results[g] = moved if results[g] is None else results[g] + moved
            for g in range(group):
                out_ref[pl.ds(base + g * side, side), :] = results[g]
            return carry

        lax.fori_loop(0, side // group, some_rows, 0)


def back_conv(cells, kernel, parts):
    total = cells.shape[0]
    shape = jax.ShapeDtypeStruct((total, lanes), f32)
    return pl.pallas_call(
        functools.partial(back_conv_body, parts),
        out_shape=(shape,) * len(parts),
        in_specs=[whole] * 2,
        out_specs=[whole] * len(parts),
        scratch_shapes=[
            pltpu.VMEM((total + 2 * reach * side, lanes), bf16),
            pltpu.VMEM((49, 16, lanes), bf16),
        ],
        compiler_params=params(6),
        cost_estimate=cost(1.5 * len(parts)),
        name="back_conv",
    )(cells, kernel)


def side_cols_body(cells_ref, first_ref, last_ref):
    for j in range(reach):
        first_ref[j] = cells_ref[:, j, :].astype(bf16)
        last_ref[j] = cells_ref[:, side - reach + j, :].astype(bf16)


def side_cols(cells):
    channels = cells.shape[1]
    shape = jax.ShapeDtypeStruct((reach, side, channels), bf16)
    return pl.pallas_call(
        side_cols_body,
        out_shape=(shape, shape),
        in_specs=[whole],
        out_specs=[whole] * 2,
        compiler_params=params(4),
        cost_estimate=cost(0.3),
        name="side_cols",
    )(cells.reshape(side, side, channels))


def side_rows_body(cells_ref, left_ref, right_ref, up_ref, down_ref):
    channels = cells_ref.shape[1]
    place = lax.broadcasted_iota(jnp.int32, (8, channels), 0)
    blank = jnp.zeros((8, channels), f32)
    left = [left_ref[h].astype(f32) for h in range(reach)]
    right = [right_ref[h].astype(f32) for h in range(reach)]
    for r in range(reach):
        for row, ref in ((r, up_ref), (side - reach + r, down_ref)):
            corner = blank
            for h in range(reach):
                corner = jnp.where(place == h, right[h][row : row + 1], corner)
                corner = jnp.where(place == 8 - reach + h, left[h][row : row + 1], corner)
            body = cells_ref[row * side : (row + 1) * side]
            ref[r] = jnp.concatenate([body, corner, blank], axis=0).astype(bf16)


def side_rows(cells, left, right):
    channels = cells.shape[1]
    shape = jax.ShapeDtypeStruct((reach, side + 16, channels), bf16)
    return pl.pallas_call(
        side_rows_body,
        out_shape=(shape, shape),
        in_specs=[whole] * 3,
        out_specs=[whole] * 2,
        compiler_params=params(6),
        cost_estimate=cost(0.5),
        name="side_rows",
    )(cells, left, right)


def beyond_steps(low, r):
    if low:
        return [(h, h - r) for h in range(r, reach)]
    return [(h, 6 + h - r) for h in range(0, r + 1)]


def add_rows(flipped, kernel_ref, top_ref, bottom_ref, rows_sum):
    lat = lax.axis_index("lat")
    channels = kernel_ref.shape[2]
    for c in range(channels // lanes):
        cols = slice(c * lanes, (c + 1) * lanes)
        for low, ref in ((True, top_ref), (False, bottom_ref)):
            outside = lat == (0 if low else lax.axis_size("lat") - 1)
            beyond = [
                jnp.where(outside, 0.0, ref[h, :, cols].astype(f32)[: side + 8]) for h in range(reach)
            ]
            for r in range(reach):
                result = None
                for q in range(7):
                    summed = None
                    for h, p in beyond_steps(low, r):
                        term = tap_row(kernel_ref, flipped, p, q, cols) * beyond[h]
                        summed = term if summed is None else summed + term
                    summed = pltpu.roll(summed, (reach - q) % (side + 8), 0) if q != reach else summed
                    result = summed if result is None else result + summed
                rows_sum[r if low else reach + r, :, cols] = result[:side]


def add_cols(flipped, kernel_ref, left_ref, right_ref, cols_sum):
    channels = kernel_ref.shape[2]
    for c in range(channels // lanes):
        cols = slice(c * lanes, (c + 1) * lanes)
        for low, ref in ((True, left_ref), (False, right_ref)):
            beyond = [ref[h, :, cols].astype(f32) for h in range(reach)]
            for r in range(reach):
                result = None
                for p in range(7):
                    summed = None
                    for h, q in beyond_steps(low, r):
                        term = tap_row(kernel_ref, flipped, p, q, cols) * beyond[h]
                        summed = term if summed is None else summed + term
                    summed = shift_cols(summed, p - reach)
                    result = summed if result is None else result + summed
                cols_sum[r if low else reach + r, :, cols] = result


def edged_row(i, conv_row, cols_sum):
    channels = conv_row.shape[1]
    place = lax.broadcasted_iota(jnp.int32, (8, channels), 0)
    first, last = conv_row[:8], conv_row[side - 8 :]
    for r in range(reach):
        first = first + jnp.where(place == r, cols_sum[r, pl.ds(i, 1), :], 0.0)
        last = last + jnp.where(place == 8 - reach + r, cols_sum[reach + r, pl.ds(i, 1), :], 0.0)
    return jnp.concatenate([first, conv_row[8 : side - 8], last], axis=0)


def each_row(step):
    def low(i, carry):
        step(i, i)
        return carry

    def middle(i, carry):
        step(i, None)
        return carry

    def high(i, carry):
        step(i, i - (side - 2 * reach))
        return carry

    lax.fori_loop(0, reach, low, 0, unroll=reach)
    lax.fori_loop(reach, side - reach, middle, 0, unroll=side // 2 - reach)
    lax.fori_loop(side - reach, side, high, 0, unroll=reach)


def conv_rows(refs, at):
    return jnp.concatenate([ref[at, :] for ref in refs], axis=1)


def normalise_body(
    conv0_ref, conv1_ref, conv2_ref, kernel_ref, left_ref, right_ref, top_ref, bottom_ref, bias_ref, gain_ref, shift_ref,
    unit_ref, spread_ref, normed_ref, rows_sum, cols_sum,
):
    channels = kernel_ref.shape[2]
    conv_refs = (conv0_ref, conv1_ref, conv2_ref)
    add_rows(False, kernel_ref, top_ref, bottom_ref, rows_sum)
    add_cols(False, kernel_ref, left_ref, right_ref, cols_sum)
    share = 1.0 / channels

    def step(i, outer):
        at = pl.ds(pl.multiple_of(i * side, side), side)
        value = edged_row(i, conv_rows(conv_refs, at), cols_sum)
        if outer is not None:
            value = value + rows_sum[outer]
        value = value + bias_ref[...]
        mean = jnp.sum(value, axis=1, keepdims=True) * share
        centred = value - mean
        spread = lax.rsqrt(jnp.sum(centred * centred, axis=1, keepdims=True) * share + norm_eps)
        unit = centred * spread
        unit_ref[at, :] = unit
        spread_ref[at, :] = jnp.broadcast_to(spread, (side, lanes))
        normed_ref[at, :] = (unit * gain_ref[...] + shift_ref[...]).astype(bf16)

    each_row(step)


def turn(source_ref, target_ref):
    for b in range(source_ref.shape[0] // 256):
        at = slice(b * 256, (b + 1) * 256)
        target_ref[:, at] = source_ref[at, :].T


def normalise(conv, kernel, left, right, top, bottom, bias, gain, shift):
    total, channels = conv[0].shape[0], kernel.shape[2]
    return pl.pallas_call(
        normalise_body,
        out_shape=(
            jax.ShapeDtypeStruct((total, channels), f32),
            jax.ShapeDtypeStruct((total, lanes), f32),
            jax.ShapeDtypeStruct((total, channels), bf16),
        ),
        in_specs=[whole] * 11,
        out_specs=[whole] * 3,
        scratch_shapes=[pltpu.VMEM((2 * reach, side, channels), f32)] * 2,
        compiler_params=params(12),
        cost_estimate=cost(2.8),
        name="normalise",
    )(*conv, kernel, left, right, top, bottom, bias, gain, shift)


def wet_row(i, counts_ref):
    place = lax.broadcasted_iota(jnp.int32, (8, lanes), 0) + (i % 8) * 8
    pieces = []
    for t in range(side // 8):
        pieces.append(place < counts_ref[i // 8, t])
    return pieces


def masked_row(i, grad_row, counts_ref):
    channels = grad_row.shape[1]
    parts = []
    for t, wet in enumerate(wet_row(i, counts_ref)):
        piece = grad_row[t * 8 : (t + 1) * 8]
        parts.append(
            jnp.concatenate(
                [
                    jnp.where(wet, piece[:, c * lanes : (c + 1) * lanes], 0.0)
                    for c in range(channels // lanes)
                ],
                axis=1,
            )
        )
    return jnp.concatenate(parts, axis=0)


def mask_rows_body(counts_ref, grad_ref, rows_ref):
    def step(i, carry):
        at = pl.ds(pl.multiple_of(i * side, side), side)
        rows_ref[at, :] = masked_row(i, grad_ref[at, :], counts_ref).astype(bf16)
        return carry

    lax.fori_loop(0, side, step, 0, unroll=side)


def mask_rows(counts, grad):
    total, channels = grad.shape
    return pl.pallas_call(
        mask_rows_body,
        out_shape=jax.ShapeDtypeStruct((total, channels), bf16),
        in_specs=[pl.BlockSpec(memory_space=pltpu.SMEM), whole],
        out_specs=whole,
        compiler_params=params(8),
        cost_estimate=cost(0.9),
        name="mask_rows",
    )(counts, grad)


def arrange_body(expand_ref, reduce_ref, bias_ref, expand_out, reduce_out, turned_out, bias_out):
    channels = expand_ref.shape[1]
    new = lax.broadcasted_iota(jnp.int32, (96, 96), 0)
    old = lax.broadcasted_iota(jnp.int32, (96, 96), 1)
    lo, rest = new // 48, new % 48
    pick = old == (rest // 6) * 12 + lo * 6 + rest % 6
    chosen = pick.astype(f32).astype(bf16)
    for hi, y, core in itertools.product(range(2), range(4), range(2)):
        unit = (hi * 4 + y) * 2 + core
        at = slice(unit * 96, (unit + 1) * 96)
        both = jnp.concatenate([expand_ref[at, :], reduce_ref[at, :]], axis=1)
        moved = jnp.dot(chosen, both, preferred_element_type=f32).astype(bf16)
        column = jnp.sum(jnp.where(pick, bias_ref[:, at], 0.0), axis=1, keepdims=True)
        column = jnp.broadcast_to(column, (96, lanes))
        for lo_place in range(2):
            x = 2 * hi + lo_place
            place = core * 16 + (y * 4 + x if core == 0 else x * 4 + y)
            to = slice(place * 48, (place + 1) * 48)
            half = slice(lo_place * 48, (lo_place + 1) * 48)
            expand_out[to, :] = moved[half, :channels]
            reduce_out[to, :] = moved[half, channels:]
            bias_out[to, :] = column[half]
    turn(expand_out, turned_out)


def arrange(expand, reduce, bias):
    units, channels = expand.shape
    shape = jax.ShapeDtypeStruct((units, channels), bf16)
    return pl.pallas_call(
        arrange_body,
        out_shape=(
            shape,
            shape,
            jax.ShapeDtypeStruct((channels, units), bf16),
            jax.ShapeDtypeStruct((units, lanes), f32),
        ),
        in_specs=[whole] * 3,
        out_specs=[whole] * 4,
        compiler_params=params(12),
        cost_estimate=cost(1.5),
        name="arrange",
    )(expand, reduce, bias)


tail_slope = 0.3275911 * 0.7071067811865476
tail_terms = [
    0.5 * a for a in (0.254829592, -0.284496736, 1.421413741, -1.453152027, 1.061405429)
]
exp_scale = -0.5 * 1.4426950408889634


def gelu_pair(v):
    d = 1.0 + tail_slope * jnp.abs(v)
    t = pltpu.reciprocal(d, approx=True)
    poly = tail_terms[4]
    for a in reversed(tail_terms[:4]):
        poly = poly * t + a
    bell = jnp.exp2(v * v * exp_scale)
    tail = poly * t * bell
    below = jnp.where(v >= 0.0, 1.0 - tail, tail)
    return v * below, below + v * bell * inv_root_two_pi


def own_place():
    lat, lon = lax.axis_index("lat"), lax.axis_index("lon")
    x = 2 * lax.axis_index("dp") + (lon & 1)
    return lat & 1, x, lat >> 1, lon >> 1


def phase_place(second):
    core, x, y, _ = own_place()
    along_y = core == (1 if second else 0)
    return jnp.where(along_y, y, x)


def dot_rows(left, right):
    return lax.dot_general(left, right, (((1,), (1,)), ((), ())), preferred_element_type=f32)


class HiddenBlock:

    def __init__(self, cells, sources, rows, grad_pre_ref, places, scratch):
        self.normed, self.grad, self.expand, self.reduce, self.bias = cells
        self.sources, self.rows, self.places = sources, rows, places
        self.grad_pre = grad_pre_ref
        self.preact, self.grad_hidden, self.hidden, self.terms = scratch
        self.total = self.normed.shape[0]

    def gather(self, ref):
        return jnp.concatenate([ref[pl.ds(s, self.rows), :] for s in self.sources], axis=0)

    def dots(self, at):
        self.preact[:, at] = dot_rows(self.gather(self.expand), self.normed[at, :])
        self.grad_hidden[:, at] = dot_rows(self.gather(self.reduce), self.grad[at, :])

    def activate(self, at):
        bias = jnp.concatenate([self.gather(self.bias)] * ((at.stop - at.start) // lanes), axis=1)
        value, slope = gelu_pair(self.preact[:, at] + bias)
        self.hidden[:, at] = value.astype(bf16)
        grad_pre = (self.grad_hidden[:, at] * slope).astype(bf16)
        self.terms[:, at] = grad_pre
        for n, place in enumerate(self.places):
            self.grad_pre[pl.ds(place, self.rows), at] = grad_pre[n * self.rows : (n + 1) * self.rows]

    def expand_sum(self):
        return jnp.dot(self.terms[...], self.normed[...], preferred_element_type=f32)

    def reduce_sum(self):
        return jnp.dot(self.hidden[...], self.grad[...], preferred_element_type=f32)


def hidden_scratch(rows, total):
    return [
        pltpu.VMEM((rows, total), f32),
        pltpu.VMEM((rows, total), f32),
        pltpu.VMEM((rows, total), bf16),
        pltpu.VMEM((rows, total), bf16),
    ]


def far_body(*refs):
    cells, (sent_ref, grad_pre_ref), scratch = refs[:5], refs[5:7], refs[7:]
    half, total = grad_pre_ref.shape
    channels = refs[0].shape[1]
    base = (1 - own_place()[0]) * half
    rows = half // 2
    blocks = [
        HiddenBlock(
            cells, [pl.multiple_of(base + b * rows, rows)], rows, grad_pre_ref, [b * rows],
            scratch[4 * b : 4 * b + 4],
        )
        for b in range(2)
    ]
    first, second = blocks
    pieces = [slice(c, c + 256) for c in range(0, total, 256)]
    for at in pieces:
        first.dots(at)
    for at in pieces:
        first.activate(at)
        second.dots(at)
    second.activate(pieces[0])
    sent_ref[:rows, :channels] = first.expand_sum().astype(bf16)
    second.activate(pieces[1])
    sent_ref[:rows, channels:] = first.reduce_sum().astype(bf16)
    for at in pieces[2:]:
        second.activate(at)
    sent_ref[rows:, :channels] = second.expand_sum().astype(bf16)
    sent_ref[rows:, channels:] = second.reduce_sum().astype(bf16)


def hidden_far(*cells):
    total, channels = cells[0].shape
    half = cells[2].shape[0] // 2
    return pl.pallas_call(
        far_body,
        out_shape=(
            jax.ShapeDtypeStruct((half, 2 * channels), bf16),
            jax.ShapeDtypeStruct((half, total), bf16),
        ),
        in_specs=[whole] * 5,
        out_specs=[whole] * 2,
        scratch_shapes=hidden_scratch(half // 2, total) * 2,
        compiler_params=params(20),
        cost_estimate=cost(5.0),
        name="hidden_far",
    )(*cells)


def near_first_body(*refs):
    cells, (sums_ref, grad_pre_ref), scratch = refs[:5], refs[5:7], refs[7:]
    half = grad_pre_ref.shape[0]
    channels = refs[0].shape[1]
    size = half // 4
    core, place = own_place()[0], phase_place(False)
    chunks = [pl.multiple_of(lax.rem(place + step, 4) * size, size) for step in (1, 2)]
    sources = [pl.multiple_of(core * half + chunk, size) for chunk in chunks]
    block = HiddenBlock(cells, sources, size, grad_pre_ref, chunks, scratch)
    block.dots(slice(0, block.total))
    block.activate(slice(0, block.total))
    sums_ref[:, :channels] = block.expand_sum()
    sums_ref[:, channels:] = block.reduce_sum()


def near_first(*cells):
    total, channels = cells[0].shape
    half = cells[2].shape[0] // 2
    return pl.pallas_call(
        near_first_body,
        out_shape=(
            jax.ShapeDtypeStruct((half // 2, 2 * channels), f32),
            jax.ShapeDtypeStruct((half, total), bf16),
        ),
        in_specs=[whole] * 5,
        out_specs=[whole] * 2,
        scratch_shapes=hidden_scratch(half // 2, total),
        compiler_params=params(16),
        cost_estimate=cost(3.0),
        name="near_first",
    )(*cells)


def near_sends_body(sums_ref, arrived_ref, *sent_refs):
    size = sent_refs[0].shape[0]
    place = phase_place(False)
    for n, step in enumerate((1, 2)):
        chunk = pl.multiple_of(lax.rem(place + step, 4) * size, size)
        total = sums_ref[n * size : (n + 1) * size] + arrived_ref[pl.ds(chunk, size), :].astype(f32)
        sent_refs[n][...] = total.astype(bf16)


def near_sends(sums, arrived):
    size, width = sums.shape[0] // 2, sums.shape[1]
    sent = jax.ShapeDtypeStruct((size, width), bf16)
    return pl.pallas_call(
        near_sends_body,
        out_shape=(sent, sent),
        in_specs=[whole] * 2,
        out_specs=[whole] * 2,
        compiler_params=params(6),
        cost_estimate=cost(0.3),
        name="near_sends",
    )(sums, arrived)


def near_last_body(*refs):
    cells, (arrived_ref, _, own_ref, sent_ref, grad_pre_ref) = refs[:5], refs[5:10]
    half = grad_pre_ref.shape[0]
    channels = refs[0].shape[1]
    size = half // 4
    core, place = own_place()[0], phase_place(False)
    chunks = [pl.multiple_of(lax.rem(place + step, 4) * size, size) for step in (3, 0)]
    sources = [pl.multiple_of(core * half + chunk, size) for chunk in chunks]
    block = HiddenBlock(cells, sources, size, grad_pre_ref, chunks, refs[10:])
    block.dots(slice(0, block.total))
    block.activate(slice(0, block.total))
    expand, reduce = block.expand_sum(), block.reduce_sum()
    for n, (chunk, ref) in enumerate(zip(chunks, (sent_ref, own_ref))):
        at = slice(n * size, (n + 1) * size)
        other = arrived_ref[pl.ds(chunk, size), :].astype(f32)
        ref[:, :channels] = (expand[at] + other[:, :channels]).astype(ref.dtype)
        ref[:, channels:] = (reduce[at] + other[:, channels:]).astype(ref.dtype)


def near_last(*inputs):
    cells, grad_pre = inputs[:5], inputs[6]
    channels = cells[0].shape[1]
    size = cells[2].shape[0] // 8
    return pl.pallas_call(
        near_last_body,
        out_shape=(
            jax.ShapeDtypeStruct((size, 2 * channels), f32),
            jax.ShapeDtypeStruct((size, 2 * channels), bf16),
            jax.ShapeDtypeStruct(grad_pre.shape, bf16),
        ),
        in_specs=[whole] * 7,
        out_specs=[whole] * 3,
        input_output_aliases={6: 2},
        scratch_shapes=hidden_scratch(2 * size, cells[0].shape[0]),
        compiler_params=params(16),
        cost_estimate=cost(3.0),
        name="near_last",
    )(*inputs)


def norm_back_body(
    turned_ref, other_ref, mine_ref, unit_ref, spread_ref, gain_ref,
    conv_grad_ref, first_ref, last_ref,
):
    total, channels = unit_ref.shape
    half = turned_ref.shape[1] // 2
    core = own_place()[0]
    block = 256
    share = 1.0 / channels
    mine_weight = turned_ref[:, pl.ds(pl.multiple_of(core * half, half), half)]
    other_weight = turned_ref[:, pl.ds(pl.multiple_of((1 - core) * half, half), half)]
    for b in range(total // block):
        at = slice(b * block, (b + 1) * block)
        summed = jnp.dot(mine_weight, mine_ref[:, at], preferred_element_type=f32)
        summed = summed + jnp.dot(other_weight, other_ref[:, at], preferred_element_type=f32)
        grad_normed = summed.astype(bf16).T.astype(f32)
        unit = unit_ref[at, :]
        grad_unit = grad_normed * gain_ref[...]
        mean_grad = jnp.sum(grad_unit, axis=1, keepdims=True) * share
        mean_cross = jnp.sum(grad_unit * unit, axis=1, keepdims=True) * share
        spread = jnp.concatenate([spread_ref[at, :]] * (channels // lanes), axis=1)
        value = (grad_unit - mean_grad - unit * mean_cross) * spread
        conv_grad_ref[b * 8 : (b + 1) * 8] = value.reshape(block // side, side, channels)
    for j in range(reach):
        first_ref[j] = conv_grad_ref[:, j, :].astype(bf16)
        last_ref[j] = conv_grad_ref[:, side - reach + j, :].astype(bf16)


def norm_back(turned, other, mine, unit, spread, gain):
    total, channels = unit.shape
    shape = jax.ShapeDtypeStruct((reach, side, channels), bf16)
    found, first, last = pl.pallas_call(
        norm_back_body,
        out_shape=(jax.ShapeDtypeStruct((side, side, channels), f32), shape, shape),
        in_specs=[whole] * 6,
        out_specs=[whole] * 3,
        compiler_params=params(14),
        cost_estimate=cost(0.2),
        name="norm_back",
    )(turned, other, mine, unit, spread, gain)
    return found.reshape(total, channels), first, last


def finish_inner_body(
    counts_ref, conv0_ref, conv1_ref, conv2_ref, kernel_ref, left_ref, right_ref, grad_ref,
    out_ref, cols_sum, done, sems,
):
    conv_refs = (conv0_ref, conv1_ref, conv2_ref)
    add_cols(True, kernel_ref, left_ref, right_ref, cols_sum)
    bounds = [reach, 9, 16, 23, side - reach]
    copies = []
    for n, (low, high) in enumerate(zip(bounds[:-1], bounds[1:])):
        for i in range(low, high):
            at = slice(i * side, (i + 1) * side)
            value = edged_row(i, conv_rows(conv_refs, at), cols_sum)
            done[at, :] = value + masked_row(i, grad_ref[at, :], counts_ref)
        part = pl.ds(low * side, (high - low) * side)
        copies.append(pltpu.make_async_copy(done.at[part, :], out_ref.at[part, :], sems.at[n]))
        copies[-1].start()
    for copy in copies:
        copy.wait()


def finish_inner(counts, conv, kernel, left, right, grad):
    total, channels = grad.shape
    return pl.pallas_call(
        finish_inner_body,
        out_shape=(
            jax.ShapeDtypeStruct((total, channels), f32),
            jax.ShapeDtypeStruct((2 * reach, side, channels), f32),
        ),
        in_specs=[pl.BlockSpec(memory_space=pltpu.SMEM)] + [whole] * 7,
        out_specs=[pl.BlockSpec(memory_space=pltpu.HBM), whole],
        scratch_shapes=[pltpu.VMEM((total, channels), f32), pltpu.SemaphoreType.DMA((4,))],
        compiler_params=params(12),
        cost_estimate=cost(2.2),
        name="finish_inner",
    )(counts, *conv, kernel, left, right, grad)


def finish_outer_body(
    counts_ref, conv0_ref, conv1_ref, conv2_ref, kernel_ref, top_ref, bottom_ref, cols_ref,
    grad_ref, _, out_ref, rows_sum, done, sems,
):
    conv_refs = (conv0_ref, conv1_ref, conv2_ref)
    add_rows(True, kernel_ref, top_ref, bottom_ref, rows_sum)
    copies = []
    for n, start in enumerate((0, side - reach)):
        for r in range(reach):
            i = start + r
            at = slice(i * side, (i + 1) * side)
            value = edged_row(i, conv_rows(conv_refs, at), cols_ref) + rows_sum[n * reach + r]
            done[n, r * side : (r + 1) * side, :] = value + masked_row(i, grad_ref[at, :], counts_ref)
        part = pl.ds(start * side, reach * side)
        copies.append(pltpu.make_async_copy(done.at[n], out_ref.at[part, :], sems.at[n]))
        copies[-1].start()
    for copy in copies:
        copy.wait()


def finish_outer(counts, conv, kernel, top, bottom, cols_sum, grad, inner):
    channels = grad.shape[1]
    return pl.pallas_call(
        finish_outer_body,
        out_shape=jax.ShapeDtypeStruct(inner.shape, f32),
        in_specs=[pl.BlockSpec(memory_space=pltpu.SMEM)]
        + [whole] * 8
        + [pl.BlockSpec(memory_space=pltpu.HBM)],
        out_specs=pl.BlockSpec(memory_space=pltpu.HBM),
        input_output_aliases={9: 0},
        scratch_shapes=[
            pltpu.VMEM((2 * reach, side, channels), f32),
            pltpu.VMEM((2, reach * side, channels), f32),
            pltpu.SemaphoreType.DMA((2,)),
        ],
        compiler_params=params(12),
        cost_estimate=cost(1.0),
        name="finish_outer",
    )(counts, *conv, kernel, top, bottom, cols_sum, grad, inner)


def split_four_body(own_ref, first_ref, second_ref, third_ref, kept_ref, *sent_refs):
    size = kept_ref.shape[0]
    place = phase_place(True)
    for step in range(4):
        at = pl.ds(pl.multiple_of(lax.rem(place + step, 4) * size, size), size)
        total = own_ref[at, :]
        for ref in (first_ref, second_ref, third_ref):
            total = total + ref[at, :].astype(f32)
        if step == 0:
            kept_ref[...] = total
        else:
            sent_refs[step - 1][...] = total.astype(bf16)


def split_four(own, parts):
    size, width = own.shape[0] // 4, own.shape[1]
    sent = jax.ShapeDtypeStruct((size, width), bf16)
    return pl.pallas_call(
        split_four_body,
        out_shape=(jax.ShapeDtypeStruct((size, width), f32), sent, sent, sent),
        in_specs=[whole] * 4,
        out_specs=[whole] * 4,
        compiler_params=params(4),
        cost_estimate=cost(0.3),
        name="split_four",
    )(own, *parts)


def split_two_body(own_ref, *refs):
    part_refs, (kept_ref, sent_ref) = refs[:-2], refs[-2:]
    size = kept_ref.shape[0]
    total = own_ref[...]
    for ref in part_refs:
        total = total + ref[...].astype(f32)
    low, high = total[:size], total[size:]
    upper = (own_place()[3] & 1) != 0
    kept_ref[...] = jnp.where(upper, high, low)
    sent_ref[...] = jnp.where(upper, low, high)


def split_two(own, parts):
    shape = jax.ShapeDtypeStruct((own.shape[0] // 2, own.shape[1]), f32)
    return pl.pallas_call(
        split_two_body,
        out_shape=(shape, shape),
        in_specs=[whole] * (1 + len(parts)),
        out_specs=[whole] * 2,
        compiler_params=params(4),
        cost_estimate=cost(0.2),
        name="split_two",
    )(own, *parts)


def split_ring_body(own_ref, first_ref, second_ref, third_ref, kept_ref, *sent_refs):
    size = kept_ref.shape[0]
    total = own_ref[...]
    for ref in (first_ref, second_ref, third_ref):
        total = total + ref[...].astype(f32)
    chunks = [total[c * size : (c + 1) * size] for c in range(4)]
    place = own_place()[3] >> 1
    for step, ref in enumerate((kept_ref, *sent_refs)):
        wanted = (place + step) & 3
        found = chunks[0]
        for c in range(1, 4):
            found = jnp.where(wanted == c, chunks[c], found)
        ref[...] = found.astype(ref.dtype)


def split_ring(own, parts):
    size, width = own.shape[0] // 4, own.shape[1]
    sent = jax.ShapeDtypeStruct((size, width), bf16)
    return pl.pallas_call(
        split_ring_body,
        out_shape=(jax.ShapeDtypeStruct((size, width), f32), sent, sent, sent),
        in_specs=[whole] * 4,
        out_specs=[whole] * 4,
        compiler_params=params(4),
        cost_estimate=cost(0.2),
        name="split_ring",
    )(own, *parts)


def last_sum_body(scale, own_ref, arrived_ref, expand_ref, reduce_ref):
    channels = expand_ref.shape[2]
    total = (own_ref[...] + arrived_ref[...]) * scale
    for r in range(total.shape[0]):
        expand_ref[r] = total[r : r + 1, :channels]
        reduce_ref[r] = total[r : r + 1, channels:]


def last_sum(own, arrived, scale):
    size, width = own.shape
    shape = jax.ShapeDtypeStruct((size, 1, width // 2), f32)
    expand, reduce = pl.pallas_call(
        functools.partial(last_sum_body, scale),
        out_shape=(shape, shape),
        in_specs=[whole] * 2,
        out_specs=[whole] * 2,
        compiler_params=params(4),
        cost_estimate=cost(0.4),
        name="last_sum",
    )(own, arrived)
    return expand.transpose(1, 0, 2), reduce.transpose(1, 0, 2)


every_axis = ("dp", "lat", "lon")


def device_pairs(move):
    def flat(hi, y, core, z, lo):
        return (hi * 8 + y * 2 + core) * 16 + z * 2 + lo

    found = []
    for hi, y, core, z, lo in itertools.product(range(2), range(4), range(2), range(8), range(2)):
        found.append((flat(hi, y, core, z, lo), flat(*move(hi, y, core, z, lo))))
    return found


def plane_pairs(step, first):
    def move(hi, y, core, z, lo):
        if (core == 0) == first:
            return (hi, (y + step) % 4, core, z, lo)
        x = (2 * hi + lo + step) % 4
        return (x // 2, y, core, z, x % 2)

    return device_pairs(move)


def ring_pairs(step):
    return device_pairs(lambda hi, y, core, z, lo: (hi, y, core, (z + 2 * step) % 8, lo))


def last_pairs():
    return device_pairs(lambda hi, y, core, z, lo: (hi, y, core, z ^ 1, lo))


def shifted(axis, step):
    count = lax.axis_size(axis)
    return [(i, (i + step) % count) for i in range(count)]


def lon_halo(first, last):
    left = lax.ppermute(last, "lon", shifted("lon", 1))
    right = lax.ppermute(first, "lon", shifted("lon", -1))
    return left, right


def lat_halo(up, down):
    top = lax.ppermute(down, "lat", shifted("lat", 1))
    bottom = lax.ppermute(up, "lat", shifted("lat", -1))
    return top, bottom


def after(value, *others):
    return lax.optimization_barrier((value, others))[0]


def local(
    state, cotangent, counts, dw_kernel, dw_bias, norm_gain, norm_bias, w_expand, b_expand, w_reduce
):
    channels = state.shape[-1]
    cells = state.reshape(-1, channels)
    grad = cotangent.reshape(-1, channels)
    total = cells.shape[0]
    kernel = dw_kernel.transpose(1, 0, 2)

    first, last = side_cols(cells)
    left, right = lon_halo(first, last)
    grad, w_expand, w_reduce = after((grad, w_expand, w_reduce), first, last)
    rows = mask_rows(counts, grad)
    conv = inner_conv(after(cells, rows), kernel, (0,))
    expand, reduce, expand_t, bias = arrange(w_expand[0], w_reduce[0], b_expand)
    left, right = after((left, right), rows, bias, conv)
    up, down = side_rows(cells, left, right)
    top, bottom = lat_halo(up, down)
    conv += inner_conv(after(cells, up, down), kernel, (1, 2))
    unit, spread, normed = normalise(
        conv, kernel, left, right, top, bottom, dw_bias, norm_gain, norm_bias
    )

    inputs = (normed, rows, expand, reduce, bias)
    sent, far_pre = hidden_far(*inputs)
    arrived = lax.ppermute(sent, "lat", [(i, i ^ 1) for i in range(8)])
    sums, near_pre = near_first(*inputs)
    one, two = near_sends(sums, arrived)
    part_one = lax.ppermute(one, every_axis, plane_pairs(1, True))
    part_two = lax.ppermute(two, every_axis, plane_pairs(2, True))
    own, three, near_pre = near_last(*inputs, arrived, after(near_pre, one, two))
    part_three = lax.ppermute(three, every_axis, plane_pairs(3, True))

    far_pre, part_one = after((far_pre, part_one), three)
    conv_grad, first, last = norm_back(expand_t, far_pre, near_pre, unit, spread, norm_gain)
    last, part_two = after((last, part_two))
    left, right = lon_halo(first, last)
    own, parts = after((own, (part_one, part_two, part_three)), first, last)
    own, *sent = split_four(own, parts)
    parts = [lax.ppermute(sent[i], every_axis, plane_pairs(i + 1, False)) for i in (1, 0, 2)]
    back = back_conv(after(conv_grad, sent), kernel, (0, 1))
    (conv_grad, left, right), parts = after(((conv_grad, left, right), parts), back)
    up, down = side_rows(conv_grad, left, right)

    own, *sent = split_ring(*after((own, parts), up, down))
    parts = [lax.ppermute(sent[i], every_axis, ring_pairs(i + 1)) for i in (1, 0, 2)]
    top, bottom = lat_halo(up, down)
    back += back_conv(after(conv_grad, sent, top, bottom), kernel, (2,))

    inner, cols_sum = finish_inner(counts, back, kernel, left, right, grad)

    own, sent = split_two(*after((own, parts), inner))
    arrived = lax.ppermute(sent, every_axis, last_pairs())
    inner = after(inner, sent)
    gradient = finish_outer(counts, back, kernel, top, bottom, cols_sum, grad, inner)

    cells_all = lax.axis_size("dp") * lax.axis_size("lat") * lax.axis_size("lon") * total
    kept = last_sum(own, arrived, 1.0 / math.sqrt(cells_all))
    return (gradient.reshape(state.shape), *kept)


def solution(mesh):
    in_specs = (
        P("dp", "lat", "lon", None),
        P("dp", "lat", "lon", None),
        P("lat", "lon"),
        P(),
        P(),
        P(),
        P(),
        P(),
        P(),
        P(),
    )
    out_specs = (
        P("dp", "lat", "lon", None),
        P(None, ("dp", "lat", "lon"), None),
        P(None, ("dp", "lat", "lon"), None),
    )
    return jax.shard_map(local, mesh=mesh, in_specs=in_specs, out_specs=out_specs, check_vma=False)
```
